32 devices in a mesh: rows: 8 (over y, x, core), grp: 4 (over z).
Axes of the slice: x: 2, y: 2, z: 4, core: 2. Of those that a mesh axis runs over, the one named last changes fastest.
Arguments:
- single: bfloat16 [768, 384], P('grp'), may hold values from -6 to 6
- pair: bfloat16 [768, 768, 128], P('rows', 'grp'), may hold values from -6 to 6
- chains: int32 [768], replicated, may hold values from 0 to 3, as said below
- noised: bfloat16 [8, 768, 768], P('rows', 'grp'), may hold values from -6 to 6
- w_gamma: bfloat16 [384, 768], replicated, may hold values from -0.3125 to 0.3125
- w_beta: bfloat16 [384, 768], replicated, may hold values from -0.3125 to 0.3125
- w_outgate: bfloat16 [384, 768], replicated, may hold values from -0.3125 to 0.3125
- w_query: bfloat16 [768, 768], replicated, may hold values from -0.21875 to 0.21875
- w_key: bfloat16 [768, 768], replicated, may hold values from -0.21875 to 0.21875
- w_value: bfloat16 [768, 768], replicated, may hold values from -0.21875 to 0.21875
- w_out: bfloat16 [768, 768], replicated, may hold values from -0.21875 to 0.21875
- w_pair: bfloat16 [128, 16], replicated, may hold values from -0.5 to 0.5
- chain_gain: float32 [16], replicated, may hold values from -3 to 6
- cotangent: bfloat16 [8, 768, 768], P('rows', 'grp'), may hold values from -6 to 6
Outputs:
- updated: bfloat16 [8, 768, 768], P('rows', 'grp')
- d_single: float32 [768, 384], P('grp')
- d_pair: bfloat16 [768, 768, 128], P('rows', 'grp')
The draws below stay inside these ranges and needn't reach their ends.
Inputs may be any that keep to these rules, and one draw needn't show every extreme that they name: `chains`: chain numbers never fall along the tokens; each chain has 1 to 384 tokens, one exactly 384.
All inputs are finite; a program needn't handle non-finite values.
Results may differ from the reference program's by a relative error of at most 0.022.
Values may be sent and summed in bfloat16 or wider, within the bound.
No kernel may reach another device: no remote copies, remote signals or barrier semaphores. Data moves between devices by JAX's collectives and lax.ppermute only.
A program may use at most 128 MiB of HBM per device.

```python
import math
import jax
import jax.numpy as jnp
from jax import lax

D = 768
HEADS = 16
CS = 384
CZ = 128
TOKENS = 768
SAMPLES = 8


def chain_numbers(key):
    half_count = TOKENS // 2
    key_first, key_second, key_place = jax.random.split(key, 3)
    first_cut = jax.random.randint(key_first, (), 1, half_count - 1)
    second_cut = jax.random.randint(key_second, (), first_cut + 1, half_count)
    small_lengths = jnp.stack([first_cut, second_cut - first_cut, half_count - second_cut]).astype(jnp.int32)
    big_slot = jax.random.randint(key_place, (), 0, 4)
    slot_index = jnp.arange(4, dtype=jnp.int32)
    pick_index = jnp.clip(jnp.where(slot_index > big_slot, slot_index - 1, slot_index), 0, 2)
    lengths = jnp.where(slot_index == big_slot, half_count, jnp.take(small_lengths, pick_index)).astype(jnp.int32)
    chain_ends = jnp.cumsum(lengths).astype(jnp.int32)
    positions = jnp.arange(TOKENS, dtype=jnp.int32)
    return jnp.sum((positions[:, None] >= chain_ends[None, :3]).astype(jnp.int32), axis=1).astype(jnp.int32)


def draw_chains(key, part):
    numbers = chain_numbers(key)
    return numbers.astype(jnp.int32)


def draw_pair(key, part):
    key = jax.random.fold_in(key, 11)
    key_normal = jax.random.fold_in(key, 0)
    values = jax.random.normal(key_normal, (TOKENS, TOKENS, CZ), jnp.float32)
    return jnp.clip(values, -6.0, 6.0).astype(jnp.bfloat16)


def draw_chain_gain(key, part):
    key = jax.random.fold_in(key, 13)
    gains = jnp.clip(jax.random.normal(key, (HEADS,), jnp.float32), -3.0, 3.0)
    return gains.astype(jnp.float32)


def steps_of(stream_key, extent, cuts, least, high):
    level = 1.0
    for position, blocks in cuts:
        draws = jax.random.uniform(jax.random.fold_in(jax.random.fold_in(stream_key, 6), position), (blocks,), jnp.float32, least / len(cuts), high / len(cuts))
        level = level * jnp.repeat(jnp.exp(draws), extent[position] // blocks).reshape((-1,) + (1,) * (len(extent) - 1 - position))
    return level


def bell_draw(own_key, dims, width, bound, shards=(), kind=jnp.bfloat16):
    loudness = steps_of(own_key, dims, shards, -0.22, 0.18) if shards else 1.0
    drawn = jax.random.normal(own_key, dims, jnp.float32) * width * loudness
    return jnp.minimum(jnp.maximum(drawn, -bound), bound).astype(kind)


def setup_inputs(seed: int = 0) -> dict:
    splits = jax.random.split(jax.random.key(seed), 15)
    return {
        "single": bell_draw(splits[0], (TOKENS, CS), 1.0, 6.0, ((0, 4),)),
        "pair": draw_pair(jax.random.fold_in(splits[14], 71), 0),
        "chains": draw_chains(jax.random.fold_in(splits[14], 71), 0),
        "noised": bell_draw(splits[3], (SAMPLES, TOKENS, D), 1.0, 6.0, ((0, 8), (1, 4))),
        "w_gamma": bell_draw(splits[4], (CS, D), CS ** -0.5, 0.3125),
        "w_beta": bell_draw(splits[5], (CS, D), CS ** -0.5, 0.3125),
        "w_outgate": bell_draw(splits[6], (CS, D), CS ** -0.5, 0.3125),
        "w_query": bell_draw(splits[7], (D, D), D ** -0.5, 0.21875),
        "w_key": bell_draw(splits[8], (D, D), D ** -0.5, 0.21875),
        "w_value": bell_draw(splits[9], (D, D), D ** -0.5, 0.21875),
        "w_out": bell_draw(splits[10], (D, D), D ** -0.5, 0.21875),
        "w_pair": bell_draw(splits[11], (CZ, HEADS), CZ ** -0.5, 0.5),
        "chain_gain": draw_chain_gain(jax.random.fold_in(splits[14], 71), 0),
        "cotangent": bell_draw(splits[13], (SAMPLES, TOKENS, D), 1.0, 6.0, ((0, 8), (1, 4))),
    }


EPSILON = 1e-05

def norm_rows(values):
    center = values - lax.optimization_barrier(jnp.mean(values, axis=-1, keepdims=True))
    inverse = lax.rsqrt(lax.optimization_barrier(jnp.mean(center * center, axis=-1, keepdims=True)) + EPSILON)
    return (center * inverse, inverse)

def norm_back(grad_in, normed, inverse):
    grad_mean = lax.optimization_barrier(jnp.mean(grad_in, axis=-1, keepdims=True))
    cross_mean = lax.optimization_barrier(jnp.mean(grad_in * normed, axis=-1, keepdims=True))
    return inverse * (grad_in - grad_mean - normed * cross_mean)

def matmul(left, right):
    return jnp.dot(left, right, preferred_element_type=jnp.float32)

def reference(single, pair, chains, noised, w_gamma, w_beta, w_outgate, w_query, w_key, w_value, w_out, w_pair, chain_gain, cotangent):
    head_size = D // HEADS
    score_scale = 1.0 / math.sqrt(head_size)
    single_norm, single_inv = norm_rows(single.astype(jnp.float32))
    single_b = single_norm.astype(jnp.bfloat16)
    cond_gamma = jax.nn.sigmoid(matmul(single_b, w_gamma))
    cond_beta = matmul(single_b, w_beta)
    out_gate = jax.nn.sigmoid(matmul(single_b, w_outgate))

    def project_row(pair_row):
        normed, inverse_row = norm_rows(pair_row.astype(jnp.float32))
        return matmul(normed.astype(jnp.bfloat16), w_pair)
    projected = lax.map(project_row, pair)
    same_chain = (chains[:, None] == chains[None, :]).astype(jnp.float32)
    bias = (jnp.transpose(projected, (2, 0, 1)) + chain_gain[:, None, None] * same_chain[None]).astype(jnp.bfloat16)
    bias_f = bias.astype(jnp.float32)

    def sample_step(carry, inputs):
        bias_sum, gamma_sum, beta_sum, gate_sum = carry
        sample_in, sample_grad = inputs
        noised_f = sample_in.astype(jnp.float32)
        noised_norm, noised_inv = norm_rows(noised_f)
        x_b = (noised_norm * cond_gamma + cond_beta).astype(jnp.bfloat16)
        queries = matmul(x_b, w_query).astype(jnp.bfloat16)
        keys = matmul(x_b, w_key).astype(jnp.bfloat16)
        values = matmul(x_b, w_value).astype(jnp.bfloat16)
        query_heads = queries.reshape(TOKENS, HEADS, head_size).astype(jnp.float32)
        key_heads = keys.reshape(TOKENS, HEADS, head_size).astype(jnp.float32)
        value_heads = values.reshape(TOKENS, HEADS, head_size).astype(jnp.float32)
        scores = jnp.einsum('ihe,jhe->hij', query_heads, key_heads) * score_scale + bias_f
        exp_scores = jnp.exp(scores)
        attn_prob = exp_scores / lax.optimization_barrier(jnp.sum(exp_scores, axis=-1, keepdims=True))
        prob_b = attn_prob.astype(jnp.bfloat16)
        attended = jnp.einsum('hij,jhe->ihe', prob_b.astype(jnp.float32), value_heads).reshape(TOKENS, D).astype(jnp.bfloat16)
        block_update = matmul(attended, w_out)
        updated = (noised_f + out_gate * block_update).astype(jnp.bfloat16)
        grad_out = sample_grad.astype(jnp.float32)
        gate_part = grad_out * block_update
        grad_update = (grad_out * out_gate).astype(jnp.bfloat16)
        grad_attn = matmul(grad_update, w_out.T).astype(jnp.bfloat16)
        grad_heads = grad_attn.reshape(TOKENS, HEADS, head_size).astype(jnp.float32)
        grad_prob = jnp.einsum('ihe,jhe->hij', grad_heads, value_heads)
        row_delta = lax.optimization_barrier(jnp.sum(attn_prob * grad_prob, axis=-1, keepdims=True))
        grad_score = attn_prob * (grad_prob - row_delta)
        score_b = grad_score.astype(jnp.bfloat16).astype(jnp.float32)
        grad_query = (jnp.einsum('hij,jhe->ihe', score_b, key_heads) * score_scale).reshape(TOKENS, D).astype(jnp.bfloat16)
        grad_key = (jnp.einsum('hij,ihe->jhe', score_b, query_heads) * score_scale).reshape(TOKENS, D).astype(jnp.bfloat16)
        grad_value = jnp.einsum('hij,ihe->jhe', prob_b.astype(jnp.float32), grad_heads).reshape(TOKENS, D).astype(jnp.bfloat16)
        grad_input = matmul(grad_query, w_query.T) + matmul(grad_key, w_key.T) + matmul(grad_value, w_value.T)
        new_carry = (bias_sum + score_b, gamma_sum + grad_input * noised_norm, beta_sum + grad_input, gate_sum + gate_part)
        return (new_carry, updated)
    start = (jnp.zeros((HEADS, TOKENS, TOKENS), jnp.float32), jnp.zeros((TOKENS, D), jnp.float32), jnp.zeros((TOKENS, D), jnp.float32), jnp.zeros((TOKENS, D), jnp.float32))
    finals, updated = lax.scan(sample_step, start, (noised, cotangent))
    bias_sum, gamma_sum, beta_sum, gate_sum = finals
    pre_gamma = (gamma_sum * cond_gamma * (1.0 - cond_gamma)).astype(jnp.bfloat16)
    pre_gate = (gate_sum * out_gate * (1.0 - out_gate)).astype(jnp.bfloat16)
    grad_snorm = matmul(pre_gamma, w_gamma.T) + matmul(beta_sum.astype(jnp.bfloat16), w_beta.T) + matmul(pre_gate, w_outgate.T)
    d_single = norm_back(grad_snorm, single_norm, single_inv)
    bias_grad = jnp.transpose((bias_sum * TOKENS).astype(jnp.bfloat16), (1, 2, 0))

    def pair_row_back(inputs):
        pair_row, grad_row = inputs
        normed, inverse_row = norm_rows(pair_row.astype(jnp.float32))
        grad_pairn = matmul(grad_row, w_pair.T)
        return norm_back(grad_pairn, normed, inverse_row).astype(jnp.bfloat16)
    d_pair = lax.map(pair_row_back, (pair, bias_grad))
    return (updated, d_single, d_pair)
```

```python
import functools
import math

import jax
import jax.numpy as jnp
from jax import lax
from jax.experimental import pallas as pl
from jax.experimental.pallas import tpu as pltpu
from jax.sharding import PartitionSpec as P

EPSILON = 1e-05
BF16 = jnp.bfloat16
F32 = jnp.float32
VMEM_LIMIT = 56 * 1024 * 1024


def norm_rows(values):
    center = values - jnp.mean(values, axis=-1, keepdims=True)
    inverse = lax.rsqrt(jnp.mean(center * center, axis=-1, keepdims=True) + EPSILON)
    return (center * inverse, inverse)


def norm_back(grad_in, normed, inverse):
    grad_mean = jnp.mean(grad_in, axis=-1, keepdims=True)
    cross_mean = jnp.mean(grad_in * normed, axis=-1, keepdims=True)
    return inverse * (grad_in - grad_mean - normed * cross_mean)


def mm(left, right):
    return lax.dot_general(left, right, (((1,), (0,)), ((), ())), preferred_element_type=F32)


def mm_nt(left, right):
    return lax.dot_general(left, right, (((1,), (1,)), ((), ())), preferred_element_type=F32)


def mm_tn(left, right):
    return lax.dot_general(left, right, (((0,), (0,)), ((), ())), preferred_element_type=F32)


def sigmoid(values):
    return 1.0 / (1.0 + jnp.exp(-values))


def params():
    return pltpu.CompilerParams(vmem_limit_bytes=VMEM_LIMIT)


def project_kernel(
    single_ref,
    noised_ref,
    cot_ref,
    w_gamma_ref,
    w_beta_ref,
    w_outgate_ref,
    w_query_ref,
    w_key_ref,
    w_value_ref,
    w_out_ref,
    send_ref,
    gamma_ref,
    gate_ref,
):
    groups, _, width = send_ref.shape
    part = width // 4
    single_norm, _ = norm_rows(single_ref[...].astype(F32))
    single_b = single_norm.astype(BF16)
    cond_gamma = sigmoid(mm(single_b, w_gamma_ref[...]))
    gamma_ref[...] = cond_gamma
    out_gate = sigmoid(mm(single_b, w_outgate_ref[...]))
    gate_ref[...] = out_gate
    cond_beta = mm(single_b, w_beta_ref[...])
    noised_norm, _ = norm_rows(noised_ref[...].astype(F32))
    x_b = (noised_norm * cond_gamma + cond_beta).astype(BF16)

    def put(slot, values):
        rounded = values.astype(BF16)
        for group in range(groups):
            send_ref[group, :, slot * part : (slot + 1) * part] = rounded[
                :, group * part : (group + 1) * part
            ]

    put(0, mm(x_b, w_query_ref[...]))
    put(1, mm(x_b, w_key_ref[...]))
    put(2, mm(x_b, w_value_ref[...]))
    grad_update = (cot_ref[...].astype(F32) * out_gate).astype(BF16)
    put(3, mm_nt(grad_update, w_out_ref[...]))


def pair_norm(block, ones):
    center = block.astype(F32) - mm(block, ones)
    square = (center * center).astype(BF16)
    inverse = lax.rsqrt(mm(square, ones) + EPSILON)
    return center * inverse, inverse


def lane_tiles(cols):
    return [(tile, tile * 128, min(cols, tile * 128 + 128)) for tile in range(-(-cols // 128))]


def bias_kernel(gain_ref, pair_ref, w_pair_ref, rows_ref, cols_ref, bias_ref, flat_ref):
    _, step, cols, channels = pair_ref.shape
    heads = gain_ref.shape[0]
    groups, per_group = bias_ref.shape[:2]
    ones = jnp.full((channels, channels), 1.0 / channels, BF16)
    weight = w_pair_ref[...]
    chain_cols = cols_ref[...]
    for half in range(2):

        def one_row(row, carry):
            normed, _ = pair_norm(pair_ref[half, row], ones)
            values = mm_nt(weight, normed.astype(BF16))
            for tile, start, end in lane_tiles(cols):
                piece = values[:, start:end]
                if end - start < 128:
                    blank = jnp.zeros((heads, 128 - end + start), F32)
                    piece = jnp.concatenate([piece, blank], axis=1)
                flat_ref[tile, pl.ds(row, heads, stride=step), :] = piece
            return carry

        lax.fori_loop(0, step, one_row, 0, unroll=4)
        same = (rows_ref[half] == chain_cols).astype(F32)
        for head in range(heads):
            values = jnp.concatenate(
                [
                    flat_ref[tile, head * step : (head + 1) * step, : end - start]
                    for tile, start, end in lane_tiles(cols)
                ],
                axis=1,
            )
            values = values + gain_ref[head] * same
            bias_ref[head // per_group, head % per_group, :, half * cols : (half + 1) * cols] = (
                values.astype(BF16)
            )


def pair_bias(pair, w_pair, chain_gain, chain_rows, chain_cols, groups):
    rows, cols, channels = pair.shape
    heads = w_pair.shape[1]
    half = rows // 2
    step = 16
    return pl.pallas_call(
        bias_kernel,
        grid=(half // step,),
        in_specs=[
            pl.BlockSpec(memory_space=pltpu.SMEM),
            pl.BlockSpec((2, step, cols, channels), lambda t: (0, t, 0, 0)),
            pl.BlockSpec((heads, channels), lambda t: (0, 0)),
            pl.BlockSpec((2, step, 1), lambda t: (0, t, 0)),
            pl.BlockSpec((1, cols), lambda t: (0, 0)),
        ],
        out_specs=pl.BlockSpec(
            (groups, heads // groups, step, 2 * cols), lambda t: (0, 0, t, 0)
        ),
        out_shape=jax.ShapeDtypeStruct((groups, heads // groups, half, 2 * cols), BF16),
        scratch_shapes=[pltpu.VMEM((-(-cols // 128), heads * step, 128), F32)],
        compiler_params=params(),
    )(
        chain_gain,
        pair.reshape(2, half, cols, channels),
        w_pair.T,
        chain_rows.reshape(2, half, 1),
        chain_cols.reshape(1, cols),
    )


def pair_back_kernel(pair_ref, grad_ref, w_pair_ref, out_ref, flat_ref, *, factor):
    _, step, cols, channels = pair_ref.shape
    groups, per_group = grad_ref.shape[:2]
    heads = groups * per_group
    ones = jnp.full((channels, channels), 1.0 / channels, BF16)
    weight = w_pair_ref[...].astype(F32)
    weight = weight - jnp.mean(weight, axis=-1, keepdims=True)
    high = weight.astype(BF16)
    low = (weight - high.astype(F32)).astype(BF16)
    weights = jnp.concatenate([high, low], axis=0)
    for half in range(2):
        for head in range(heads):
            values = grad_ref[
                head // per_group, head % per_group, :, half * cols : (half + 1) * cols
            ].astype(F32)
            for tile, start, end in lane_tiles(cols):
                flat_ref[tile, head * step : (head + 1) * step, : end - start] = values[
                    :, start:end
                ]

        def one_row(row, carry):
            normed, inverse = pair_norm(pair_ref[half, row], ones)
            grads = jnp.concatenate(
                [
                    flat_ref[tile, pl.ds(row, heads, stride=step), :][:, : end - start]
                    for tile, start, end in lane_tiles(cols)
                ],
                axis=1,
            )
            grads = jnp.concatenate([grads, grads], axis=0).astype(BF16)
            grad_pair = mm_tn(grads, weights)
            cross = mm((grad_pair * normed).astype(BF16), ones)
            out_ref[half, row] = (
                (factor * inverse) * (grad_pair - normed * cross)
            ).astype(BF16)
            return carry

        lax.fori_loop(0, step, one_row, 0, unroll=4)


def pair_back(pair, grad, w_pair, factor):
    rows, cols, channels = pair.shape
    groups, per_group = grad.shape[:2]
    heads = groups * per_group
    half = rows // 2
    step = 16
    out = pl.pallas_call(
        functools.partial(pair_back_kernel, factor=factor),
        grid=(half // step,),
        in_specs=[
            pl.BlockSpec((2, step, cols, channels), lambda t: (0, t, 0, 0)),
            pl.BlockSpec((groups, per_group, step, 2 * cols), lambda t: (0, 0, t, 0)),
            pl.BlockSpec((heads, channels), lambda t: (0, 0)),
        ],
        out_specs=pl.BlockSpec((2, step, cols, channels), lambda t: (0, t, 0, 0)),
        out_shape=jax.ShapeDtypeStruct((2, half, cols, channels), BF16),
        scratch_shapes=[pltpu.VMEM((-(-cols // 128), heads * step, 128), F32)],
        compiler_params=params(),
    )(pair.reshape(2, half, cols, channels), grad, w_pair.T)
    return out.reshape(rows, cols, channels)


def attention_kernel(
    acts_ref,
    bias_ref,
    out_ref,
    dbias_ref,
    keys_t_ref,
    values_t_ref,
    query_t_ref,
    grads_t_ref,
    bias_full,
    score_full,
    att_sum,
    gq_sum,
    gk_sum,
    gv_sum,
    *,
    head_size,
    row_block,
):
    head = pl.program_id(0)
    heads = pl.num_programs(0)
    groups, cols, width = acts_ref.shape
    tokens = groups * cols
    part = width // 4
    row_parts = bias_ref.shape[0]
    half = bias_ref.shape[3]
    scale = 1.0 / math.sqrt(head_size)
    extra = att_sum.shape[1] - part

    def piece(slot):
        return acts_ref[:, :, slot * part : (slot + 1) * part].reshape(tokens, part)

    @pl.when(head == 0)
    def _():
        query_t_ref[...] = piece(0).T
        keys_t_ref[...] = piece(1).T
        values_t_ref[...] = piece(2).T
        grads_t_ref[...] = piece(3).T
        att_sum[...] = jnp.zeros_like(att_sum)
        gq_sum[...] = jnp.zeros_like(gq_sum)

    for row_part in range(row_parts):
        for group in range(groups):
            for side in range(2):
                top = row_part * 2 * half + side * half
                bias_full[top : top + half, group * cols : (group + 1) * cols] = bias_ref[
                    row_part, group, 0, :, side * cols : (side + 1) * cols
                ]

    lane = lax.broadcasted_iota(jnp.int32, (1, part), 1)
    mine = (lane >= head * head_size) & (lane < (head + 1) * head_size)
    zero = jnp.zeros((), BF16)
    keys_m = jnp.where(mine, piece(1), zero)
    values_m = jnp.concatenate(
        [jnp.where(mine, piece(2), zero), jnp.ones((tokens, extra), BF16)], axis=1
    )
    feature = pl.multiple_of(head * head_size, head_size)
    query_t = query_t_ref[pl.ds(feature, head_size), :]
    grads_t = grads_t_ref[pl.ds(feature, head_size), :]
    gk_t = jnp.zeros((head_size, tokens), F32)
    gv_t = jnp.zeros((head_size, tokens), F32)
    for top in range(0, tokens, row_block):
        rows = slice(top, top + row_block)
        query = jnp.where(mine, piece(0)[rows], zero)
        grads = jnp.where(mine, piece(3)[rows], zero)
        scores = mm(query, keys_t_ref[...]) * scale + bias_full[rows, :].astype(F32)
        weights = jnp.exp(scores)
        attended = mm(weights.astype(BF16), values_m)
        inverse = 1.0 / attended[:, part : part + 1]
        attended = attended[:, :part] * inverse
        att_sum[rows, :part] += attended
        delta = jnp.sum(attended * grads.astype(F32), axis=-1, keepdims=True)
        prob = weights * inverse
        grad_prob = mm(grads, values_t_ref[...])
        score = (prob * (grad_prob - delta)).astype(BF16)
        score_full[rows, :] = score
        gq_sum[rows, :] += mm(score, keys_m)
        gk_t = gk_t + mm(query_t[:, rows], score)
        gv_t = gv_t + mm(grads_t[:, rows], prob.astype(BF16))
    gk_sum[pl.ds(feature, head_size), :] = gk_t
    gv_sum[pl.ds(feature, head_size), :] = gv_t

    for row_part in range(row_parts):
        for group in range(groups):
            for side in range(2):
                top = row_part * 2 * half + side * half
                dbias_ref[row_part, group, 0, :, side * cols : (side + 1) * cols] = score_full[
                    top : top + half, group * cols : (group + 1) * cols
                ]

    @pl.when(head == heads - 1)
    def _():
        results = (
            gq_sum[...] * scale,
            (gk_sum[...] * scale).T,
            gv_sum[...].T,
            att_sum[:, :part],
        )
        for slot, values in enumerate(results):
            out_ref[:, :, slot * part : (slot + 1) * part] = values.astype(BF16).reshape(
                groups, cols, part
            )


def attention(acts, bias, head_size):
    groups, cols, width = acts.shape
    tokens = groups * cols
    part = width // 4
    row_parts, _, heads, half, lanes = bias.shape
    row_block = 256 if tokens % 256 == 0 else cols
    spread = (row_parts, groups, 1, half, lanes)
    padded = (part // 128 + 1) * 128
    return pl.pallas_call(
        functools.partial(attention_kernel, head_size=head_size, row_block=row_block),
        grid=(heads,),
        in_specs=[
            pl.BlockSpec((groups, cols, width), lambda h: (0, 0, 0)),
            pl.BlockSpec(spread, lambda h: (0, 0, h, 0, 0)),
        ],
        out_specs=[
            pl.BlockSpec((groups, cols, width), lambda h: (0, 0, 0)),
            pl.BlockSpec(spread, lambda h: (0, 0, h, 0, 0)),
        ],
        out_shape=[
            jax.ShapeDtypeStruct((groups, cols, width), BF16),
            jax.ShapeDtypeStruct(bias.shape, BF16),
        ],
        scratch_shapes=[
            pltpu.VMEM((part, tokens), BF16),
            pltpu.VMEM((part, tokens), BF16),
            pltpu.VMEM((part, tokens), BF16),
            pltpu.VMEM((part, tokens), BF16),
            pltpu.VMEM((tokens, tokens), BF16),
            pltpu.VMEM((tokens, tokens), BF16),
            pltpu.VMEM((tokens, padded), F32),
            pltpu.VMEM((tokens, part), F32),
            pltpu.VMEM((part, tokens), F32),
            pltpu.VMEM((part, tokens), F32),
        ],
        compiler_params=params(),
    )(acts, bias)


def finish_kernel(
    got_ref,
    single_ref,
    noised_ref,
    cot_ref,
    gamma_ref,
    gate_ref,
    w_gamma_ref,
    w_beta_ref,
    w_outgate_ref,
    w_query_ref,
    w_key_ref,
    w_value_ref,
    w_out_ref,
    updated_ref,
    d_single_ref,
):
    groups, _, width = got_ref.shape
    part = width // 4

    def take(slot):
        return jnp.concatenate(
            [got_ref[group, :, slot * part : (slot + 1) * part] for group in range(groups)], axis=1
        )

    out_gate = gate_ref[...]
    cond_gamma = gamma_ref[...]
    block_update = mm(take(3), w_out_ref[...])
    noised = noised_ref[...].astype(F32)
    updated_ref[...] = (noised + out_gate * block_update).astype(BF16)
    gate_part = cot_ref[...].astype(F32) * block_update
    pre_gate = (gate_part * out_gate * (1.0 - out_gate)).astype(BF16)
    grad_input = mm_nt(take(0), w_query_ref[...])
    grad_input += mm_nt(take(1), w_key_ref[...])
    grad_input += mm_nt(take(2), w_value_ref[...])
    noised_norm, _ = norm_rows(noised)
    pre_gamma = (grad_input * noised_norm * cond_gamma * (1.0 - cond_gamma)).astype(BF16)
    grad_snorm = mm_nt(pre_gamma, w_gamma_ref[...])
    grad_snorm += mm_nt(grad_input.astype(BF16), w_beta_ref[...])
    grad_snorm += mm_nt(pre_gate, w_outgate_ref[...])
    single_norm, single_inv = norm_rows(single_ref[...].astype(F32))
    d_single_ref[...] = norm_back(grad_snorm, single_norm, single_inv)


def split_heads(
    single,
    pair,
    chains,
    noised,
    w_gamma,
    w_beta,
    w_outgate,
    w_query,
    w_key,
    w_value,
    w_out,
    w_pair,
    chain_gain,
    cotangent,
    *,
    groups,
):
    cols, _ = single.shape
    rows = pair.shape[0]
    tokens = chains.shape[0]
    width = noised.shape[2]
    head_size = width // w_pair.shape[1]
    row_index = lax.axis_index("rows")
    group_index = lax.axis_index("grp")
    chain_rows = lax.dynamic_slice_in_dim(chains, row_index * rows, rows)
    chain_cols = lax.dynamic_slice_in_dim(chains, group_index * cols, cols)
    bias_send = pair_bias(pair, w_pair, chain_gain, chain_rows, chain_cols, groups)
    bias_own = lax.all_to_all(bias_send, "grp", 0, 0)
    bias_all = lax.all_gather(bias_own, "rows", axis=0)
    noised = noised[0]
    cotangent = cotangent[0]
    acts_send, cond_gamma, out_gate = pl.pallas_call(
        project_kernel,
        out_shape=[
            jax.ShapeDtypeStruct((groups, cols, 4 * width // groups), BF16),
            jax.ShapeDtypeStruct((cols, width), F32),
            jax.ShapeDtypeStruct((cols, width), F32),
        ],
        compiler_params=params(),
    )(
        single,
        noised,
        cotangent,
        w_gamma,
        w_beta,
        w_outgate,
        w_query,
        w_key,
        w_value,
        w_out,
    )
    acts = lax.all_to_all(acts_send, "grp", 0, 0)
    grads_send, dbias = attention(acts, bias_all, head_size)
    grads = lax.all_to_all(grads_send, "grp", 0, 0)
    dbias_own = lax.psum_scatter(dbias, "rows", scatter_dimension=0, tiled=False)
    dbias_back = lax.all_to_all(dbias_own, "grp", 0, 0)
    updated, d_part = pl.pallas_call(
        finish_kernel,
        out_shape=[
            jax.ShapeDtypeStruct((cols, width), BF16),
            jax.ShapeDtypeStruct(single.shape, F32),
        ],
        compiler_params=params(),
    )(
        grads,
        single,
        noised,
        cotangent,
        cond_gamma,
        out_gate,
        w_gamma,
        w_beta,
        w_outgate,
        w_query,
        w_key,
        w_value,
        w_out,
    )
    d_single = lax.psum(d_part, "rows")
    d_pair = pair_back(pair, dbias_back, w_pair, float(tokens))
    return (updated[None], d_single, d_pair)


def project(acts, weight):
    return jnp.einsum("std,de->ste", acts, weight, preferred_element_type=F32)


def project_back(acts, weight):
    return jnp.einsum("ste,de->std", acts, weight, preferred_element_type=F32)


def split_keys(
    single,
    pair,
    chains,
    noised,
    w_gamma,
    w_beta,
    w_outgate,
    w_query,
    w_key,
    w_value,
    w_out,
    w_pair,
    chain_gain,
    cotangent,
):
    col_count = single.shape[0]
    row_count = pair.shape[0]
    head_count = w_pair.shape[1]
    model_width = w_query.shape[0]
    head_size = model_width // head_count
    sample_count = noised.shape[0]
    token_total = chains.shape[0]
    score_scale = 1.0 / math.sqrt(head_size)
    row_index = lax.axis_index("rows")
    group_index = lax.axis_index("grp")
    chain_rows = lax.dynamic_slice_in_dim(chains, row_index * row_count, row_count)
    chain_cols = lax.dynamic_slice_in_dim(chains, group_index * col_count, col_count)
    pair_norm, pair_inv = norm_rows(pair.astype(jnp.float32))
    projected = jnp.einsum(
        "ijc,ch->hij", pair_norm.astype(jnp.bfloat16), w_pair, preferred_element_type=jnp.float32
    )
    same_chain = (chain_rows[:, None] == chain_cols[None, :]).astype(jnp.float32)
    bias_block = (projected + chain_gain[:, None, None] * same_chain[None]).astype(jnp.bfloat16)
    bias_keys = lax.all_gather(bias_block, "rows", axis=1, tiled=True)
    single_norm, single_inv = norm_rows(single.astype(jnp.float32))
    single_b = single_norm.astype(jnp.bfloat16)
    cond_gamma = jax.nn.sigmoid(jnp.dot(single_b, w_gamma, preferred_element_type=jnp.float32))
    cond_beta = jnp.dot(single_b, w_beta, preferred_element_type=jnp.float32)
    out_gate = jax.nn.sigmoid(jnp.dot(single_b, w_outgate, preferred_element_type=jnp.float32))
    noised_f = noised.astype(jnp.float32)
    noised_norm, noised_inv = norm_rows(noised_f)
    x_b = (noised_norm * cond_gamma[None] + cond_beta[None]).astype(jnp.bfloat16)
    queries = project(x_b, w_query).astype(jnp.bfloat16)
    keys_own = project(x_b, w_key).astype(jnp.bfloat16)
    values_own = project(x_b, w_value).astype(jnp.bfloat16)
    queries_all = lax.all_gather(queries, "grp", axis=1, tiled=True)
    query_heads = queries_all.reshape(sample_count, token_total, head_count, head_size)
    key_heads = keys_own.reshape(sample_count, col_count, head_count, head_size)
    value_heads = values_own.reshape(sample_count, col_count, head_count, head_size)
    scores = (
        jnp.einsum("sihe,sjhe->shij", query_heads, key_heads, preferred_element_type=jnp.float32)
        * score_scale
        + bias_keys.astype(jnp.float32)[None]
    )
    exp_scores = jnp.exp(scores)
    exp_total = lax.psum(jnp.sum(exp_scores, axis=-1).astype(jnp.bfloat16), "grp").astype(
        jnp.float32
    )
    attn_prob = exp_scores / exp_total[..., None]
    prob_b = attn_prob.astype(jnp.bfloat16)
    attended_part = jnp.einsum(
        "shij,sjhe->sihe", prob_b, value_heads, preferred_element_type=jnp.float32
    )
    attended_part = attended_part.reshape(sample_count, token_total, model_width)
    attended = lax.psum_scatter(
        attended_part.astype(jnp.bfloat16), "grp", scatter_dimension=1, tiled=True
    )
    block_update = project(attended, w_out)
    updated = (noised_f + out_gate[None] * block_update).astype(jnp.bfloat16)
    grad_out = cotangent.astype(jnp.float32)
    gate_part = jnp.sum(grad_out * block_update, axis=0)
    grad_update = (grad_out * out_gate[None]).astype(jnp.bfloat16)
    grad_attn = project_back(grad_update, w_out).astype(jnp.bfloat16)
    grads_all = lax.all_gather(grad_attn, "grp", axis=1, tiled=True)
    grad_heads = grads_all.reshape(sample_count, token_total, head_count, head_size)
    grad_prob = jnp.einsum(
        "sihe,sjhe->shij", grad_heads, value_heads, preferred_element_type=jnp.float32
    )
    row_delta = lax.psum(
        jnp.sum(attn_prob * grad_prob, axis=-1).astype(jnp.bfloat16), "grp"
    ).astype(jnp.float32)
    grad_score = attn_prob * (grad_prob - row_delta[..., None])
    score_b = grad_score.astype(jnp.bfloat16)
    query_part = (
        jnp.einsum("shij,sjhe->sihe", score_b, key_heads, preferred_element_type=jnp.float32)
        * score_scale
    )
    query_part = query_part.reshape(sample_count, token_total, model_width)
    grad_query = lax.psum_scatter(
        query_part.astype(jnp.bfloat16), "grp", scatter_dimension=1, tiled=True
    )
    grad_key = (
        jnp.einsum("shij,sihe->sjhe", score_b, query_heads, preferred_element_type=jnp.float32)
        * score_scale
    )
    grad_value = jnp.einsum(
        "shij,sihe->sjhe", prob_b, grad_heads, preferred_element_type=jnp.float32
    )
    grad_key = grad_key.reshape(sample_count, col_count, model_width).astype(jnp.bfloat16)
    grad_value = grad_value.reshape(sample_count, col_count, model_width).astype(jnp.bfloat16)
    grad_input = (
        project_back(grad_query, w_query)
        + project_back(grad_key, w_key)
        + project_back(grad_value, w_value)
    )
    gamma_part = jnp.sum(grad_input * noised_norm, axis=0)
    beta_part = jnp.sum(grad_input, axis=0)
    gamma_sum, beta_sum, gate_sum = lax.psum((gamma_part, beta_part, gate_part), "rows")
    pre_gamma = (gamma_sum * cond_gamma * (1.0 - cond_gamma)).astype(jnp.bfloat16)
    pre_gate = (gate_sum * out_gate * (1.0 - out_gate)).astype(jnp.bfloat16)
    grad_snorm = jnp.dot(pre_gamma, w_gamma.T, preferred_element_type=jnp.float32)
    grad_snorm = grad_snorm + jnp.dot(
        beta_sum.astype(jnp.bfloat16), w_beta.T, preferred_element_type=jnp.float32
    )
    grad_snorm = grad_snorm + jnp.dot(pre_gate, w_outgate.T, preferred_element_type=jnp.float32)
    d_single = norm_back(grad_snorm, single_norm, single_inv)
    bias_part = jnp.sum(score_b, axis=0, dtype=jnp.float32)
    bias_own = lax.psum_scatter(bias_part, "rows", scatter_dimension=1, tiled=True)
    bias_grad = (bias_own * token_total).astype(jnp.bfloat16)
    grad_pairn = jnp.einsum("hij,ch->ijc", bias_grad, w_pair, preferred_element_type=jnp.float32)
    d_pair = norm_back(grad_pairn, pair_norm, pair_inv).astype(jnp.bfloat16)
    return (updated, d_single, d_pair)


def solution(mesh):
    in_specs = (
        P("grp", None),
        P("rows", "grp", None),
        P(),
        P("rows", "grp", None),
        P(),
        P(),
        P(),
        P(),
        P(),
        P(),
        P(),
        P(),
        P(),
        P("rows", "grp", None),
    )
    out_specs = (P("rows", "grp", None), P("grp", None), P("rows", "grp", None))
    groups = mesh.shape["grp"]

    def on_device(*args):
        pair, noised, w_pair = args[1], args[3], args[11]
        fits = (
            pair.shape[0] % 32 == 0
            and noised.shape[0] == 1
            and noised.shape[1] % 64 == 0
            and w_pair.shape[1] % groups == 0
        )
        if fits:
            return split_heads(*args, groups=groups)
        return split_keys(*args)

    return jax.shard_map(
        on_device, mesh=mesh, in_specs=in_specs, out_specs=out_specs, check_vma=False
    )
```

```python
import functools
import math

import jax
import jax.numpy as jnp
from jax import lax
from jax.experimental import pallas as pl
from jax.experimental.pallas import tpu as pltpu
from jax.sharding import PartitionSpec as P

EPSILON = 1e-05
BF16 = jnp.bfloat16
F32 = jnp.float32
VMEM_LIMIT = 56 * 1024 * 1024


def norm_rows(values):
    center = values - jnp.mean(values, axis=-1, keepdims=True)
    inverse = lax.rsqrt(jnp.mean(center * center, axis=-1, keepdims=True) + EPSILON)
    return (center * inverse, inverse)


def norm_back(grad_in, normed, inverse):
    grad_mean = jnp.mean(grad_in, axis=-1, keepdims=True)
    cross_mean = jnp.mean(grad_in * normed, axis=-1, keepdims=True)
    return inverse * (grad_in - grad_mean - normed * cross_mean)


def mm(left, right):
    return lax.dot_general(left, right, (((1,), (0,)), ((), ())), preferred_element_type=F32)


def mm_nt(left, right):
    return lax.dot_general(left, right, (((1,), (1,)), ((), ())), preferred_element_type=F32)


def mm_tn(left, right):
    return lax.dot_general(left, right, (((0,), (0,)), ((), ())), preferred_element_type=F32)


def sigmoid(values):
    return 1.0 / (1.0 + jnp.exp(-values))


def params():
    return pltpu.CompilerParams(vmem_limit_bytes=VMEM_LIMIT)


def smem():
    return pl.BlockSpec(memory_space=pltpu.SMEM)


def vmem():
    return pl.BlockSpec(memory_space=pltpu.VMEM)


def project_kernel(
    group_ref,
    single_ref,
    noised_ref,
    cot_ref,
    w_gamma_ref,
    w_beta_ref,
    w_outgate_ref,
    w_query_ref,
    w_key_ref,
    w_value_ref,
    w_out_ref,
    *rest,
    groups,
):
    send_refs = rest[:groups]
    gamma_ref, gate_ref, stage_ref = rest[groups:]
    width = stage_ref.shape[2]
    part = width // 4
    group_own = group_ref[0]
    single_norm, _ = norm_rows(single_ref[...].astype(F32))
    single_b = single_norm.astype(BF16)
    cond_gamma = sigmoid(mm(single_b, w_gamma_ref[...]))
    gamma_ref[...] = cond_gamma
    out_gate = sigmoid(mm(single_b, w_outgate_ref[...]))
    gate_ref[...] = out_gate
    cond_beta = mm(single_b, w_beta_ref[...])
    noised_norm, _ = norm_rows(noised_ref[...].astype(F32))
    x_b = (noised_norm * cond_gamma + cond_beta).astype(BF16)

    def put(kind, values):
        rounded = values.astype(BF16)
        for group in range(groups):
            slot = lax.rem(group - group_own + groups, groups)
            stage_ref[slot, :, kind * part : (kind + 1) * part] = rounded[
                :, group * part : (group + 1) * part
            ]

    put(0, mm(x_b, w_query_ref[...]))
    put(1, mm(x_b, w_key_ref[...]))
    put(2, mm(x_b, w_value_ref[...]))
    grad_update = (cot_ref[...].astype(F32) * out_gate).astype(BF16)
    put(3, mm_nt(grad_update, w_out_ref[...]))
    for slot in range(groups):
        send_refs[slot][...] = stage_ref[slot]


def lane_tiles(cols):
    return [(tile, tile * 128, min(cols, tile * 128 + 128)) for tile in range(-(-cols // 128))]


def mean_matrix(channels):
    first = lax.broadcasted_iota(jnp.int32, (2 * channels, 2 * channels), 0) >= channels
    second = lax.broadcasted_iota(jnp.int32, (2 * channels, 2 * channels), 1) >= channels
    return jnp.where(first == second, 1.0 / channels, 0.0).astype(BF16)


def center_rows(pair_ref, first, batch, means):
    _, _, cols, channels = pair_ref.shape
    both = jnp.concatenate(
        [pair_ref[side, pl.ds(first, batch)].reshape(batch * cols, channels) for side in range(2)],
        axis=1,
    )
    return both.astype(F32) - mm(both, means)


def bias_kernel(
    group_ref,
    rows_ref,
    chains_ref,
    gain_ref,
    pair_ref,
    w_pair_ref,
    cols_ref,
    *rest,
    groups,
    batch,
):
    send_refs = rest[:groups]
    stats_ref, flat_ref, gains_ref, stage_ref = rest[groups:]
    _, step, cols, channels = pair_ref.shape
    heads = gain_ref.shape[0]
    per_group = heads // groups
    half = step * pl.num_programs(0)
    group_own = group_ref[0]
    row_base = rows_ref[0] * 2 * half + pl.program_id(0) * step
    means = mean_matrix(channels)
    weight = w_pair_ref[...].astype(F32).T.astype(BF16)
    left = jnp.concatenate(
        [
            jnp.concatenate([weight, jnp.zeros((heads, channels), BF16)], axis=1),
            jnp.concatenate(
                [
                    jnp.zeros((heads, channels), BF16),
                    jnp.full((heads, channels), 1.0 / channels, BF16),
                ],
                axis=1,
            ),
        ],
        axis=0,
    )
    chain_cols = cols_ref[pl.ds(group_own, 1), :]
    for head in range(heads):
        gains_ref[head : head + 1, :] = jnp.full((1, cols), gain_ref[head], F32)

    def some_rows(index, carry):
        first = index * batch
        center = center_rows(pair_ref, first, batch, means)
        center_b = center.astype(BF16)
        square = (center * center).astype(BF16)
        for inner in range(batch):
            rows = slice(inner * cols, (inner + 1) * cols)
            for side in range(2):
                lanes = slice(side * channels, (side + 1) * channels)
                right = jnp.concatenate([center_b[rows, lanes], square[rows, lanes]], axis=1)
                sums = mm_nt(left, right)
                inverse = lax.rsqrt(sums[heads : heads + 8] + EPSILON)
                projected = sums[:heads] * inverse[:1]
                stats_ref[side, first + inner, :heads, :] = projected
                stats_ref[side, first + inner, heads:, :] = inverse
                chain = chains_ref[row_base + side * half + first + inner]
                same = (chain_cols == chain).astype(F32)
                values = projected + gains_ref[...] * same
                for tile, start, end in lane_tiles(cols):
                    piece = values[:, start:end]
                    if end - start < 128:
                        blank = jnp.zeros((heads, 128 - end + start), F32)
                        piece = jnp.concatenate([piece, blank], axis=1)
                    flat_ref[side, tile, pl.ds(first + inner, heads, stride=step), :] = piece
        return carry

    lax.fori_loop(0, step // batch, some_rows, 0)
    for head in range(heads):
        slot = lax.rem(head // per_group - group_own + groups, groups)
        values = jnp.concatenate(
            [
                flat_ref[side, tile, head * step : (head + 1) * step, : end - start]
                for side in range(2)
                for tile, start, end in lane_tiles(cols)
            ],
            axis=1,
        )
        stage_ref[slot, head % per_group] = values.astype(BF16)
    for slot in range(groups):
        send_refs[slot][...] = stage_ref[slot]


def pair_bias(pair, w_pair, chain_gain, chains, group_index, row_index, groups):
    rows, cols, channels = pair.shape
    heads = w_pair.shape[1]
    per_group = heads // groups
    half = rows // 2
    step = 16
    tiles = -(-cols // 128)
    *sends, stats = pl.pallas_call(
        functools.partial(bias_kernel, groups=groups, batch=4),
        grid=(half // step,),
        in_specs=[
            smem(),
            smem(),
            smem(),
            smem(),
            pl.BlockSpec((2, step, cols, channels), lambda t: (0, t, 0, 0)),
            pl.BlockSpec((channels, heads), lambda t: (0, 0)),
            pl.BlockSpec((groups, cols), lambda t: (0, 0)),
        ],
        out_specs=[
            pl.BlockSpec((per_group, step, 2 * cols), lambda t: (0, t, 0)) for _ in range(groups)
        ]
        + [pl.BlockSpec((2, step, heads + 8, cols), lambda t: (0, t, 0, 0))],
        out_shape=[
            jax.ShapeDtypeStruct((per_group, half, 2 * cols), BF16) for _ in range(groups)
        ]
        + [jax.ShapeDtypeStruct((2, half, heads + 8, cols), F32)],
        scratch_shapes=[
            pltpu.VMEM((2, tiles, heads * step, 128), F32),
            pltpu.VMEM((heads, cols), F32),
            pltpu.VMEM((groups, per_group, step, 2 * cols), BF16),
        ],
        compiler_params=params(),
    )(
        group_index,
        row_index,
        chains,
        chain_gain,
        pair.reshape(2, half, cols, channels),
        w_pair,
        chains.reshape(groups, cols),
    )
    return sends, stats


def pair_back_kernel(group_ref, pair_ref, stats_ref, w_pair_ref, *rest, groups, factor, batch):
    grad_refs = rest[:groups]
    out_ref, flat_ref = rest[groups:]
    _, step, cols, channels = pair_ref.shape
    per_group = grad_refs[0].shape[0]
    heads = groups * per_group
    group_own = group_ref[0]
    means = mean_matrix(channels)
    weight = w_pair_ref[...].astype(F32).T
    weight = weight - jnp.mean(weight, axis=-1, keepdims=True)
    high = weight.astype(BF16)
    low = (weight - high.astype(F32)).astype(BF16)
    weights = jnp.concatenate([high, low, jnp.zeros((16, channels), BF16)], axis=0)
    spread = lax.broadcasted_iota(jnp.int32, (2 * heads + 16, channels), 0)
    spread = ((spread >= 2 * heads) & (spread < 2 * heads + 2)).astype(F32).astype(BF16)
    weights = jnp.concatenate([weights, spread], axis=1)
    blank = jnp.zeros((14, cols), F32)
    for slot in range(groups):
        source = lax.rem(group_own + slot, groups)
        for head in range(per_group):
            values = grad_refs[slot][head].astype(F32)
            top = pl.multiple_of((source * per_group + head) * step, step)
            for side in range(2):
                for tile, start, end in lane_tiles(cols):
                    flat_ref[side, tile, pl.ds(top, step), : end - start] = values[
                        :, side * cols + start : side * cols + end
                    ]

    def some_rows(index, carry):
        first = index * batch
        center = center_rows(pair_ref, first, batch, means)
        for side in range(2):
            lefts = []
            for inner in range(batch):
                grads = jnp.concatenate(
                    [
                        flat_ref[side, tile, pl.ds(first + inner, heads, stride=step), :][
                            :, : end - start
                        ]
                        for tile, start, end in lane_tiles(cols)
                    ],
                    axis=1,
                )
                projected = stats_ref[side, first + inner, :heads, :]
                inverse = stats_ref[side, first + inner, heads : heads + 1, :]
                cross = jnp.sum(grads * projected, axis=0, keepdims=True) * (1.0 / channels)
                scaled = grads * (inverse * factor)
                cross = cross * (inverse * inverse * factor)
                cross_high = cross.astype(BF16).astype(F32)
                lefts.append(
                    jnp.concatenate(
                        [scaled, scaled, cross_high, cross - cross_high, blank], axis=0
                    )
                )
            for inner in range(batch):
                rows = slice(inner * cols, (inner + 1) * cols)
                lanes = slice(side * channels, (side + 1) * channels)
                both = mm_tn(lefts[inner].astype(BF16), weights)
                out_ref[side, first + inner] = (
                    both[:, :channels] - center[rows, lanes] * both[:, channels:]
                ).astype(BF16)
        return carry

    lax.fori_loop(0, step // batch, some_rows, 0)


def pair_back(pair, stats, grads, w_pair, group_index, factor):
    rows, cols, channels = pair.shape
    groups = len(grads)
    per_group = grads[0].shape[0]
    heads = groups * per_group
    half = rows // 2
    step = 16
    tiles = -(-cols // 128)
    out = pl.pallas_call(
        functools.partial(pair_back_kernel, groups=groups, factor=factor, batch=4),
        grid=(half // step,),
        in_specs=[
            smem(),
            pl.BlockSpec((2, step, cols, channels), lambda t: (0, t, 0, 0)),
            pl.BlockSpec((2, step, heads + 8, cols), lambda t: (0, t, 0, 0)),
            pl.BlockSpec((channels, heads), lambda t: (0, 0)),
        ]
        + [pl.BlockSpec((per_group, step, 2 * cols), lambda t: (0, t, 0)) for _ in range(groups)],
        out_specs=pl.BlockSpec((2, step, cols, channels), lambda t: (0, t, 0, 0)),
        out_shape=jax.ShapeDtypeStruct((2, half, cols, channels), BF16),
        scratch_shapes=[pltpu.VMEM((2, tiles, heads * step, 128), F32)],
        compiler_params=params(),
    )(group_index, pair.reshape(2, half, cols, channels), stats, w_pair, *grads)
    return out.reshape(rows, cols, channels)


def attention_kernel(group_ref, bias_ref, *rest, groups, head_size, row_block):
    acts_refs = rest[:groups]
    out_refs = rest[groups : 2 * groups]
    (
        dbias_ref,
        query_ref,
        keys_ref,
        values_ref,
        grads_ref,
        query_t_ref,
        keys_t_ref,
        values_t_ref,
        grads_t_ref,
        bias_full,
        score_full,
        att_sum,
        gq_sum,
        gk_sum,
        gv_sum,
    ) = rest[2 * groups :]
    head = pl.program_id(0)
    heads = pl.num_programs(0)
    group_own = group_ref[0]
    cols, width = acts_refs[0].shape
    tokens = groups * cols
    part = width // 4
    row_parts = bias_ref.shape[0]
    half = bias_ref.shape[3]
    scale = 1.0 / math.sqrt(head_size)
    extra = att_sum.shape[1] - part
    plain = (query_ref, keys_ref, values_ref, grads_ref)
    turned = (query_t_ref, keys_t_ref, values_t_ref, grads_t_ref)

    @pl.when(head == 0)
    def _():
        for kind in range(4):
            for slot in range(groups):
                plain[kind][slot * cols : (slot + 1) * cols, :] = acts_refs[slot][
                    :, kind * part : (kind + 1) * part
                ]
            turned[kind][...] = plain[kind][...].T
        att_sum[...] = jnp.zeros_like(att_sum)
        gq_sum[...] = jnp.zeros_like(gq_sum)

    def places():
        for row_part in range(row_parts):
            owner, inside = divmod(row_part * 2 * half, cols)
            slot = lax.rem(group_own - owner + groups, groups)
            for side in range(2):
                top = pl.multiple_of(slot * cols + inside + side * half, 16)
                for column in range(groups):
                    yield row_part, column, side, pl.ds(top, half)

    for row_part, column, side, rows in places():
        bias_full[rows, column * cols : (column + 1) * cols] = bias_ref[
            row_part, column, 0, :, side * cols : (side + 1) * cols
        ]

    lane = lax.broadcasted_iota(jnp.int32, (1, part), 1)
    mine = (lane >= head * head_size) & (lane < (head + 1) * head_size)
    zero = jnp.zeros((), BF16)
    keys_m = jnp.where(mine, keys_ref[...], zero)
    values_m = jnp.concatenate(
        [jnp.where(mine, values_ref[...], zero), jnp.ones((tokens, extra), BF16)], axis=1
    )
    feature = pl.multiple_of(head * head_size, head_size)
    query_t = query_t_ref[pl.ds(feature, head_size), :]
    grads_t = grads_t_ref[pl.ds(feature, head_size), :]
    gk_t = jnp.zeros((head_size, tokens), F32)
    gv_t = jnp.zeros((head_size, tokens), F32)
    for top in range(0, tokens, row_block):
        rows = slice(top, top + row_block)
        query = jnp.where(mine, query_ref[rows, :], zero)
        grads = jnp.where(mine, grads_ref[rows, :], zero)
        scores = mm(query, keys_t_ref[...]) * scale + bias_full[rows, :].astype(F32)
        weights = jnp.exp(scores)
        attended = mm(weights.astype(BF16), values_m)
        inverse = 1.0 / attended[:, part : part + 1]
        attended = attended[:, :part] * inverse
        att_sum[rows, :part] += attended
        delta = jnp.sum(attended * grads.astype(F32), axis=-1, keepdims=True)
        prob = weights * inverse
        grad_prob = mm(grads, values_t_ref[...])
        score = (prob * (grad_prob - delta)).astype(BF16)
        score_full[rows, :] = score
        gq_sum[rows, :] += mm(score, keys_m)
        gk_t = gk_t + mm(query_t[:, rows], score)
        gv_t = gv_t + mm(grads_t[:, rows], prob.astype(BF16))
    gk_sum[pl.ds(feature, head_size), :] = gk_t
    gv_sum[pl.ds(feature, head_size), :] = gv_t

    for row_part, column, side, rows in places():
        dbias_ref[row_part, column, 0, :, side * cols : (side + 1) * cols] = score_full[
            rows, column * cols : (column + 1) * cols
        ]

    @pl.when(head == heads - 1)
    def _():
        results = (
            gq_sum[...] * scale,
            (gk_sum[...] * scale).T,
            gv_sum[...].T,
            att_sum[:, :part],
        )
        for kind, values in enumerate(results):
            rounded = values.astype(BF16)
            for slot in range(groups):
                out_refs[slot][:, kind * part : (kind + 1) * part] = rounded[
                    slot * cols : (slot + 1) * cols
                ]


def attention(group_index, acts, bias, head_size):
    groups = len(acts)
    cols, width = acts[0].shape
    tokens = groups * cols
    part = width // 4
    row_parts, _, heads, half, lanes = bias.shape
    row_block = 256 if tokens % 256 == 0 else cols
    spread = (row_parts, groups, 1, half, lanes)
    padded = (part // 128 + 1) * 128
    slots = [pl.BlockSpec((cols, width), lambda h: (0, 0)) for _ in range(groups)]
    *grads, dbias = pl.pallas_call(
        functools.partial(
            attention_kernel, groups=groups, head_size=head_size, row_block=row_block
        ),
        grid=(heads,),
        in_specs=[smem(), pl.BlockSpec(spread, lambda h: (0, 0, h, 0, 0))] + slots,
        out_specs=slots + [pl.BlockSpec(spread, lambda h: (0, 0, h, 0, 0))],
        out_shape=[jax.ShapeDtypeStruct((cols, width), BF16) for _ in range(groups)]
        + [jax.ShapeDtypeStruct(bias.shape, BF16)],
        scratch_shapes=[pltpu.VMEM((tokens, part), BF16) for _ in range(4)]
        + [pltpu.VMEM((part, tokens), BF16) for _ in range(4)]
        + [
            pltpu.VMEM((tokens, tokens), BF16),
            pltpu.VMEM((tokens, tokens), BF16),
            pltpu.VMEM((tokens, padded), F32),
            pltpu.VMEM((tokens, part), F32),
            pltpu.VMEM((part, tokens), F32),
            pltpu.VMEM((part, tokens), F32),
        ],
        compiler_params=params(),
    )(group_index, bias, *acts)
    return grads, dbias


def finish_kernel(
    group_ref,
    single_ref,
    noised_ref,
    cot_ref,
    gamma_ref,
    gate_ref,
    w_gamma_ref,
    w_beta_ref,
    w_outgate_ref,
    w_query_ref,
    w_key_ref,
    w_value_ref,
    w_out_ref,
    *rest,
    groups,
):
    got_refs = rest[:groups]
    updated_ref, d_single_ref, stage_ref = rest[groups:]
    width = stage_ref.shape[2]
    part = width // 4
    for slot in range(groups):
        stage_ref[lax.rem(group_ref[0] + slot, groups)] = got_refs[slot][...]

    def take(kind):
        return jnp.concatenate(
            [stage_ref[group, :, kind * part : (kind + 1) * part] for group in range(groups)],
            axis=1,
        )

    out_gate = gate_ref[...]
    cond_gamma = gamma_ref[...]
    block_update = mm(take(3), w_out_ref[...])
    noised = noised_ref[...].astype(F32)
    updated_ref[...] = (noised + out_gate * block_update).astype(BF16)
    gate_part = cot_ref[...].astype(F32) * block_update
    pre_gate = (gate_part * out_gate * (1.0 - out_gate)).astype(BF16)
    grad_input = mm_nt(take(0), w_query_ref[...])
    grad_input += mm_nt(take(1), w_key_ref[...])
    grad_input += mm_nt(take(2), w_value_ref[...])
    noised_norm, _ = norm_rows(noised)
    pre_gamma = (grad_input * noised_norm * cond_gamma * (1.0 - cond_gamma)).astype(BF16)
    grad_snorm = mm_nt(pre_gamma, w_gamma_ref[...])
    grad_snorm += mm_nt(grad_input.astype(BF16), w_beta_ref[...])
    grad_snorm += mm_nt(pre_gate, w_outgate_ref[...])
    single_norm, single_inv = norm_rows(single_ref[...].astype(F32))
    d_single_ref[...] = norm_back(grad_snorm, single_norm, single_inv)


def swap_groups(sends, direction):
    groups = len(sends)
    got = [sends[0]]
    for shift in range(1, groups):
        perm = [(index, (index + direction * shift) % groups) for index in range(groups)]
        got.append(lax.ppermute(sends[shift], "grp", perm))
    return got


def sum_rows(values, row_total):
    bit = 1
    while bit < row_total:
        perm = [(index, index ^ bit) for index in range(row_total)]
        mine = values.astype(BF16)
        values = mine.astype(F32) + lax.ppermute(mine, "rows", perm).astype(F32)
        bit *= 2
    return values


def split_heads(
    single,
    pair,
    chains,
    noised,
    w_gamma,
    w_beta,
    w_outgate,
    w_query,
    w_key,
    w_value,
    w_out,
    w_pair,
    chain_gain,
    cotangent,
    *,
    groups,
    row_total,
):
    cols, _ = single.shape
    tokens = chains.shape[0]
    width = noised.shape[2]
    head_size = width // w_pair.shape[1]
    row_index = lax.axis_index("rows").reshape(1)
    group_index = lax.axis_index("grp").reshape(1)
    bias_send, stats = pair_bias(
        pair, w_pair, chain_gain, chains, group_index, row_index, groups
    )
    bias_own = jnp.stack(swap_groups(bias_send, 1))
    bias_all = lax.all_gather(bias_own, "rows", axis=0)
    noised = noised[0]
    cotangent = cotangent[0]
    *acts_send, cond_gamma, out_gate = pl.pallas_call(
        functools.partial(project_kernel, groups=groups),
        in_specs=[smem()] + [vmem()] * 10,
        out_shape=[
            jax.ShapeDtypeStruct((cols, 4 * width // groups), BF16) for _ in range(groups)
        ]
        + [
            jax.ShapeDtypeStruct((cols, width), F32),
            jax.ShapeDtypeStruct((cols, width), F32),
        ],
        scratch_shapes=[pltpu.VMEM((groups, cols, 4 * width // groups), BF16)],
        compiler_params=params(),
    )(
        group_index,
        single,
        noised,
        cotangent,
        w_gamma,
        w_beta,
        w_outgate,
        w_query,
        w_key,
        w_value,
        w_out,
    )
    acts = swap_groups(acts_send, 1)
    grads_send, dbias = attention(group_index, acts, bias_all, head_size)
    grads = swap_groups(grads_send, -1)
    dbias_own = lax.psum_scatter(dbias, "rows", scatter_dimension=0, tiled=False)
    dbias_back = swap_groups([dbias_own[slot] for slot in range(groups)], -1)
    updated, d_part = pl.pallas_call(
        functools.partial(finish_kernel, groups=groups),
        in_specs=[smem()] + [vmem()] * (12 + groups),
        out_shape=[
            jax.ShapeDtypeStruct((cols, width), BF16),
            jax.ShapeDtypeStruct(single.shape, F32),
        ],
        scratch_shapes=[pltpu.VMEM((groups, cols, 4 * width // groups), BF16)],
        compiler_params=params(),
    )(
        group_index,
        single,
        noised,
        cotangent,
        cond_gamma,
        out_gate,
        w_gamma,
        w_beta,
        w_outgate,
        w_query,
        w_key,
        w_value,
        w_out,
        *grads,
    )
    d_single = sum_rows(d_part, row_total)
    d_pair = pair_back(pair, stats, dbias_back, w_pair, group_index, float(tokens))
    return (updated[None], d_single, d_pair)


def project(acts, weight):
    return jnp.einsum("std,de->ste", acts, weight, preferred_element_type=F32)


def project_back(acts, weight):
    return jnp.einsum("ste,de->std", acts, weight, preferred_element_type=F32)


def split_keys(
    single,
    pair,
    chains,
    noised,
    w_gamma,
    w_beta,
    w_outgate,
    w_query,
    w_key,
    w_value,
    w_out,
    w_pair,
    chain_gain,
    cotangent,
):
    col_count = single.shape[0]
    row_count = pair.shape[0]
    head_count = w_pair.shape[1]
    model_width = w_query.shape[0]
    head_size = model_width // head_count
    sample_count = noised.shape[0]
    token_total = chains.shape[0]
    score_scale = 1.0 / math.sqrt(head_size)
    row_index = lax.axis_index("rows")
    group_index = lax.axis_index("grp")
    chain_rows = lax.dynamic_slice_in_dim(chains, row_index * row_count, row_count)
    chain_cols = lax.dynamic_slice_in_dim(chains, group_index * col_count, col_count)
    pair_norm, pair_inv = norm_rows(pair.astype(jnp.float32))
    projected = jnp.einsum(
        "ijc,ch->hij", pair_norm.astype(jnp.bfloat16), w_pair, preferred_element_type=jnp.float32
    )
    same_chain = (chain_rows[:, None] == chain_cols[None, :]).astype(jnp.float32)
    bias_block = (projected + chain_gain[:, None, None] * same_chain[None]).astype(jnp.bfloat16)
    bias_keys = lax.all_gather(bias_block, "rows", axis=1, tiled=True)
    single_norm, single_inv = norm_rows(single.astype(jnp.float32))
    single_b = single_norm.astype(jnp.bfloat16)
    cond_gamma = jax.nn.sigmoid(jnp.dot(single_b, w_gamma, preferred_element_type=jnp.float32))
    cond_beta = jnp.dot(single_b, w_beta, preferred_element_type=jnp.float32)
    out_gate = jax.nn.sigmoid(jnp.dot(single_b, w_outgate, preferred_element_type=jnp.float32))
    noised_f = noised.astype(jnp.float32)
    noised_norm, noised_inv = norm_rows(noised_f)
    x_b = (noised_norm * cond_gamma[None] + cond_beta[None]).astype(jnp.bfloat16)
    queries = project(x_b, w_query).astype(jnp.bfloat16)
    keys_own = project(x_b, w_key).astype(jnp.bfloat16)
    values_own = project(x_b, w_value).astype(jnp.bfloat16)
    queries_all = lax.all_gather(queries, "grp", axis=1, tiled=True)
    query_heads = queries_all.reshape(sample_count, token_total, head_count, head_size)
    key_heads = keys_own.reshape(sample_count, col_count, head_count, head_size)
    value_heads = values_own.reshape(sample_count, col_count, head_count, head_size)
    scores = (
        jnp.einsum("sihe,sjhe->shij", query_heads, key_heads, preferred_element_type=jnp.float32)
        * score_scale
        + bias_keys.astype(jnp.float32)[None]
    )
    exp_scores = jnp.exp(scores)
    exp_total = lax.psum(jnp.sum(exp_scores, axis=-1).astype(jnp.bfloat16), "grp").astype(
        jnp.float32
    )
    attn_prob = exp_scores / exp_total[..., None]
    prob_b = attn_prob.astype(jnp.bfloat16)
    attended_part = jnp.einsum(
        "shij,sjhe->sihe", prob_b, value_heads, preferred_element_type=jnp.float32
    )
    attended_part = attended_part.reshape(sample_count, token_total, model_width)
    attended = lax.psum_scatter(
        attended_part.astype(jnp.bfloat16), "grp", scatter_dimension=1, tiled=True
    )
    block_update = project(attended, w_out)
    updated = (noised_f + out_gate[None] * block_update).astype(jnp.bfloat16)
    grad_out = cotangent.astype(jnp.float32)
    gate_part = jnp.sum(grad_out * block_update, axis=0)
    grad_update = (grad_out * out_gate[None]).astype(jnp.bfloat16)
    grad_attn = project_back(grad_update, w_out).astype(jnp.bfloat16)
    grads_all = lax.all_gather(grad_attn, "grp", axis=1, tiled=True)
    grad_heads = grads_all.reshape(sample_count, token_total, head_count, head_size)
    grad_prob = jnp.einsum(
        "sihe,sjhe->shij", grad_heads, value_heads, preferred_element_type=jnp.float32
    )
    row_delta = lax.psum(
        jnp.sum(attn_prob * grad_prob, axis=-1).astype(jnp.bfloat16), "grp"
    ).astype(jnp.float32)
    grad_score = attn_prob * (grad_prob - row_delta[..., None])
    score_b = grad_score.astype(jnp.bfloat16)
    query_part = (
        jnp.einsum("shij,sjhe->sihe", score_b, key_heads, preferred_element_type=jnp.float32)
        * score_scale
    )
    query_part = query_part.reshape(sample_count, token_total, model_width)
    grad_query = lax.psum_scatter(
        query_part.astype(jnp.bfloat16), "grp", scatter_dimension=1, tiled=True
    )
    grad_key = (
        jnp.einsum("shij,sihe->sjhe", score_b, query_heads, preferred_element_type=jnp.float32)
        * score_scale
    )
    grad_value = jnp.einsum(
        "shij,sihe->sjhe", prob_b, grad_heads, preferred_element_type=jnp.float32
    )
    grad_key = grad_key.reshape(sample_count, col_count, model_width).astype(jnp.bfloat16)
    grad_value = grad_value.reshape(sample_count, col_count, model_width).astype(jnp.bfloat16)
    grad_input = (
        project_back(grad_query, w_query)
        + project_back(grad_key, w_key)
        + project_back(grad_value, w_value)
    )
    gamma_part = jnp.sum(grad_input * noised_norm, axis=0)
    beta_part = jnp.sum(grad_input, axis=0)
    gamma_sum, beta_sum, gate_sum = lax.psum((gamma_part, beta_part, gate_part), "rows")
    pre_gamma = (gamma_sum * cond_gamma * (1.0 - cond_gamma)).astype(jnp.bfloat16)
    pre_gate = (gate_sum * out_gate * (1.0 - out_gate)).astype(jnp.bfloat16)
    grad_snorm = jnp.dot(pre_gamma, w_gamma.T, preferred_element_type=jnp.float32)
    grad_snorm = grad_snorm + jnp.dot(
        beta_sum.astype(jnp.bfloat16), w_beta.T, preferred_element_type=jnp.float32
    )
    grad_snorm = grad_snorm + jnp.dot(pre_gate, w_outgate.T, preferred_element_type=jnp.float32)
    d_single = norm_back(grad_snorm, single_norm, single_inv)
    bias_part = jnp.sum(score_b, axis=0, dtype=jnp.float32)
    bias_own = lax.psum_scatter(bias_part, "rows", scatter_dimension=1, tiled=True)
    bias_grad = (bias_own * token_total).astype(jnp.bfloat16)
    grad_pairn = jnp.einsum("hij,ch->ijc", bias_grad, w_pair, preferred_element_type=jnp.float32)
    d_pair = norm_back(grad_pairn, pair_norm, pair_inv).astype(jnp.bfloat16)
    return (updated, d_single, d_pair)


def solution(mesh):
    in_specs = (
        P("grp", None),
        P("rows", "grp", None),
        P(),
        P("rows", "grp", None),
        P(),
        P(),
        P(),
        P(),
        P(),
        P(),
        P(),
        P(),
        P(),
        P("rows", "grp", None),
    )
    out_specs = (P("rows", "grp", None), P("grp", None), P("rows", "grp", None))
    groups = mesh.shape["grp"]
    row_total = mesh.shape["rows"]

    def on_device(*args):
        pair, noised, w_pair = args[1], args[3], args[11]
        fits = (
            pair.shape[0] % 32 == 0
            and pair.shape[1] % pair.shape[0] == 0
            and row_total == 8
            and noised.shape[0] == 1
            and noised.shape[1] % 64 == 0
            and w_pair.shape[1] % groups == 0
        )
        if fits:
            return split_heads(*args, groups=groups, row_total=row_total)
        return split_keys(*args)

    return jax.shard_map(
        on_device, mesh=mesh, in_specs=in_specs, out_specs=out_specs, check_vma=False
    )
```

```python
import functools
import math

import jax
import jax.numpy as jnp
from jax import lax
from jax.experimental import pallas as pl
from jax.experimental.pallas import tpu as pltpu
from jax.sharding import PartitionSpec as P

EPSILON = 1e-05
BF16 = jnp.bfloat16
F32 = jnp.float32
VMEM_LIMIT = 56 * 1024 * 1024


def norm_rows(values):
    center = values - jnp.mean(values, axis=-1, keepdims=True)
    inverse = lax.rsqrt(jnp.mean(center * center, axis=-1, keepdims=True) + EPSILON)
    return (center * inverse, inverse)


def norm_back(grad_in, normed, inverse):
    grad_mean = jnp.mean(grad_in, axis=-1, keepdims=True)
    cross_mean = jnp.mean(grad_in * normed, axis=-1, keepdims=True)
    return inverse * (grad_in - grad_mean - normed * cross_mean)


def mm(left, right):
    return lax.dot_general(left, right, (((1,), (0,)), ((), ())), preferred_element_type=F32)


def mm_nt(left, right):
    return lax.dot_general(left, right, (((1,), (1,)), ((), ())), preferred_element_type=F32)


def mm_tn(left, right):
    return lax.dot_general(left, right, (((0,), (0,)), ((), ())), preferred_element_type=F32)


def sigmoid(values):
    return 1.0 / (1.0 + jnp.exp(-values))


def params():
    return pltpu.CompilerParams(vmem_limit_bytes=VMEM_LIMIT)


def smem():
    return pl.BlockSpec(memory_space=pltpu.SMEM)


def vmem():
    return pl.BlockSpec(memory_space=pltpu.VMEM)


def project_kernel(
    group_ref,
    single_ref,
    noised_ref,
    cot_ref,
    w_gamma_ref,
    w_beta_ref,
    w_outgate_ref,
    w_query_ref,
    w_key_ref,
    w_value_ref,
    w_out_ref,
    *rest,
    groups,
    calls,
):
    send_refs = rest[:groups]
    gamma_ref, gate_ref, stage_ref = rest[groups:]
    width = stage_ref.shape[2]
    part = width // (4 * calls)
    group_own = group_ref[0]
    single_norm, _ = norm_rows(single_ref[...].astype(F32))
    single_b = single_norm.astype(BF16)
    cond_gamma = sigmoid(mm(single_b, w_gamma_ref[...]))
    gamma_ref[...] = cond_gamma
    out_gate = sigmoid(mm(single_b, w_outgate_ref[...]))
    gate_ref[...] = out_gate
    cond_beta = mm(single_b, w_beta_ref[...])
    noised_norm, _ = norm_rows(noised_ref[...].astype(F32))
    x_b = (noised_norm * cond_gamma + cond_beta).astype(BF16)

    def put(kind, values):
        rounded = values.astype(BF16)
        for group in range(groups):
            slot = lax.rem(group - group_own + groups, groups)
            for call in range(calls):
                feature = (group * calls + call) * part
                lane = (call * 4 + kind) * part
                stage_ref[slot, :, lane : lane + part] = rounded[:, feature : feature + part]

    put(0, mm(x_b, w_query_ref[...]))
    put(1, mm(x_b, w_key_ref[...]))
    put(2, mm(x_b, w_value_ref[...]))
    grad_update = (cot_ref[...].astype(F32) * out_gate).astype(BF16)
    put(3, mm_nt(grad_update, w_out_ref[...]))
    for slot in range(groups):
        send_refs[slot][...] = stage_ref[slot]


def lane_tiles(cols):
    return [(tile, tile * 128, min(cols, tile * 128 + 128)) for tile in range(-(-cols // 128))]


def mean_matrix(channels):
    first = lax.broadcasted_iota(jnp.int32, (2 * channels, 2 * channels), 0) >= channels
    second = lax.broadcasted_iota(jnp.int32, (2 * channels, 2 * channels), 1) >= channels
    return jnp.where(first == second, 1.0 / channels, 0.0).astype(BF16)


def center_rows(pair_ref, first, batch, means):
    _, _, cols, channels = pair_ref.shape
    both = jnp.concatenate(
        [pair_ref[side, pl.ds(first, batch)].reshape(batch * cols, channels) for side in range(2)],
        axis=1,
    )
    return both.astype(F32) - mm(both, means)


def bias_kernel(
    group_ref,
    rows_ref,
    chains_ref,
    gain_ref,
    pair_ref,
    w_pair_ref,
    cols_ref,
    *rest,
    groups,
    batch,
):
    send_refs = rest[:groups]
    stats_ref, flat_ref, gains_ref, stage_ref = rest[groups:]
    _, step, cols, channels = pair_ref.shape
    heads = gain_ref.shape[0]
    per_group = heads // groups
    half = step * pl.num_programs(0)
    group_own = group_ref[0]
    row_base = rows_ref[0] * 2 * half + pl.program_id(0) * step
    means = mean_matrix(channels)
    weight = w_pair_ref[...]
    left = jnp.concatenate(
        [
            jnp.concatenate([weight, jnp.zeros((heads, channels), BF16)], axis=1),
            jnp.concatenate(
                [
                    jnp.zeros((heads, channels), BF16),
                    jnp.full((heads, channels), 1.0 / channels, BF16),
                ],
                axis=1,
            ),
        ],
        axis=0,
    )
    chain_cols = cols_ref[:, :cols]
    for group in range(1, groups):
        here = cols_ref[:, group * cols : (group + 1) * cols]
        chain_cols = jnp.where(group_own == group, here, chain_cols)
    for head in range(heads):
        gains_ref[head : head + 1, :] = jnp.full((1, cols), gain_ref[head], F32)

    def some_rows(index, carry):
        first = index * batch
        center = center_rows(pair_ref, first, batch, means)
        center_b = center.astype(BF16)
        square = (center * center).astype(BF16)
        for inner in range(batch):
            rows = slice(inner * cols, (inner + 1) * cols)
            for side in range(2):
                lanes = slice(side * channels, (side + 1) * channels)
                right = jnp.concatenate([center_b[rows, lanes], square[rows, lanes]], axis=1)
                sums = mm_nt(left, right)
                inverse = lax.rsqrt(sums[heads : heads + 8] + EPSILON)
                projected = sums[:heads] * inverse[:1]
                stats_ref[side, first + inner, :heads, :] = projected
                stats_ref[side, first + inner, heads:, :] = inverse
                chain = chains_ref[row_base + side * half + first + inner]
                same = (chain_cols == chain).astype(F32)
                values = projected + gains_ref[...] * same
                for tile, start, end in lane_tiles(cols):
                    piece = values[:, start:end]
                    if end - start < 128:
                        blank = jnp.zeros((heads, 128 - end + start), F32)
                        piece = jnp.concatenate([piece, blank], axis=1)
                    flat_ref[side, tile, pl.ds(first + inner, heads, stride=step), :] = piece
        return carry

    lax.fori_loop(0, step // batch, some_rows, 0)
    for head in range(heads):
        slot = lax.rem(head // per_group - group_own + groups, groups)
        values = jnp.concatenate(
            [
                flat_ref[side, tile, head * step : (head + 1) * step, : end - start]
                for side in range(2)
                for tile, start, end in lane_tiles(cols)
            ],
            axis=1,
        )
        stage_ref[slot, head % per_group] = values.astype(BF16)
    for slot in range(groups):
        send_refs[slot][...] = stage_ref[slot]


def pair_bias(pair, w_pair, chain_gain, chains, group_index, row_index, groups):
    rows, cols, channels = pair.shape
    heads = w_pair.shape[1]
    per_group = heads // groups
    half = rows // 2
    step = 16
    tiles = -(-cols // 128)
    *sends, stats = pl.pallas_call(
        functools.partial(bias_kernel, groups=groups, batch=4),
        grid=(half // step,),
        in_specs=[
            smem(),
            smem(),
            smem(),
            smem(),
            pl.BlockSpec((2, step, cols, channels), lambda t: (0, t, 0, 0)),
            pl.BlockSpec((heads, channels), lambda t: (0, 0)),
            pl.BlockSpec((1, groups * cols), lambda t: (0, 0)),
        ],
        out_specs=[
            pl.BlockSpec((per_group, step, 2 * cols), lambda t: (0, t, 0)) for _ in range(groups)
        ]
        + [pl.BlockSpec((2, step, heads + 8, cols), lambda t: (0, t, 0, 0))],
        out_shape=[
            jax.ShapeDtypeStruct((per_group, half, 2 * cols), BF16) for _ in range(groups)
        ]
        + [jax.ShapeDtypeStruct((2, half, heads + 8, cols), F32)],
        scratch_shapes=[
            pltpu.VMEM((2, tiles, heads * step, 128), F32),
            pltpu.VMEM((heads, cols), F32),
            pltpu.VMEM((groups, per_group, step, 2 * cols), BF16),
        ],
        compiler_params=params(),
    )(
        group_index,
        row_index,
        chains,
        chain_gain,
        pair.reshape(2, half, cols, channels),
        w_pair.T,
        chains.reshape(1, groups * cols),
    )
    return sends, stats


def pair_back_kernel(
    group_ref, pair_ref, stats_ref, w_pair_ref, *rest, groups, calls, factor, batch
):
    grad_refs = rest[: groups * calls]
    out_ref, flat_ref = rest[groups * calls :]
    _, step, cols, channels = pair_ref.shape
    per_call = grad_refs[0].shape[0]
    heads = groups * calls * per_call
    group_own = group_ref[0]
    means = mean_matrix(channels)
    weight = w_pair_ref[...].astype(F32)
    weight = weight - jnp.mean(weight, axis=-1, keepdims=True)
    high = weight.astype(BF16)
    low = (weight - high.astype(F32)).astype(BF16)
    weights = jnp.concatenate([high, low, jnp.zeros((16, channels), BF16)], axis=0)
    spread = lax.broadcasted_iota(jnp.int32, (2 * heads + 16, channels), 0)
    spread = ((spread >= 2 * heads) & (spread < 2 * heads + 2)).astype(F32).astype(BF16)
    weights = jnp.concatenate([weights, spread], axis=1)
    blank = jnp.zeros((14, cols), F32)
    for number in range(groups * calls):
        call, slot = divmod(number, groups)
        source = lax.rem(group_own + slot, groups) * calls + call
        for head in range(per_call):
            values = grad_refs[number][head].astype(F32)
            top = pl.multiple_of((source * per_call + head) * step, step)
            for side in range(2):
                for tile, start, end in lane_tiles(cols):
                    flat_ref[side, tile, pl.ds(top, step), : end - start] = values[
                        :, side * cols + start : side * cols + end
                    ]

    def some_rows(index, carry):
        first = index * batch
        center = center_rows(pair_ref, first, batch, means)
        for side in range(2):
            lefts = []
            for inner in range(batch):
                grads = jnp.concatenate(
                    [
                        flat_ref[side, tile, pl.ds(first + inner, heads, stride=step), :][
                            :, : end - start
                        ]
                        for tile, start, end in lane_tiles(cols)
                    ],
                    axis=1,
                )
                projected = stats_ref[side, first + inner, :heads, :]
                inverse = stats_ref[side, first + inner, heads : heads + 1, :]
                cross = jnp.sum(grads * projected, axis=0, keepdims=True) * (1.0 / channels)
                scaled = grads * (inverse * factor)
                cross = cross * (inverse * inverse * factor)
                cross_high = cross.astype(BF16).astype(F32)
                lefts.append(
                    jnp.concatenate(
                        [scaled, scaled, cross_high, cross - cross_high, blank], axis=0
                    )
                )
            for inner in range(batch):
                rows = slice(inner * cols, (inner + 1) * cols)
                lanes = slice(side * channels, (side + 1) * channels)
                both = mm_tn(lefts[inner].astype(BF16), weights)
                out_ref[side, first + inner] = (
                    both[:, :channels] - center[rows, lanes] * both[:, channels:]
                ).astype(BF16)
        return carry

    lax.fori_loop(0, step // batch, some_rows, 0)


def pair_back(pair, stats, grads, w_pair, group_index, groups, factor):
    rows, cols, channels = pair.shape
    per_call = grads[0].shape[0]
    heads = len(grads) * per_call
    half = rows // 2
    step = 16
    tiles = -(-cols // 128)
    out = pl.pallas_call(
        functools.partial(
            pair_back_kernel, groups=groups, calls=len(grads) // groups, factor=factor, batch=4
        ),
        grid=(half // step,),
        in_specs=[
            smem(),
            pl.BlockSpec((2, step, cols, channels), lambda t: (0, t, 0, 0)),
            pl.BlockSpec((2, step, heads + 8, cols), lambda t: (0, t, 0, 0)),
            pl.BlockSpec((heads, channels), lambda t: (0, 0)),
        ]
        + [pl.BlockSpec((per_call, step, 2 * cols), lambda t: (0, t, 0)) for _ in grads],
        out_specs=pl.BlockSpec((2, step, cols, channels), lambda t: (0, t, 0, 0)),
        out_shape=jax.ShapeDtypeStruct((2, half, cols, channels), BF16),
        scratch_shapes=[pltpu.VMEM((2, tiles, heads * step, 128), F32)],
        compiler_params=params(),
    )(group_index, pair.reshape(2, half, cols, channels), stats, w_pair.T, *grads)
    return out.reshape(rows, cols, channels)


def attention_kernel(group_ref, row_ref, *rest, groups, row_parts, head_size, row_block):
    bias_refs = rest[:row_parts]
    acts_refs = rest[row_parts : row_parts + groups]
    rest = rest[row_parts + groups :]
    out_refs = rest[:groups]
    (
        keep_ref,
        give_ref,
        query_ref,
        keys_ref,
        values_ref,
        grads_ref,
        query_t_ref,
        keys_t_ref,
        values_t_ref,
        grads_t_ref,
        bias_full,
        score_full,
        att_sum,
        gq_sum,
        gk_sum,
        gv_sum,
    ) = rest[groups:]
    head = pl.program_id(0)
    heads = pl.num_programs(0)
    group_own = group_ref[0]
    cols, width = acts_refs[0].shape
    tokens = groups * cols
    part = width // 4
    half = bias_refs[0].shape[2]
    scale = 1.0 / math.sqrt(head_size)
    extra = att_sum.shape[1] - part
    plain = (query_ref, keys_ref, values_ref, grads_ref)
    turned = (query_t_ref, keys_t_ref, values_t_ref, grads_t_ref)

    @pl.when(head == 0)
    def _():
        for kind in range(4):
            for slot in range(groups):
                plain[kind][slot * cols : (slot + 1) * cols, :] = acts_refs[slot][
                    :, kind * part : (kind + 1) * part
                ]
            turned[kind][...] = plain[kind][...].T
        att_sum[...] = jnp.zeros_like(att_sum)
        gq_sum[...] = jnp.zeros_like(gq_sum)

    def places():
        for other in range(row_parts):
            first = (row_ref[0] ^ other) * (2 * half)
            slot = lax.rem(group_own - first // cols + groups, groups)
            for side in range(2):
                top = slot * cols + lax.rem(first, cols) + side * half
                top = pl.multiple_of(top, 16)
                for column in range(groups):
                    yield other, column, side, pl.ds(top, half)

    for other, column, side, rows in places():
        bias_full[rows, column * cols : (column + 1) * cols] = bias_refs[other][
            column, 0, :, side * cols : (side + 1) * cols
        ]

    lane = lax.broadcasted_iota(jnp.int32, (1, part), 1)
    mine = (lane >= head * head_size) & (lane < (head + 1) * head_size)
    zero = jnp.zeros((), BF16)
    keys_m = jnp.where(mine, keys_ref[...], zero)
    values_m = jnp.concatenate(
        [jnp.where(mine, values_ref[...], zero), jnp.ones((tokens, extra), BF16)], axis=1
    )
    feature = pl.multiple_of(head * head_size, head_size)
    query_t = query_t_ref[pl.ds(feature, head_size), :]
    grads_t = grads_t_ref[pl.ds(feature, head_size), :]
    gk_t = jnp.zeros((head_size, tokens), F32)
    gv_t = jnp.zeros((head_size, tokens), F32)
    for top in range(0, tokens, row_block):
        rows = slice(top, top + row_block)
        query = jnp.where(mine, query_ref[rows, :], zero)
        grads = jnp.where(mine, grads_ref[rows, :], zero)
        scores = mm(query, keys_t_ref[...]) * scale + bias_full[rows, :].astype(F32)
        weights = jnp.exp(scores)
        attended = mm(weights.astype(BF16), values_m)
        inverse = 1.0 / attended[:, part : part + 1]
        attended = attended[:, :part] * inverse
        att_sum[rows, :part] += attended
        delta = jnp.sum(attended * grads.astype(F32), axis=-1, keepdims=True)
        prob = weights * inverse
        grad_prob = mm(grads, values_t_ref[...])
        score = (prob * (grad_prob - delta)).astype(BF16)
        score_full[rows, :] = score
        gq_sum[rows, :] += mm(score, keys_m)
        gk_t = gk_t + mm(query_t[:, rows], score)
        gv_t = gv_t + mm(grads_t[:, rows], prob.astype(BF16))
    gk_sum[pl.ds(feature, head_size), :] = gk_t
    gv_sum[pl.ds(feature, head_size), :] = gv_t

    for other, column, side, rows in places():
        dbias_ref = give_ref if other % 2 else keep_ref
        dbias_ref[other // 2, column, 0, :, side * cols : (side + 1) * cols] = score_full[
            rows, column * cols : (column + 1) * cols
        ]

    @pl.when(head == heads - 1)
    def _():
        results = (
            gq_sum[...] * scale,
            (gk_sum[...] * scale).T,
            gv_sum[...].T,
            att_sum[:, :part],
        )
        for kind, values in enumerate(results):
            rounded = values.astype(BF16)
            for slot in range(groups):
                out_refs[slot][:, kind * part : (kind + 1) * part] = rounded[
                    slot * cols : (slot + 1) * cols
                ]


def attention(group_index, row_index, acts, bias, head_size, call, calls):
    groups = len(acts)
    row_parts = len(bias)
    cols, width = acts[0].shape
    width = width // calls
    tokens = groups * cols
    part = width // 4
    _, heads, half, lanes = bias[0].shape
    heads = heads // calls
    row_block = 256 if tokens % 256 == 0 else cols
    padded = (part // 128 + 1) * 128
    halves = (row_parts // 2, groups, heads, half, lanes)
    *grads, keep, give = pl.pallas_call(
        functools.partial(
            attention_kernel,
            groups=groups,
            row_parts=row_parts,
            head_size=head_size,
            row_block=row_block,
        ),
        grid=(heads,),
        in_specs=[smem(), smem()]
        + [pl.BlockSpec((groups, 1, half, lanes), lambda h: (0, call * heads + h, 0, 0))]
        * row_parts
        + [pl.BlockSpec((cols, width), lambda h: (0, call))] * groups,
        out_specs=[pl.BlockSpec((cols, width), lambda h: (0, 0))] * groups
        + [
            pl.BlockSpec((row_parts // 2, groups, 1, half, lanes), lambda h: (0, 0, h, 0, 0))
        ]
        * 2,
        out_shape=[jax.ShapeDtypeStruct((cols, width), BF16)] * groups
        + [jax.ShapeDtypeStruct(halves, BF16)] * 2,
        scratch_shapes=[pltpu.VMEM((tokens, part), BF16) for _ in range(4)]
        + [pltpu.VMEM((part, tokens), BF16) for _ in range(4)]
        + [
            pltpu.VMEM((tokens, tokens), BF16),
            pltpu.VMEM((tokens, tokens), BF16),
            pltpu.VMEM((tokens, padded), F32),
            pltpu.VMEM((tokens, part), F32),
            pltpu.VMEM((part, tokens), F32),
            pltpu.VMEM((part, tokens), F32),
        ],
        compiler_params=params(),
    )(group_index, row_index, *bias, *acts)
    return grads, keep, give


def finish_kernel(
    group_ref,
    single_ref,
    noised_ref,
    cot_ref,
    gamma_ref,
    gate_ref,
    w_gamma_ref,
    w_beta_ref,
    w_outgate_ref,
    w_query_ref,
    w_key_ref,
    w_value_ref,
    w_out_ref,
    *rest,
    groups,
    calls,
):
    got_refs = rest[: groups * calls]
    updated_ref, d_single_ref, stage_ref = rest[groups * calls :]
    width = stage_ref.shape[3]
    part = width // 4
    for slot in range(groups):
        for call in range(calls):
            stage_ref[lax.rem(group_ref[0] + slot, groups), call] = got_refs[
                call * groups + slot
            ][...]

    def take(kind):
        return jnp.concatenate(
            [
                stage_ref[group, call, :, kind * part : (kind + 1) * part]
                for group in range(groups)
                for call in range(calls)
            ],
            axis=1,
        )

    out_gate = gate_ref[...]
    cond_gamma = gamma_ref[...]
    block_update = mm(take(3), w_out_ref[...])
    noised = noised_ref[...].astype(F32)
    updated_ref[...] = (noised + out_gate * block_update).astype(BF16)
    gate_part = cot_ref[...].astype(F32) * block_update
    pre_gate = (gate_part * out_gate * (1.0 - out_gate)).astype(BF16)
    grad_input = mm_nt(take(0), w_query_ref[...])
    grad_input += mm_nt(take(1), w_key_ref[...])
    grad_input += mm_nt(take(2), w_value_ref[...])
    noised_norm, _ = norm_rows(noised)
    pre_gamma = (grad_input * noised_norm * cond_gamma * (1.0 - cond_gamma)).astype(BF16)
    grad_snorm = mm_nt(pre_gamma, w_gamma_ref[...])
    grad_snorm += mm_nt(grad_input.astype(BF16), w_beta_ref[...])
    grad_snorm += mm_nt(pre_gate, w_outgate_ref[...])
    single_norm, single_inv = norm_rows(single_ref[...].astype(F32))
    d_single_ref[...] = norm_back(grad_snorm, single_norm, single_inv)


def swap_groups(sends, direction):
    groups = len(sends)
    got = [sends[0]]
    for shift in range(1, groups):
        perm = [(index, (index + direction * shift) % groups) for index in range(groups)]
        got.append(lax.ppermute(sends[shift], "grp", perm))
    return got


def flip_rows(values, bits, row_total):
    return lax.ppermute(values, "rows", [(index, index ^ bits) for index in range(row_total)])


def gather_rows(own, row_total):
    blocks = [None] * row_total
    for bits in range(0, row_total, 2):
        blocks[bits] = flip_rows(own, bits, row_total) if bits else own
    for bits in range(0, row_total, 2):
        blocks[bits + 1] = flip_rows(blocks[bits], 1, row_total)
    return blocks


def scatter_rows(keep, give, row_total):
    both = keep.astype(F32) + flip_rows(give, 1, row_total).astype(F32)
    total = both[0]
    for bits in range(2, row_total, 2):
        total += flip_rows(both[bits // 2].astype(BF16), bits, row_total).astype(F32)
    return total.astype(BF16)


def sum_rows(values, row_total):
    bit = 1
    while bit < row_total:
        mine = values.astype(BF16)
        values = mine.astype(F32) + flip_rows(mine, bit, row_total).astype(F32)
        bit *= 2
    return values


def split_heads(
    single,
    pair,
    chains,
    noised,
    w_gamma,
    w_beta,
    w_outgate,
    w_query,
    w_key,
    w_value,
    w_out,
    w_pair,
    chain_gain,
    cotangent,
    *,
    groups,
    row_total,
):
    cols, _ = single.shape
    tokens = chains.shape[0]
    width = noised.shape[2]
    head_size = width // w_pair.shape[1]
    calls = 2
    row_index = lax.axis_index("rows").reshape(1)
    group_index = lax.axis_index("grp").reshape(1)
    bias_send, stats = pair_bias(
        pair, w_pair, chain_gain, chains, group_index, row_index, groups
    )
    bias_got = swap_groups(bias_send, 1)
    noised = noised[0]
    cotangent = cotangent[0]
    *acts_send, cond_gamma, out_gate = pl.pallas_call(
        functools.partial(project_kernel, groups=groups, calls=calls),
        in_specs=[smem()] + [vmem()] * 10,
        out_shape=[
            jax.ShapeDtypeStruct((cols, 4 * width // groups), BF16) for _ in range(groups)
        ]
        + [
            jax.ShapeDtypeStruct((cols, width), F32),
            jax.ShapeDtypeStruct((cols, width), F32),
        ],
        scratch_shapes=[pltpu.VMEM((groups, cols, 4 * width // groups), BF16)],
        compiler_params=params(),
    )(
        group_index,
        single,
        noised,
        cotangent,
        w_gamma,
        w_beta,
        w_outgate,
        w_query,
        w_key,
        w_value,
        w_out,
    )
    bias_got, acts_send = lax.optimization_barrier((bias_got, acts_send))
    acts = swap_groups(acts_send, 1)
    bias_all = gather_rows(jnp.stack(bias_got), row_total)
    grads = []
    dbias_back = []
    for call in range(calls):
        grads_send, keep, give = attention(
            group_index, row_index, acts, bias_all, head_size, call, calls
        )
        dbias_own = scatter_rows(keep, give, row_total)
        grads.append(swap_groups(grads_send, -1))
        dbias_back += swap_groups([dbias_own[slot] for slot in range(groups)], -1)
    updated, d_part = pl.pallas_call(
        functools.partial(finish_kernel, groups=groups, calls=calls),
        in_specs=[smem()] + [vmem()] * (12 + groups * calls),
        out_shape=[
            jax.ShapeDtypeStruct((cols, width), BF16),
            jax.ShapeDtypeStruct(single.shape, F32),
        ],
        scratch_shapes=[pltpu.VMEM((groups, calls, cols, 4 * width // (groups * calls)), BF16)],
        compiler_params=params(),
    )(
        group_index,
        single,
        noised,
        cotangent,
        cond_gamma,
        out_gate,
        w_gamma,
        w_beta,
        w_outgate,
        w_query,
        w_key,
        w_value,
        w_out,
        *grads[0],
        *grads[1],
    )
    d_single = sum_rows(d_part, row_total)
    d_pair = pair_back(pair, stats, dbias_back, w_pair, group_index, groups, float(tokens))
    return (updated[None], d_single, d_pair)


def project(acts, weight):
    return jnp.einsum("std,de->ste", acts, weight, preferred_element_type=F32)


def project_back(acts, weight):
    return jnp.einsum("ste,de->std", acts, weight, preferred_element_type=F32)


def split_keys(
    single,
    pair,
    chains,
    noised,
    w_gamma,
    w_beta,
    w_outgate,
    w_query,
    w_key,
    w_value,
    w_out,
    w_pair,
    chain_gain,
    cotangent,
):
    col_count = single.shape[0]
    row_count = pair.shape[0]
    head_count = w_pair.shape[1]
    model_width = w_query.shape[0]
    head_size = model_width // head_count
    sample_count = noised.shape[0]
    token_total = chains.shape[0]
    score_scale = 1.0 / math.sqrt(head_size)
    row_index = lax.axis_index("rows")
    group_index = lax.axis_index("grp")
    chain_rows = lax.dynamic_slice_in_dim(chains, row_index * row_count, row_count)
    chain_cols = lax.dynamic_slice_in_dim(chains, group_index * col_count, col_count)
    pair_norm, pair_inv = norm_rows(pair.astype(jnp.float32))
    projected = jnp.einsum(
        "ijc,ch->hij", pair_norm.astype(jnp.bfloat16), w_pair, preferred_element_type=jnp.float32
    )
    same_chain = (chain_rows[:, None] == chain_cols[None, :]).astype(jnp.float32)
    bias_block = (projected + chain_gain[:, None, None] * same_chain[None]).astype(jnp.bfloat16)
    bias_keys = lax.all_gather(bias_block, "rows", axis=1, tiled=True)
    single_norm, single_inv = norm_rows(single.astype(jnp.float32))
    single_b = single_norm.astype(jnp.bfloat16)
    cond_gamma = jax.nn.sigmoid(jnp.dot(single_b, w_gamma, preferred_element_type=jnp.float32))
    cond_beta = jnp.dot(single_b, w_beta, preferred_element_type=jnp.float32)
    out_gate = jax.nn.sigmoid(jnp.dot(single_b, w_outgate, preferred_element_type=jnp.float32))
    noised_f = noised.astype(jnp.float32)
    noised_norm, noised_inv = norm_rows(noised_f)
    x_b = (noised_norm * cond_gamma[None] + cond_beta[None]).astype(jnp.bfloat16)
    queries = project(x_b, w_query).astype(jnp.bfloat16)
    keys_own = project(x_b, w_key).astype(jnp.bfloat16)
    values_own = project(x_b, w_value).astype(jnp.bfloat16)
    queries_all = lax.all_gather(queries, "grp", axis=1, tiled=True)
    query_heads = queries_all.reshape(sample_count, token_total, head_count, head_size)
    key_heads = keys_own.reshape(sample_count, col_count, head_count, head_size)
    value_heads = values_own.reshape(sample_count, col_count, head_count, head_size)
    scores = (
        jnp.einsum("sihe,sjhe->shij", query_heads, key_heads, preferred_element_type=jnp.float32)
        * score_scale
        + bias_keys.astype(jnp.float32)[None]
    )
    exp_scores = jnp.exp(scores)
    exp_total = lax.psum(jnp.sum(exp_scores, axis=-1).astype(jnp.bfloat16), "grp").astype(
        jnp.float32
    )
    attn_prob = exp_scores / exp_total[..., None]
    prob_b = attn_prob.astype(jnp.bfloat16)
    attended_part = jnp.einsum(
        "shij,sjhe->sihe", prob_b, value_heads, preferred_element_type=jnp.float32
    )
    attended_part = attended_part.reshape(sample_count, token_total, model_width)
    attended = lax.psum_scatter(
        attended_part.astype(jnp.bfloat16), "grp", scatter_dimension=1, tiled=True
    )
    block_update = project(attended, w_out)
    updated = (noised_f + out_gate[None] * block_update).astype(jnp.bfloat16)
    grad_out = cotangent.astype(jnp.float32)
    gate_part = jnp.sum(grad_out * block_update, axis=0)
    grad_update = (grad_out * out_gate[None]).astype(jnp.bfloat16)
    grad_attn = project_back(grad_update, w_out).astype(jnp.bfloat16)
    grads_all = lax.all_gather(grad_attn, "grp", axis=1, tiled=True)
    grad_heads = grads_all.reshape(sample_count, token_total, head_count, head_size)
    grad_prob = jnp.einsum(
        "sihe,sjhe->shij", grad_heads, value_heads, preferred_element_type=jnp.float32
    )
    row_delta = lax.psum(
        jnp.sum(attn_prob * grad_prob, axis=-1).astype(jnp.bfloat16), "grp"
    ).astype(jnp.float32)
    grad_score = attn_prob * (grad_prob - row_delta[..., None])
    score_b = grad_score.astype(jnp.bfloat16)
    query_part = (
        jnp.einsum("shij,sjhe->sihe", score_b, key_heads, preferred_element_type=jnp.float32)
        * score_scale
    )
    query_part = query_part.reshape(sample_count, token_total, model_width)
    grad_query = lax.psum_scatter(
        query_part.astype(jnp.bfloat16), "grp", scatter_dimension=1, tiled=True
    )
    grad_key = (
        jnp.einsum("shij,sihe->sjhe", score_b, query_heads, preferred_element_type=jnp.float32)
        * score_scale
    )
    grad_value = jnp.einsum(
        "shij,sihe->sjhe", prob_b, grad_heads, preferred_element_type=jnp.float32
    )
    grad_key = grad_key.reshape(sample_count, col_count, model_width).astype(jnp.bfloat16)
    grad_value = grad_value.reshape(sample_count, col_count, model_width).astype(jnp.bfloat16)
    grad_input = (
        project_back(grad_query, w_query)
        + project_back(grad_key, w_key)
        + project_back(grad_value, w_value)
    )
    gamma_part = jnp.sum(grad_input * noised_norm, axis=0)
    beta_part = jnp.sum(grad_input, axis=0)
    gamma_sum, beta_sum, gate_sum = lax.psum((gamma_part, beta_part, gate_part), "rows")
    pre_gamma = (gamma_sum * cond_gamma * (1.0 - cond_gamma)).astype(jnp.bfloat16)
    pre_gate = (gate_sum * out_gate * (1.0 - out_gate)).astype(jnp.bfloat16)
    grad_snorm = jnp.dot(pre_gamma, w_gamma.T, preferred_element_type=jnp.float32)
    grad_snorm = grad_snorm + jnp.dot(
        beta_sum.astype(jnp.bfloat16), w_beta.T, preferred_element_type=jnp.float32
    )
    grad_snorm = grad_snorm + jnp.dot(pre_gate, w_outgate.T, preferred_element_type=jnp.float32)
    d_single = norm_back(grad_snorm, single_norm, single_inv)
    bias_part = jnp.sum(score_b, axis=0, dtype=jnp.float32)
    bias_own = lax.psum_scatter(bias_part, "rows", scatter_dimension=1, tiled=True)
    bias_grad = (bias_own * token_total).astype(jnp.bfloat16)
    grad_pairn = jnp.einsum("hij,ch->ijc", bias_grad, w_pair, preferred_element_type=jnp.float32)
    d_pair = norm_back(grad_pairn, pair_norm, pair_inv).astype(jnp.bfloat16)
    return (updated, d_single, d_pair)


def solution(mesh):
    in_specs = (
        P("grp", None),
        P("rows", "grp", None),
        P(),
        P("rows", "grp", None),
        P(),
        P(),
        P(),
        P(),
        P(),
        P(),
        P(),
        P(),
        P(),
        P("rows", "grp", None),
    )
    out_specs = (P("rows", "grp", None), P("grp", None), P("rows", "grp", None))
    groups = mesh.shape["grp"]
    row_total = mesh.shape["rows"]

    def on_device(*args):
        pair, noised, w_pair = args[1], args[3], args[11]
        fits = (
            pair.shape[0] % 32 == 0
            and pair.shape[1] % pair.shape[0] == 0
            and row_total == 8
            and noised.shape[0] == 1
            and noised.shape[1] % 64 == 0
            and w_pair.shape[1] % (2 * groups) == 0
        )
        if fits:
            return split_heads(*args, groups=groups, row_total=row_total)
        return split_keys(*args)

    return jax.shard_map(
        on_device, mesh=mesh, in_specs=in_specs, out_specs=out_specs, check_vma=False
    )
```

```python
import functools
import math

import jax
import jax.numpy as jnp
from jax import lax
from jax.experimental import pallas as pl
from jax.experimental.pallas import tpu as pltpu
from jax.sharding import PartitionSpec as P

EPSILON = 1e-05
BF16 = jnp.bfloat16
F32 = jnp.float32
VMEM_LIMIT = 56 * 1024 * 1024


def norm_rows(values):
    center = values - jnp.mean(values, axis=-1, keepdims=True)
    inverse = lax.rsqrt(jnp.mean(center * center, axis=-1, keepdims=True) + EPSILON)
    return (center * inverse, inverse)


def norm_back(grad_in, normed, inverse):
    grad_mean = jnp.mean(grad_in, axis=-1, keepdims=True)
    cross_mean = jnp.mean(grad_in * normed, axis=-1, keepdims=True)
    return inverse * (grad_in - grad_mean - normed * cross_mean)


def mm(left, right):
    return lax.dot_general(left, right, (((1,), (0,)), ((), ())), preferred_element_type=F32)


def mm_nt(left, right):
    return lax.dot_general(left, right, (((1,), (1,)), ((), ())), preferred_element_type=F32)


def mm_tn(left, right):
    return lax.dot_general(left, right, (((0,), (0,)), ((), ())), preferred_element_type=F32)


def sigmoid(values):
    return 1.0 / (1.0 + jnp.exp(-values))


def params():
    return pltpu.CompilerParams(vmem_limit_bytes=VMEM_LIMIT)


def smem():
    return pl.BlockSpec(memory_space=pltpu.SMEM)


def vmem():
    return pl.BlockSpec(memory_space=pltpu.VMEM)


def project_kernel(
    group_ref,
    single_ref,
    noised_ref,
    cot_ref,
    w_gamma_ref,
    w_beta_ref,
    w_outgate_ref,
    w_query_ref,
    w_key_ref,
    w_value_ref,
    w_out_ref,
    *rest,
    groups,
    calls,
):
    send_refs = rest[:groups]
    gamma_ref, gate_ref, stage_ref = rest[groups:]
    width = stage_ref.shape[2]
    part = width // (4 * calls)
    group_own = group_ref[0]
    single_norm, _ = norm_rows(single_ref[...].astype(F32))
    single_b = single_norm.astype(BF16)
    cond_gamma = sigmoid(mm(single_b, w_gamma_ref[...]))
    gamma_ref[...] = cond_gamma
    out_gate = sigmoid(mm(single_b, w_outgate_ref[...]))
    gate_ref[...] = out_gate
    cond_beta = mm(single_b, w_beta_ref[...])
    noised_norm, _ = norm_rows(noised_ref[...].astype(F32))
    x_b = (noised_norm * cond_gamma + cond_beta).astype(BF16)

    def put(kind, values):
        rounded = values.astype(BF16)
        for group in range(groups):
            slot = lax.rem(group - group_own + groups, groups)
            for call in range(calls):
                feature = (group * calls + call) * part
                lane = (call * 4 + kind) * part
                stage_ref[slot, :, lane : lane + part] = rounded[:, feature : feature + part]

    put(0, mm(x_b, w_query_ref[...]))
    put(1, mm(x_b, w_key_ref[...]))
    put(2, mm(x_b, w_value_ref[...]))
    grad_update = (cot_ref[...].astype(F32) * out_gate).astype(BF16)
    put(3, mm_nt(grad_update, w_out_ref[...]))
    for slot in range(groups):
        send_refs[slot][...] = stage_ref[slot]


def lane_tiles(cols):
    return [(tile, tile * 128, min(cols, tile * 128 + 128)) for tile in range(-(-cols // 128))]


def mean_matrix(channels):
    first = lax.broadcasted_iota(jnp.int32, (2 * channels, 2 * channels), 0) >= channels
    second = lax.broadcasted_iota(jnp.int32, (2 * channels, 2 * channels), 1) >= channels
    return jnp.where(first == second, 1.0 / channels, 0.0).astype(BF16)


def center_rows(pair_ref, first, batch, means):
    _, _, cols, channels = pair_ref.shape
    both = jnp.concatenate(
        [pair_ref[side, pl.ds(first, batch)].reshape(batch * cols, channels) for side in range(2)],
        axis=1,
    )
    return both.astype(F32) - mm(both, means)


def bias_kernel(
    group_ref,
    rows_ref,
    chains_ref,
    gain_ref,
    pair_ref,
    w_pair_ref,
    cols_ref,
    *rest,
    groups,
    batch,
):
    send_refs = rest[:groups]
    stats_ref, flat_ref, gains_ref, stage_ref = rest[groups:]
    _, step, cols, channels = pair_ref.shape
    heads = gain_ref.shape[0]
    per_group = heads // groups
    half = step * pl.num_programs(0)
    group_own = group_ref[0]
    row_base = rows_ref[0] * 2 * half + pl.program_id(0) * step
    means = mean_matrix(channels)
    weight = w_pair_ref[...]
    left = jnp.concatenate(
        [
            jnp.concatenate([weight, jnp.zeros((heads, channels), BF16)], axis=1),
            jnp.concatenate(
                [
                    jnp.zeros((heads, channels), BF16),
                    jnp.full((heads, channels), 1.0 / channels, BF16),
                ],
                axis=1,
            ),
        ],
        axis=0,
    )
    chain_cols = cols_ref[:, :cols]
    for group in range(1, groups):
        here = cols_ref[:, group * cols : (group + 1) * cols]
        chain_cols = jnp.where(group_own == group, here, chain_cols)
    for head in range(heads):
        gains_ref[head : head + 1, :] = jnp.full((1, cols), gain_ref[head], F32)

    def some_rows(index, carry):
        first = index * batch
        center = center_rows(pair_ref, first, batch, means)
        center_b = center.astype(BF16)
        square = (center * center).astype(BF16)
        for inner in range(batch):
            rows = slice(inner * cols, (inner + 1) * cols)
            for side in range(2):
                lanes = slice(side * channels, (side + 1) * channels)
                right = jnp.concatenate([center_b[rows, lanes], square[rows, lanes]], axis=1)
                sums = mm_nt(left, right)
                inverse = lax.rsqrt(sums[heads : heads + 8] + EPSILON)
                projected = sums[:heads] * inverse[:1]
                stats_ref[side, first + inner, :heads, :] = projected
                stats_ref[side, first + inner, heads:, :] = inverse
                chain = chains_ref[row_base + side * half + first + inner]
                same = (chain_cols == chain).astype(F32)
                values = projected + gains_ref[...] * same
                for tile, start, end in lane_tiles(cols):
                    piece = values[:, start:end]
                    if end - start < 128:
                        blank = jnp.zeros((heads, 128 - end + start), F32)
                        piece = jnp.concatenate([piece, blank], axis=1)
                    flat_ref[side, tile, pl.ds(first + inner, heads, stride=step), :] = piece
        return carry

    lax.fori_loop(0, step // batch, some_rows, 0)
    for head in range(heads):
        slot = lax.rem(head // per_group - group_own + groups, groups)
        values = jnp.concatenate(
            [
                flat_ref[side, tile, head * step : (head + 1) * step, : end - start]
                for side in range(2)
                for tile, start, end in lane_tiles(cols)
            ],
            axis=1,
        )
        stage_ref[slot, head % per_group] = values.astype(BF16)
    for slot in range(groups):
        send_refs[slot][...] = stage_ref[slot]


def pair_bias(pair, w_pair, chain_gain, chains, group_index, row_index, groups):
    rows, cols, channels = pair.shape
    heads = w_pair.shape[1]
    per_group = heads // groups
    half = rows // 2
    step = 16
    tiles = -(-cols // 128)
    *sends, stats = pl.pallas_call(
        functools.partial(bias_kernel, groups=groups, batch=4),
        grid=(half // step,),
        in_specs=[
            smem(),
            smem(),
            smem(),
            smem(),
            pl.BlockSpec((2, step, cols, channels), lambda t: (0, t, 0, 0)),
            pl.BlockSpec((heads, channels), lambda t: (0, 0)),
            pl.BlockSpec((1, groups * cols), lambda t: (0, 0)),
        ],
        out_specs=[
            pl.BlockSpec((per_group, step, 2 * cols), lambda t: (0, t, 0)) for _ in range(groups)
        ]
        + [pl.BlockSpec((2, step, heads + 8, cols), lambda t: (0, t, 0, 0))],
        out_shape=[
            jax.ShapeDtypeStruct((per_group, half, 2 * cols), BF16) for _ in range(groups)
        ]
        + [jax.ShapeDtypeStruct((2, half, heads + 8, cols), F32)],
        scratch_shapes=[
            pltpu.VMEM((2, tiles, heads * step, 128), F32),
            pltpu.VMEM((heads, cols), F32),
            pltpu.VMEM((groups, per_group, step, 2 * cols), BF16),
        ],
        compiler_params=params(),
    )(
        group_index,
        row_index,
        chains,
        chain_gain,
        pair.reshape(2, half, cols, channels),
        w_pair.T,
        chains.reshape(1, groups * cols),
    )
    return sends, stats


def pair_back_kernel(
    group_ref, pair_ref, stats_ref, w_pair_ref, *rest, groups, calls, factor, batch
):
    grad_refs = rest[: groups * calls]
    out_ref, flat_ref = rest[groups * calls :]
    _, step, cols, channels = pair_ref.shape
    per_call = grad_refs[0].shape[0]
    heads = groups * calls * per_call
    group_own = group_ref[0]
    means = mean_matrix(channels)
    weight = w_pair_ref[...].astype(F32)
    weight = weight - jnp.mean(weight, axis=-1, keepdims=True)
    high = weight.astype(BF16)
    low = (weight - high.astype(F32)).astype(BF16)
    weights = jnp.concatenate([high, low, jnp.zeros((16, channels), BF16)], axis=0)
    spread = lax.broadcasted_iota(jnp.int32, (2 * heads + 16, channels), 0)
    spread = ((spread >= 2 * heads) & (spread < 2 * heads + 2)).astype(F32).astype(BF16)
    weights = jnp.concatenate([weights, spread], axis=1)
    blank = jnp.zeros((14, cols), F32)
    for number in range(groups * calls):
        call, slot = divmod(number, groups)
        source = lax.rem(group_own + slot, groups) * calls + call
        for head in range(per_call):
            values = grad_refs[number][head].astype(F32)
            top = pl.multiple_of((source * per_call + head) * step, step)
            for side in range(2):
                for tile, start, end in lane_tiles(cols):
                    flat_ref[side, tile, pl.ds(top, step), : end - start] = values[
                        :, side * cols + start : side * cols + end
                    ]

    def some_rows(index, carry):
        first = index * batch
        center = center_rows(pair_ref, first, batch, means)
        for side in range(2):
            lefts = []
            for inner in range(batch):
                grads = jnp.concatenate(
                    [
                        flat_ref[side, tile, pl.ds(first + inner, heads, stride=step), :][
                            :, : end - start
                        ]
                        for tile, start, end in lane_tiles(cols)
                    ],
                    axis=1,
                )
                projected = stats_ref[side, first + inner, :heads, :]
                inverse = stats_ref[side, first + inner, heads : heads + 1, :]
                cross = jnp.sum(grads * projected, axis=0, keepdims=True) * (1.0 / channels)
                scaled = grads * (inverse * factor)
                cross = cross * (inverse * inverse * factor)
                cross_high = cross.astype(BF16).astype(F32)
                lefts.append(
                    jnp.concatenate(
                        [scaled, scaled, cross_high, cross - cross_high, blank], axis=0
                    )
                )
            for inner in range(batch):
                rows = slice(inner * cols, (inner + 1) * cols)
                lanes = slice(side * channels, (side + 1) * channels)
                both = mm_tn(lefts[inner].astype(BF16), weights)
                out_ref[side, first + inner] = (
                    both[:, :channels] - center[rows, lanes] * both[:, channels:]
                ).astype(BF16)
        return carry

    lax.fori_loop(0, step // batch, some_rows, 0)


def pair_back(pair, stats, grads, w_pair, group_index, groups, factor):
    rows, cols, channels = pair.shape
    per_call = grads[0].shape[0]
    heads = len(grads) * per_call
    half = rows // 2
    step = 16
    tiles = -(-cols // 128)
    out = pl.pallas_call(
        functools.partial(
            pair_back_kernel, groups=groups, calls=len(grads) // groups, factor=factor, batch=4
        ),
        grid=(half // step,),
        in_specs=[
            smem(),
            pl.BlockSpec((2, step, cols, channels), lambda t: (0, t, 0, 0)),
            pl.BlockSpec((2, step, heads + 8, cols), lambda t: (0, t, 0, 0)),
            pl.BlockSpec((heads, channels), lambda t: (0, 0)),
        ]
        + [pl.BlockSpec((per_call, step, 2 * cols), lambda t: (0, t, 0)) for _ in grads],
        out_specs=pl.BlockSpec((2, step, cols, channels), lambda t: (0, t, 0, 0)),
        out_shape=jax.ShapeDtypeStruct((2, half, cols, channels), BF16),
        scratch_shapes=[pltpu.VMEM((2, tiles, heads * step, 128), F32)],
        compiler_params=params(),
    )(group_index, pair.reshape(2, half, cols, channels), stats, w_pair.T, *grads)
    return out.reshape(rows, cols, channels)


def unit_order(heads):
    first, second = range(heads // 2), range(heads // 2, heads)
    order = [(0, head) for head in range(heads)]
    order += [(1, head) for head in first] + [(3, head) for head in first]
    order += [(2, head) for head in second] + [(3, head) for head in second]
    order += [(2, head) for head in first] + [(1, head) for head in second]
    return order


def attention_kernel(group_ref, row_ref, *rest, groups, row_parts, head_size, row_block):
    bias_refs = rest[:2]
    acts_refs = rest[2 : 2 + groups]
    rest = rest[2 + groups :]
    out_refs = rest[:groups]
    (
        keep_ref,
        give_ref,
        query_ref,
        keys_ref,
        values_ref,
        grads_ref,
        query_t_ref,
        keys_t_ref,
        values_t_ref,
        grads_t_ref,
        bias_full,
        score_full,
        att_sum,
        gq_sum,
        gk_sum,
        gv_sum,
    ) = rest[groups:]
    head = pl.program_id(0)
    heads = keep_ref.shape[0] * 2 // row_parts
    group_own = group_ref[0]
    cols, width = acts_refs[0].shape
    tokens = groups * cols
    part = width // 4
    half = bias_refs[0].shape[3]
    scale = 1.0 / math.sqrt(head_size)
    extra = att_sum.shape[1] - part
    plain = (query_ref, keys_ref, values_ref, grads_ref)
    turned = (query_t_ref, keys_t_ref, values_t_ref, grads_t_ref)

    @pl.when(head == 0)
    def _():
        for kind in range(4):
            for slot in range(groups):
                plain[kind][slot * cols : (slot + 1) * cols, :] = acts_refs[slot][
                    :, kind * part : (kind + 1) * part
                ]
            turned[kind][...] = plain[kind][...].T
        att_sum[...] = jnp.zeros_like(att_sum)
        gq_sum[...] = jnp.zeros_like(gq_sum)

    def places(row_part):
        first = row_part * (2 * half)
        slot = lax.rem(group_own - first // cols + groups, groups)
        for side in range(2):
            top = slot * cols + lax.rem(first, cols) + side * half
            top = pl.multiple_of(top, 16)
            for column in range(groups):
                yield column, side, pl.ds(top, half)

    for other in range(2):
        for chip in range(row_parts // 2):
            for column, side, rows in places(2 * chip + (row_ref[0] + other) % 2):
                bias_full[rows, column * cols : (column + 1) * cols] = bias_refs[other][
                    chip, column, 0, :, side * cols : (side + 1) * cols
                ]

    lane = lax.broadcasted_iota(jnp.int32, (1, part), 1)
    mine = (lane >= head * head_size) & (lane < (head + 1) * head_size)
    zero = jnp.zeros((), BF16)
    keys_m = jnp.where(mine, keys_ref[...], zero)
    values_m = jnp.concatenate(
        [jnp.where(mine, values_ref[...], zero), jnp.ones((tokens, extra), BF16)], axis=1
    )
    feature = pl.multiple_of(head * head_size, head_size)
    query_t = query_t_ref[pl.ds(feature, head_size), :]
    grads_t = grads_t_ref[pl.ds(feature, head_size), :]
    gk_t = jnp.zeros((head_size, tokens), F32)
    gv_t = jnp.zeros((head_size, tokens), F32)
    for top in range(0, tokens, row_block):
        rows = slice(top, top + row_block)
        query = jnp.where(mine, query_ref[rows, :], zero)
        grads = jnp.where(mine, grads_ref[rows, :], zero)
        scores = mm(query, keys_t_ref[...]) * scale + bias_full[rows, :].astype(F32)
        weights = jnp.exp(scores)
        attended = mm(weights.astype(BF16), values_m)
        inverse = 1.0 / attended[:, part : part + 1]
        attended = attended[:, :part] * inverse
        att_sum[rows, :part] += attended
        delta = jnp.sum(attended * grads.astype(F32), axis=-1, keepdims=True)
        prob = weights * inverse
        grad_prob = mm(grads, values_t_ref[...])
        score = (prob * (grad_prob - delta)).astype(BF16)
        score_full[rows, :] = score
        gq_sum[rows, :] += mm(score, keys_m)
        gk_t = gk_t + mm(query_t[:, rows], score)
        gv_t = gv_t + mm(grads_t[:, rows], prob.astype(BF16))
    gk_sum[pl.ds(feature, head_size), :] = gk_t
    gv_sum[pl.ds(feature, head_size), :] = gv_t

    for other in range(row_parts):
        dbias_ref = give_ref if other % 2 else keep_ref
        unit = 0
        for place, (chip, unit_head) in enumerate(unit_order(heads)):
            if chip == other // 2:
                unit = jnp.where(head == unit_head, place, unit)
        for column, side, rows in places(row_ref[0] ^ other):
            dbias_ref[unit, column, :, side * cols : (side + 1) * cols] = score_full[
                rows, column * cols : (column + 1) * cols
            ]

    @pl.when(head == heads - 1)
    def _():
        results = (
            gq_sum[...] * scale,
            (gk_sum[...] * scale).T,
            gv_sum[...].T,
            att_sum[:, :part],
        )
        for kind, values in enumerate(results):
            rounded = values.astype(BF16)
            for slot in range(groups):
                out_refs[slot][:, kind * part : (kind + 1) * part] = rounded[
                    slot * cols : (slot + 1) * cols
                ]


def attention(group_index, row_index, acts, bias, head_size):
    groups = len(acts)
    row_parts = 2 * bias[0].shape[0]
    cols, width = acts[0].shape
    tokens = groups * cols
    part = width // 4
    _, _, heads, half, lanes = bias[0].shape
    spread = pl.BlockSpec((row_parts // 2, groups, 1, half, lanes), lambda h: (0, 0, h, 0, 0))
    row_block = 256 if tokens % 256 == 0 else cols
    padded = (part // 128 + 1) * 128
    units = (row_parts // 2 * heads, groups, half, lanes)
    *grads, keep, give = pl.pallas_call(
        functools.partial(
            attention_kernel,
            groups=groups,
            row_parts=row_parts,
            head_size=head_size,
            row_block=row_block,
        ),
        grid=(heads,),
        in_specs=[smem(), smem()]
        + [spread] * 2
        + [pl.BlockSpec((cols, width), lambda h: (0, 0))] * groups,
        out_specs=[pl.BlockSpec((cols, width), lambda h: (0, 0))] * groups
        + [pl.BlockSpec(units, lambda h: (0, 0, 0, 0))] * 2,
        out_shape=[jax.ShapeDtypeStruct((cols, width), BF16)] * groups
        + [jax.ShapeDtypeStruct(units, BF16)] * 2,
        scratch_shapes=[pltpu.VMEM((tokens, part), BF16) for _ in range(4)]
        + [pltpu.VMEM((part, tokens), BF16) for _ in range(4)]
        + [
            pltpu.VMEM((tokens, tokens), BF16),
            pltpu.VMEM((tokens, tokens), BF16),
            pltpu.VMEM((tokens, padded), F32),
            pltpu.VMEM((tokens, part), F32),
            pltpu.VMEM((part, tokens), F32),
            pltpu.VMEM((part, tokens), F32),
        ],
        compiler_params=params(),
    )(group_index, row_index, *bias, *acts)
    return grads, keep, give


def add_kernel(*refs, terms):
    inputs = refs[: len(refs) - len(terms)]
    outputs = refs[len(refs) - len(terms) :]
    for out_ref, pairs in zip(outputs, terms):
        blocks = out_ref.shape[0]
        total = None
        for number, first in pairs:
            value = inputs[number][first : first + blocks].astype(F32)
            total = value if total is None else total + value
        out_ref[...] = total.astype(BF16)


def add_blocks(inputs, blocks, terms):
    shapes = [(count,) + inputs[0].shape[1:] for count in blocks]
    return pl.pallas_call(
        functools.partial(add_kernel, terms=terms),
        in_specs=[vmem()] * len(inputs),
        out_shape=[jax.ShapeDtypeStruct(shape, BF16) for shape in shapes],
        compiler_params=params(),
    )(*inputs)


def add_last_kernel(keep_ref, got_ref, near_ref, far_ref, near_two_ref, far_two_ref, *out_refs):
    heads = out_refs[0].shape[0]
    half = heads // 2
    for head in range(heads):
        first, second = (near_ref, far_two_ref) if head < half else (far_ref, near_two_ref)
        inside = head if head < half else head - half
        total = keep_ref[head].astype(F32) + got_ref[head].astype(F32)
        total += first[inside].astype(F32) + second[inside].astype(F32)
        total = total.astype(BF16)
        for slot, out_ref in enumerate(out_refs):
            out_ref[head] = total[slot]


def finish_kernel(
    group_ref,
    single_ref,
    noised_ref,
    cot_ref,
    gamma_ref,
    gate_ref,
    w_gamma_ref,
    w_beta_ref,
    w_outgate_ref,
    w_query_ref,
    w_key_ref,
    w_value_ref,
    w_out_ref,
    *rest,
    groups,
    calls,
):
    got_refs = rest[: groups * calls]
    updated_ref, d_single_ref, stage_ref = rest[groups * calls :]
    width = stage_ref.shape[3]
    part = width // 4
    for slot in range(groups):
        for call in range(calls):
            stage_ref[lax.rem(group_ref[0] + slot, groups), call] = got_refs[
                call * groups + slot
            ][...]

    def take(kind):
        return jnp.concatenate(
            [
                stage_ref[group, call, :, kind * part : (kind + 1) * part]
                for group in range(groups)
                for call in range(calls)
            ],
            axis=1,
        )

    out_gate = gate_ref[...]
    cond_gamma = gamma_ref[...]
    block_update = mm(take(3), w_out_ref[...])
    noised = noised_ref[...].astype(F32)
    updated_ref[...] = (noised + out_gate * block_update).astype(BF16)
    gate_part = cot_ref[...].astype(F32) * block_update
    pre_gate = (gate_part * out_gate * (1.0 - out_gate)).astype(BF16)
    grad_input = mm_nt(take(0), w_query_ref[...])
    grad_input += mm_nt(take(1), w_key_ref[...])
    grad_input += mm_nt(take(2), w_value_ref[...])
    noised_norm, _ = norm_rows(noised)
    pre_gamma = (grad_input * noised_norm * cond_gamma * (1.0 - cond_gamma)).astype(BF16)
    grad_snorm = mm_nt(pre_gamma, w_gamma_ref[...])
    grad_snorm += mm_nt(grad_input.astype(BF16), w_beta_ref[...])
    grad_snorm += mm_nt(pre_gate, w_outgate_ref[...])
    single_norm, single_inv = norm_rows(single_ref[...].astype(F32))
    d_single_ref[...] = norm_back(grad_snorm, single_norm, single_inv)


def swap_groups(sends, direction):
    groups = len(sends)
    got = [sends[0]]
    for shift in range(1, groups):
        perm = [(index, (index + direction * shift) % groups) for index in range(groups)]
        got.append(lax.ppermute(sends[shift], "grp", perm))
    return got


def flip_rows(values, bits, row_total):
    return lax.ppermute(values, "rows", [(index, index ^ bits) for index in range(row_total)])


def gather_rows(own, acts, row_total):
    groups = [list(range(core, row_total, 2)) for core in range(2)]
    mine = lax.all_gather(own, "rows", axis_index_groups=groups)
    mine, acts = lax.optimization_barrier((mine, acts))
    return (mine, flip_rows(mine, 1, row_total)), acts


def scatter_rows(keep, give, grads, row_total):
    got = flip_rows(give, 1, row_total)
    units, groups, half, lanes = keep.shape
    heads = units // 4
    part = heads // 2
    near_send, far_send = add_blocks(
        [keep, got],
        [heads, heads],
        [[(0, heads), (1, heads)], [(0, 2 * heads), (1, 2 * heads)]],
    )
    near = flip_rows(near_send, 2, row_total)
    far = flip_rows(far_send, 4, row_total)
    far_two, near_two = add_blocks(
        [keep, got, near, far],
        [part, part],
        [
            [(0, 3 * heads), (1, 3 * heads), (2, part)],
            [(0, 3 * heads + part), (1, 3 * heads + part), (3, part)],
        ],
    )
    far_two, near_two, grads = lax.optimization_barrier((far_two, near_two, grads))
    far_two = flip_rows(far_two, 4, row_total)
    near_two = flip_rows(near_two, 2, row_total)
    sums = pl.pallas_call(
        add_last_kernel,
        grid=(1,),
        in_specs=[
            pl.BlockSpec((count, groups, half, lanes), lambda t: (0, 0, 0, 0))
            for count in (heads, heads, heads, heads, part, part)
        ],
        out_specs=[pl.BlockSpec((heads, half, lanes), lambda t: (0, 0, 0))] * groups,
        out_shape=[jax.ShapeDtypeStruct((heads, half, lanes), BF16)] * groups,
        compiler_params=params(),
    )(keep, got, near, far, near_two, far_two)
    return sums, grads


def sum_rows(values, row_total):
    bit = 1
    while bit < row_total:
        mine = values.astype(BF16)
        values = mine.astype(F32) + flip_rows(mine, bit, row_total).astype(F32)
        bit *= 2
    return values


def split_heads(
    single,
    pair,
    chains,
    noised,
    w_gamma,
    w_beta,
    w_outgate,
    w_query,
    w_key,
    w_value,
    w_out,
    w_pair,
    chain_gain,
    cotangent,
    *,
    groups,
    row_total,
):
    cols, _ = single.shape
    tokens = chains.shape[0]
    width = noised.shape[2]
    head_size = width // w_pair.shape[1]
    calls = 1
    row_index = lax.axis_index("rows").reshape(1)
    group_index = lax.axis_index("grp").reshape(1)
    bias_send, stats = pair_bias(
        pair, w_pair, chain_gain, chains, group_index, row_index, groups
    )
    bias_got = swap_groups(bias_send, 1)
    noised = noised[0]
    cotangent = cotangent[0]
    *acts_send, cond_gamma, out_gate = pl.pallas_call(
        functools.partial(project_kernel, groups=groups, calls=calls),
        in_specs=[smem()] + [vmem()] * 10,
        out_shape=[
            jax.ShapeDtypeStruct((cols, 4 * width // groups), BF16) for _ in range(groups)
        ]
        + [
            jax.ShapeDtypeStruct((cols, width), F32),
            jax.ShapeDtypeStruct((cols, width), F32),
        ],
        scratch_shapes=[pltpu.VMEM((groups, cols, 4 * width // groups), BF16)],
        compiler_params=params(),
    )(
        group_index,
        single,
        noised,
        cotangent,
        w_gamma,
        w_beta,
        w_outgate,
        w_query,
        w_key,
        w_value,
        w_out,
    )
    bias_got, acts_send = lax.optimization_barrier((bias_got, acts_send))
    acts = swap_groups(acts_send, 1)
    bias_all, acts = gather_rows(jnp.stack(bias_got), acts, row_total)
    grads_send, keep, give = attention(group_index, row_index, acts, bias_all, head_size)
    grads = swap_groups(grads_send, -1)
    dbias_own, grads = scatter_rows(keep, give, grads, row_total)
    dbias_back = swap_groups(dbias_own, -1)
    updated, d_part = pl.pallas_call(
        functools.partial(finish_kernel, groups=groups, calls=calls),
        in_specs=[smem()] + [vmem()] * (12 + groups * calls),
        out_shape=[
            jax.ShapeDtypeStruct((cols, width), BF16),
            jax.ShapeDtypeStruct(single.shape, F32),
        ],
        scratch_shapes=[pltpu.VMEM((groups, calls, cols, 4 * width // (groups * calls)), BF16)],
        compiler_params=params(),
    )(
        group_index,
        single,
        noised,
        cotangent,
        cond_gamma,
        out_gate,
        w_gamma,
        w_beta,
        w_outgate,
        w_query,
        w_key,
        w_value,
        w_out,
        *grads,
    )
    d_single = sum_rows(d_part, row_total)
    d_pair = pair_back(pair, stats, dbias_back, w_pair, group_index, groups, float(tokens))
    return (updated[None], d_single, d_pair)


def project(acts, weight):
    return jnp.einsum("std,de->ste", acts, weight, preferred_element_type=F32)


def project_back(acts, weight):
    return jnp.einsum("ste,de->std", acts, weight, preferred_element_type=F32)


def split_keys(
    single,
    pair,
    chains,
    noised,
    w_gamma,
    w_beta,
    w_outgate,
    w_query,
    w_key,
    w_value,
    w_out,
    w_pair,
    chain_gain,
    cotangent,
):
    col_count = single.shape[0]
    row_count = pair.shape[0]
    head_count = w_pair.shape[1]
    model_width = w_query.shape[0]
    head_size = model_width // head_count
    sample_count = noised.shape[0]
    token_total = chains.shape[0]
    score_scale = 1.0 / math.sqrt(head_size)
    row_index = lax.axis_index("rows")
    group_index = lax.axis_index("grp")
    chain_rows = lax.dynamic_slice_in_dim(chains, row_index * row_count, row_count)
    chain_cols = lax.dynamic_slice_in_dim(chains, group_index * col_count, col_count)
    pair_norm, pair_inv = norm_rows(pair.astype(jnp.float32))
    projected = jnp.einsum(
        "ijc,ch->hij", pair_norm.astype(jnp.bfloat16), w_pair, preferred_element_type=jnp.float32
    )
    same_chain = (chain_rows[:, None] == chain_cols[None, :]).astype(jnp.float32)
    bias_block = (projected + chain_gain[:, None, None] * same_chain[None]).astype(jnp.bfloat16)
    bias_keys = lax.all_gather(bias_block, "rows", axis=1, tiled=True)
    single_norm, single_inv = norm_rows(single.astype(jnp.float32))
    single_b = single_norm.astype(jnp.bfloat16)
    cond_gamma = jax.nn.sigmoid(jnp.dot(single_b, w_gamma, preferred_element_type=jnp.float32))
    cond_beta = jnp.dot(single_b, w_beta, preferred_element_type=jnp.float32)
    out_gate = jax.nn.sigmoid(jnp.dot(single_b, w_outgate, preferred_element_type=jnp.float32))
    noised_f = noised.astype(jnp.float32)
    noised_norm, noised_inv = norm_rows(noised_f)
    x_b = (noised_norm * cond_gamma[None] + cond_beta[None]).astype(jnp.bfloat16)
    queries = project(x_b, w_query).astype(jnp.bfloat16)
    keys_own = project(x_b, w_key).astype(jnp.bfloat16)
    values_own = project(x_b, w_value).astype(jnp.bfloat16)
    queries_all = lax.all_gather(queries, "grp", axis=1, tiled=True)
    query_heads = queries_all.reshape(sample_count, token_total, head_count, head_size)
    key_heads = keys_own.reshape(sample_count, col_count, head_count, head_size)
    value_heads = values_own.reshape(sample_count, col_count, head_count, head_size)
    scores = (
        jnp.einsum("sihe,sjhe->shij", query_heads, key_heads, preferred_element_type=jnp.float32)
        * score_scale
        + bias_keys.astype(jnp.float32)[None]
    )
    exp_scores = jnp.exp(scores)
    exp_total = lax.psum(jnp.sum(exp_scores, axis=-1).astype(jnp.bfloat16), "grp").astype(
        jnp.float32
    )
    attn_prob = exp_scores / exp_total[..., None]
    prob_b = attn_prob.astype(jnp.bfloat16)
    attended_part = jnp.einsum(
        "shij,sjhe->sihe", prob_b, value_heads, preferred_element_type=jnp.float32
    )
    attended_part = attended_part.reshape(sample_count, token_total, model_width)
    attended = lax.psum_scatter(
        attended_part.astype(jnp.bfloat16), "grp", scatter_dimension=1, tiled=True
    )
    block_update = project(attended, w_out)
    updated = (noised_f + out_gate[None] * block_update).astype(jnp.bfloat16)
    grad_out = cotangent.astype(jnp.float32)
    gate_part = jnp.sum(grad_out * block_update, axis=0)
    grad_update = (grad_out * out_gate[None]).astype(jnp.bfloat16)
    grad_attn = project_back(grad_update, w_out).astype(jnp.bfloat16)
    grads_all = lax.all_gather(grad_attn, "grp", axis=1, tiled=True)
    grad_heads = grads_all.reshape(sample_count, token_total, head_count, head_size)
    grad_prob = jnp.einsum(
        "sihe,sjhe->shij", grad_heads, value_heads, preferred_element_type=jnp.float32
    )
    row_delta = lax.psum(
        jnp.sum(attn_prob * grad_prob, axis=-1).astype(jnp.bfloat16), "grp"
    ).astype(jnp.float32)
    grad_score = attn_prob * (grad_prob - row_delta[..., None])
    score_b = grad_score.astype(jnp.bfloat16)
    query_part = (
        jnp.einsum("shij,sjhe->sihe", score_b, key_heads, preferred_element_type=jnp.float32)
        * score_scale
    )
    query_part = query_part.reshape(sample_count, token_total, model_width)
    grad_query = lax.psum_scatter(
        query_part.astype(jnp.bfloat16), "grp", scatter_dimension=1, tiled=True
    )
    grad_key = (
        jnp.einsum("shij,sihe->sjhe", score_b, query_heads, preferred_element_type=jnp.float32)
        * score_scale
    )
    grad_value = jnp.einsum(
        "shij,sihe->sjhe", prob_b, grad_heads, preferred_element_type=jnp.float32
    )
    grad_key = grad_key.reshape(sample_count, col_count, model_width).astype(jnp.bfloat16)
    grad_value = grad_value.reshape(sample_count, col_count, model_width).astype(jnp.bfloat16)
    grad_input = (
        project_back(grad_query, w_query)
        + project_back(grad_key, w_key)
        + project_back(grad_value, w_value)
    )
    gamma_part = jnp.sum(grad_input * noised_norm, axis=0)
    beta_part = jnp.sum(grad_input, axis=0)
    gamma_sum, beta_sum, gate_sum = lax.psum((gamma_part, beta_part, gate_part), "rows")
    pre_gamma = (gamma_sum * cond_gamma * (1.0 - cond_gamma)).astype(jnp.bfloat16)
    pre_gate = (gate_sum * out_gate * (1.0 - out_gate)).astype(jnp.bfloat16)
    grad_snorm = jnp.dot(pre_gamma, w_gamma.T, preferred_element_type=jnp.float32)
    grad_snorm = grad_snorm + jnp.dot(
        beta_sum.astype(jnp.bfloat16), w_beta.T, preferred_element_type=jnp.float32
    )
    grad_snorm = grad_snorm + jnp.dot(pre_gate, w_outgate.T, preferred_element_type=jnp.float32)
    d_single = norm_back(grad_snorm, single_norm, single_inv)
    bias_part = jnp.sum(score_b, axis=0, dtype=jnp.float32)
    bias_own = lax.psum_scatter(bias_part, "rows", scatter_dimension=1, tiled=True)
    bias_grad = (bias_own * token_total).astype(jnp.bfloat16)
    grad_pairn = jnp.einsum("hij,ch->ijc", bias_grad, w_pair, preferred_element_type=jnp.float32)
    d_pair = norm_back(grad_pairn, pair_norm, pair_inv).astype(jnp.bfloat16)
    return (updated, d_single, d_pair)


def solution(mesh):
    in_specs = (
        P("grp", None),
        P("rows", "grp", None),
        P(),
        P("rows", "grp", None),
        P(),
        P(),
        P(),
        P(),
        P(),
        P(),
        P(),
        P(),
        P(),
        P("rows", "grp", None),
    )
    out_specs = (P("rows", "grp", None), P("grp", None), P("rows", "grp", None))
    groups = mesh.shape["grp"]
    row_total = mesh.shape["rows"]

    def on_device(*args):
        pair, noised, w_pair = args[1], args[3], args[11]
        fits = (
            pair.shape[0] % 32 == 0
            and pair.shape[1] % pair.shape[0] == 0
            and row_total == 8
            and noised.shape[0] == 1
            and noised.shape[1] % 64 == 0
            and w_pair.shape[1] % (2 * groups) == 0
        )
        if fits:
            return split_heads(*args, groups=groups, row_total=row_total)
        return split_keys(*args)

    return jax.shard_map(
        on_device, mesh=mesh, in_specs=in_specs, out_specs=out_specs, check_vma=False
    )
```

```python
import functools
import math

import jax
import jax.numpy as jnp
from jax import lax
from jax.experimental import pallas as pl
from jax.experimental.pallas import tpu as pltpu
from jax.sharding import PartitionSpec as P

EPSILON = 1e-05
BF16 = jnp.bfloat16
F32 = jnp.float32
VMEM_LIMIT = 56 * 1024 * 1024


def norm_rows(values):
    center = values - jnp.mean(values, axis=-1, keepdims=True)
    inverse = lax.rsqrt(jnp.mean(center * center, axis=-1, keepdims=True) + EPSILON)
    return (center * inverse, inverse)


def norm_back(grad_in, normed, inverse):
    grad_mean = jnp.mean(grad_in, axis=-1, keepdims=True)
    cross_mean = jnp.mean(grad_in * normed, axis=-1, keepdims=True)
    return inverse * (grad_in - grad_mean - normed * cross_mean)


def mm(left, right):
    return lax.dot_general(left, right, (((1,), (0,)), ((), ())), preferred_element_type=F32)


def mm_nt(left, right):
    return lax.dot_general(left, right, (((1,), (1,)), ((), ())), preferred_element_type=F32)


def mm_tn(left, right):
    return lax.dot_general(left, right, (((0,), (0,)), ((), ())), preferred_element_type=F32)


def sigmoid(values):
    return 1.0 / (1.0 + jnp.exp(-values))


def params():
    return pltpu.CompilerParams(vmem_limit_bytes=VMEM_LIMIT)


def smem():
    return pl.BlockSpec(memory_space=pltpu.SMEM)


def vmem():
    return pl.BlockSpec(memory_space=pltpu.VMEM)


def project_kernel(
    group_ref,
    single_ref,
    noised_ref,
    cot_ref,
    w_gamma_ref,
    w_beta_ref,
    w_outgate_ref,
    w_query_ref,
    w_key_ref,
    w_value_ref,
    w_out_ref,
    *rest,
    groups,
    calls,
):
    send_refs = rest[:groups]
    gamma_ref, gate_ref, stage_ref = rest[groups:]
    width = stage_ref.shape[2]
    part = width // (4 * calls)
    group_own = group_ref[0]
    single_norm, _ = norm_rows(single_ref[...].astype(F32))
    single_b = single_norm.astype(BF16)
    cond_gamma = sigmoid(mm(single_b, w_gamma_ref[...]))
    gamma_ref[...] = cond_gamma
    out_gate = sigmoid(mm(single_b, w_outgate_ref[...]))
    gate_ref[...] = out_gate
    cond_beta = mm(single_b, w_beta_ref[...])
    noised_norm, _ = norm_rows(noised_ref[...].astype(F32))
    x_b = (noised_norm * cond_gamma + cond_beta).astype(BF16)

    def put(kind, values):
        rounded = values.astype(BF16)
        for group in range(groups):
            slot = lax.rem(group - group_own + groups, groups)
            for call in range(calls):
                feature = (group * calls + call) * part
                lane = (call * 4 + kind) * part
                stage_ref[slot, :, lane : lane + part] = rounded[:, feature : feature + part]

    put(0, mm(x_b, w_query_ref[...]))
    put(1, mm(x_b, w_key_ref[...]))
    put(2, mm(x_b, w_value_ref[...]))
    grad_update = (cot_ref[...].astype(F32) * out_gate).astype(BF16)
    put(3, mm_nt(grad_update, w_out_ref[...]))
    for slot in range(groups):
        send_refs[slot][...] = stage_ref[slot]


def lane_tiles(cols):
    return [(tile, tile * 128, min(cols, tile * 128 + 128)) for tile in range(-(-cols // 128))]


def mean_matrix(channels):
    first = lax.broadcasted_iota(jnp.int32, (2 * channels, 2 * channels), 0) >= channels
    second = lax.broadcasted_iota(jnp.int32, (2 * channels, 2 * channels), 1) >= channels
    return jnp.where(first == second, 1.0 / channels, 0.0).astype(BF16)


def center_rows(pair_ref, first, batch, means):
    _, _, cols, channels = pair_ref.shape
    both = jnp.concatenate(
        [pair_ref[side, pl.ds(first, batch)].reshape(batch * cols, channels) for side in range(2)],
        axis=1,
    )
    return both.astype(F32) - mm(both, means)


def bias_kernel(
    group_ref,
    rows_ref,
    chains_ref,
    gain_ref,
    pair_ref,
    w_pair_ref,
    cols_ref,
    *rest,
    groups,
    batch,
):
    send_refs = rest[:groups]
    stats_ref, flat_ref, gains_ref, stage_ref = rest[groups:]
    _, step, cols, channels = pair_ref.shape
    heads = gain_ref.shape[0]
    per_group = heads // groups
    half = step * pl.num_programs(0)
    group_own = group_ref[0]
    row_base = rows_ref[0] * 2 * half + pl.program_id(0) * step
    means = mean_matrix(channels)
    weight = w_pair_ref[...]
    left = jnp.concatenate(
        [
            jnp.concatenate([weight, jnp.zeros((heads, channels), BF16)], axis=1),
            jnp.concatenate(
                [
                    jnp.zeros((heads, channels), BF16),
                    jnp.full((heads, channels), 1.0 / channels, BF16),
                ],
                axis=1,
            ),
        ],
        axis=0,
    )
    chain_cols = cols_ref[:, :cols]
    for group in range(1, groups):
        here = cols_ref[:, group * cols : (group + 1) * cols]
        chain_cols = jnp.where(group_own == group, here, chain_cols)
    for head in range(heads):
        gains_ref[head : head + 1, :] = jnp.full((1, cols), gain_ref[head], F32)

    def some_rows(index, carry):
        first = index * batch
        center = center_rows(pair_ref, first, batch, means)
        center_b = center.astype(BF16)
        square = (center * center).astype(BF16)
        for inner in range(batch):
            rows = slice(inner * cols, (inner + 1) * cols)
            for side in range(2):
                lanes = slice(side * channels, (side + 1) * channels)
                right = jnp.concatenate([center_b[rows, lanes], square[rows, lanes]], axis=1)
                sums = mm_nt(left, right)
                inverse = lax.rsqrt(sums[heads : heads + 8] + EPSILON)
                projected = sums[:heads] * inverse[:1]
                stats_ref[side, first + inner, :heads, :] = projected
                stats_ref[side, first + inner, heads:, :] = inverse
                chain = chains_ref[row_base + side * half + first + inner]
                same = (chain_cols == chain).astype(F32)
                values = projected + gains_ref[...] * same
                for tile, start, end in lane_tiles(cols):
                    piece = values[:, start:end]
                    if end - start < 128:
                        blank = jnp.zeros((heads, 128 - end + start), F32)
                        piece = jnp.concatenate([piece, blank], axis=1)
                    flat_ref[side, tile, pl.ds(first + inner, heads, stride=step), :] = piece
        return carry

    lax.fori_loop(0, step // batch, some_rows, 0)
    for head in range(heads):
        slot = lax.rem(head // per_group - group_own + groups, groups)
        values = jnp.concatenate(
            [
                flat_ref[side, tile, head * step : (head + 1) * step, : end - start]
                for side in range(2)
                for tile, start, end in lane_tiles(cols)
            ],
            axis=1,
        )
        stage_ref[slot, head % per_group] = values.astype(BF16)
    for slot in range(groups):
        send_refs[slot][...] = stage_ref[slot]


def pair_bias(pair, w_pair, chain_gain, chains, group_index, row_index, groups):
    rows, cols, channels = pair.shape
    heads = w_pair.shape[1]
    per_group = heads // groups
    half = rows // 2
    step = 16
    tiles = -(-cols // 128)
    *sends, stats = pl.pallas_call(
        functools.partial(bias_kernel, groups=groups, batch=4),
        grid=(half // step,),
        in_specs=[
            smem(),
            smem(),
            smem(),
            smem(),
            pl.BlockSpec((2, step, cols, channels), lambda t: (0, t, 0, 0)),
            pl.BlockSpec((heads, channels), lambda t: (0, 0)),
            pl.BlockSpec((1, groups * cols), lambda t: (0, 0)),
        ],
        out_specs=[
            pl.BlockSpec((per_group, step, 2 * cols), lambda t: (0, t, 0)) for _ in range(groups)
        ]
        + [pl.BlockSpec((2, step, heads + 8, cols), lambda t: (0, t, 0, 0))],
        out_shape=[
            jax.ShapeDtypeStruct((per_group, half, 2 * cols), BF16) for _ in range(groups)
        ]
        + [jax.ShapeDtypeStruct((2, half, heads + 8, cols), F32)],
        scratch_shapes=[
            pltpu.VMEM((2, tiles, heads * step, 128), F32),
            pltpu.VMEM((heads, cols), F32),
            pltpu.VMEM((groups, per_group, step, 2 * cols), BF16),
        ],
        compiler_params=params(),
    )(
        group_index,
        row_index,
        chains,
        chain_gain,
        pair.reshape(2, half, cols, channels),
        w_pair.T,
        chains.reshape(1, groups * cols),
    )
    return sends, stats


def pair_back_kernel(
    group_ref, pair_ref, stats_ref, w_pair_ref, *rest, groups, calls, factor, batch
):
    grad_refs = rest[: groups * calls]
    out_ref, flat_ref = rest[groups * calls :]
    _, step, cols, channels = pair_ref.shape
    per_call = grad_refs[0].shape[0]
    heads = groups * calls * per_call
    group_own = group_ref[0]
    means = mean_matrix(channels)
    weight = w_pair_ref[...].astype(F32)
    weight = weight - jnp.mean(weight, axis=-1, keepdims=True)
    high = weight.astype(BF16)
    low = (weight - high.astype(F32)).astype(BF16)
    weights = jnp.concatenate([high, low, jnp.zeros((16, channels), BF16)], axis=0)
    spread = lax.broadcasted_iota(jnp.int32, (2 * heads + 16, channels), 0)
    spread = ((spread >= 2 * heads) & (spread < 2 * heads + 2)).astype(F32).astype(BF16)
    weights = jnp.concatenate([weights, spread], axis=1)
    blank = jnp.zeros((14, cols), F32)
    for number in range(groups * calls):
        call, slot = divmod(number, groups)
        source = lax.rem(group_own + slot, groups) * calls + call
        for head in range(per_call):
            values = grad_refs[number][head].astype(F32)
            top = pl.multiple_of((source * per_call + head) * step, step)
            for side in range(2):
                for tile, start, end in lane_tiles(cols):
                    flat_ref[side, tile, pl.ds(top, step), : end - start] = values[
                        :, side * cols + start : side * cols + end
                    ]

    def some_rows(index, carry):
        first = index * batch
        center = center_rows(pair_ref, first, batch, means)
        for side in range(2):
            lefts = []
            for inner in range(batch):
                grads = jnp.concatenate(
                    [
                        flat_ref[side, tile, pl.ds(first + inner, heads, stride=step), :][
                            :, : end - start
                        ]
                        for tile, start, end in lane_tiles(cols)
                    ],
                    axis=1,
                )
                projected = stats_ref[side, first + inner, :heads, :]
                inverse = stats_ref[side, first + inner, heads : heads + 1, :]
                cross = jnp.sum(grads * projected, axis=0, keepdims=True) * (1.0 / channels)
                scaled = grads * (inverse * factor)
                cross = cross * (inverse * inverse * factor)
                cross_high = cross.astype(BF16).astype(F32)
                lefts.append(
                    jnp.concatenate(
                        [scaled, scaled, cross_high, cross - cross_high, blank], axis=0
                    )
                )
            for inner in range(batch):
                rows = slice(inner * cols, (inner + 1) * cols)
                lanes = slice(side * channels, (side + 1) * channels)
                both = mm_tn(lefts[inner].astype(BF16), weights)
                out_ref[side, first + inner] = (
                    both[:, :channels] - center[rows, lanes] * both[:, channels:]
                ).astype(BF16)
        return carry

    lax.fori_loop(0, step // batch, some_rows, 0)


def pair_back(pair, stats, grads, w_pair, group_index, groups, factor):
    rows, cols, channels = pair.shape
    per_call = grads[0].shape[0]
    heads = len(grads) * per_call
    half = rows // 2
    step = 16
    tiles = -(-cols // 128)
    out = pl.pallas_call(
        functools.partial(
            pair_back_kernel, groups=groups, calls=len(grads) // groups, factor=factor, batch=4
        ),
        grid=(half // step,),
        in_specs=[
            smem(),
            pl.BlockSpec((2, step, cols, channels), lambda t: (0, t, 0, 0)),
            pl.BlockSpec((2, step, heads + 8, cols), lambda t: (0, t, 0, 0)),
            pl.BlockSpec((heads, channels), lambda t: (0, 0)),
        ]
        + [pl.BlockSpec((per_call, step, 2 * cols), lambda t: (0, t, 0)) for _ in grads],
        out_specs=pl.BlockSpec((2, step, cols, channels), lambda t: (0, t, 0, 0)),
        out_shape=jax.ShapeDtypeStruct((2, half, cols, channels), BF16),
        scratch_shapes=[pltpu.VMEM((2, tiles, heads * step, 128), F32)],
        compiler_params=params(),
    )(group_index, pair.reshape(2, half, cols, channels), stats, w_pair.T, *grads)
    return out.reshape(rows, cols, channels)


def unit_order(heads):
    first, second = range(heads // 2), range(heads // 2, heads)
    order = [(0, head) for head in range(heads)]
    order += [(1, head) for head in first] + [(3, head) for head in first]
    order += [(2, head) for head in second] + [(3, head) for head in second]
    order += [(2, head) for head in first] + [(1, head) for head in second]
    return order


def attention_kernel(group_ref, row_ref, *rest, groups, row_parts, head_size, row_block):
    bias_refs = rest[: row_parts + 2]
    acts_refs = rest[row_parts + 2 : row_parts + 2 + groups]
    rest = rest[row_parts + 2 + groups :]
    out_refs = rest[:groups]
    (
        keep_ref,
        give_ref,
        query_ref,
        keys_ref,
        values_ref,
        grads_ref,
        query_t_ref,
        keys_t_ref,
        values_t_ref,
        grads_t_ref,
        bias_full,
        score_full,
        att_sum,
        gq_sum,
        gk_sum,
        gv_sum,
    ) = rest[groups:]
    head = pl.program_id(0)
    heads = keep_ref.shape[0] * 2 // row_parts
    group_own = group_ref[0]
    cols, width = acts_refs[0].shape
    tokens = groups * cols
    part = width // 4
    half = bias_refs[0].shape[2]
    scale = 1.0 / math.sqrt(head_size)
    extra = att_sum.shape[1] - part
    plain = (query_ref, keys_ref, values_ref, grads_ref)
    turned = (query_t_ref, keys_t_ref, values_t_ref, grads_t_ref)

    @pl.when(head == 0)
    def _():
        for kind in range(4):
            for slot in range(groups):
                plain[kind][slot * cols : (slot + 1) * cols, :] = acts_refs[slot][
                    :, kind * part : (kind + 1) * part
                ]
            turned[kind][...] = plain[kind][...].T
        att_sum[...] = jnp.zeros_like(att_sum)
        gq_sum[...] = jnp.zeros_like(gq_sum)

    def places(row_part):
        first = row_part * (2 * half)
        slot = lax.rem(group_own - first // cols + groups, groups)
        for side in range(2):
            top = slot * cols + lax.rem(first, cols) + side * half
            top = pl.multiple_of(top, 16)
            for column in range(groups):
                yield column, side, pl.ds(top, half)

    for other in range(row_parts):
        for column, side, rows in places(row_ref[0] ^ other):
            block, place = bias_refs[other], column
            if other >= row_parts - 2 and column >= groups // 2:
                block, place = bias_refs[other + 2], column - groups // 2
            bias_full[rows, column * cols : (column + 1) * cols] = block[
                place, 0, :, side * cols : (side + 1) * cols
            ]

    lane = lax.broadcasted_iota(jnp.int32, (1, part), 1)
    mine = (lane >= head * head_size) & (lane < (head + 1) * head_size)
    zero = jnp.zeros((), BF16)
    keys_m = jnp.where(mine, keys_ref[...], zero)
    values_m = jnp.concatenate(
        [jnp.where(mine, values_ref[...], zero), jnp.ones((tokens, extra), BF16)], axis=1
    )
    feature = pl.multiple_of(head * head_size, head_size)
    query_t = query_t_ref[pl.ds(feature, head_size), :]
    grads_t = grads_t_ref[pl.ds(feature, head_size), :]
    gk_t = jnp.zeros((head_size, tokens), F32)
    gv_t = jnp.zeros((head_size, tokens), F32)
    for top in range(0, tokens, row_block):
        rows = slice(top, top + row_block)
        query = jnp.where(mine, query_ref[rows, :], zero)
        grads = jnp.where(mine, grads_ref[rows, :], zero)
        scores = mm(query, keys_t_ref[...]) * scale + bias_full[rows, :].astype(F32)
        weights = jnp.exp(scores)
        attended = mm(weights.astype(BF16), values_m)
        inverse = 1.0 / attended[:, part : part + 1]
        attended = attended[:, :part] * inverse
        att_sum[rows, :part] += attended
        delta = jnp.sum(attended * grads.astype(F32), axis=-1, keepdims=True)
        prob = weights * inverse
        grad_prob = mm(grads, values_t_ref[...])
        score = (prob * (grad_prob - delta)).astype(BF16)
        score_full[rows, :] = score
        gq_sum[rows, :] += mm(score, keys_m)
        gk_t = gk_t + mm(query_t[:, rows], score)
        gv_t = gv_t + mm(grads_t[:, rows], prob.astype(BF16))
    gk_sum[pl.ds(feature, head_size), :] = gk_t
    gv_sum[pl.ds(feature, head_size), :] = gv_t

    for other in range(row_parts):
        dbias_ref = give_ref if other % 2 else keep_ref
        unit = 0
        for place, (chip, unit_head) in enumerate(unit_order(heads)):
            if chip == other // 2:
                unit = jnp.where(head == unit_head, place, unit)
        for column, side, rows in places(row_ref[0] ^ other):
            dbias_ref[unit, column, :, side * cols : (side + 1) * cols] = score_full[
                rows, column * cols : (column + 1) * cols
            ]

    @pl.when(head == heads - 1)
    def _():
        results = (
            gq_sum[...] * scale,
            (gk_sum[...] * scale).T,
            gv_sum[...].T,
            att_sum[:, :part],
        )
        for kind, values in enumerate(results):
            rounded = values.astype(BF16)
            for slot in range(groups):
                out_refs[slot][:, kind * part : (kind + 1) * part] = rounded[
                    slot * cols : (slot + 1) * cols
                ]


def attention(group_index, row_index, acts, bias, head_size):
    groups = len(acts)
    row_parts = len(bias) - 2
    cols, width = acts[0].shape
    tokens = groups * cols
    part = width // 4
    _, heads, half, lanes = bias[0].shape
    row_block = 256 if tokens % 256 == 0 else cols
    padded = (part // 128 + 1) * 128
    units = (row_parts // 2 * heads, groups, half, lanes)
    *grads, keep, give = pl.pallas_call(
        functools.partial(
            attention_kernel,
            groups=groups,
            row_parts=row_parts,
            head_size=head_size,
            row_block=row_block,
        ),
        grid=(heads,),
        in_specs=[smem(), smem()]
        + [
            pl.BlockSpec((block.shape[0], 1, half, lanes), lambda h: (0, h, 0, 0))
            for block in bias
        ]
        + [pl.BlockSpec((cols, width), lambda h: (0, 0))] * groups,
        out_specs=[pl.BlockSpec((cols, width), lambda h: (0, 0))] * groups
        + [pl.BlockSpec(units, lambda h: (0, 0, 0, 0))] * 2,
        out_shape=[jax.ShapeDtypeStruct((cols, width), BF16)] * groups
        + [jax.ShapeDtypeStruct(units, BF16)] * 2,
        scratch_shapes=[pltpu.VMEM((tokens, part), BF16) for _ in range(4)]
        + [pltpu.VMEM((part, tokens), BF16) for _ in range(4)]
        + [
            pltpu.VMEM((tokens, tokens), BF16),
            pltpu.VMEM((tokens, tokens), BF16),
            pltpu.VMEM((tokens, padded), F32),
            pltpu.VMEM((tokens, part), F32),
            pltpu.VMEM((part, tokens), F32),
            pltpu.VMEM((part, tokens), F32),
        ],
        compiler_params=params(),
    )(group_index, row_index, *bias, *acts)
    return grads, keep, give


def finish_kernel(
    group_ref,
    single_ref,
    noised_ref,
    cot_ref,
    gamma_ref,
    gate_ref,
    w_gamma_ref,
    w_beta_ref,
    w_outgate_ref,
    w_query_ref,
    w_key_ref,
    w_value_ref,
    w_out_ref,
    *rest,
    groups,
    calls,
):
    got_refs = rest[: groups * calls]
    updated_ref, d_single_ref, stage_ref = rest[groups * calls :]
    width = stage_ref.shape[3]
    part = width // 4
    for slot in range(groups):
        for call in range(calls):
            stage_ref[lax.rem(group_ref[0] + slot, groups), call] = got_refs[
                call * groups + slot
            ][...]

    def take(kind):
        return jnp.concatenate(
            [
                stage_ref[group, call, :, kind * part : (kind + 1) * part]
                for group in range(groups)
                for call in range(calls)
            ],
            axis=1,
        )

    out_gate = gate_ref[...]
    cond_gamma = gamma_ref[...]
    block_update = mm(take(3), w_out_ref[...])
    noised = noised_ref[...].astype(F32)
    updated_ref[...] = (noised + out_gate * block_update).astype(BF16)
    gate_part = cot_ref[...].astype(F32) * block_update
    pre_gate = (gate_part * out_gate * (1.0 - out_gate)).astype(BF16)
    grad_input = mm_nt(take(0), w_query_ref[...])
    grad_input += mm_nt(take(1), w_key_ref[...])
    grad_input += mm_nt(take(2), w_value_ref[...])
    noised_norm, _ = norm_rows(noised)
    pre_gamma = (grad_input * noised_norm * cond_gamma * (1.0 - cond_gamma)).astype(BF16)
    grad_snorm = mm_nt(pre_gamma, w_gamma_ref[...])
    grad_snorm += mm_nt(grad_input.astype(BF16), w_beta_ref[...])
    grad_snorm += mm_nt(pre_gate, w_outgate_ref[...])
    single_norm, single_inv = norm_rows(single_ref[...].astype(F32))
    d_single_ref[...] = norm_back(grad_snorm, single_norm, single_inv)


def swap_groups(sends, direction):
    groups = len(sends)
    got = [sends[0]]
    for shift in range(1, groups):
        perm = [(index, (index + direction * shift) % groups) for index in range(groups)]
        got.append(lax.ppermute(sends[shift], "grp", perm))
    return got


def flip_rows(values, bits, row_total):
    return lax.ppermute(values, "rows", [(index, index ^ bits) for index in range(row_total)])


def gather_rows(own, acts, row_total):
    half = own.shape[0] // 2
    near = flip_rows(own, 2, row_total)
    far = flip_rows(own, 4, row_total)
    first = flip_rows(near[:half], 4, row_total)
    second = flip_rows(far[half:], 2, row_total)
    first, second, acts[1], acts[2], acts[3] = lax.optimization_barrier(
        (first, second, acts[1], acts[2], acts[3])
    )
    blocks = []
    for block in (own, near, far, first, second):
        blocks += [block, flip_rows(block, 1, row_total)]
    return blocks, acts


def add_last_kernel(keep_ref, got_ref, near_ref, far_ref, near_two_ref, far_two_ref, *out_refs):
    head = pl.program_id(0)
    lower = head < pl.num_programs(0) // 2
    total = keep_ref[0].astype(F32) + got_ref[0].astype(F32)
    total += jnp.where(lower, near_ref[0].astype(F32), far_ref[0].astype(F32))
    total += jnp.where(lower, far_two_ref[0].astype(F32), near_two_ref[0].astype(F32))
    total = total.astype(BF16)
    for slot, out_ref in enumerate(out_refs):
        out_ref[0] = total[slot]


def scatter_rows(keep, give, grads, row_total):
    got = flip_rows(give, 1, row_total)
    units, groups, half, lanes = keep.shape
    heads = units // 4
    part = heads // 2

    def add(first, count, *others):
        total = keep[first : first + count].astype(F32) + got[first : first + count].astype(F32)
        for other in others:
            total += other.astype(F32)
        return total.astype(BF16)

    near = flip_rows(add(heads, heads), 2, row_total)
    far = flip_rows(add(2 * heads, heads), 4, row_total)
    far_two = add(3 * heads, part, near[part:])
    near_two = add(3 * heads + part, part, far[part:])
    far_two = flip_rows(far_two, 4, row_total)
    near_two = flip_rows(near_two, 2, row_total)
    far_two, near_two, grads = lax.optimization_barrier((far_two, near_two, grads))
    block = (1, groups, half, lanes)
    whole = pl.BlockSpec(block, lambda h: (h, 0, 0, 0))
    wrapped = pl.BlockSpec(block, lambda h: (lax.rem(h, part), 0, 0, 0))
    sums = pl.pallas_call(
        add_last_kernel,
        grid=(heads,),
        in_specs=[whole, whole] + [wrapped] * 4,
        out_specs=[pl.BlockSpec((1, half, lanes), lambda h: (h, 0, 0))] * groups,
        out_shape=[jax.ShapeDtypeStruct((heads, half, lanes), BF16)] * groups,
        compiler_params=params(),
    )(keep, got, near, far, near_two, far_two)
    sums, grads = lax.optimization_barrier((sums, grads))
    return sums, grads


def sum_rows(values, row_total):
    mine = values.astype(BF16)
    both = (mine.astype(F32) + flip_rows(mine, 1, row_total).astype(F32)).astype(BF16)
    near, far, last = (flip_rows(both, bits, row_total).astype(F32) for bits in (2, 4, 6))
    return (both.astype(F32) + near) + (far + last)


def split_heads(
    single,
    pair,
    chains,
    noised,
    w_gamma,
    w_beta,
    w_outgate,
    w_query,
    w_key,
    w_value,
    w_out,
    w_pair,
    chain_gain,
    cotangent,
    *,
    groups,
    row_total,
):
    cols, _ = single.shape
    tokens = chains.shape[0]
    width = noised.shape[2]
    head_size = width // w_pair.shape[1]
    calls = 1
    row_index = lax.axis_index("rows").reshape(1)
    group_index = lax.axis_index("grp").reshape(1)
    bias_send, stats = pair_bias(
        pair, w_pair, chain_gain, chains, group_index, row_index, groups
    )
    bias_got = swap_groups(bias_send, 1)
    noised = noised[0]
    cotangent = cotangent[0]
    *acts_send, cond_gamma, out_gate = pl.pallas_call(
        functools.partial(project_kernel, groups=groups, calls=calls),
        in_specs=[smem()] + [vmem()] * 10,
        out_shape=[
            jax.ShapeDtypeStruct((cols, 4 * width // groups), BF16) for _ in range(groups)
        ]
        + [
            jax.ShapeDtypeStruct((cols, width), F32),
            jax.ShapeDtypeStruct((cols, width), F32),
        ],
        scratch_shapes=[pltpu.VMEM((groups, cols, 4 * width // groups), BF16)],
        compiler_params=params(),
    )(
        group_index,
        single,
        noised,
        cotangent,
        w_gamma,
        w_beta,
        w_outgate,
        w_query,
        w_key,
        w_value,
        w_out,
    )
    bias_got, _ = lax.optimization_barrier((bias_got, acts_send))
    acts = swap_groups(acts_send, 1)
    bias_all, acts = gather_rows(jnp.stack(bias_got), acts, row_total)
    grads_send, keep, give = attention(group_index, row_index, acts, bias_all, head_size)
    grads = swap_groups(grads_send, -1)
    dbias_own, grads = scatter_rows(keep, give, grads, row_total)
    dbias_back = swap_groups(dbias_own, -1)
    updated, d_part = pl.pallas_call(
        functools.partial(finish_kernel, groups=groups, calls=calls),
        in_specs=[smem()] + [vmem()] * (12 + groups * calls),
        out_shape=[
            jax.ShapeDtypeStruct((cols, width), BF16),
            jax.ShapeDtypeStruct(single.shape, F32),
        ],
        scratch_shapes=[pltpu.VMEM((groups, calls, cols, 4 * width // (groups * calls)), BF16)],
        compiler_params=params(),
    )(
        group_index,
        single,
        noised,
        cotangent,
        cond_gamma,
        out_gate,
        w_gamma,
        w_beta,
        w_outgate,
        w_query,
        w_key,
        w_value,
        w_out,
        *grads,
    )
    d_part, dbias_back = lax.optimization_barrier((d_part, dbias_back))
    d_single = sum_rows(d_part, row_total)
    d_pair = pair_back(pair, stats, dbias_back, w_pair, group_index, groups, float(tokens))
    return (updated[None], d_single, d_pair)


def project(acts, weight):
    return jnp.einsum("std,de->ste", acts, weight, preferred_element_type=F32)


def project_back(acts, weight):
    return jnp.einsum("ste,de->std", acts, weight, preferred_element_type=F32)


def split_keys(
    single,
    pair,
    chains,
    noised,
    w_gamma,
    w_beta,
    w_outgate,
    w_query,
    w_key,
    w_value,
    w_out,
    w_pair,
    chain_gain,
    cotangent,
):
    col_count = single.shape[0]
    row_count = pair.shape[0]
    head_count = w_pair.shape[1]
    model_width = w_query.shape[0]
    head_size = model_width // head_count
    sample_count = noised.shape[0]
    token_total = chains.shape[0]
    score_scale = 1.0 / math.sqrt(head_size)
    row_index = lax.axis_index("rows")
    group_index = lax.axis_index("grp")
    chain_rows = lax.dynamic_slice_in_dim(chains, row_index * row_count, row_count)
    chain_cols = lax.dynamic_slice_in_dim(chains, group_index * col_count, col_count)
    pair_norm, pair_inv = norm_rows(pair.astype(jnp.float32))
    projected = jnp.einsum(
        "ijc,ch->hij", pair_norm.astype(jnp.bfloat16), w_pair, preferred_element_type=jnp.float32
    )
    same_chain = (chain_rows[:, None] == chain_cols[None, :]).astype(jnp.float32)
    bias_block = (projected + chain_gain[:, None, None] * same_chain[None]).astype(jnp.bfloat16)
    bias_keys = lax.all_gather(bias_block, "rows", axis=1, tiled=True)
    single_norm, single_inv = norm_rows(single.astype(jnp.float32))
    single_b = single_norm.astype(jnp.bfloat16)
    cond_gamma = jax.nn.sigmoid(jnp.dot(single_b, w_gamma, preferred_element_type=jnp.float32))
    cond_beta = jnp.dot(single_b, w_beta, preferred_element_type=jnp.float32)
    out_gate = jax.nn.sigmoid(jnp.dot(single_b, w_outgate, preferred_element_type=jnp.float32))
    noised_f = noised.astype(jnp.float32)
    noised_norm, noised_inv = norm_rows(noised_f)
    x_b = (noised_norm * cond_gamma[None] + cond_beta[None]).astype(jnp.bfloat16)
    queries = project(x_b, w_query).astype(jnp.bfloat16)
    keys_own = project(x_b, w_key).astype(jnp.bfloat16)
    values_own = project(x_b, w_value).astype(jnp.bfloat16)
    queries_all = lax.all_gather(queries, "grp", axis=1, tiled=True)
    query_heads = queries_all.reshape(sample_count, token_total, head_count, head_size)
    key_heads = keys_own.reshape(sample_count, col_count, head_count, head_size)
    value_heads = values_own.reshape(sample_count, col_count, head_count, head_size)
    scores = (
        jnp.einsum("sihe,sjhe->shij", query_heads, key_heads, preferred_element_type=jnp.float32)
        * score_scale
        + bias_keys.astype(jnp.float32)[None]
    )
    exp_scores = jnp.exp(scores)
    exp_total = lax.psum(jnp.sum(exp_scores, axis=-1).astype(jnp.bfloat16), "grp").astype(
        jnp.float32
    )
    attn_prob = exp_scores / exp_total[..., None]
    prob_b = attn_prob.astype(jnp.bfloat16)
    attended_part = jnp.einsum(
        "shij,sjhe->sihe", prob_b, value_heads, preferred_element_type=jnp.float32
    )
    attended_part = attended_part.reshape(sample_count, token_total, model_width)
    attended = lax.psum_scatter(
        attended_part.astype(jnp.bfloat16), "grp", scatter_dimension=1, tiled=True
    )
    block_update = project(attended, w_out)
    updated = (noised_f + out_gate[None] * block_update).astype(jnp.bfloat16)
    grad_out = cotangent.astype(jnp.float32)
    gate_part = jnp.sum(grad_out * block_update, axis=0)
    grad_update = (grad_out * out_gate[None]).astype(jnp.bfloat16)
    grad_attn = project_back(grad_update, w_out).astype(jnp.bfloat16)
    grads_all = lax.all_gather(grad_attn, "grp", axis=1, tiled=True)
    grad_heads = grads_all.reshape(sample_count, token_total, head_count, head_size)
    grad_prob = jnp.einsum(
        "sihe,sjhe->shij", grad_heads, value_heads, preferred_element_type=jnp.float32
    )
    row_delta = lax.psum(
        jnp.sum(attn_prob * grad_prob, axis=-1).astype(jnp.bfloat16), "grp"
    ).astype(jnp.float32)
    grad_score = attn_prob * (grad_prob - row_delta[..., None])
    score_b = grad_score.astype(jnp.bfloat16)
    query_part = (
        jnp.einsum("shij,sjhe->sihe", score_b, key_heads, preferred_element_type=jnp.float32)
        * score_scale
    )
    query_part = query_part.reshape(sample_count, token_total, model_width)
    grad_query = lax.psum_scatter(
        query_part.astype(jnp.bfloat16), "grp", scatter_dimension=1, tiled=True
    )
    grad_key = (
        jnp.einsum("shij,sihe->sjhe", score_b, query_heads, preferred_element_type=jnp.float32)
        * score_scale
    )
    grad_value = jnp.einsum(
        "shij,sihe->sjhe", prob_b, grad_heads, preferred_element_type=jnp.float32
    )
    grad_key = grad_key.reshape(sample_count, col_count, model_width).astype(jnp.bfloat16)
    grad_value = grad_value.reshape(sample_count, col_count, model_width).astype(jnp.bfloat16)
    grad_input = (
        project_back(grad_query, w_query)
        + project_back(grad_key, w_key)
        + project_back(grad_value, w_value)
    )
    gamma_part = jnp.sum(grad_input * noised_norm, axis=0)
    beta_part = jnp.sum(grad_input, axis=0)
    gamma_sum, beta_sum, gate_sum = lax.psum((gamma_part, beta_part, gate_part), "rows")
    pre_gamma = (gamma_sum * cond_gamma * (1.0 - cond_gamma)).astype(jnp.bfloat16)
    pre_gate = (gate_sum * out_gate * (1.0 - out_gate)).astype(jnp.bfloat16)
    grad_snorm = jnp.dot(pre_gamma, w_gamma.T, preferred_element_type=jnp.float32)
    grad_snorm = grad_snorm + jnp.dot(
        beta_sum.astype(jnp.bfloat16), w_beta.T, preferred_element_type=jnp.float32
    )
    grad_snorm = grad_snorm + jnp.dot(pre_gate, w_outgate.T, preferred_element_type=jnp.float32)
    d_single = norm_back(grad_snorm, single_norm, single_inv)
    bias_part = jnp.sum(score_b, axis=0, dtype=jnp.float32)
    bias_own = lax.psum_scatter(bias_part, "rows", scatter_dimension=1, tiled=True)
    bias_grad = (bias_own * token_total).astype(jnp.bfloat16)
    grad_pairn = jnp.einsum("hij,ch->ijc", bias_grad, w_pair, preferred_element_type=jnp.float32)
    d_pair = norm_back(grad_pairn, pair_norm, pair_inv).astype(jnp.bfloat16)
    return (updated, d_single, d_pair)


def solution(mesh):
    in_specs = (
        P("grp", None),
        P("rows", "grp", None),
        P(),
        P("rows", "grp", None),
        P(),
        P(),
        P(),
        P(),
        P(),
        P(),
        P(),
        P(),
        P(),
        P("rows", "grp", None),
    )
    out_specs = (P("rows", "grp", None), P("grp", None), P("rows", "grp", None))
    groups = mesh.shape["grp"]
    row_total = mesh.shape["rows"]

    def on_device(*args):
        pair, noised, w_pair = args[1], args[3], args[11]
        fits = (
            pair.shape[0] % 32 == 0
            and pair.shape[1] % pair.shape[0] == 0
            and row_total == 8
            and noised.shape[0] == 1
            and noised.shape[1] % 64 == 0
            and w_pair.shape[1] % (2 * groups) == 0
        )
        if fits:
            return split_heads(*args, groups=groups, row_total=row_total)
        return split_keys(*args)

    return jax.shard_map(
        on_device, mesh=mesh, in_specs=in_specs, out_specs=out_specs, check_vma=False
    )
```

```python
import functools
import math

import jax
import jax.numpy as jnp
from jax import lax
from jax.experimental import pallas as pl
from jax.experimental.pallas import tpu as pltpu
from jax.sharding import PartitionSpec as P

EPSILON = 1e-05
BF16 = jnp.bfloat16
F32 = jnp.float32
VMEM_LIMIT = 56 * 1024 * 1024


def norm_rows(values):
    center = values - jnp.mean(values, axis=-1, keepdims=True)
    inverse = lax.rsqrt(jnp.mean(center * center, axis=-1, keepdims=True) + EPSILON)
    return (center * inverse, inverse)


def norm_back(grad_in, normed, inverse):
    grad_mean = jnp.mean(grad_in, axis=-1, keepdims=True)
    cross_mean = jnp.mean(grad_in * normed, axis=-1, keepdims=True)
    return inverse * (grad_in - grad_mean - normed * cross_mean)


def mm(left, right):
    return lax.dot_general(left, right, (((1,), (0,)), ((), ())), preferred_element_type=F32)


def mm_nt(left, right):
    return lax.dot_general(left, right, (((1,), (1,)), ((), ())), preferred_element_type=F32)


def mm_tn(left, right):
    return lax.dot_general(left, right, (((0,), (0,)), ((), ())), preferred_element_type=F32)


def sigmoid(values):
    return 1.0 / (1.0 + jnp.exp(-values))


def params():
    return pltpu.CompilerParams(vmem_limit_bytes=VMEM_LIMIT)


def smem():
    return pl.BlockSpec(memory_space=pltpu.SMEM)


def vmem():
    return pl.BlockSpec(memory_space=pltpu.VMEM)


def project_kernel(
    group_ref,
    single_ref,
    noised_ref,
    cot_ref,
    w_gamma_ref,
    w_beta_ref,
    w_outgate_ref,
    w_query_ref,
    w_key_ref,
    w_value_ref,
    w_out_ref,
    *rest,
    groups,
    calls,
):
    send_refs = rest[:groups]
    gamma_ref, gate_ref, stage_ref = rest[groups:]
    width = stage_ref.shape[2]
    part = width // (4 * calls)
    group_own = group_ref[0]
    single_norm, _ = norm_rows(single_ref[...].astype(F32))
    single_b = single_norm.astype(BF16)
    cond_gamma = sigmoid(mm(single_b, w_gamma_ref[...]))
    gamma_ref[...] = cond_gamma
    out_gate = sigmoid(mm(single_b, w_outgate_ref[...]))
    gate_ref[...] = out_gate
    cond_beta = mm(single_b, w_beta_ref[...])
    noised_norm, _ = norm_rows(noised_ref[...].astype(F32))
    x_b = (noised_norm * cond_gamma + cond_beta).astype(BF16)

    def put(kind, values):
        rounded = values.astype(BF16)
        for group in range(groups):
            slot = lax.rem(group - group_own + groups, groups)
            for call in range(calls):
                feature = (group * calls + call) * part
                lane = (call * 4 + kind) * part
                stage_ref[slot, :, lane : lane + part] = rounded[:, feature : feature + part]

    put(0, mm(x_b, w_query_ref[...]))
    put(1, mm(x_b, w_key_ref[...]))
    put(2, mm(x_b, w_value_ref[...]))
    grad_update = (cot_ref[...].astype(F32) * out_gate).astype(BF16)
    put(3, mm_nt(grad_update, w_out_ref[...]))
    for slot in range(groups):
        send_refs[slot][...] = stage_ref[slot]


def lane_tiles(cols):
    return [(tile, tile * 128, min(cols, tile * 128 + 128)) for tile in range(-(-cols // 128))]


def mean_matrix(channels):
    first = lax.broadcasted_iota(jnp.int32, (2 * channels, 2 * channels), 0) >= channels
    second = lax.broadcasted_iota(jnp.int32, (2 * channels, 2 * channels), 1) >= channels
    return jnp.where(first == second, 1.0 / channels, 0.0).astype(BF16)


def center_rows(pair_ref, first, batch, means):
    _, _, cols, channels = pair_ref.shape
    both = jnp.concatenate(
        [pair_ref[side, pl.ds(first, batch)].reshape(batch * cols, channels) for side in range(2)],
        axis=1,
    )
    return both.astype(F32) - mm(both, means)


def lane_pad(block, before, total):
    rows, width = block.shape
    pieces = [block]
    if before:
        pieces = [jnp.zeros((rows, before), block.dtype)] + pieces
    if total > before + width:
        pieces = pieces + [jnp.zeros((rows, total - before - width), block.dtype)]
    return jnp.concatenate(pieces, axis=1)


def bias_kernel(
    group_ref,
    rows_ref,
    chains_ref,
    gain_ref,
    pair_ref,
    w_pair_ref,
    cols_ref,
    *rest,
    groups,
    batch,
):
    send_refs = rest[:groups]
    stats_ref, flat_ref, gains_ref, stage_ref = rest[groups:]
    _, step, cols, channels = pair_ref.shape
    heads = gain_ref.shape[0]
    per_group = heads // groups
    half = step * pl.num_programs(0)
    group_own = group_ref[0]
    row_base = rows_ref[0] * 2 * half + pl.program_id(0) * step
    means = mean_matrix(channels)
    weight = w_pair_ref[...].astype(F32).T.astype(BF16)
    mean_part = jnp.full((channels, heads), 1.0 / channels, BF16)
    mixed = []
    for inner in range(2):
        for part, offset in ((weight, 0), (mean_part, heads)):
            for side in range(2):
                mixed.append(lane_pad(part, 2 * heads * (2 * inner + side) + offset, 8 * heads))
    mixed = jnp.concatenate(mixed, axis=0)
    chain_all = cols_ref[...].reshape(1, groups * cols)
    chain_cols = chain_all[:, :cols]
    for group in range(1, groups):
        here = chain_all[:, group * cols : (group + 1) * cols]
        chain_cols = jnp.where(group_own == group, here, chain_cols)
    for head in range(heads):
        gains_ref[head : head + 1, :] = jnp.full((1, cols), gain_ref[head], F32)

    def some_rows(index, carry):
        first = index * batch
        center = center_rows(pair_ref, first, batch, means)
        center_b = center.astype(BF16)
        square = (center * center).astype(BF16)
        for base in range(0, batch, 2):
            one = slice(base * cols, (base + 1) * cols)
            two = slice((base + 1) * cols, (base + 2) * cols)
            left = jnp.concatenate(
                [center_b[one], square[one], center_b[two], square[two]], axis=1
            )
            sums = mm(left, mixed).T
            for inner in range(2):
                row = first + base + inner
                for side in range(2):
                    top = 2 * heads * (2 * inner + side)
                    inverse = lax.rsqrt(sums[top + heads : top + 2 * heads] + EPSILON)
                    projected = sums[top : top + heads] * inverse
                    stats_ref[side, row, :heads, :] = projected
                    stats_ref[side, row, heads:, :] = inverse[:8]
                    chain = chains_ref[row_base + side * half + row]
                    same = (chain_cols == chain).astype(F32)
                    values = projected + gains_ref[...] * same
                    for tile, start, end in lane_tiles(cols):
                        piece = lane_pad(values[:, start:end], 0, 128)
                        flat_ref[side, tile, pl.ds(row, heads, stride=step), :] = piece
        return carry

    lax.fori_loop(0, step // batch, some_rows, 0)
    for head in range(heads):
        slot = lax.rem(head // per_group - group_own + groups, groups)
        values = jnp.concatenate(
            [
                flat_ref[side, tile, head * step : (head + 1) * step, : end - start]
                for side in range(2)
                for tile, start, end in lane_tiles(cols)
            ],
            axis=1,
        )
        stage_ref[slot, head % per_group] = values.astype(BF16)
    for slot in range(groups):
        send_refs[slot][...] = stage_ref[slot]


def pair_bias(pair, w_pair, chain_gain, chains, group_index, row_index, groups):
    rows, cols, channels = pair.shape
    heads = w_pair.shape[1]
    per_group = heads // groups
    half = rows // 2
    step = 16
    tiles = -(-cols // 128)
    *sends, stats = pl.pallas_call(
        functools.partial(bias_kernel, groups=groups, batch=4),
        grid=(half // step,),
        in_specs=[
            smem(),
            smem(),
            smem(),
            smem(),
            pl.BlockSpec((2, step, cols, channels), lambda t: (0, t, 0, 0)),
            pl.BlockSpec((heads, channels), lambda t: (0, 0)),
            pl.BlockSpec((groups * cols,), lambda t: (0,)),
        ],
        out_specs=[
            pl.BlockSpec((per_group, step, 2 * cols), lambda t: (0, t, 0)) for _ in range(groups)
        ]
        + [pl.BlockSpec((2, step, heads + 8, cols), lambda t: (0, t, 0, 0))],
        out_shape=[
            jax.ShapeDtypeStruct((per_group, half, 2 * cols), BF16) for _ in range(groups)
        ]
        + [jax.ShapeDtypeStruct((2, half, heads + 8, cols), F32)],
        scratch_shapes=[
            pltpu.VMEM((2, tiles, heads * step, 128), F32),
            pltpu.VMEM((heads, cols), F32),
            pltpu.VMEM((groups, per_group, step, 2 * cols), BF16),
        ],
        compiler_params=params(),
    )(
        group_index,
        row_index,
        chains,
        chain_gain,
        pair.reshape(2, half, cols, channels),
        w_pair.T,
        chains,
    )
    return sends, stats


def pair_back_kernel(
    group_ref, pair_ref, stats_ref, w_pair_ref, *rest, groups, calls, factor, batch
):
    grad_refs = rest[: groups * calls]
    out_ref, flat_ref = rest[groups * calls :]
    _, step, cols, channels = pair_ref.shape
    per_call = grad_refs[0].shape[0]
    heads = groups * calls * per_call
    group_own = group_ref[0]
    means = mean_matrix(channels)
    weight = w_pair_ref[...].astype(F32)
    weight = (weight - jnp.mean(weight, axis=-1, keepdims=True)).astype(BF16)
    spread = lax.broadcasted_iota(jnp.int32, (heads, channels), 0)
    spread = (spread < 2).astype(F32).astype(BF16)
    block = jnp.concatenate(
        [lane_pad(weight, 0, 2 * channels), lane_pad(spread, channels, 2 * channels)], axis=0
    )
    weights = jnp.concatenate(
        [lane_pad(block, 2 * channels * place, 8 * channels) for place in range(4)], axis=0
    )
    blank = jnp.zeros((heads - 2, cols), F32)
    for number in range(groups * calls):
        call, slot = divmod(number, groups)
        source = lax.rem(group_own + slot, groups) * calls + call
        for head in range(per_call):
            values = grad_refs[number][head].astype(F32)
            top = pl.multiple_of((source * per_call + head) * step, step)
            for side in range(2):
                for tile, start, end in lane_tiles(cols):
                    flat_ref[side, tile, pl.ds(top, step), : end - start] = values[
                        :, side * cols + start : side * cols + end
                    ]

    def some_rows(index, carry):
        first = index * batch
        center = center_rows(pair_ref, first, batch, means)
        for base in range(0, batch, 2):
            places = [(base + inner, side) for inner in range(2) for side in range(2)]
            left = []
            for inner, side in places:
                grads = jnp.concatenate(
                    [
                        flat_ref[side, tile, pl.ds(first + inner, heads, stride=step), :][
                            :, : end - start
                        ]
                        for tile, start, end in lane_tiles(cols)
                    ],
                    axis=1,
                )
                projected = stats_ref[side, first + inner, :heads, :]
                inverse = stats_ref[side, first + inner, heads : heads + 1, :]
                cross = jnp.sum(grads * projected, axis=0, keepdims=True) * (1.0 / channels)
                scaled = grads * (inverse * factor)
                cross = cross * (inverse * inverse * factor)
                cross_high = cross.astype(BF16).astype(F32)
                left += [scaled, cross_high, cross - cross_high, blank]
            both = mm_tn(jnp.concatenate(left, axis=0).astype(BF16), weights)
            for place, (inner, side) in enumerate(places):
                rows = slice(inner * cols, (inner + 1) * cols)
                lanes = slice(side * channels, (side + 1) * channels)
                start = 2 * channels * place
                middle, end = start + channels, start + 2 * channels
                out_ref[side, first + inner] = (
                    both[:, start:middle] - center[rows, lanes] * both[:, middle:end]
                ).astype(BF16)
        return carry

    lax.fori_loop(0, step // batch, some_rows, 0)


def pair_back(pair, stats, grads, w_pair, group_index, groups, factor):
    rows, cols, channels = pair.shape
    per_call = grads[0].shape[0]
    heads = len(grads) * per_call
    half = rows // 2
    step = 16
    tiles = -(-cols // 128)
    out = pl.pallas_call(
        functools.partial(
            pair_back_kernel, groups=groups, calls=len(grads) // groups, factor=factor, batch=4
        ),
        grid=(half // step,),
        in_specs=[
            smem(),
            pl.BlockSpec((2, step, cols, channels), lambda t: (0, t, 0, 0)),
            pl.BlockSpec((2, step, heads + 8, cols), lambda t: (0, t, 0, 0)),
            pl.BlockSpec((heads, channels), lambda t: (0, 0)),
        ]
        + [pl.BlockSpec((per_call, step, 2 * cols), lambda t: (0, t, 0)) for _ in grads],
        out_specs=pl.BlockSpec((2, step, cols, channels), lambda t: (0, t, 0, 0)),
        out_shape=jax.ShapeDtypeStruct((2, half, cols, channels), BF16),
        scratch_shapes=[pltpu.VMEM((2, tiles, heads * step, 128), F32)],
        compiler_params=params(),
    )(group_index, pair.reshape(2, half, cols, channels), stats, w_pair.T, *grads)
    return out.reshape(rows, cols, channels)


def unit_order(heads):
    first, second = range(heads // 2), range(heads // 2, heads)
    order = [(0, head) for head in range(heads)]
    order += [(1, head) for head in first] + [(3, head) for head in first]
    order += [(2, head) for head in second] + [(3, head) for head in second]
    order += [(2, head) for head in first] + [(1, head) for head in second]
    return order


def attention_kernel(group_ref, row_ref, *rest, groups, row_parts, head_size, row_block):
    bias_refs = rest[: row_parts + 2]
    acts_refs = rest[row_parts + 2 : row_parts + 2 + groups]
    rest = rest[row_parts + 2 + groups :]
    out_refs = rest[:groups]
    (
        keep_ref,
        give_ref,
        query_ref,
        keys_ref,
        values_ref,
        grads_ref,
        query_t_ref,
        keys_t_ref,
        values_t_ref,
        grads_t_ref,
        bias_full,
        score_full,
        att_sum,
        gq_sum,
        gk_sum,
        gv_sum,
    ) = rest[groups:]
    head = pl.program_id(0)
    heads = keep_ref.shape[0] * 2 // row_parts
    group_own = group_ref[0]
    cols, width = acts_refs[0].shape
    tokens = groups * cols
    part = width // 4
    half = bias_refs[0].shape[2]
    scale = 1.0 / math.sqrt(head_size)
    extra = att_sum.shape[1] - part
    plain = (query_ref, keys_ref, values_ref, grads_ref)
    turned = (query_t_ref, keys_t_ref, values_t_ref, grads_t_ref)

    @pl.when(head == 0)
    def _():
        for kind in range(4):
            for slot in range(groups):
                plain[kind][slot * cols : (slot + 1) * cols, :] = acts_refs[slot][
                    :, kind * part : (kind + 1) * part
                ]
            turned[kind][...] = plain[kind][...].T
        att_sum[...] = jnp.zeros_like(att_sum)
        gq_sum[...] = jnp.zeros_like(gq_sum)

    def places(row_part):
        first = row_part * (2 * half)
        slot = lax.rem(group_own - first // cols + groups, groups)
        for side in range(2):
            top = slot * cols + lax.rem(first, cols) + side * half
            top = pl.multiple_of(top, 16)
            for column in range(groups):
                yield column, side, pl.ds(top, half)

    for other in range(row_parts):
        for column, side, rows in places(row_ref[0] ^ other):
            block, place = bias_refs[other], column
            if other >= row_parts - 2 and column >= groups // 2:
                block, place = bias_refs[other + 2], column - groups // 2
            bias_full[rows, column * cols : (column + 1) * cols] = block[
                place, 0, :, side * cols : (side + 1) * cols
            ]

    lane = lax.broadcasted_iota(jnp.int32, (1, part), 1)
    mine = (lane >= head * head_size) & (lane < (head + 1) * head_size)
    zero = jnp.zeros((), BF16)
    keys_m = jnp.where(mine, keys_ref[...], zero)
    values_m = jnp.concatenate(
        [jnp.where(mine, values_ref[...], zero), jnp.ones((tokens, extra), BF16)], axis=1
    )
    feature = pl.multiple_of(head * head_size, head_size)
    query_t = query_t_ref[pl.ds(feature, head_size), :]
    grads_t = grads_t_ref[pl.ds(feature, head_size), :]
    gk_t = jnp.zeros((head_size, tokens), F32)
    gv_t = jnp.zeros((head_size, tokens), F32)
    for top in range(0, tokens, row_block):
        rows = slice(top, top + row_block)
        query = jnp.where(mine, query_ref[rows, :], zero)
        grads = jnp.where(mine, grads_ref[rows, :], zero)
        scores = mm(query, keys_t_ref[...]) * scale + bias_full[rows, :].astype(F32)
        weights = jnp.exp(scores)
        attended = mm(weights.astype(BF16), values_m)
        inverse = 1.0 / attended[:, part : part + 1]
        attended = attended[:, :part] * inverse
        att_sum[rows, :part] += attended
        delta = jnp.sum(attended * grads.astype(F32), axis=-1, keepdims=True)
        prob = weights * inverse
        grad_prob = mm(grads, values_t_ref[...])
        score = (prob * (grad_prob - delta)).astype(BF16)
        score_full[rows, :] = score
        gq_sum[rows, :] += mm(score, keys_m)
        gk_t = gk_t + mm(query_t[:, rows], score)
        gv_t = gv_t + mm(grads_t[:, rows], prob.astype(BF16))
    gk_sum[pl.ds(feature, head_size), :] = gk_t
    gv_sum[pl.ds(feature, head_size), :] = gv_t

    for other in range(row_parts):
        dbias_ref = give_ref if other % 2 else keep_ref
        unit = 0
        for place, (chip, unit_head) in enumerate(unit_order(heads)):
            if chip == other // 2:
                unit = jnp.where(head == unit_head, place, unit)
        for column, side, rows in places(row_ref[0] ^ other):
            dbias_ref[unit, column, :, side * cols : (side + 1) * cols] = score_full[
                rows, column * cols : (column + 1) * cols
            ]

    @pl.when(head == heads - 1)
    def _():
        results = (
            gq_sum[...] * scale,
            (gk_sum[...] * scale).T,
            gv_sum[...].T,
            att_sum[:, :part],
        )
        for kind, values in enumerate(results):
            rounded = values.astype(BF16)
            for slot in range(groups):
                out_refs[slot][:, kind * part : (kind + 1) * part] = rounded[
                    slot * cols : (slot + 1) * cols
                ]


def attention(group_index, row_index, acts, bias, head_size):
    groups = len(acts)
    row_parts = len(bias) - 2
    cols, width = acts[0].shape
    tokens = groups * cols
    part = width // 4
    _, heads, half, lanes = bias[0].shape
    row_block = 256 if tokens % 256 == 0 else cols
    padded = (part // 128 + 1) * 128
    units = (row_parts // 2 * heads, groups, half, lanes)
    *grads, keep, give = pl.pallas_call(
        functools.partial(
            attention_kernel,
            groups=groups,
            row_parts=row_parts,
            head_size=head_size,
            row_block=row_block,
        ),
        grid=(heads,),
        in_specs=[smem(), smem()]
        + [
            pl.BlockSpec((block.shape[0], 1, half, lanes), lambda h: (0, h, 0, 0))
            for block in bias
        ]
        + [pl.BlockSpec((cols, width), lambda h: (0, 0))] * groups,
        out_specs=[pl.BlockSpec((cols, width), lambda h: (0, 0))] * groups
        + [pl.BlockSpec(units, lambda h: (0, 0, 0, 0))] * 2,
        out_shape=[jax.ShapeDtypeStruct((cols, width), BF16)] * groups
        + [jax.ShapeDtypeStruct(units, BF16)] * 2,
        scratch_shapes=[pltpu.VMEM((tokens, part), BF16) for _ in range(4)]
        + [pltpu.VMEM((part, tokens), BF16) for _ in range(4)]
        + [
            pltpu.VMEM((tokens, tokens), BF16),
            pltpu.VMEM((tokens, tokens), BF16),
            pltpu.VMEM((tokens, padded), F32),
            pltpu.VMEM((tokens, part), F32),
            pltpu.VMEM((part, tokens), F32),
            pltpu.VMEM((part, tokens), F32),
        ],
        compiler_params=params(),
    )(group_index, row_index, *bias, *acts)
    return grads, keep, give


def finish_kernel(
    group_ref,
    single_ref,
    noised_ref,
    cot_ref,
    gamma_ref,
    gate_ref,
    w_gamma_ref,
    w_beta_ref,
    w_outgate_ref,
    w_query_ref,
    w_key_ref,
    w_value_ref,
    w_out_ref,
    *rest,
    groups,
    calls,
):
    got_refs = rest[: groups * calls]
    updated_ref, d_single_ref, stage_ref = rest[groups * calls :]
    width = stage_ref.shape[3]
    part = width // 4
    for slot in range(groups):
        for call in range(calls):
            stage_ref[lax.rem(group_ref[0] + slot, groups), call] = got_refs[
                call * groups + slot
            ][...]

    def take(kind):
        return jnp.concatenate(
            [
                stage_ref[group, call, :, kind * part : (kind + 1) * part]
                for group in range(groups)
                for call in range(calls)
            ],
            axis=1,
        )

    out_gate = gate_ref[...]
    cond_gamma = gamma_ref[...]
    block_update = mm(take(3), w_out_ref[...])
    noised = noised_ref[...].astype(F32)
    updated_ref[...] = (noised + out_gate * block_update).astype(BF16)
    gate_part = cot_ref[...].astype(F32) * block_update
    pre_gate = (gate_part * out_gate * (1.0 - out_gate)).astype(BF16)
    grad_input = mm_nt(take(0), w_query_ref[...])
    grad_input += mm_nt(take(1), w_key_ref[...])
    grad_input += mm_nt(take(2), w_value_ref[...])
    noised_norm, _ = norm_rows(noised)
    pre_gamma = (grad_input * noised_norm * cond_gamma * (1.0 - cond_gamma)).astype(BF16)
    grad_snorm = mm_nt(pre_gamma, w_gamma_ref[...])
    grad_snorm += mm_nt(grad_input.astype(BF16), w_beta_ref[...])
    grad_snorm += mm_nt(pre_gate, w_outgate_ref[...])
    single_norm, single_inv = norm_rows(single_ref[...].astype(F32))
    d_single_ref[...] = norm_back(grad_snorm, single_norm, single_inv)


def swap_groups(sends, direction):
    groups = len(sends)
    got = [sends[0]]
    for shift in range(1, groups):
        perm = [(index, (index + direction * shift) % groups) for index in range(groups)]
        got.append(lax.ppermute(sends[shift], "grp", perm))
    return got


def flip_rows(values, bits, row_total):
    return lax.ppermute(values, "rows", [(index, index ^ bits) for index in range(row_total)])


def gather_rows(own, acts, row_total):
    half = own.shape[0] // 2
    near = flip_rows(own, 2, row_total)
    far = flip_rows(own, 4, row_total)
    first = flip_rows(near[:half], 4, row_total)
    second = flip_rows(far[half:], 2, row_total)
    first, second, acts[1], acts[2], acts[3] = lax.optimization_barrier(
        (first, second, acts[1], acts[2], acts[3])
    )
    blocks = []
    for block in (own, near, far, first, second):
        blocks += [block, flip_rows(block, 1, row_total)]
    return blocks, acts


def add_last_kernel(own_ref, far_ref, near_ref, *out_refs):
    heads = own_ref.shape[0]
    half = heads // 2
    for head in range(heads):
        other = far_ref[head] if head < half else near_ref[head - half]
        total = (own_ref[head].astype(F32) + other.astype(F32)).astype(BF16)
        for slot, out_ref in enumerate(out_refs):
            out_ref[head] = total[slot]


def scatter_rows(keep, give, row_total):
    got = flip_rows(give, 1, row_total)
    heads = keep.shape[0] // 4
    part = heads // 2

    def add(first, count, *others):
        total = keep[first : first + count].astype(F32) + got[first : first + count].astype(F32)
        for other in others:
            total += other.astype(F32)
        return total.astype(BF16)

    near = flip_rows(add(heads, heads), 2, row_total)
    far = flip_rows(add(2 * heads, heads), 4, row_total)
    far_two = flip_rows(add(3 * heads, part, near[part:]), 4, row_total)
    near_two = flip_rows(add(3 * heads + part, part, far[part:]), 2, row_total)
    own = add(0, heads, jnp.concatenate([near[:part], far[:part]]))
    return own, far_two, near_two


def add_last(own, far_two, near_two):
    heads, groups, half, lanes = own.shape
    return pl.pallas_call(
        add_last_kernel,
        in_specs=[vmem()] * 3,
        out_specs=[vmem()] * groups,
        out_shape=[jax.ShapeDtypeStruct((heads, half, lanes), BF16)] * groups,
        compiler_params=params(),
    )(own, far_two, near_two)


def sum_rows(values, row_total):
    mine = values.astype(BF16)
    both = (mine.astype(F32) + flip_rows(mine, 1, row_total).astype(F32)).astype(BF16)
    near, far, last = (flip_rows(both, bits, row_total).astype(F32) for bits in (2, 4, 6))
    return (both.astype(F32) + near) + (far + last)


def split_heads(
    single,
    pair,
    chains,
    noised,
    w_gamma,
    w_beta,
    w_outgate,
    w_query,
    w_key,
    w_value,
    w_out,
    w_pair,
    chain_gain,
    cotangent,
    *,
    groups,
    row_total,
):
    cols, _ = single.shape
    tokens = chains.shape[0]
    width = noised.shape[2]
    head_size = width // w_pair.shape[1]
    calls = 1
    row_index = lax.axis_index("rows").reshape(1)
    group_index = lax.axis_index("grp").reshape(1)
    bias_send, stats = pair_bias(
        pair, w_pair, chain_gain, chains, group_index, row_index, groups
    )
    bias_got = swap_groups(bias_send, 1)
    noised = noised[0]
    cotangent = cotangent[0]
    *acts_send, cond_gamma, out_gate = pl.pallas_call(
        functools.partial(project_kernel, groups=groups, calls=calls),
        in_specs=[smem()] + [vmem()] * 10,
        out_shape=[
            jax.ShapeDtypeStruct((cols, 4 * width // groups), BF16) for _ in range(groups)
        ]
        + [
            jax.ShapeDtypeStruct((cols, width), F32),
            jax.ShapeDtypeStruct((cols, width), F32),
        ],
        scratch_shapes=[pltpu.VMEM((groups, cols, 4 * width // groups), BF16)],
        compiler_params=params(),
    )(
        group_index,
        single,
        noised,
        cotangent,
        w_gamma,
        w_beta,
        w_outgate,
        w_query,
        w_key,
        w_value,
        w_out,
    )
    bias_got, _ = lax.optimization_barrier((bias_got, acts_send))
    acts = swap_groups(acts_send, 1)
    bias_all, acts = gather_rows(jnp.stack(bias_got), acts, row_total)
    grads_send, keep, give = attention(group_index, row_index, acts, bias_all, head_size)
    grads = swap_groups(grads_send, -1)
    own, far_two, near_two = scatter_rows(keep, give, row_total)
    own, grads = lax.optimization_barrier((own, grads))
    updated, d_part = pl.pallas_call(
        functools.partial(finish_kernel, groups=groups, calls=calls),
        in_specs=[smem()] + [vmem()] * (12 + groups * calls),
        out_shape=[
            jax.ShapeDtypeStruct((cols, width), BF16),
            jax.ShapeDtypeStruct(single.shape, F32),
        ],
        scratch_shapes=[pltpu.VMEM((groups, calls, cols, 4 * width // (groups * calls)), BF16)],
        compiler_params=params(),
    )(
        group_index,
        single,
        noised,
        cotangent,
        cond_gamma,
        out_gate,
        w_gamma,
        w_beta,
        w_outgate,
        w_query,
        w_key,
        w_value,
        w_out,
        *grads,
    )
    far_two, near_two, d_part = lax.optimization_barrier((far_two, near_two, d_part))
    dbias_back = swap_groups(add_last(own, far_two, near_two), -1)
    d_single = sum_rows(d_part, row_total)
    d_pair = pair_back(pair, stats, dbias_back, w_pair, group_index, groups, float(tokens))
    return (updated[None], d_single, d_pair)


def project(acts, weight):
    return jnp.einsum("std,de->ste", acts, weight, preferred_element_type=F32)


def project_back(acts, weight):
    return jnp.einsum("ste,de->std", acts, weight, preferred_element_type=F32)


def split_keys(
    single,
    pair,
    chains,
    noised,
    w_gamma,
    w_beta,
    w_outgate,
    w_query,
    w_key,
    w_value,
    w_out,
    w_pair,
    chain_gain,
    cotangent,
):
    col_count = single.shape[0]
    row_count = pair.shape[0]
    head_count = w_pair.shape[1]
    model_width = w_query.shape[0]
    head_size = model_width // head_count
    sample_count = noised.shape[0]
    token_total = chains.shape[0]
    score_scale = 1.0 / math.sqrt(head_size)
    row_index = lax.axis_index("rows")
    group_index = lax.axis_index("grp")
    chain_rows = lax.dynamic_slice_in_dim(chains, row_index * row_count, row_count)
    chain_cols = lax.dynamic_slice_in_dim(chains, group_index * col_count, col_count)
    pair_norm, pair_inv = norm_rows(pair.astype(jnp.float32))
    projected = jnp.einsum(
        "ijc,ch->hij", pair_norm.astype(jnp.bfloat16), w_pair, preferred_element_type=jnp.float32
    )
    same_chain = (chain_rows[:, None] == chain_cols[None, :]).astype(jnp.float32)
    bias_block = (projected + chain_gain[:, None, None] * same_chain[None]).astype(jnp.bfloat16)
    bias_keys = lax.all_gather(bias_block, "rows", axis=1, tiled=True)
    single_norm, single_inv = norm_rows(single.astype(jnp.float32))
    single_b = single_norm.astype(jnp.bfloat16)
    cond_gamma = jax.nn.sigmoid(jnp.dot(single_b, w_gamma, preferred_element_type=jnp.float32))
    cond_beta = jnp.dot(single_b, w_beta, preferred_element_type=jnp.float32)
    out_gate = jax.nn.sigmoid(jnp.dot(single_b, w_outgate, preferred_element_type=jnp.float32))
    noised_f = noised.astype(jnp.float32)
    noised_norm, noised_inv = norm_rows(noised_f)
    x_b = (noised_norm * cond_gamma[None] + cond_beta[None]).astype(jnp.bfloat16)
    queries = project(x_b, w_query).astype(jnp.bfloat16)
    keys_own = project(x_b, w_key).astype(jnp.bfloat16)
    values_own = project(x_b, w_value).astype(jnp.bfloat16)
    queries_all = lax.all_gather(queries, "grp", axis=1, tiled=True)
    query_heads = queries_all.reshape(sample_count, token_total, head_count, head_size)
    key_heads = keys_own.reshape(sample_count, col_count, head_count, head_size)
    value_heads = values_own.reshape(sample_count, col_count, head_count, head_size)
    scores = (
        jnp.einsum("sihe,sjhe->shij", query_heads, key_heads, preferred_element_type=jnp.float32)
        * score_scale
        + bias_keys.astype(jnp.float32)[None]
    )
    exp_scores = jnp.exp(scores)
    exp_total = lax.psum(jnp.sum(exp_scores, axis=-1).astype(jnp.bfloat16), "grp").astype(
        jnp.float32
    )
    attn_prob = exp_scores / exp_total[..., None]
    prob_b = attn_prob.astype(jnp.bfloat16)
    attended_part = jnp.einsum(
        "shij,sjhe->sihe", prob_b, value_heads, preferred_element_type=jnp.float32
    )
    attended_part = attended_part.reshape(sample_count, token_total, model_width)
    attended = lax.psum_scatter(
        attended_part.astype(jnp.bfloat16), "grp", scatter_dimension=1, tiled=True
    )
    block_update = project(attended, w_out)
    updated = (noised_f + out_gate[None] * block_update).astype(jnp.bfloat16)
    grad_out = cotangent.astype(jnp.float32)
    gate_part = jnp.sum(grad_out * block_update, axis=0)
    grad_update = (grad_out * out_gate[None]).astype(jnp.bfloat16)
    grad_attn = project_back(grad_update, w_out).astype(jnp.bfloat16)
    grads_all = lax.all_gather(grad_attn, "grp", axis=1, tiled=True)
    grad_heads = grads_all.reshape(sample_count, token_total, head_count, head_size)
    grad_prob = jnp.einsum(
        "sihe,sjhe->shij", grad_heads, value_heads, preferred_element_type=jnp.float32
    )
    row_delta = lax.psum(
        jnp.sum(attn_prob * grad_prob, axis=-1).astype(jnp.bfloat16), "grp"
    ).astype(jnp.float32)
    grad_score = attn_prob * (grad_prob - row_delta[..., None])
    score_b = grad_score.astype(jnp.bfloat16)
    query_part = (
        jnp.einsum("shij,sjhe->sihe", score_b, key_heads, preferred_element_type=jnp.float32)
        * score_scale
    )
    query_part = query_part.reshape(sample_count, token_total, model_width)
    grad_query = lax.psum_scatter(
        query_part.astype(jnp.bfloat16), "grp", scatter_dimension=1, tiled=True
    )
    grad_key = (
        jnp.einsum("shij,sihe->sjhe", score_b, query_heads, preferred_element_type=jnp.float32)
        * score_scale
    )
    grad_value = jnp.einsum(
        "shij,sihe->sjhe", prob_b, grad_heads, preferred_element_type=jnp.float32
    )
    grad_key = grad_key.reshape(sample_count, col_count, model_width).astype(jnp.bfloat16)
    grad_value = grad_value.reshape(sample_count, col_count, model_width).astype(jnp.bfloat16)
    grad_input = (
        project_back(grad_query, w_query)
        + project_back(grad_key, w_key)
        + project_back(grad_value, w_value)
    )
    gamma_part = jnp.sum(grad_input * noised_norm, axis=0)
    beta_part = jnp.sum(grad_input, axis=0)
    gamma_sum, beta_sum, gate_sum = lax.psum((gamma_part, beta_part, gate_part), "rows")
    pre_gamma = (gamma_sum * cond_gamma * (1.0 - cond_gamma)).astype(jnp.bfloat16)
    pre_gate = (gate_sum * out_gate * (1.0 - out_gate)).astype(jnp.bfloat16)
    grad_snorm = jnp.dot(pre_gamma, w_gamma.T, preferred_element_type=jnp.float32)
    grad_snorm = grad_snorm + jnp.dot(
        beta_sum.astype(jnp.bfloat16), w_beta.T, preferred_element_type=jnp.float32
    )
    grad_snorm = grad_snorm + jnp.dot(pre_gate, w_outgate.T, preferred_element_type=jnp.float32)
    d_single = norm_back(grad_snorm, single_norm, single_inv)
    bias_part = jnp.sum(score_b, axis=0, dtype=jnp.float32)
    bias_own = lax.psum_scatter(bias_part, "rows", scatter_dimension=1, tiled=True)
    bias_grad = (bias_own * token_total).astype(jnp.bfloat16)
    grad_pairn = jnp.einsum("hij,ch->ijc", bias_grad, w_pair, preferred_element_type=jnp.float32)
    d_pair = norm_back(grad_pairn, pair_norm, pair_inv).astype(jnp.bfloat16)
    return (updated, d_single, d_pair)


def solution(mesh):
    in_specs = (
        P("grp", None),
        P("rows", "grp", None),
        P(),
        P("rows", "grp", None),
        P(),
        P(),
        P(),
        P(),
        P(),
        P(),
        P(),
        P(),
        P(),
        P("rows", "grp", None),
    )
    out_specs = (P("rows", "grp", None), P("grp", None), P("rows", "grp", None))
    groups = mesh.shape["grp"]
    row_total = mesh.shape["rows"]

    def on_device(*args):
        pair, noised, w_pair = args[1], args[3], args[11]
        fits = (
            pair.shape[0] % 32 == 0
            and pair.shape[1] % pair.shape[0] == 0
            and row_total == 8
            and noised.shape[0] == 1
            and noised.shape[1] % 64 == 0
            and w_pair.shape[1] % (2 * groups) == 0
        )
        if fits:
            return split_heads(*args, groups=groups, row_total=row_total)
        return split_keys(*args)

    return jax.shard_map(
        on_device, mesh=mesh, in_specs=in_specs, out_specs=out_specs, check_vma=False
    )
```

```python
import functools
import math

import jax
import jax.numpy as jnp
from jax import lax
from jax.experimental import pallas as pl
from jax.experimental.pallas import tpu as pltpu
from jax.sharding import PartitionSpec as P

EPSILON = 1e-05
BF16 = jnp.bfloat16
F32 = jnp.float32
VMEM_LIMIT = 56 * 1024 * 1024


def norm_rows(values):
    center = values - jnp.mean(values, axis=-1, keepdims=True)
    inverse = lax.rsqrt(jnp.mean(center * center, axis=-1, keepdims=True) + EPSILON)
    return (center * inverse, inverse)


def norm_back(grad_in, normed, inverse):
    grad_mean = jnp.mean(grad_in, axis=-1, keepdims=True)
    cross_mean = jnp.mean(grad_in * normed, axis=-1, keepdims=True)
    return inverse * (grad_in - grad_mean - normed * cross_mean)


def mm(left, right):
    return lax.dot_general(left, right, (((1,), (0,)), ((), ())), preferred_element_type=F32)


def mm_nt(left, right):
    return lax.dot_general(left, right, (((1,), (1,)), ((), ())), preferred_element_type=F32)


def mm_tn(left, right):
    return lax.dot_general(left, right, (((0,), (0,)), ((), ())), preferred_element_type=F32)


def sigmoid(values):
    return 1.0 / (1.0 + jnp.exp(-values))


def params():
    return pltpu.CompilerParams(vmem_limit_bytes=VMEM_LIMIT)


def smem():
    return pl.BlockSpec(memory_space=pltpu.SMEM)


def vmem():
    return pl.BlockSpec(memory_space=pltpu.VMEM)


def project_kernel(
    group_ref,
    single_ref,
    noised_ref,
    cot_ref,
    w_gamma_ref,
    w_beta_ref,
    w_outgate_ref,
    w_query_ref,
    w_key_ref,
    w_value_ref,
    w_out_ref,
    *rest,
    groups,
    calls,
):
    send_refs = rest[:groups]
    gamma_ref, gate_ref, stage_ref = rest[groups:]
    width = stage_ref.shape[2]
    part = width // (4 * calls)
    group_own = group_ref[0]
    single_norm, _ = norm_rows(single_ref[...].astype(F32))
    single_b = single_norm.astype(BF16)
    cond_gamma = sigmoid(mm(single_b, w_gamma_ref[...]))
    gamma_ref[...] = cond_gamma
    out_gate = sigmoid(mm(single_b, w_outgate_ref[...]))
    gate_ref[...] = out_gate
    cond_beta = mm(single_b, w_beta_ref[...])
    noised_norm, _ = norm_rows(noised_ref[...].astype(F32))
    x_b = (noised_norm * cond_gamma + cond_beta).astype(BF16)

    def put(kind, values):
        rounded = values.astype(BF16)
        for group in range(groups):
            slot = group_own ^ group
            for call in range(calls):
                feature = (group * calls + call) * part
                lane = (call * 4 + kind) * part
                stage_ref[slot, :, lane : lane + part] = rounded[:, feature : feature + part]

    put(0, mm(x_b, w_query_ref[...]))
    put(1, mm(x_b, w_key_ref[...]))
    put(2, mm(x_b, w_value_ref[...]))
    grad_update = (cot_ref[...].astype(F32) * out_gate).astype(BF16)
    put(3, mm_nt(grad_update, w_out_ref[...]))
    for slot in range(groups):
        send_refs[slot][...] = stage_ref[slot]


def lane_tiles(cols):
    return [(tile, tile * 128, min(cols, tile * 128 + 128)) for tile in range(-(-cols // 128))]


def mean_matrix(channels):
    first = lax.broadcasted_iota(jnp.int32, (2 * channels, 2 * channels), 0) >= channels
    second = lax.broadcasted_iota(jnp.int32, (2 * channels, 2 * channels), 1) >= channels
    return jnp.where(first == second, 1.0 / channels, 0.0).astype(BF16)


def center_rows(pair_ref, first, batch, means):
    _, _, cols, channels = pair_ref.shape
    both = jnp.concatenate(
        [pair_ref[side, first : first + batch].reshape(batch * cols, channels) for side in range(2)],
        axis=1,
    )
    return both.astype(F32) - mm(both, means)


def lane_pad(block, before, total):
    rows, width = block.shape
    pieces = [block]
    if before:
        pieces = [jnp.zeros((rows, before), block.dtype)] + pieces
    if total > before + width:
        pieces = pieces + [jnp.zeros((rows, total - before - width), block.dtype)]
    return jnp.concatenate(pieces, axis=1)


def bias_kernel(
    group_ref,
    rows_ref,
    chains_ref,
    gain_ref,
    pair_ref,
    w_pair_ref,
    cols_ref,
    *rest,
    groups,
    batch,
):
    send_refs = rest[:groups]
    stats_ref, flat_ref, gains_ref, stage_ref = rest[groups:]
    _, step, cols, channels = pair_ref.shape
    heads = gain_ref.shape[0]
    per_group = heads // groups
    half = step * pl.num_programs(0)
    group_own = group_ref[0]
    row_base = rows_ref[0] * 2 * half + pl.program_id(0) * step
    means = mean_matrix(channels)
    weight = w_pair_ref[...].astype(F32).T.astype(BF16)
    mean_part = jnp.full((channels, heads), 1.0 / channels, BF16)
    mixed = []
    for inner in range(2):
        for part, offset in ((weight, 0), (mean_part, heads)):
            for side in range(2):
                mixed.append(lane_pad(part, 2 * heads * (2 * inner + side) + offset, 8 * heads))
    mixed = jnp.concatenate(mixed, axis=0)
    chain_all = cols_ref[...].reshape(1, groups * cols)
    chain_cols = chain_all[:, :cols]
    for group in range(1, groups):
        here = chain_all[:, group * cols : (group + 1) * cols]
        chain_cols = jnp.where(group_own == group, here, chain_cols)
    for head in range(heads):
        gains_ref[head : head + 1, :] = jnp.full((1, cols), gain_ref[head], F32)

    for first in range(0, step, batch):
        center = center_rows(pair_ref, first, batch, means)
        center_b = center.astype(BF16)
        square = (center * center).astype(BF16)
        for base in range(0, batch, 2):
            one = slice(base * cols, (base + 1) * cols)
            two = slice((base + 1) * cols, (base + 2) * cols)
            left = jnp.concatenate(
                [center_b[one], square[one], center_b[two], square[two]], axis=1
            )
            sums = mm(left, mixed).T
            for inner in range(2):
                row = first + base + inner
                for side in range(2):
                    top = 2 * heads * (2 * inner + side)
                    inverse = lax.rsqrt(sums[top + heads : top + 2 * heads] + EPSILON)
                    projected = sums[top : top + heads] * inverse
                    stats_ref[side, row, :heads, :] = projected
                    stats_ref[side, row, heads:, :] = inverse[:8]
                    chain = chains_ref[row_base + side * half + row]
                    same = (chain_cols == chain).astype(F32)
                    values = projected + gains_ref[...] * same
                    for tile, start, end in lane_tiles(cols):
                        piece = lane_pad(values[:, start:end], 0, 128)
                        flat_ref[side, tile, pl.ds(row, heads, stride=step), :] = piece
    for head in range(heads):
        slot = group_own ^ (head // per_group)
        values = jnp.concatenate(
            [
                flat_ref[side, tile, head * step : (head + 1) * step, : end - start]
                for side in range(2)
                for tile, start, end in lane_tiles(cols)
            ],
            axis=1,
        )
        stage_ref[slot, head % per_group] = values.astype(BF16)
    for slot in range(groups):
        send_refs[slot][...] = stage_ref[slot]


def pair_bias(pair, w_pair, chain_gain, chains, group_index, row_index, groups):
    rows, cols, channels = pair.shape
    heads = w_pair.shape[1]
    per_group = heads // groups
    half = rows // 2
    step = 16
    tiles = -(-cols // 128)
    *sends, stats = pl.pallas_call(
        functools.partial(bias_kernel, groups=groups, batch=4),
        grid=(half // step,),
        in_specs=[
            smem(),
            smem(),
            smem(),
            smem(),
            pl.BlockSpec((2, step, cols, channels), lambda t: (0, t, 0, 0)),
            pl.BlockSpec((heads, channels), lambda t: (0, 0)),
            pl.BlockSpec((groups * cols,), lambda t: (0,)),
        ],
        out_specs=[
            pl.BlockSpec((per_group, step, 2 * cols), lambda t: (0, t, 0)) for _ in range(groups)
        ]
        + [pl.BlockSpec((2, step, heads + 8, cols), lambda t: (0, t, 0, 0))],
        out_shape=[
            jax.ShapeDtypeStruct((per_group, half, 2 * cols), BF16) for _ in range(groups)
        ]
        + [jax.ShapeDtypeStruct((2, half, heads + 8, cols), F32)],
        scratch_shapes=[
            pltpu.VMEM((2, tiles, heads * step, 128), F32),
            pltpu.VMEM((heads, cols), F32),
            pltpu.VMEM((groups, per_group, step, 2 * cols), BF16),
        ],
        compiler_params=params(),
    )(
        group_index,
        row_index,
        chains,
        chain_gain,
        pair.reshape(2, half, cols, channels),
        w_pair.T,
        chains,
    )
    return sends, stats


def pair_back_kernel(
    group_ref, pair_ref, stats_ref, w_pair_ref, *rest, groups, calls, factor, batch
):
    grad_refs = rest[: groups * calls]
    out_ref, flat_ref = rest[groups * calls :]
    _, step, cols, channels = pair_ref.shape
    per_call = grad_refs[0].shape[0]
    heads = groups * calls * per_call
    group_own = group_ref[0]
    means = mean_matrix(channels)
    weight = w_pair_ref[...].astype(F32)
    weight = (weight - jnp.mean(weight, axis=-1, keepdims=True)).astype(BF16)
    spread = lax.broadcasted_iota(jnp.int32, (heads, channels), 0)
    spread = (spread < 2).astype(F32).astype(BF16)
    block = jnp.concatenate(
        [lane_pad(weight, 0, 2 * channels), lane_pad(spread, channels, 2 * channels)], axis=0
    )
    weights = jnp.concatenate(
        [lane_pad(block, 2 * channels * place, 8 * channels) for place in range(4)], axis=0
    )
    blank = jnp.zeros((heads - 2, cols), F32)
    for number in range(groups * calls):
        call, slot = divmod(number, groups)
        source = (group_own ^ slot) * calls + call
        for head in range(per_call):
            values = grad_refs[number][head].astype(F32)
            top = pl.multiple_of((source * per_call + head) * step, step)
            for side in range(2):
                for tile, start, end in lane_tiles(cols):
                    flat_ref[side, tile, pl.ds(top, step), : end - start] = values[
                        :, side * cols + start : side * cols + end
                    ]

    for first in range(0, step, batch):
        center = center_rows(pair_ref, first, batch, means)
        for base in range(0, batch, 2):
            places = [(base + inner, side) for inner in range(2) for side in range(2)]
            left = []
            for inner, side in places:
                grads = jnp.concatenate(
                    [
                        flat_ref[side, tile, pl.ds(first + inner, heads, stride=step), :][
                            :, : end - start
                        ]
                        for tile, start, end in lane_tiles(cols)
                    ],
                    axis=1,
                )
                projected = stats_ref[side, first + inner, :heads, :]
                inverse = stats_ref[side, first + inner, heads : heads + 1, :]
                cross = jnp.sum(grads * projected, axis=0, keepdims=True) * (1.0 / channels)
                scaled = grads * (inverse * factor)
                cross = cross * (inverse * inverse * factor)
                cross_high = cross.astype(BF16).astype(F32)
                left += [scaled, cross_high, cross - cross_high, blank]
            both = mm_tn(jnp.concatenate(left, axis=0).astype(BF16), weights)
            for place, (inner, side) in enumerate(places):
                rows = slice(inner * cols, (inner + 1) * cols)
                lanes = slice(side * channels, (side + 1) * channels)
                start = 2 * channels * place
                middle, end = start + channels, start + 2 * channels
                out_ref[side, first + inner] = (
                    both[:, start:middle] - center[rows, lanes] * both[:, middle:end]
                ).astype(BF16)


def pair_back(pair, stats, grads, w_pair, group_index, groups, factor):
    rows, cols, channels = pair.shape
    per_call = grads[0].shape[0]
    heads = len(grads) * per_call
    half = rows // 2
    step = 16
    tiles = -(-cols // 128)
    out = pl.pallas_call(
        functools.partial(
            pair_back_kernel, groups=groups, calls=len(grads) // groups, factor=factor, batch=4
        ),
        grid=(half // step,),
        in_specs=[
            smem(),
            pl.BlockSpec((2, step, cols, channels), lambda t: (0, t, 0, 0)),
            pl.BlockSpec((2, step, heads + 8, cols), lambda t: (0, t, 0, 0)),
            pl.BlockSpec((heads, channels), lambda t: (0, 0)),
        ]
        + [pl.BlockSpec((per_call, step, 2 * cols), lambda t: (0, t, 0)) for _ in grads],
        out_specs=pl.BlockSpec((2, step, cols, channels), lambda t: (0, t, 0, 0)),
        out_shape=jax.ShapeDtypeStruct((2, half, cols, channels), BF16),
        scratch_shapes=[pltpu.VMEM((2, tiles, heads * step, 128), F32)],
        compiler_params=params(),
    )(group_index, pair.reshape(2, half, cols, channels), stats, w_pair.T, *grads)
    return out.reshape(rows, cols, channels)


def unit_order(heads):
    first, second = range(heads // 2), range(heads // 2, heads)
    order = [(0, head) for head in range(heads)]
    order += [(1, head) for head in first] + [(3, head) for head in first]
    order += [(2, head) for head in second] + [(3, head) for head in second]
    order += [(2, head) for head in first] + [(1, head) for head in second]
    return order


def attention_kernel(group_ref, row_ref, *rest, groups, row_parts, head_size, row_block):
    bias_refs = rest[: row_parts + 2]
    acts_refs = rest[row_parts + 2 : row_parts + 2 + groups]
    rest = rest[row_parts + 2 + groups :]
    out_refs = rest[:groups]
    (
        keep_ref,
        give_ref,
        query_ref,
        keys_ref,
        values_ref,
        grads_ref,
        query_t_ref,
        keys_t_ref,
        values_t_ref,
        grads_t_ref,
        bias_full,
        score_full,
        att_sum,
        gq_sum,
        gk_sum,
        gv_sum,
    ) = rest[groups:]
    head = pl.program_id(0)
    heads = keep_ref.shape[0] * 2 // row_parts
    group_own = group_ref[0]
    cols, width = acts_refs[0].shape
    tokens = groups * cols
    part = width // 4
    half = bias_refs[0].shape[2]
    scale = 1.0 / math.sqrt(head_size)
    extra = att_sum.shape[1] - part
    plain = (query_ref, keys_ref, values_ref, grads_ref)
    turned = (query_t_ref, keys_t_ref, values_t_ref, grads_t_ref)

    @pl.when(head == 0)
    def _():
        for kind in range(4):
            for slot in range(groups):
                plain[kind][slot * cols : (slot + 1) * cols, :] = acts_refs[slot][
                    :, kind * part : (kind + 1) * part
                ]
            turned[kind][...] = plain[kind][...].T
        att_sum[...] = jnp.zeros_like(att_sum)
        gq_sum[...] = jnp.zeros_like(gq_sum)

    def places(row_part):
        first = row_part * (2 * half)
        slot = group_own ^ (first // cols)
        for side in range(2):
            top = slot * cols + lax.rem(first, cols) + side * half
            top = pl.multiple_of(top, 16)
            for column in range(groups):
                yield column, side, pl.ds(top, half)

    for other in range(row_parts):
        for column, side, rows in places(row_ref[0] ^ other):
            block, place = bias_refs[other], column
            if other >= row_parts - 2 and column >= groups // 2:
                block, place = bias_refs[other + 2], column - groups // 2
            bias_full[rows, column * cols : (column + 1) * cols] = block[
                place, 0, :, side * cols : (side + 1) * cols
            ]

    lane = lax.broadcasted_iota(jnp.int32, (1, part), 1)
    mine = (lane >= head * head_size) & (lane < (head + 1) * head_size)
    zero = jnp.zeros((), BF16)
    keys_m = jnp.where(mine, keys_ref[...], zero)
    values_m = jnp.concatenate(
        [jnp.where(mine, values_ref[...], zero), jnp.ones((tokens, extra), BF16)], axis=1
    )
    feature = pl.multiple_of(head * head_size, head_size)
    query_t = query_t_ref[pl.ds(feature, head_size), :]
    grads_t = grads_t_ref[pl.ds(feature, head_size), :]
    gk_t = jnp.zeros((head_size, tokens), F32)
    gv_t = jnp.zeros((head_size, tokens), F32)
    for top in range(0, tokens, row_block):
        rows = slice(top, top + row_block)
        query = jnp.where(mine, query_ref[rows, :], zero)
        grads = jnp.where(mine, grads_ref[rows, :], zero)
        scores = mm(query, keys_t_ref[...]) * scale + bias_full[rows, :].astype(F32)
        weights = jnp.exp(scores)
        attended = mm(weights.astype(BF16), values_m)
        inverse = 1.0 / attended[:, part : part + 1]
        attended = attended[:, :part] * inverse
        att_sum[rows, :part] += attended
        delta = jnp.sum(attended * grads.astype(F32), axis=-1, keepdims=True)
        prob = weights * inverse
        grad_prob = mm(grads, values_t_ref[...])
        score = (prob * (grad_prob - delta)).astype(BF16)
        score_full[rows, :] = score
        gq_sum[rows, :] += mm(score, keys_m)
        gk_t = gk_t + mm(query_t[:, rows], score)
        gv_t = gv_t + mm(grads_t[:, rows], prob.astype(BF16))
    gk_sum[pl.ds(feature, head_size), :] = gk_t
    gv_sum[pl.ds(feature, head_size), :] = gv_t

    for other in range(row_parts):
        dbias_ref = give_ref if other % 2 else keep_ref
        unit = 0
        for place, (chip, unit_head) in enumerate(unit_order(heads)):
            if chip == other // 2:
                unit = jnp.where(head == unit_head, place, unit)
        for column, side, rows in places(row_ref[0] ^ other):
            dbias_ref[unit, column, :, side * cols : (side + 1) * cols] = score_full[
                rows, column * cols : (column + 1) * cols
            ]

    @pl.when(head == heads - 1)
    def _():
        results = (
            gq_sum[...] * scale,
            (gk_sum[...] * scale).T,
            gv_sum[...].T,
            att_sum[:, :part],
        )
        for kind, values in enumerate(results):
            rounded = values.astype(BF16)
            for slot in range(groups):
                out_refs[slot][:, kind * part : (kind + 1) * part] = rounded[
                    slot * cols : (slot + 1) * cols
                ]


def attention(group_index, row_index, acts, bias, head_size):
    groups = len(acts)
    row_parts = len(bias) - 2
    cols, width = acts[0].shape
    tokens = groups * cols
    part = width // 4
    _, heads, half, lanes = bias[0].shape
    row_block = 256 if tokens % 256 == 0 else cols
    padded = (part // 128 + 1) * 128
    units = (row_parts // 2 * heads, groups, half, lanes)
    *grads, keep, give = pl.pallas_call(
        functools.partial(
            attention_kernel,
            groups=groups,
            row_parts=row_parts,
            head_size=head_size,
            row_block=row_block,
        ),
        grid=(heads,),
        in_specs=[smem(), smem()]
        + [
            pl.BlockSpec((block.shape[0], 1, half, lanes), lambda h: (0, h, 0, 0))
            for block in bias
        ]
        + [pl.BlockSpec((cols, width), lambda h: (0, 0))] * groups,
        out_specs=[pl.BlockSpec((cols, width), lambda h: (0, 0))] * groups
        + [pl.BlockSpec(units, lambda h: (0, 0, 0, 0))] * 2,
        out_shape=[jax.ShapeDtypeStruct((cols, width), BF16)] * groups
        + [jax.ShapeDtypeStruct(units, BF16)] * 2,
        scratch_shapes=[pltpu.VMEM((tokens, part), BF16) for _ in range(4)]
        + [pltpu.VMEM((part, tokens), BF16) for _ in range(4)]
        + [
            pltpu.VMEM((tokens, tokens), BF16),
            pltpu.VMEM((tokens, tokens), BF16),
            pltpu.VMEM((tokens, padded), F32),
            pltpu.VMEM((tokens, part), F32),
            pltpu.VMEM((part, tokens), F32),
            pltpu.VMEM((part, tokens), F32),
        ],
        compiler_params=params(),
    )(group_index, row_index, *bias, *acts)
    return grads, keep, give


def finish_kernel(
    group_ref,
    single_ref,
    noised_ref,
    cot_ref,
    gamma_ref,
    gate_ref,
    w_gamma_ref,
    w_beta_ref,
    w_outgate_ref,
    w_query_ref,
    w_key_ref,
    w_value_ref,
    w_out_ref,
    *rest,
    groups,
    calls,
):
    got_refs = rest[: groups * calls]
    updated_ref, d_single_ref, stage_ref = rest[groups * calls :]
    width = stage_ref.shape[3]
    part = width // 4
    for slot in range(groups):
        for call in range(calls):
            stage_ref[group_ref[0] ^ slot, call] = got_refs[
                call * groups + slot
            ][...]

    def take(kind):
        return jnp.concatenate(
            [
                stage_ref[group, call, :, kind * part : (kind + 1) * part]
                for group in range(groups)
                for call in range(calls)
            ],
            axis=1,
        )

    out_gate = gate_ref[...]
    cond_gamma = gamma_ref[...]
    block_update = mm(take(3), w_out_ref[...])
    noised = noised_ref[...].astype(F32)
    updated_ref[...] = (noised + out_gate * block_update).astype(BF16)
    gate_part = cot_ref[...].astype(F32) * block_update
    pre_gate = (gate_part * out_gate * (1.0 - out_gate)).astype(BF16)
    grad_input = mm_nt(take(0), w_query_ref[...])
    grad_input += mm_nt(take(1), w_key_ref[...])
    grad_input += mm_nt(take(2), w_value_ref[...])
    noised_norm, _ = norm_rows(noised)
    pre_gamma = (grad_input * noised_norm * cond_gamma * (1.0 - cond_gamma)).astype(BF16)
    grad_snorm = mm_nt(pre_gamma, w_gamma_ref[...])
    grad_snorm += mm_nt(grad_input.astype(BF16), w_beta_ref[...])
    grad_snorm += mm_nt(pre_gate, w_outgate_ref[...])
    single_norm, single_inv = norm_rows(single_ref[...].astype(F32))
    d_single_ref[...] = norm_back(grad_snorm, single_norm, single_inv).astype(BF16)


def swap_groups(sends):
    groups = len(sends)
    got = [sends[0]]
    for bits in range(1, groups):
        perm = [(index, index ^ bits) for index in range(groups)]
        got.append(lax.ppermute(sends[bits], "grp", perm))
    return got


def flip_rows(values, bits, row_total):
    return lax.ppermute(values, "rows", [(index, index ^ bits) for index in range(row_total)])


def gather_rows(own, acts, row_total):
    half = own.shape[0] // 2
    near = flip_rows(own, 2, row_total)
    far = flip_rows(own, 4, row_total)
    first = flip_rows(near[:half], 4, row_total)
    second = flip_rows(far[half:], 2, row_total)
    first, second, acts[1], acts[2], acts[3] = lax.optimization_barrier(
        (first, second, acts[1], acts[2], acts[3])
    )
    blocks = []
    for block in (own, near, far, first, second):
        blocks += [block, flip_rows(block, 1, row_total)]
    return blocks, acts


def add_last_kernel(own_ref, far_ref, near_ref, *out_refs):
    heads = own_ref.shape[0]
    half = heads // 2
    for head in range(heads):
        other = far_ref[head] if head < half else near_ref[head - half]
        total = (own_ref[head].astype(F32) + other.astype(F32)).astype(BF16)
        for slot, out_ref in enumerate(out_refs):
            out_ref[head] = total[slot]


def scatter_rows(keep, give, row_total):
    got = flip_rows(give, 1, row_total)
    heads = keep.shape[0] // 4
    part = heads // 2

    def add(first, count, *others):
        total = keep[first : first + count].astype(F32) + got[first : first + count].astype(F32)
        for other in others:
            total += other.astype(F32)
        return total.astype(BF16)

    near = flip_rows(add(heads, heads), 2, row_total)
    far = flip_rows(add(2 * heads, heads), 4, row_total)
    far_two = flip_rows(add(3 * heads, part, near[part:]), 4, row_total)
    near_two = flip_rows(add(3 * heads + part, part, far[part:]), 2, row_total)
    own = add(0, heads, jnp.concatenate([near[:part], far[:part]]))
    return own, far_two, near_two


def add_last(own, far_two, near_two):
    heads, groups, half, lanes = own.shape
    return pl.pallas_call(
        add_last_kernel,
        in_specs=[vmem()] * 3,
        out_specs=[vmem()] * groups,
        out_shape=[jax.ShapeDtypeStruct((heads, half, lanes), BF16)] * groups,
        compiler_params=params(),
    )(own, far_two, near_two)


def sum_cores(mine, row_total):
    return (mine.astype(F32) + flip_rows(mine, 1, row_total).astype(F32)).astype(BF16)


def sum_chips(both, row_total):
    near, far, last = (flip_rows(both, bits, row_total).astype(F32) for bits in (2, 4, 6))
    return (both.astype(F32) + near) + (far + last)


def split_heads(
    single,
    pair,
    chains,
    noised,
    w_gamma,
    w_beta,
    w_outgate,
    w_query,
    w_key,
    w_value,
    w_out,
    w_pair,
    chain_gain,
    cotangent,
    *,
    groups,
    row_total,
):
    cols, _ = single.shape
    tokens = chains.shape[0]
    width = noised.shape[2]
    head_size = width // w_pair.shape[1]
    calls = 1
    row_index = lax.axis_index("rows").reshape(1)
    group_index = lax.axis_index("grp").reshape(1)
    bias_send, stats = pair_bias(
        pair, w_pair, chain_gain, chains, group_index, row_index, groups
    )
    bias_got = swap_groups(bias_send)
    noised = noised[0]
    cotangent = cotangent[0]
    *acts_send, cond_gamma, out_gate = pl.pallas_call(
        functools.partial(project_kernel, groups=groups, calls=calls),
        in_specs=[smem()] + [vmem()] * 10,
        out_shape=[
            jax.ShapeDtypeStruct((cols, 4 * width // groups), BF16) for _ in range(groups)
        ]
        + [
            jax.ShapeDtypeStruct((cols, width), F32),
            jax.ShapeDtypeStruct((cols, width), F32),
        ],
        scratch_shapes=[pltpu.VMEM((groups, cols, 4 * width // groups), BF16)],
        compiler_params=params(),
    )(
        group_index,
        single,
        noised,
        cotangent,
        w_gamma,
        w_beta,
        w_outgate,
        w_query,
        w_key,
        w_value,
        w_out,
    )
    bias_got, _ = lax.optimization_barrier((bias_got, acts_send))
    acts = swap_groups(acts_send)
    bias_all, acts = gather_rows(jnp.stack(bias_got), acts, row_total)
    grads_send, keep, give = attention(group_index, row_index, acts, bias_all, head_size)
    grads = swap_groups(grads_send)
    own, far_two, near_two = scatter_rows(keep, give, row_total)
    far_two, near_two, grads = lax.optimization_barrier((far_two, near_two, grads))
    dbias_own, grads = lax.optimization_barrier((add_last(own, far_two, near_two), grads))
    dbias_back = swap_groups(dbias_own)
    updated, d_part = pl.pallas_call(
        functools.partial(finish_kernel, groups=groups, calls=calls),
        in_specs=[smem()] + [vmem()] * (12 + groups * calls),
        out_shape=[
            jax.ShapeDtypeStruct((cols, width), BF16),
            jax.ShapeDtypeStruct(single.shape, BF16),
        ],
        scratch_shapes=[pltpu.VMEM((groups, calls, cols, 4 * width // (groups * calls)), BF16)],
        compiler_params=params(),
    )(
        group_index,
        single,
        noised,
        cotangent,
        cond_gamma,
        out_gate,
        w_gamma,
        w_beta,
        w_outgate,
        w_query,
        w_key,
        w_value,
        w_out,
        *grads,
    )
    d_part, dbias_back = lax.optimization_barrier((d_part, dbias_back))
    d_both = sum_cores(d_part, row_total)
    d_single = sum_chips(d_both, row_total)
    d_pair = pair_back(pair, stats, dbias_back, w_pair, group_index, groups, float(tokens))
    return (updated[None], d_single, d_pair)


def project(acts, weight):
    return jnp.einsum("std,de->ste", acts, weight, preferred_element_type=F32)


def project_back(acts, weight):
    return jnp.einsum("ste,de->std", acts, weight, preferred_element_type=F32)


def split_keys(
    single,
    pair,
    chains,
    noised,
    w_gamma,
    w_beta,
    w_outgate,
    w_query,
    w_key,
    w_value,
    w_out,
    w_pair,
    chain_gain,
    cotangent,
):
    col_count = single.shape[0]
    row_count = pair.shape[0]
    head_count = w_pair.shape[1]
    model_width = w_query.shape[0]
    head_size = model_width // head_count
    sample_count = noised.shape[0]
    token_total = chains.shape[0]
    score_scale = 1.0 / math.sqrt(head_size)
    row_index = lax.axis_index("rows")
    group_index = lax.axis_index("grp")
    chain_rows = lax.dynamic_slice_in_dim(chains, row_index * row_count, row_count)
    chain_cols = lax.dynamic_slice_in_dim(chains, group_index * col_count, col_count)
    pair_norm, pair_inv = norm_rows(pair.astype(jnp.float32))
    projected = jnp.einsum(
        "ijc,ch->hij", pair_norm.astype(jnp.bfloat16), w_pair, preferred_element_type=jnp.float32
    )
    same_chain = (chain_rows[:, None] == chain_cols[None, :]).astype(jnp.float32)
    bias_block = (projected + chain_gain[:, None, None] * same_chain[None]).astype(jnp.bfloat16)
    bias_keys = lax.all_gather(bias_block, "rows", axis=1, tiled=True)
    single_norm, single_inv = norm_rows(single.astype(jnp.float32))
    single_b = single_norm.astype(jnp.bfloat16)
    cond_gamma = jax.nn.sigmoid(jnp.dot(single_b, w_gamma, preferred_element_type=jnp.float32))
    cond_beta = jnp.dot(single_b, w_beta, preferred_element_type=jnp.float32)
    out_gate = jax.nn.sigmoid(jnp.dot(single_b, w_outgate, preferred_element_type=jnp.float32))
    noised_f = noised.astype(jnp.float32)
    noised_norm, noised_inv = norm_rows(noised_f)
    x_b = (noised_norm * cond_gamma[None] + cond_beta[None]).astype(jnp.bfloat16)
    queries = project(x_b, w_query).astype(jnp.bfloat16)
    keys_own = project(x_b, w_key).astype(jnp.bfloat16)
    values_own = project(x_b, w_value).astype(jnp.bfloat16)
    queries_all = lax.all_gather(queries, "grp", axis=1, tiled=True)
    query_heads = queries_all.reshape(sample_count, token_total, head_count, head_size)
    key_heads = keys_own.reshape(sample_count, col_count, head_count, head_size)
    value_heads = values_own.reshape(sample_count, col_count, head_count, head_size)
    scores = (
        jnp.einsum("sihe,sjhe->shij", query_heads, key_heads, preferred_element_type=jnp.float32)
        * score_scale
        + bias_keys.astype(jnp.float32)[None]
    )
    exp_scores = jnp.exp(scores)
    exp_total = lax.psum(jnp.sum(exp_scores, axis=-1).astype(jnp.bfloat16), "grp").astype(
        jnp.float32
    )
    attn_prob = exp_scores / exp_total[..., None]
    prob_b = attn_prob.astype(jnp.bfloat16)
    attended_part = jnp.einsum(
        "shij,sjhe->sihe", prob_b, value_heads, preferred_element_type=jnp.float32
    )
    attended_part = attended_part.reshape(sample_count, token_total, model_width)
    attended = lax.psum_scatter(
        attended_part.astype(jnp.bfloat16), "grp", scatter_dimension=1, tiled=True
    )
    block_update = project(attended, w_out)
    updated = (noised_f + out_gate[None] * block_update).astype(jnp.bfloat16)
    grad_out = cotangent.astype(jnp.float32)
    gate_part = jnp.sum(grad_out * block_update, axis=0)
    grad_update = (grad_out * out_gate[None]).astype(jnp.bfloat16)
    grad_attn = project_back(grad_update, w_out).astype(jnp.bfloat16)
    grads_all = lax.all_gather(grad_attn, "grp", axis=1, tiled=True)
    grad_heads = grads_all.reshape(sample_count, token_total, head_count, head_size)
    grad_prob = jnp.einsum(
        "sihe,sjhe->shij", grad_heads, value_heads, preferred_element_type=jnp.float32
    )
    row_delta = lax.psum(
        jnp.sum(attn_prob * grad_prob, axis=-1).astype(jnp.bfloat16), "grp"
    ).astype(jnp.float32)
    grad_score = attn_prob * (grad_prob - row_delta[..., None])
    score_b = grad_score.astype(jnp.bfloat16)
    query_part = (
        jnp.einsum("shij,sjhe->sihe", score_b, key_heads, preferred_element_type=jnp.float32)
        * score_scale
    )
    query_part = query_part.reshape(sample_count, token_total, model_width)
    grad_query = lax.psum_scatter(
        query_part.astype(jnp.bfloat16), "grp", scatter_dimension=1, tiled=True
    )
    grad_key = (
        jnp.einsum("shij,sihe->sjhe", score_b, query_heads, preferred_element_type=jnp.float32)
        * score_scale
    )
    grad_value = jnp.einsum(
        "shij,sihe->sjhe", prob_b, grad_heads, preferred_element_type=jnp.float32
    )
    grad_key = grad_key.reshape(sample_count, col_count, model_width).astype(jnp.bfloat16)
    grad_value = grad_value.reshape(sample_count, col_count, model_width).astype(jnp.bfloat16)
    grad_input = (
        project_back(grad_query, w_query)
        + project_back(grad_key, w_key)
        + project_back(grad_value, w_value)
    )
    gamma_part = jnp.sum(grad_input * noised_norm, axis=0)
    beta_part = jnp.sum(grad_input, axis=0)
    gamma_sum, beta_sum, gate_sum = lax.psum((gamma_part, beta_part, gate_part), "rows")
    pre_gamma = (gamma_sum * cond_gamma * (1.0 - cond_gamma)).astype(jnp.bfloat16)
    pre_gate = (gate_sum * out_gate * (1.0 - out_gate)).astype(jnp.bfloat16)
    grad_snorm = jnp.dot(pre_gamma, w_gamma.T, preferred_element_type=jnp.float32)
    grad_snorm = grad_snorm + jnp.dot(
        beta_sum.astype(jnp.bfloat16), w_beta.T, preferred_element_type=jnp.float32
    )
    grad_snorm = grad_snorm + jnp.dot(pre_gate, w_outgate.T, preferred_element_type=jnp.float32)
    d_single = norm_back(grad_snorm, single_norm, single_inv)
    bias_part = jnp.sum(score_b, axis=0, dtype=jnp.float32)
    bias_own = lax.psum_scatter(bias_part, "rows", scatter_dimension=1, tiled=True)
    bias_grad = (bias_own * token_total).astype(jnp.bfloat16)
    grad_pairn = jnp.einsum("hij,ch->ijc", bias_grad, w_pair, preferred_element_type=jnp.float32)
    d_pair = norm_back(grad_pairn, pair_norm, pair_inv).astype(jnp.bfloat16)
    return (updated, d_single, d_pair)


def solution(mesh):
    in_specs = (
        P("grp", None),
        P("rows", "grp", None),
        P(),
        P("rows", "grp", None),
        P(),
        P(),
        P(),
        P(),
        P(),
        P(),
        P(),
        P(),
        P(),
        P("rows", "grp", None),
    )
    out_specs = (P("rows", "grp", None), P("grp", None), P("rows", "grp", None))
    groups = mesh.shape["grp"]
    row_total = mesh.shape["rows"]

    def on_device(*args):
        pair, noised, w_pair = args[1], args[3], args[11]
        fits = (
            groups in (2, 4)
            and pair.shape[0] % 32 == 0
            and pair.shape[1] % pair.shape[0] == 0
            and row_total == 8
            and noised.shape[0] == 1
            and noised.shape[1] % 64 == 0
            and w_pair.shape[1] % (2 * groups) == 0
        )
        if fits:
            return split_heads(*args, groups=groups, row_total=row_total)
        return split_keys(*args)

    return jax.shard_map(
        on_device, mesh=mesh, in_specs=in_specs, out_specs=out_specs, check_vma=False
    )
```

```python
import functools
import math

import jax
import jax.numpy as jnp
from jax import lax
from jax.experimental import pallas as pl
from jax.experimental.pallas import tpu as pltpu
from jax.sharding import PartitionSpec as P

EPSILON = 1e-05
BF16 = jnp.bfloat16
F32 = jnp.float32
VMEM_LIMIT = 56 * 1024 * 1024


def norm_rows(values):
    center = values - jnp.mean(values, axis=-1, keepdims=True)
    inverse = lax.rsqrt(jnp.mean(center * center, axis=-1, keepdims=True) + EPSILON)
    return (center * inverse, inverse)


def norm_back(grad_in, normed, inverse):
    grad_mean = jnp.mean(grad_in, axis=-1, keepdims=True)
    cross_mean = jnp.mean(grad_in * normed, axis=-1, keepdims=True)
    return inverse * (grad_in - grad_mean - normed * cross_mean)


def mm(left, right):
    return lax.dot_general(left, right, (((1,), (0,)), ((), ())), preferred_element_type=F32)


def mm_nt(left, right):
    return lax.dot_general(left, right, (((1,), (1,)), ((), ())), preferred_element_type=F32)


def mm_tn(left, right):
    return lax.dot_general(left, right, (((0,), (0,)), ((), ())), preferred_element_type=F32)


def sigmoid(values):
    return 1.0 / (1.0 + jnp.exp(-values))


def params():
    return pltpu.CompilerParams(vmem_limit_bytes=VMEM_LIMIT)


def smem():
    return pl.BlockSpec(memory_space=pltpu.SMEM)


def vmem():
    return pl.BlockSpec(memory_space=pltpu.VMEM)


def project_kernel(
    group_ref,
    single_ref,
    noised_ref,
    cot_ref,
    w_gamma_ref,
    w_beta_ref,
    w_outgate_ref,
    w_query_ref,
    w_key_ref,
    w_value_ref,
    w_out_ref,
    *rest,
    groups,
    calls,
):
    send_refs = rest[:groups]
    gamma_ref, gate_ref, stage_ref = rest[groups:]
    width = stage_ref.shape[2]
    part = width // (4 * calls)
    group_own = group_ref[0]
    single_norm, _ = norm_rows(single_ref[...].astype(F32))
    single_b = single_norm.astype(BF16)
    cond_gamma = sigmoid(mm(single_b, w_gamma_ref[...]))
    gamma_ref[...] = cond_gamma
    out_gate = sigmoid(mm(single_b, w_outgate_ref[...]))
    gate_ref[...] = out_gate
    cond_beta = mm(single_b, w_beta_ref[...])
    noised_norm, _ = norm_rows(noised_ref[...].astype(F32))
    x_b = (noised_norm * cond_gamma + cond_beta).astype(BF16)

    def put(kind, values):
        rounded = values.astype(BF16)
        for group in range(groups):
            slot = group_own ^ group
            for call in range(calls):
                feature = (group * calls + call) * part
                lane = (call * 4 + kind) * part
                stage_ref[slot, :, lane : lane + part] = rounded[:, feature : feature + part]

    put(0, mm(x_b, w_query_ref[...]))
    put(1, mm(x_b, w_key_ref[...]))
    put(2, mm(x_b, w_value_ref[...]))
    grad_update = (cot_ref[...].astype(F32) * out_gate).astype(BF16)
    put(3, mm_nt(grad_update, w_out_ref[...]))
    for slot in range(groups):
        send_refs[slot][...] = stage_ref[slot]


def lane_tiles(cols):
    return [(tile, tile * 128, min(cols, tile * 128 + 128)) for tile in range(-(-cols // 128))]


def mean_matrix(channels):
    first = lax.broadcasted_iota(jnp.int32, (2 * channels, 2 * channels), 0) >= channels
    second = lax.broadcasted_iota(jnp.int32, (2 * channels, 2 * channels), 1) >= channels
    return jnp.where(first == second, 1.0 / channels, 0.0).astype(BF16)


def center_rows(pair_ref, first, batch, means):
    _, _, cols, channels = pair_ref.shape
    both = jnp.concatenate(
        [pair_ref[side, first : first + batch].reshape(batch * cols, channels) for side in range(2)],
        axis=1,
    )
    return both.astype(F32) - mm(both, means)


def lane_pad(block, before, total):
    rows, width = block.shape
    pieces = [block]
    if before:
        pieces = [jnp.zeros((rows, before), block.dtype)] + pieces
    if total > before + width:
        pieces = pieces + [jnp.zeros((rows, total - before - width), block.dtype)]
    return jnp.concatenate(pieces, axis=1)


def bias_kernel(
    group_ref,
    rows_ref,
    chains_ref,
    gain_ref,
    pair_ref,
    w_pair_ref,
    cols_ref,
    *rest,
    groups,
    batch,
):
    send_refs = rest[:groups]
    stats_ref, flat_ref, gains_ref, stage_ref = rest[groups:]
    _, step, cols, channels = pair_ref.shape
    heads = gain_ref.shape[0]
    per_group = heads // groups
    half = step * pl.num_programs(0)
    group_own = group_ref[0]
    row_base = rows_ref[0] * 2 * half + pl.program_id(0) * step
    means = mean_matrix(channels)
    weight = w_pair_ref[...].astype(F32).T.astype(BF16)
    mean_part = jnp.full((channels, heads), 1.0 / channels, BF16)
    mixed = []
    for inner in range(2):
        for part, offset in ((weight, 0), (mean_part, heads)):
            for side in range(2):
                mixed.append(lane_pad(part, 2 * heads * (2 * inner + side) + offset, 8 * heads))
    mixed = jnp.concatenate(mixed, axis=0)
    chain_all = cols_ref[...].reshape(1, groups * cols)
    chain_cols = chain_all[:, :cols]
    for group in range(1, groups):
        here = chain_all[:, group * cols : (group + 1) * cols]
        chain_cols = jnp.where(group_own == group, here, chain_cols)
    for head in range(heads):
        gains_ref[head : head + 1, :] = jnp.full((1, cols), gain_ref[head], F32)

    for first in range(0, step, batch):
        center = center_rows(pair_ref, first, batch, means)
        center_b = center.astype(BF16)
        square = (center * center).astype(BF16)
        for base in range(0, batch, 2):
            one = slice(base * cols, (base + 1) * cols)
            two = slice((base + 1) * cols, (base + 2) * cols)
            left = jnp.concatenate(
                [center_b[one], square[one], center_b[two], square[two]], axis=1
            )
            sums = mm(left, mixed).T
            for inner in range(2):
                row = first + base + inner
                for side in range(2):
                    top = 2 * heads * (2 * inner + side)
                    inverse = lax.rsqrt(sums[top + heads : top + 2 * heads] + EPSILON)
                    projected = sums[top : top + heads] * inverse
                    stats_ref[side, row, :heads, :] = projected
                    stats_ref[side, row, heads:, :] = inverse[:8]
                    chain = chains_ref[row_base + side * half + row]
                    same = (chain_cols == chain).astype(F32)
                    values = projected + gains_ref[...] * same
                    for tile, start, end in lane_tiles(cols):
                        piece = lane_pad(values[:, start:end], 0, 128)
                        flat_ref[side, tile, pl.ds(row, heads, stride=step), :] = piece
    for head in range(heads):
        slot = group_own ^ (head // per_group)
        values = jnp.concatenate(
            [
                flat_ref[side, tile, head * step : (head + 1) * step, : end - start]
                for side in range(2)
                for tile, start, end in lane_tiles(cols)
            ],
            axis=1,
        )
        stage_ref[slot, head % per_group] = values.astype(BF16)
    for slot in range(groups):
        send_refs[slot][...] = stage_ref[slot]


def pair_bias(pair, w_pair, chain_gain, chains, group_index, row_index, groups):
    rows, cols, channels = pair.shape
    heads = w_pair.shape[1]
    per_group = heads // groups
    half = rows // 2
    step = 16
    tiles = -(-cols // 128)
    *sends, stats = pl.pallas_call(
        functools.partial(bias_kernel, groups=groups, batch=4),
        grid=(half // step,),
        in_specs=[
            smem(),
            smem(),
            smem(),
            smem(),
            pl.BlockSpec((2, step, cols, channels), lambda t: (0, t, 0, 0)),
            pl.BlockSpec((heads, channels), lambda t: (0, 0)),
            pl.BlockSpec((groups * cols,), lambda t: (0,)),
        ],
        out_specs=[
            pl.BlockSpec((per_group, step, 2 * cols), lambda t: (0, t, 0)) for _ in range(groups)
        ]
        + [pl.BlockSpec((2, step, heads + 8, cols), lambda t: (0, t, 0, 0))],
        out_shape=[
            jax.ShapeDtypeStruct((per_group, half, 2 * cols), BF16) for _ in range(groups)
        ]
        + [jax.ShapeDtypeStruct((2, half, heads + 8, cols), F32)],
        scratch_shapes=[
            pltpu.VMEM((2, tiles, heads * step, 128), F32),
            pltpu.VMEM((heads, cols), F32),
            pltpu.VMEM((groups, per_group, step, 2 * cols), BF16),
        ],
        compiler_params=params(),
    )(
        group_index,
        row_index,
        chains,
        chain_gain,
        pair.reshape(2, half, cols, channels),
        w_pair.T,
        chains,
    )
    return sends, stats


def pair_back_kernel(
    group_ref, pair_ref, stats_ref, w_pair_ref, *rest, groups, calls, factor, batch
):
    grad_refs = rest[: groups * calls]
    out_ref, flat_ref = rest[groups * calls :]
    _, step, cols, channels = pair_ref.shape
    per_call = grad_refs[0].shape[0]
    heads = groups * calls * per_call
    group_own = group_ref[0]
    means = mean_matrix(channels)
    weight = w_pair_ref[...].astype(F32)
    weight = (weight - jnp.mean(weight, axis=-1, keepdims=True)).astype(BF16)
    spread = lax.broadcasted_iota(jnp.int32, (heads, channels), 0)
    spread = (spread < 2).astype(F32).astype(BF16)
    block = jnp.concatenate(
        [lane_pad(weight, 0, 2 * channels), lane_pad(spread, channels, 2 * channels)], axis=0
    )
    weights = jnp.concatenate(
        [lane_pad(block, 2 * channels * place, 8 * channels) for place in range(4)], axis=0
    )
    blank = jnp.zeros((heads - 2, cols), F32)
    for number in range(groups * calls):
        call, slot = divmod(number, groups)
        source = (group_own ^ slot) * calls + call
        for head in range(per_call):
            values = grad_refs[number][head].astype(F32)
            top = pl.multiple_of((source * per_call + head) * step, step)
            for side in range(2):
                for tile, start, end in lane_tiles(cols):
                    flat_ref[side, tile, pl.ds(top, step), : end - start] = values[
                        :, side * cols + start : side * cols + end
                    ]

    for first in range(0, step, batch):
        center = center_rows(pair_ref, first, batch, means)
        for base in range(0, batch, 2):
            places = [(base + inner, side) for inner in range(2) for side in range(2)]
            left = []
            for inner, side in places:
                grads = jnp.concatenate(
                    [
                        flat_ref[side, tile, pl.ds(first + inner, heads, stride=step), :][
                            :, : end - start
                        ]
                        for tile, start, end in lane_tiles(cols)
                    ],
                    axis=1,
                )
                projected = stats_ref[side, first + inner, :heads, :]
                inverse = stats_ref[side, first + inner, heads : heads + 1, :]
                cross = jnp.sum(grads * projected, axis=0, keepdims=True) * (1.0 / channels)
                scaled = grads * (inverse * factor)
                cross = cross * (inverse * inverse * factor)
                cross_high = cross.astype(BF16).astype(F32)
                left += [scaled, cross_high, cross - cross_high, blank]
            both = mm_tn(jnp.concatenate(left, axis=0).astype(BF16), weights)
            for place, (inner, side) in enumerate(places):
                rows = slice(inner * cols, (inner + 1) * cols)
                lanes = slice(side * channels, (side + 1) * channels)
                start = 2 * channels * place
                middle, end = start + channels, start + 2 * channels
                out_ref[side, first + inner] = (
                    both[:, start:middle] - center[rows, lanes] * both[:, middle:end]
                ).astype(BF16)


def pair_back(pair, stats, grads, w_pair, group_index, groups, factor):
    rows, cols, channels = pair.shape
    per_call = grads[0].shape[0]
    heads = len(grads) * per_call
    half = rows // 2
    step = 16
    tiles = -(-cols // 128)
    out = pl.pallas_call(
        functools.partial(
            pair_back_kernel, groups=groups, calls=len(grads) // groups, factor=factor, batch=4
        ),
        grid=(half // step,),
        in_specs=[
            smem(),
            pl.BlockSpec((2, step, cols, channels), lambda t: (0, t, 0, 0)),
            pl.BlockSpec((2, step, heads + 8, cols), lambda t: (0, t, 0, 0)),
            pl.BlockSpec((heads, channels), lambda t: (0, 0)),
        ]
        + [pl.BlockSpec((per_call, step, 2 * cols), lambda t: (0, t, 0)) for _ in grads],
        out_specs=pl.BlockSpec((2, step, cols, channels), lambda t: (0, t, 0, 0)),
        out_shape=jax.ShapeDtypeStruct((2, half, cols, channels), BF16),
        scratch_shapes=[pltpu.VMEM((2, tiles, heads * step, 128), F32)],
        compiler_params=params(),
    )(group_index, pair.reshape(2, half, cols, channels), stats, w_pair.T, *grads)
    return out.reshape(rows, cols, channels)


def unit_order(heads):
    first, second = range(heads // 2), range(heads // 2, heads)
    order = [(1, head) for head in first] + [(3, head) for head in first]
    order += [(2, head) for head in second] + [(3, head) for head in second]
    order += [(0, head) for head in range(heads)]
    order += [(2, head) for head in first] + [(1, head) for head in second]
    return order


def attention_kernel(group_ref, row_ref, *rest, groups, row_parts, head_size, row_block):
    bias_refs = rest[: row_parts + 2]
    acts_refs = rest[row_parts + 2 : row_parts + 2 + groups]
    rest = rest[row_parts + 2 + groups :]
    out_refs = rest[:groups]
    (
        keep_ref,
        give_ref,
        give_late_ref,
        query_ref,
        keys_ref,
        values_ref,
        grads_ref,
        query_t_ref,
        keys_t_ref,
        values_t_ref,
        grads_t_ref,
        bias_full,
        score_full,
        att_sum,
        gq_sum,
        gk_sum,
        gv_sum,
    ) = rest[groups:]
    head = pl.program_id(0)
    heads = keep_ref.shape[0] * 2 // row_parts
    group_own = group_ref[0]
    cols, width = acts_refs[0].shape
    tokens = groups * cols
    part = width // 4
    half = bias_refs[0].shape[2]
    scale = 1.0 / math.sqrt(head_size)
    extra = att_sum.shape[1] - part
    plain = (query_ref, keys_ref, values_ref, grads_ref)
    turned = (query_t_ref, keys_t_ref, values_t_ref, grads_t_ref)

    @pl.when(head == 0)
    def _():
        for kind in range(4):
            for slot in range(groups):
                plain[kind][slot * cols : (slot + 1) * cols, :] = acts_refs[slot][
                    :, kind * part : (kind + 1) * part
                ]
            turned[kind][...] = plain[kind][...].T
        att_sum[...] = jnp.zeros_like(att_sum)
        gq_sum[...] = jnp.zeros_like(gq_sum)

    def places(row_part):
        first = row_part * (2 * half)
        slot = group_own ^ (first // cols)
        for side in range(2):
            top = slot * cols + lax.rem(first, cols) + side * half
            top = pl.multiple_of(top, 16)
            for column in range(groups):
                yield column, side, pl.ds(top, half)

    for other in range(row_parts):
        for column, side, rows in places(row_ref[0] ^ other):
            block, place = bias_refs[other], column
            if other >= row_parts - 2 and column >= groups // 2:
                block, place = bias_refs[other + 2], column - groups // 2
            bias_full[rows, column * cols : (column + 1) * cols] = block[
                place, 0, :, side * cols : (side + 1) * cols
            ]

    lane = lax.broadcasted_iota(jnp.int32, (1, part), 1)
    mine = (lane >= head * head_size) & (lane < (head + 1) * head_size)
    zero = jnp.zeros((), BF16)
    keys_m = jnp.where(mine, keys_ref[...], zero)
    values_m = jnp.concatenate(
        [jnp.where(mine, values_ref[...], zero), jnp.ones((tokens, extra), BF16)], axis=1
    )
    feature = pl.multiple_of(head * head_size, head_size)
    query_t = query_t_ref[pl.ds(feature, head_size), :]
    grads_t = grads_t_ref[pl.ds(feature, head_size), :]
    gk_t = jnp.zeros((head_size, tokens), F32)
    gv_t = jnp.zeros((head_size, tokens), F32)
    for top in range(0, tokens, row_block):
        rows = slice(top, top + row_block)
        query = jnp.where(mine, query_ref[rows, :], zero)
        grads = jnp.where(mine, grads_ref[rows, :], zero)
        scores = mm(query, keys_t_ref[...]) * scale + bias_full[rows, :].astype(F32)
        weights = jnp.exp(scores)
        attended = mm(weights.astype(BF16), values_m)
        inverse = 1.0 / attended[:, part : part + 1]
        attended = attended[:, :part] * inverse
        att_sum[rows, :part] += attended
        delta = jnp.sum(attended * grads.astype(F32), axis=-1, keepdims=True)
        prob = weights * inverse
        grad_prob = mm(grads, values_t_ref[...])
        score = (prob * (grad_prob - delta)).astype(BF16)
        score_full[rows, :] = score
        gq_sum[rows, :] += mm(score, keys_m)
        gk_t = gk_t + mm(query_t[:, rows], score)
        gv_t = gv_t + mm(grads_t[:, rows], prob.astype(BF16))
    gk_sum[pl.ds(feature, head_size), :] = gk_t
    gv_sum[pl.ds(feature, head_size), :] = gv_t

    order = unit_order(heads)
    early = len(order) // 2

    def give_back(some_heads):
        for other in range(row_parts):
            unit = order.index((other // 2, some_heads[0]))
            dbias_ref = keep_ref
            if other % 2:
                dbias_ref = give_ref if unit < early else give_late_ref
                unit = unit % early
            unit = unit + head - some_heads[0]
            for column, side, rows in places(row_ref[0] ^ other):
                dbias_ref[unit, column, :, side * cols : (side + 1) * cols] = score_full[
                    rows, column * cols : (column + 1) * cols
                ]

    @pl.when(head < heads // 2)
    def _():
        give_back(range(heads // 2))

    @pl.when(head >= heads // 2)
    def _():
        give_back(range(heads // 2, heads))

    @pl.when(head == heads - 1)
    def _():
        results = (
            gq_sum[...] * scale,
            (gk_sum[...] * scale).T,
            gv_sum[...].T,
            att_sum[:, :part],
        )
        for kind, values in enumerate(results):
            rounded = values.astype(BF16)
            for slot in range(groups):
                out_refs[slot][:, kind * part : (kind + 1) * part] = rounded[
                    slot * cols : (slot + 1) * cols
                ]


def attention(group_index, row_index, acts, bias, head_size):
    groups = len(acts)
    row_parts = len(bias) - 2
    cols, width = acts[0].shape
    tokens = groups * cols
    part = width // 4
    _, heads, half, lanes = bias[0].shape
    row_block = 256 if tokens % 256 == 0 else cols
    padded = (part // 128 + 1) * 128
    units = (row_parts // 2 * heads, groups, half, lanes)
    some = (row_parts // 4 * heads, groups, half, lanes)
    *grads, keep, give, give_late = pl.pallas_call(
        functools.partial(
            attention_kernel,
            groups=groups,
            row_parts=row_parts,
            head_size=head_size,
            row_block=row_block,
        ),
        grid=(heads,),
        in_specs=[smem(), smem()]
        + [
            pl.BlockSpec((block.shape[0], 1, half, lanes), lambda h: (0, h, 0, 0))
            for block in bias
        ]
        + [pl.BlockSpec((cols, width), lambda h: (0, 0))] * groups,
        out_specs=[pl.BlockSpec((cols, width), lambda h: (0, 0))] * groups
        + [pl.BlockSpec(shape, lambda h: (0, 0, 0, 0)) for shape in (units, some, some)],
        out_shape=[jax.ShapeDtypeStruct((cols, width), BF16)] * groups
        + [jax.ShapeDtypeStruct(shape, BF16) for shape in (units, some, some)],
        scratch_shapes=[pltpu.VMEM((tokens, part), BF16) for _ in range(4)]
        + [pltpu.VMEM((part, tokens), BF16) for _ in range(4)]
        + [
            pltpu.VMEM((tokens, tokens), BF16),
            pltpu.VMEM((tokens, tokens), BF16),
            pltpu.VMEM((tokens, padded), F32),
            pltpu.VMEM((tokens, part), F32),
            pltpu.VMEM((part, tokens), F32),
            pltpu.VMEM((part, tokens), F32),
        ],
        compiler_params=params(),
    )(group_index, row_index, *bias, *acts)
    return grads, keep, give, give_late


def finish_kernel(
    group_ref,
    single_ref,
    noised_ref,
    cot_ref,
    gamma_ref,
    gate_ref,
    w_gamma_ref,
    w_beta_ref,
    w_outgate_ref,
    w_query_ref,
    w_key_ref,
    w_value_ref,
    w_out_ref,
    *rest,
    groups,
    calls,
):
    got_refs = rest[: groups * calls]
    updated_ref, d_single_ref, stage_ref = rest[groups * calls :]
    width = stage_ref.shape[3]
    part = width // 4
    for slot in range(groups):
        for call in range(calls):
            stage_ref[group_ref[0] ^ slot, call] = got_refs[
                call * groups + slot
            ][...]

    def take(kind):
        return jnp.concatenate(
            [
                stage_ref[group, call, :, kind * part : (kind + 1) * part]
                for group in range(groups)
                for call in range(calls)
            ],
            axis=1,
        )

    out_gate = gate_ref[...]
    cond_gamma = gamma_ref[...]
    block_update = mm(take(3), w_out_ref[...])
    noised = noised_ref[...].astype(F32)
    updated_ref[...] = (noised + out_gate * block_update).astype(BF16)
    gate_part = cot_ref[...].astype(F32) * block_update
    pre_gate = (gate_part * out_gate * (1.0 - out_gate)).astype(BF16)
    grad_input = mm_nt(take(0), w_query_ref[...])
    grad_input += mm_nt(take(1), w_key_ref[...])
    grad_input += mm_nt(take(2), w_value_ref[...])
    noised_norm, _ = norm_rows(noised)
    pre_gamma = (grad_input * noised_norm * cond_gamma * (1.0 - cond_gamma)).astype(BF16)
    grad_snorm = mm_nt(pre_gamma, w_gamma_ref[...])
    grad_snorm += mm_nt(grad_input.astype(BF16), w_beta_ref[...])
    grad_snorm += mm_nt(pre_gate, w_outgate_ref[...])
    single_norm, single_inv = norm_rows(single_ref[...].astype(F32))
    d_single_ref[...] = norm_back(grad_snorm, single_norm, single_inv).astype(BF16)


def swap_groups(sends):
    groups = len(sends)
    got = list(sends)
    for bits in (*range(2, groups), 1):
        perm = [(index, index ^ bits) for index in range(groups)]
        got[bits] = lax.ppermute(sends[bits], "grp", perm)
    return got


def flip_rows(values, bits, row_total):
    return lax.ppermute(values, "rows", [(index, index ^ bits) for index in range(row_total)])


def gather_rows(own, acts, row_total):
    half = own.shape[0] // 2
    near = flip_rows(own, 2, row_total)
    far = flip_rows(own, 4, row_total)
    first = flip_rows(near[:half], 4, row_total)
    second = flip_rows(far[half:], 2, row_total)
    own, acts[2] = lax.optimization_barrier((own, acts[2]))
    own_other = flip_rows(own, 1, row_total)
    first, second, own_other, acts[1], acts[3] = lax.optimization_barrier(
        (first, second, own_other, acts[1], acts[3])
    )
    blocks = [own, own_other]
    for block in (near, far, first, second):
        blocks += [block, flip_rows(block, 1, row_total)]
    return blocks, acts


def add_last_kernel(own_ref, far_ref, near_ref, *out_refs):
    heads = own_ref.shape[0]
    half = heads // 2
    for head in range(heads):
        other = far_ref[head] if head < half else near_ref[head - half]
        total = (own_ref[head].astype(F32) + other.astype(F32)).astype(BF16)
        for slot, out_ref in enumerate(out_refs):
            out_ref[head] = total[slot]


def scatter_rows(keep, give, give_late, row_total):
    got = flip_rows(give, 1, row_total)
    got, give_late = lax.optimization_barrier((got, give_late))
    got_late = flip_rows(give_late, 1, row_total)
    early = got.shape[0]
    heads = early // 2
    part = heads // 2

    def add(first, count, *others):
        source, place = (got, first) if first < early else (got_late, first - early)
        total = keep[first : first + count].astype(F32)
        total += source[place : place + count].astype(F32)
        for other in others:
            total += other.astype(F32)
        return total.astype(BF16)

    near = flip_rows(add(0, heads), 2, row_total)
    far = flip_rows(add(heads, heads), 4, row_total)
    far_two = flip_rows(add(early + heads, part, near[part:]), 4, row_total)
    near_two = flip_rows(add(early + heads + part, part, far[part:]), 2, row_total)
    own = add(early, heads, jnp.concatenate([near[:part], far[:part]]))
    return own, far_two, near_two


def add_last(own, far_two, near_two):
    heads, groups, half, lanes = own.shape
    return pl.pallas_call(
        add_last_kernel,
        in_specs=[vmem()] * 3,
        out_specs=[vmem()] * groups,
        out_shape=[jax.ShapeDtypeStruct((heads, half, lanes), BF16)] * groups,
        compiler_params=params(),
    )(own, far_two, near_two)


def sum_cores(mine, row_total):
    return (mine.astype(F32) + flip_rows(mine, 1, row_total).astype(F32)).astype(BF16)


def sum_chips(both, row_total):
    near, far, last = (flip_rows(both, bits, row_total).astype(F32) for bits in (2, 4, 6))
    return (both.astype(F32) + near) + (far + last)


def split_heads(
    single,
    pair,
    chains,
    noised,
    w_gamma,
    w_beta,
    w_outgate,
    w_query,
    w_key,
    w_value,
    w_out,
    w_pair,
    chain_gain,
    cotangent,
    *,
    groups,
    row_total,
):
    cols, _ = single.shape
    tokens = chains.shape[0]
    width = noised.shape[2]
    head_size = width // w_pair.shape[1]
    calls = 1
    row_index = lax.axis_index("rows").reshape(1)
    group_index = lax.axis_index("grp").reshape(1)
    bias_send, stats = pair_bias(
        pair, w_pair, chain_gain, chains, group_index, row_index, groups
    )
    bias_got = swap_groups(bias_send)
    noised = noised[0]
    cotangent = cotangent[0]
    *acts_send, cond_gamma, out_gate = pl.pallas_call(
        functools.partial(project_kernel, groups=groups, calls=calls),
        in_specs=[smem()] + [vmem()] * 10,
        out_shape=[
            jax.ShapeDtypeStruct((cols, 4 * width // groups), BF16) for _ in range(groups)
        ]
        + [
            jax.ShapeDtypeStruct((cols, width), F32),
            jax.ShapeDtypeStruct((cols, width), F32),
        ],
        scratch_shapes=[pltpu.VMEM((groups, cols, 4 * width // groups), BF16)],
        compiler_params=params(),
    )(
        group_index,
        single,
        noised,
        cotangent,
        w_gamma,
        w_beta,
        w_outgate,
        w_query,
        w_key,
        w_value,
        w_out,
    )
    bias_got, _ = lax.optimization_barrier((bias_got, acts_send))
    acts = swap_groups(acts_send)
    bias_all, acts = gather_rows(jnp.stack(bias_got), acts, row_total)
    grads_send, keep, give, give_late = attention(group_index, row_index, acts, bias_all, head_size)
    grads = swap_groups(grads_send)
    own, far_two, near_two = scatter_rows(keep, give, give_late, row_total)
    far_two, near_two, grads = lax.optimization_barrier((far_two, near_two, grads))
    dbias_own, grads = lax.optimization_barrier((add_last(own, far_two, near_two), grads))
    dbias_back = swap_groups(dbias_own)
    updated, d_part = pl.pallas_call(
        functools.partial(finish_kernel, groups=groups, calls=calls),
        in_specs=[smem()] + [vmem()] * (12 + groups * calls),
        out_shape=[
            jax.ShapeDtypeStruct((cols, width), BF16),
            jax.ShapeDtypeStruct(single.shape, BF16),
        ],
        scratch_shapes=[pltpu.VMEM((groups, calls, cols, 4 * width // (groups * calls)), BF16)],
        compiler_params=params(),
    )(
        group_index,
        single,
        noised,
        cotangent,
        cond_gamma,
        out_gate,
        w_gamma,
        w_beta,
        w_outgate,
        w_query,
        w_key,
        w_value,
        w_out,
        *grads,
    )
    d_part, dbias_back = lax.optimization_barrier((d_part, dbias_back))
    d_both = sum_cores(d_part, row_total)
    d_single = sum_chips(d_both, row_total)
    d_pair = pair_back(pair, stats, dbias_back, w_pair, group_index, groups, float(tokens))
    return (updated[None], d_single, d_pair)


def project(acts, weight):
    return jnp.einsum("std,de->ste", acts, weight, preferred_element_type=F32)


def project_back(acts, weight):
    return jnp.einsum("ste,de->std", acts, weight, preferred_element_type=F32)


def split_keys(
    single,
    pair,
    chains,
    noised,
    w_gamma,
    w_beta,
    w_outgate,
    w_query,
    w_key,
    w_value,
    w_out,
    w_pair,
    chain_gain,
    cotangent,
):
    col_count = single.shape[0]
    row_count = pair.shape[0]
    head_count = w_pair.shape[1]
    model_width = w_query.shape[0]
    head_size = model_width // head_count
    sample_count = noised.shape[0]
    token_total = chains.shape[0]
    score_scale = 1.0 / math.sqrt(head_size)
    row_index = lax.axis_index("rows")
    group_index = lax.axis_index("grp")
    chain_rows = lax.dynamic_slice_in_dim(chains, row_index * row_count, row_count)
    chain_cols = lax.dynamic_slice_in_dim(chains, group_index * col_count, col_count)
    pair_norm, pair_inv = norm_rows(pair.astype(jnp.float32))
    projected = jnp.einsum(
        "ijc,ch->hij", pair_norm.astype(jnp.bfloat16), w_pair, preferred_element_type=jnp.float32
    )
    same_chain = (chain_rows[:, None] == chain_cols[None, :]).astype(jnp.float32)
    bias_block = (projected + chain_gain[:, None, None] * same_chain[None]).astype(jnp.bfloat16)
    bias_keys = lax.all_gather(bias_block, "rows", axis=1, tiled=True)
    single_norm, single_inv = norm_rows(single.astype(jnp.float32))
    single_b = single_norm.astype(jnp.bfloat16)
    cond_gamma = jax.nn.sigmoid(jnp.dot(single_b, w_gamma, preferred_element_type=jnp.float32))
    cond_beta = jnp.dot(single_b, w_beta, preferred_element_type=jnp.float32)
    out_gate = jax.nn.sigmoid(jnp.dot(single_b, w_outgate, preferred_element_type=jnp.float32))
    noised_f = noised.astype(jnp.float32)
    noised_norm, noised_inv = norm_rows(noised_f)
    x_b = (noised_norm * cond_gamma[None] + cond_beta[None]).astype(jnp.bfloat16)
    queries = project(x_b, w_query).astype(jnp.bfloat16)
    keys_own = project(x_b, w_key).astype(jnp.bfloat16)
    values_own = project(x_b, w_value).astype(jnp.bfloat16)
    queries_all = lax.all_gather(queries, "grp", axis=1, tiled=True)
    query_heads = queries_all.reshape(sample_count, token_total, head_count, head_size)
    key_heads = keys_own.reshape(sample_count, col_count, head_count, head_size)
    value_heads = values_own.reshape(sample_count, col_count, head_count, head_size)
    scores = (
        jnp.einsum("sihe,sjhe->shij", query_heads, key_heads, preferred_element_type=jnp.float32)
        * score_scale
        + bias_keys.astype(jnp.float32)[None]
    )
    exp_scores = jnp.exp(scores)
    exp_total = lax.psum(jnp.sum(exp_scores, axis=-1).astype(jnp.bfloat16), "grp").astype(
        jnp.float32
    )
    attn_prob = exp_scores / exp_total[..., None]
    prob_b = attn_prob.astype(jnp.bfloat16)
    attended_part = jnp.einsum(
        "shij,sjhe->sihe", prob_b, value_heads, preferred_element_type=jnp.float32
    )
    attended_part = attended_part.reshape(sample_count, token_total, model_width)
    attended = lax.psum_scatter(
        attended_part.astype(jnp.bfloat16), "grp", scatter_dimension=1, tiled=True
    )
    block_update = project(attended, w_out)
    updated = (noised_f + out_gate[None] * block_update).astype(jnp.bfloat16)
    grad_out = cotangent.astype(jnp.float32)
    gate_part = jnp.sum(grad_out * block_update, axis=0)
    grad_update = (grad_out * out_gate[None]).astype(jnp.bfloat16)
    grad_attn = project_back(grad_update, w_out).astype(jnp.bfloat16)
    grads_all = lax.all_gather(grad_attn, "grp", axis=1, tiled=True)
    grad_heads = grads_all.reshape(sample_count, token_total, head_count, head_size)
    grad_prob = jnp.einsum(
        "sihe,sjhe->shij", grad_heads, value_heads, preferred_element_type=jnp.float32
    )
    row_delta = lax.psum(
        jnp.sum(attn_prob * grad_prob, axis=-1).astype(jnp.bfloat16), "grp"
    ).astype(jnp.float32)
    grad_score = attn_prob * (grad_prob - row_delta[..., None])
    score_b = grad_score.astype(jnp.bfloat16)
    query_part = (
        jnp.einsum("shij,sjhe->sihe", score_b, key_heads, preferred_element_type=jnp.float32)
        * score_scale
    )
    query_part = query_part.reshape(sample_count, token_total, model_width)
    grad_query = lax.psum_scatter(
        query_part.astype(jnp.bfloat16), "grp", scatter_dimension=1, tiled=True
    )
    grad_key = (
        jnp.einsum("shij,sihe->sjhe", score_b, query_heads, preferred_element_type=jnp.float32)
        * score_scale
    )
    grad_value = jnp.einsum(
        "shij,sihe->sjhe", prob_b, grad_heads, preferred_element_type=jnp.float32
    )
    grad_key = grad_key.reshape(sample_count, col_count, model_width).astype(jnp.bfloat16)
    grad_value = grad_value.reshape(sample_count, col_count, model_width).astype(jnp.bfloat16)
    grad_input = (
        project_back(grad_query, w_query)
        + project_back(grad_key, w_key)
        + project_back(grad_value, w_value)
    )
    gamma_part = jnp.sum(grad_input * noised_norm, axis=0)
    beta_part = jnp.sum(grad_input, axis=0)
    gamma_sum, beta_sum, gate_sum = lax.psum((gamma_part, beta_part, gate_part), "rows")
    pre_gamma = (gamma_sum * cond_gamma * (1.0 - cond_gamma)).astype(jnp.bfloat16)
    pre_gate = (gate_sum * out_gate * (1.0 - out_gate)).astype(jnp.bfloat16)
    grad_snorm = jnp.dot(pre_gamma, w_gamma.T, preferred_element_type=jnp.float32)
    grad_snorm = grad_snorm + jnp.dot(
        beta_sum.astype(jnp.bfloat16), w_beta.T, preferred_element_type=jnp.float32
    )
    grad_snorm = grad_snorm + jnp.dot(pre_gate, w_outgate.T, preferred_element_type=jnp.float32)
    d_single = norm_back(grad_snorm, single_norm, single_inv)
    bias_part = jnp.sum(score_b, axis=0, dtype=jnp.float32)
    bias_own = lax.psum_scatter(bias_part, "rows", scatter_dimension=1, tiled=True)
    bias_grad = (bias_own * token_total).astype(jnp.bfloat16)
    grad_pairn = jnp.einsum("hij,ch->ijc", bias_grad, w_pair, preferred_element_type=jnp.float32)
    d_pair = norm_back(grad_pairn, pair_norm, pair_inv).astype(jnp.bfloat16)
    return (updated, d_single, d_pair)


def solution(mesh):
    in_specs = (
        P("grp", None),
        P("rows", "grp", None),
        P(),
        P("rows", "grp", None),
        P(),
        P(),
        P(),
        P(),
        P(),
        P(),
        P(),
        P(),
        P(),
        P("rows", "grp", None),
    )
    out_specs = (P("rows", "grp", None), P("grp", None), P("rows", "grp", None))
    groups = mesh.shape["grp"]
    row_total = mesh.shape["rows"]

    def on_device(*args):
        pair, noised, w_pair = args[1], args[3], args[11]
        fits = (
            groups in (2, 4)
            and pair.shape[0] % 32 == 0
            and pair.shape[1] % pair.shape[0] == 0
            and row_total == 8
            and noised.shape[0] == 1
            and noised.shape[1] % 64 == 0
            and w_pair.shape[1] % (2 * groups) == 0
        )
        if fits:
            return split_heads(*args, groups=groups, row_total=row_total)
        return split_keys(*args)

    return jax.shard_map(
        on_device, mesh=mesh, in_specs=in_specs, out_specs=out_specs, check_vma=False
    )
```

```python
import functools
import math

import jax
import jax.numpy as jnp
from jax import lax
from jax.experimental import pallas as pl
from jax.experimental.pallas import tpu as pltpu
from jax.sharding import PartitionSpec as P

EPSILON = 1e-05
BF16 = jnp.bfloat16
F32 = jnp.float32
VMEM_LIMIT = 56 * 1024 * 1024


def norm_rows(values):
    center = values - jnp.mean(values, axis=-1, keepdims=True)
    inverse = lax.rsqrt(jnp.mean(center * center, axis=-1, keepdims=True) + EPSILON)
    return (center * inverse, inverse)


def norm_back(grad_in, normed, inverse):
    grad_mean = jnp.mean(grad_in, axis=-1, keepdims=True)
    cross_mean = jnp.mean(grad_in * normed, axis=-1, keepdims=True)
    return inverse * (grad_in - grad_mean - normed * cross_mean)


def mm(left, right):
    return lax.dot_general(left, right, (((1,), (0,)), ((), ())), preferred_element_type=F32)


def mm_nt(left, right):
    return lax.dot_general(left, right, (((1,), (1,)), ((), ())), preferred_element_type=F32)


def mm_tn(left, right):
    return lax.dot_general(left, right, (((0,), (0,)), ((), ())), preferred_element_type=F32)


def sigmoid(values):
    return 1.0 / (1.0 + jnp.exp(-values))


def params():
    return pltpu.CompilerParams(vmem_limit_bytes=VMEM_LIMIT)


def smem():
    return pl.BlockSpec(memory_space=pltpu.SMEM)


def vmem():
    return pl.BlockSpec(memory_space=pltpu.VMEM)


def project_kernel(
    group_ref,
    single_ref,
    noised_ref,
    cot_ref,
    w_gamma_ref,
    w_beta_ref,
    w_outgate_ref,
    w_query_ref,
    w_key_ref,
    w_value_ref,
    w_out_ref,
    *rest,
    groups,
    calls,
):
    send_refs = rest[:groups]
    gamma_ref, gate_ref, stage_ref = rest[groups:]
    width = stage_ref.shape[2]
    part = width // (4 * calls)
    group_own = group_ref[0]
    single_norm, _ = norm_rows(single_ref[...].astype(F32))
    single_b = single_norm.astype(BF16)
    cond_gamma = sigmoid(mm(single_b, w_gamma_ref[...]))
    gamma_ref[...] = cond_gamma
    out_gate = sigmoid(mm(single_b, w_outgate_ref[...]))
    gate_ref[...] = out_gate
    cond_beta = mm(single_b, w_beta_ref[...])
    noised_norm, _ = norm_rows(noised_ref[...].astype(F32))
    x_b = (noised_norm * cond_gamma + cond_beta).astype(BF16)

    def put(kind, values):
        rounded = values.astype(BF16)
        for group in range(groups):
            slot = group_own ^ group
            for call in range(calls):
                feature = (group * calls + call) * part
                lane = (call * 4 + kind) * part
                stage_ref[slot, :, lane : lane + part] = rounded[:, feature : feature + part]

    put(0, mm(x_b, w_query_ref[...]))
    put(1, mm(x_b, w_key_ref[...]))
    put(2, mm(x_b, w_value_ref[...]))
    grad_update = (cot_ref[...].astype(F32) * out_gate).astype(BF16)
    put(3, mm_nt(grad_update, w_out_ref[...]))
    for slot in range(groups):
        send_refs[slot][...] = stage_ref[slot]


def lane_tiles(cols):
    return [(tile, tile * 128, min(cols, tile * 128 + 128)) for tile in range(-(-cols // 128))]


def mean_matrix(channels):
    first = lax.broadcasted_iota(jnp.int32, (2 * channels, 2 * channels), 0) >= channels
    second = lax.broadcasted_iota(jnp.int32, (2 * channels, 2 * channels), 1) >= channels
    return jnp.where(first == second, 1.0 / channels, 0.0).astype(BF16)


def center_rows(pair_ref, first, batch, means):
    _, _, cols, channels = pair_ref.shape
    both = jnp.concatenate(
        [pair_ref[side, first : first + batch].reshape(batch * cols, channels) for side in range(2)],
        axis=1,
    )
    return both.astype(F32) - mm(both, means)


def lane_pad(block, before, total):
    rows, width = block.shape
    pieces = [block]
    if before:
        pieces = [jnp.zeros((rows, before), block.dtype)] + pieces
    if total > before + width:
        pieces = pieces + [jnp.zeros((rows, total - before - width), block.dtype)]
    return jnp.concatenate(pieces, axis=1)


def bias_kernel(
    group_ref,
    rows_ref,
    chains_ref,
    gain_ref,
    pair_ref,
    w_pair_ref,
    cols_ref,
    *rest,
    groups,
    batch,
):
    send_refs = rest[:groups]
    stats_ref, flat_ref, gains_ref, stage_ref = rest[groups:]
    _, step, cols, channels = pair_ref.shape
    heads = gain_ref.shape[0]
    per_group = heads // groups
    half = step * pl.num_programs(0)
    group_own = group_ref[0]
    row_base = rows_ref[0] * 2 * half + pl.program_id(0) * step
    means = mean_matrix(channels)
    weight = w_pair_ref[...].astype(F32).T.astype(BF16)
    mean_part = jnp.full((channels, heads), 1.0 / channels, BF16)
    mixed = []
    for inner in range(2):
        for part, offset in ((weight, 0), (mean_part, heads)):
            for side in range(2):
                mixed.append(lane_pad(part, 2 * heads * (2 * inner + side) + offset, 8 * heads))
    mixed = jnp.concatenate(mixed, axis=0)
    chain_all = cols_ref[...].reshape(1, groups * cols)
    chain_cols = chain_all[:, :cols]
    for group in range(1, groups):
        here = chain_all[:, group * cols : (group + 1) * cols]
        chain_cols = jnp.where(group_own == group, here, chain_cols)
    for head in range(heads):
        gains_ref[head : head + 1, :] = jnp.full((1, cols), gain_ref[head], F32)

    for first in range(0, step, batch):
        center = center_rows(pair_ref, first, batch, means)
        center_b = center.astype(BF16)
        square = (center * center).astype(BF16)
        for base in range(0, batch, 2):
            one = slice(base * cols, (base + 1) * cols)
            two = slice((base + 1) * cols, (base + 2) * cols)
            left = jnp.concatenate(
                [center_b[one], square[one], center_b[two], square[two]], axis=1
            )
            sums = mm(left, mixed).T
            for inner in range(2):
                row = first + base + inner
                for side in range(2):
                    top = 2 * heads * (2 * inner + side)
                    inverse = lax.rsqrt(sums[top + heads : top + 2 * heads] + EPSILON)
                    projected = sums[top : top + heads] * inverse
                    stats_ref[side, row, :heads, :] = projected
                    stats_ref[side, row, heads:, :] = inverse[:8]
                    chain = chains_ref[row_base + side * half + row]
                    same = (chain_cols == chain).astype(F32)
                    values = projected + gains_ref[...] * same
                    for tile, start, end in lane_tiles(cols):
                        piece = lane_pad(values[:, start:end], 0, 128)
                        flat_ref[side, tile, pl.ds(row, heads, stride=step), :] = piece
    for head in range(heads):
        slot = group_own ^ (head // per_group)
        tops = slice(head * step, (head + 1) * step)
        rest_lanes = [flat_ref[side, 1, tops, : cols - 128] for side in range(2)]
        stage_ref[slot, head % per_group, 0] = flat_ref[0, 0, tops, :].astype(BF16)
        stage_ref[slot, head % per_group, 1] = flat_ref[1, 0, tops, :].astype(BF16)
        stage_ref[slot, head % per_group, 2] = jnp.concatenate(rest_lanes, axis=1).astype(BF16)
    for slot in range(groups):
        send_refs[slot][...] = stage_ref[slot]


def pair_bias(pair, w_pair, chain_gain, chains, group_index, row_index, groups):
    rows, cols, channels = pair.shape
    heads = w_pair.shape[1]
    per_group = heads // groups
    half = rows // 2
    step = 16
    tiles = -(-cols // 128)
    *sends, stats = pl.pallas_call(
        functools.partial(bias_kernel, groups=groups, batch=4),
        grid=(half // step,),
        in_specs=[
            smem(),
            smem(),
            smem(),
            smem(),
            pl.BlockSpec((2, step, cols, channels), lambda t: (0, t, 0, 0)),
            pl.BlockSpec((heads, channels), lambda t: (0, 0)),
            pl.BlockSpec((groups * cols,), lambda t: (0,)),
        ],
        out_specs=[
            pl.BlockSpec((per_group, 3, step, 128), lambda t: (0, 0, t, 0)) for _ in range(groups)
        ]
        + [pl.BlockSpec((2, step, heads + 8, cols), lambda t: (0, t, 0, 0))],
        out_shape=[
            jax.ShapeDtypeStruct((per_group, 3, half, 128), BF16) for _ in range(groups)
        ]
        + [jax.ShapeDtypeStruct((2, half, heads + 8, cols), F32)],
        scratch_shapes=[
            pltpu.VMEM((2, tiles, heads * step, 128), F32),
            pltpu.VMEM((heads, cols), F32),
            pltpu.VMEM((groups, per_group, 3, step, 128), BF16),
        ],
        compiler_params=params(),
    )(
        group_index,
        row_index,
        chains,
        chain_gain,
        pair.reshape(2, half, cols, channels),
        w_pair.T,
        chains,
    )
    return sends, stats


def pair_back_kernel(
    group_ref, pair_ref, stats_ref, w_pair_ref, *rest, groups, calls, factor, batch
):
    grad_refs = rest[: groups * calls]
    out_ref, flat_ref = rest[groups * calls :]
    _, step, cols, channels = pair_ref.shape
    per_call = grad_refs[0].shape[0]
    heads = groups * calls * per_call
    group_own = group_ref[0]
    means = mean_matrix(channels)
    weight = w_pair_ref[...].astype(F32)
    weight = (weight - jnp.mean(weight, axis=-1, keepdims=True)).astype(BF16)
    spread = lax.broadcasted_iota(jnp.int32, (heads, channels), 0)
    spread = (spread < 2).astype(F32).astype(BF16)
    block = jnp.concatenate(
        [lane_pad(weight, 0, 2 * channels), lane_pad(spread, channels, 2 * channels)], axis=0
    )
    weights = jnp.concatenate(
        [lane_pad(block, 2 * channels * place, 8 * channels) for place in range(4)], axis=0
    )
    blank = jnp.zeros((heads - 2, cols), F32)
    for number in range(groups * calls):
        call, slot = divmod(number, groups)
        source = (group_own ^ slot) * calls + call
        for head in range(per_call):
            values = grad_refs[number][head].astype(F32)
            top = pl.multiple_of((source * per_call + head) * step, step)
            for side in range(2):
                flat_ref[side, 0, pl.ds(top, step), :] = values[side]
                flat_ref[side, 1, pl.ds(top, step), : cols - 128] = values[2][
                    :, side * (cols - 128) : (side + 1) * (cols - 128)
                ]

    for first in range(0, step, batch):
        center = center_rows(pair_ref, first, batch, means)
        for base in range(0, batch, 2):
            places = [(base + inner, side) for inner in range(2) for side in range(2)]
            left = []
            for inner, side in places:
                grads = jnp.concatenate(
                    [
                        flat_ref[side, tile, pl.ds(first + inner, heads, stride=step), :][
                            :, : end - start
                        ]
                        for tile, start, end in lane_tiles(cols)
                    ],
                    axis=1,
                )
                projected = stats_ref[side, first + inner, :heads, :]
                inverse = stats_ref[side, first + inner, heads : heads + 1, :]
                cross = jnp.sum(grads * projected, axis=0, keepdims=True) * (1.0 / channels)
                scaled = grads * (inverse * factor)
                cross = cross * (inverse * inverse * factor)
                cross_high = cross.astype(BF16).astype(F32)
                left += [scaled, cross_high, cross - cross_high, blank]
            both = mm_tn(jnp.concatenate(left, axis=0).astype(BF16), weights)
            for place, (inner, side) in enumerate(places):
                rows = slice(inner * cols, (inner + 1) * cols)
                lanes = slice(side * channels, (side + 1) * channels)
                start = 2 * channels * place
                middle, end = start + channels, start + 2 * channels
                out_ref[side, first + inner] = (
                    both[:, start:middle] - center[rows, lanes] * both[:, middle:end]
                ).astype(BF16)


def pair_back(pair, stats, grads, w_pair, group_index, groups, factor):
    rows, cols, channels = pair.shape
    per_call = grads[0].shape[0]
    heads = len(grads) * per_call
    half = rows // 2
    step = 16
    tiles = -(-cols // 128)
    out = pl.pallas_call(
        functools.partial(
            pair_back_kernel, groups=groups, calls=len(grads) // groups, factor=factor, batch=4
        ),
        grid=(half // step,),
        in_specs=[
            smem(),
            pl.BlockSpec((2, step, cols, channels), lambda t: (0, t, 0, 0)),
            pl.BlockSpec((2, step, heads + 8, cols), lambda t: (0, t, 0, 0)),
            pl.BlockSpec((heads, channels), lambda t: (0, 0)),
        ]
        + [pl.BlockSpec((per_call, 3, step, 128), lambda t: (0, 0, t, 0)) for _ in grads],
        out_specs=pl.BlockSpec((2, step, cols, channels), lambda t: (0, t, 0, 0)),
        out_shape=jax.ShapeDtypeStruct((2, half, cols, channels), BF16),
        scratch_shapes=[pltpu.VMEM((2, tiles, heads * step, 128), F32)],
        compiler_params=params(),
    )(group_index, pair.reshape(2, half, cols, channels), stats, w_pair.T, *grads)
    return out.reshape(rows, cols, channels)


def unit_order(heads):
    first, second = range(heads // 2), range(heads // 2, heads)
    order = [(1, head) for head in first] + [(3, head) for head in first]
    order += [(2, head) for head in second] + [(3, head) for head in second]
    order += [(0, head) for head in range(heads)]
    order += [(2, head) for head in first] + [(1, head) for head in second]
    return order


def attention_kernel(group_ref, row_ref, *rest, groups, row_parts, head_size, row_block):
    bias_refs = rest[: row_parts + 2]
    acts_refs = rest[row_parts + 2 : row_parts + 2 + groups]
    rest = rest[row_parts + 2 + groups :]
    out_refs = rest[:groups]
    (
        keep_ref,
        give_ref,
        give_late_ref,
        query_ref,
        keys_ref,
        values_ref,
        grads_ref,
        query_t_ref,
        keys_t_ref,
        values_t_ref,
        grads_t_ref,
        bias_full,
        score_full,
        att_sum,
        gq_sum,
        gk_sum,
        gv_sum,
    ) = rest[groups:]
    head = pl.program_id(0)
    heads = keep_ref.shape[0] * 2 // row_parts
    group_own = group_ref[0]
    cols, width = acts_refs[0].shape
    tokens = groups * cols
    part = width // 4
    half = bias_refs[0].shape[3]
    rest_lanes = cols - 128
    scale = 1.0 / math.sqrt(head_size)
    extra = att_sum.shape[1] - part
    plain = (query_ref, keys_ref, values_ref, grads_ref)
    turned = (query_t_ref, keys_t_ref, values_t_ref, grads_t_ref)

    turns = [(slot * cols, slot * 128, 128) for slot in range(groups)]
    turns += [
        (slot * cols + 128, groups * 128 + slot * rest_lanes, rest_lanes) for slot in range(groups)
    ]

    @pl.when(head == 0)
    def _():
        for kind in range(4):
            lanes = slice(kind * part, (kind + 1) * part)
            if kind in (0, 3):
                for slot in range(groups):
                    plain[kind][slot * cols : (slot + 1) * cols, :] = acts_refs[slot][:, lanes]
            else:
                for token, place, count in turns:
                    slot, inside = divmod(token, cols)
                    plain[kind][place : place + count, :] = acts_refs[slot][
                        inside : inside + count, lanes
                    ]
            turned[kind][...] = plain[kind][...].T
        att_sum[...] = jnp.zeros_like(att_sum)
        gq_sum[...] = jnp.zeros_like(gq_sum)

    def places(row_part):
        first = row_part * (2 * half)
        slot = group_own ^ (first // cols)
        for side in range(2):
            top = slot * cols + lax.rem(first, cols) + side * half
            yield side, pl.ds(pl.multiple_of(top, 16), half)

    for other in range(row_parts):

        def block(column, which, other=other):
            if other >= row_parts - 2 and column >= groups // 2:
                return bias_refs[other + 2][column - groups // 2, 0, which]
            return bias_refs[other][column, 0, which]

        for side, rows in places(row_ref[0] ^ other):
            lanes = slice(side * rest_lanes, (side + 1) * rest_lanes)
            tiles = [block(column, side) for column in range(groups)]
            tiles += [block(column, 2)[:, lanes] for column in range(groups)]
            bias_full[rows, :] = jnp.concatenate(tiles, axis=1)

    lane = lax.broadcasted_iota(jnp.int32, (1, part), 1)
    mine = (lane >= head * head_size) & (lane < (head + 1) * head_size)
    zero = jnp.zeros((), BF16)
    keys_m = jnp.where(mine, keys_ref[...], zero)
    values_m = jnp.concatenate(
        [jnp.where(mine, values_ref[...], zero), jnp.ones((tokens, extra), BF16)], axis=1
    )
    feature = pl.multiple_of(head * head_size, head_size)
    query_t = query_t_ref[pl.ds(feature, head_size), :]
    grads_t = grads_t_ref[pl.ds(feature, head_size), :]
    gk_t = jnp.zeros((head_size, tokens), F32)
    gv_t = jnp.zeros((head_size, tokens), F32)
    for top in range(0, tokens, row_block):
        rows = slice(top, top + row_block)
        query = jnp.where(mine, query_ref[rows, :], zero)
        grads = jnp.where(mine, grads_ref[rows, :], zero)
        scores = mm(query, keys_t_ref[...]) * scale + bias_full[rows, :].astype(F32)
        weights = jnp.exp(scores)
        attended = mm(weights.astype(BF16), values_m)
        inverse = 1.0 / attended[:, part : part + 1]
        attended = attended[:, :part] * inverse
        att_sum[rows, :part] += attended
        delta = jnp.sum(attended * grads.astype(F32), axis=-1, keepdims=True)
        prob = weights * inverse
        grad_prob = mm(grads, values_t_ref[...])
        score = (prob * (grad_prob - delta)).astype(BF16)
        score_full[rows, :] = score
        gq_sum[rows, :] += mm(score, keys_m)
        gk_t = gk_t + mm(query_t[:, rows], score)
        gv_t = gv_t + mm(grads_t[:, rows], prob.astype(BF16))
    gk_sum[pl.ds(feature, head_size), :] = gk_t
    gv_sum[pl.ds(feature, head_size), :] = gv_t

    order = unit_order(heads)
    early = len(order) // 2

    def give_back(some_heads):
        for other in range(row_parts):
            unit = order.index((other // 2, some_heads[0]))
            dbias_ref = keep_ref
            if other % 2:
                dbias_ref = give_ref if unit < early else give_late_ref
                unit = unit % early
            unit = unit + head - some_heads[0]
            scores = [score_full[rows, :] for _, rows in places(row_ref[0] ^ other)]
            blocks = []
            for column in range(groups):
                start = groups * 128 + column * rest_lanes
                blocks += [score[:, column * 128 : (column + 1) * 128] for score in scores]
                blocks.append(
                    jnp.concatenate(
                        [score[:, start : start + rest_lanes] for score in scores], axis=1
                    )
                )
            dbias_ref[unit] = jnp.stack(blocks).reshape(dbias_ref.shape[1:])

    @pl.when(head < heads // 2)
    def _():
        give_back(range(heads // 2))

    @pl.when(head >= heads // 2)
    def _():
        give_back(range(heads // 2, heads))

    @pl.when(head == heads - 1)
    def _():
        results = (
            gq_sum[...] * scale,
            (gk_sum[...] * scale).T,
            gv_sum[...].T,
            att_sum[:, :part],
        )
        for kind, values in enumerate(results):
            rounded = values.astype(BF16)
            lanes = slice(kind * part, (kind + 1) * part)
            if kind in (0, 3):
                for slot in range(groups):
                    out_refs[slot][:, lanes] = rounded[slot * cols : (slot + 1) * cols]
            else:
                for token, place, count in turns:
                    slot, inside = divmod(token, cols)
                    out_refs[slot][inside : inside + count, lanes] = rounded[place : place + count]


def attention(group_index, row_index, acts, bias, head_size):
    groups = len(acts)
    row_parts = len(bias) - 2
    cols, width = acts[0].shape
    tokens = groups * cols
    part = width // 4
    _, heads, _, half, lanes = bias[0].shape
    row_block = 256 if tokens % 256 == 0 else cols
    padded = (part // 128 + 1) * 128
    units = (row_parts // 2 * heads, groups, 3, half, lanes)
    some = (row_parts // 4 * heads, groups, 3, half, lanes)
    *grads, keep, give, give_late = pl.pallas_call(
        functools.partial(
            attention_kernel,
            groups=groups,
            row_parts=row_parts,
            head_size=head_size,
            row_block=row_block,
        ),
        grid=(heads,),
        in_specs=[smem(), smem()]
        + [
            pl.BlockSpec((block.shape[0], 1, 3, half, lanes), lambda h: (0, h, 0, 0, 0))
            for block in bias
        ]
        + [pl.BlockSpec((cols, width), lambda h: (0, 0))] * groups,
        out_specs=[pl.BlockSpec((cols, width), lambda h: (0, 0))] * groups
        + [pl.BlockSpec(shape, lambda h: (0, 0, 0, 0, 0)) for shape in (units, some, some)],
        out_shape=[jax.ShapeDtypeStruct((cols, width), BF16)] * groups
        + [jax.ShapeDtypeStruct(shape, BF16) for shape in (units, some, some)],
        scratch_shapes=[pltpu.VMEM((tokens, part), BF16) for _ in range(4)]
        + [pltpu.VMEM((part, tokens), BF16) for _ in range(4)]
        + [
            pltpu.VMEM((tokens, tokens), BF16),
            pltpu.VMEM((tokens, tokens), BF16),
            pltpu.VMEM((tokens, padded), F32),
            pltpu.VMEM((tokens, part), F32),
            pltpu.VMEM((part, tokens), F32),
            pltpu.VMEM((part, tokens), F32),
        ],
        compiler_params=params(),
    )(group_index, row_index, *bias, *acts)
    return grads, keep, give, give_late


def finish_kernel(
    group_ref,
    single_ref,
    noised_ref,
    cot_ref,
    gamma_ref,
    gate_ref,
    w_gamma_ref,
    w_beta_ref,
    w_outgate_ref,
    w_query_ref,
    w_key_ref,
    w_value_ref,
    w_out_ref,
    *rest,
    groups,
    calls,
):
    got_refs = rest[: groups * calls]
    updated_ref, d_single_ref, stage_ref = rest[groups * calls :]
    width = stage_ref.shape[3]
    part = width // 4
    for slot in range(groups):
        for call in range(calls):
            stage_ref[group_ref[0] ^ slot, call] = got_refs[
                call * groups + slot
            ][...]

    def take(kind):
        return jnp.concatenate(
            [
                stage_ref[group, call, :, kind * part : (kind + 1) * part]
                for group in range(groups)
                for call in range(calls)
            ],
            axis=1,
        )

    out_gate = gate_ref[...]
    cond_gamma = gamma_ref[...]
    block_update = mm(take(3), w_out_ref[...])
    noised = noised_ref[...].astype(F32)
    updated_ref[...] = (noised + out_gate * block_update).astype(BF16)
    gate_part = cot_ref[...].astype(F32) * block_update
    pre_gate = (gate_part * out_gate * (1.0 - out_gate)).astype(BF16)
    grad_input = mm_nt(take(0), w_query_ref[...])
    grad_input += mm_nt(take(1), w_key_ref[...])
    grad_input += mm_nt(take(2), w_value_ref[...])
    noised_norm, _ = norm_rows(noised)
    pre_gamma = (grad_input * noised_norm * cond_gamma * (1.0 - cond_gamma)).astype(BF16)
    grad_snorm = mm_nt(pre_gamma, w_gamma_ref[...])
    grad_snorm += mm_nt(grad_input.astype(BF16), w_beta_ref[...])
    grad_snorm += mm_nt(pre_gate, w_outgate_ref[...])
    single_norm, single_inv = norm_rows(single_ref[...].astype(F32))
    d_single_ref[...] = norm_back(grad_snorm, single_norm, single_inv).astype(BF16)


def swap_groups(sends):
    groups = len(sends)
    order = (*range(2, groups), 1)
    got = []
    for bits in order:
        perm = [(index, index ^ bits) for index in range(groups)]
        got.append(lax.ppermute(sends[bits], "grp", perm))
    got = dict(zip(order, lax.optimization_barrier(got)))
    return [sends[0]] + [got[bits] for bits in range(1, groups)]


def flip_rows(values, bits, row_total):
    return lax.ppermute(values, "rows", [(index, index ^ bits) for index in range(row_total)])


def gather_rows(own, acts, row_total):
    half = own.shape[0] // 2
    near = flip_rows(own, 2, row_total)
    far = flip_rows(own, 4, row_total)
    first = flip_rows(near[:half], 4, row_total)
    second = flip_rows(far[half:], 2, row_total)
    first, second, acts = lax.optimization_barrier((first, second, acts))
    blocks = []
    for block in (own, near, far, first, second):
        blocks += [block, flip_rows(block, 1, row_total)]
    return blocks, acts


def add_last_kernel(own_ref, far_ref, near_ref, *out_refs):
    heads = own_ref.shape[0]
    half = heads // 2
    for head in range(heads):
        other = far_ref[head] if head < half else near_ref[head - half]
        total = (own_ref[head].astype(F32) + other.astype(F32)).astype(BF16)
        for slot, out_ref in enumerate(out_refs):
            out_ref[head] = total[slot]


def scatter_rows(keep, give, give_late, row_total):
    got = flip_rows(give, 1, row_total)
    got, give_late = lax.optimization_barrier((got, give_late))
    got_late = flip_rows(give_late, 1, row_total)
    early = got.shape[0]
    heads = early // 2
    part = heads // 2

    def add(first, count, *others):
        source, place = (got, first) if first < early else (got_late, first - early)
        total = keep[first : first + count].astype(F32)
        total += source[place : place + count].astype(F32)
        for other in others:
            total += other.astype(F32)
        return total.astype(BF16)

    near = flip_rows(add(0, heads), 2, row_total)
    far = flip_rows(add(heads, heads), 4, row_total)
    far_two = flip_rows(add(early + heads, part, near[part:]), 4, row_total)
    near_two = flip_rows(add(early + heads + part, part, far[part:]), 2, row_total)
    own = add(early, heads, jnp.concatenate([near[:part], far[:part]]))
    return own, far_two, near_two


def add_last(own, far_two, near_two):
    heads, groups = own.shape[:2]
    return pl.pallas_call(
        add_last_kernel,
        in_specs=[vmem()] * 3,
        out_specs=[vmem()] * groups,
        out_shape=[jax.ShapeDtypeStruct((heads,) + own.shape[2:], BF16)] * groups,
        compiler_params=params(),
    )(own, far_two, near_two)


def sum_cores(mine, row_total):
    return (mine.astype(F32) + flip_rows(mine, 1, row_total).astype(F32)).astype(BF16)


def sum_chips(both, row_total):
    near, far, last = (flip_rows(both, bits, row_total).astype(F32) for bits in (2, 4, 6))
    return (both.astype(F32) + near) + (far + last)


def split_heads(
    single,
    pair,
    chains,
    noised,
    w_gamma,
    w_beta,
    w_outgate,
    w_query,
    w_key,
    w_value,
    w_out,
    w_pair,
    chain_gain,
    cotangent,
    *,
    groups,
    row_total,
):
    cols, _ = single.shape
    tokens = chains.shape[0]
    width = noised.shape[2]
    head_size = width // w_pair.shape[1]
    calls = 1
    row_index = lax.axis_index("rows").reshape(1)
    group_index = lax.axis_index("grp").reshape(1)
    bias_send, stats = pair_bias(
        pair, w_pair, chain_gain, chains, group_index, row_index, groups
    )
    bias_got = swap_groups(bias_send)
    noised = noised[0]
    cotangent = cotangent[0]
    *acts_send, cond_gamma, out_gate = pl.pallas_call(
        functools.partial(project_kernel, groups=groups, calls=calls),
        in_specs=[smem()] + [vmem()] * 10,
        out_shape=[
            jax.ShapeDtypeStruct((cols, 4 * width // groups), BF16) for _ in range(groups)
        ]
        + [
            jax.ShapeDtypeStruct((cols, width), F32),
            jax.ShapeDtypeStruct((cols, width), F32),
        ],
        scratch_shapes=[pltpu.VMEM((groups, cols, 4 * width // groups), BF16)],
        compiler_params=params(),
    )(
        group_index,
        single,
        noised,
        cotangent,
        w_gamma,
        w_beta,
        w_outgate,
        w_query,
        w_key,
        w_value,
        w_out,
    )
    bias_got, _ = lax.optimization_barrier((bias_got, acts_send))
    acts = swap_groups(acts_send)
    bias_all, acts = gather_rows(jnp.stack(bias_got), acts, row_total)
    grads_send, keep, give, give_late = attention(group_index, row_index, acts, bias_all, head_size)
    grads = swap_groups(grads_send)
    own, far_two, near_two = scatter_rows(keep, give, give_late, row_total)
    far_two, near_two, grads = lax.optimization_barrier((far_two, near_two, grads))
    dbias_own, grads = lax.optimization_barrier((add_last(own, far_two, near_two), grads))
    dbias_back = swap_groups(dbias_own)
    updated, d_part = pl.pallas_call(
        functools.partial(finish_kernel, groups=groups, calls=calls),
        in_specs=[smem()] + [vmem()] * (12 + groups * calls),
        out_shape=[
            jax.ShapeDtypeStruct((cols, width), BF16),
            jax.ShapeDtypeStruct(single.shape, BF16),
        ],
        scratch_shapes=[pltpu.VMEM((groups, calls, cols, 4 * width // (groups * calls)), BF16)],
        compiler_params=params(),
    )(
        group_index,
        single,
        noised,
        cotangent,
        cond_gamma,
        out_gate,
        w_gamma,
        w_beta,
        w_outgate,
        w_query,
        w_key,
        w_value,
        w_out,
        *grads,
    )
    d_part, dbias_back = lax.optimization_barrier((d_part, dbias_back))
    d_both = sum_cores(d_part, row_total)
    d_single = sum_chips(d_both, row_total)
    d_pair = pair_back(pair, stats, dbias_back, w_pair, group_index, groups, float(tokens))
    return (updated[None], d_single, d_pair)


def project(acts, weight):
    return jnp.einsum("std,de->ste", acts, weight, preferred_element_type=F32)


def project_back(acts, weight):
    return jnp.einsum("ste,de->std", acts, weight, preferred_element_type=F32)


def split_keys(
    single,
    pair,
    chains,
    noised,
    w_gamma,
    w_beta,
    w_outgate,
    w_query,
    w_key,
    w_value,
    w_out,
    w_pair,
    chain_gain,
    cotangent,
):
    col_count = single.shape[0]
    row_count = pair.shape[0]
    head_count = w_pair.shape[1]
    model_width = w_query.shape[0]
    head_size = model_width // head_count
    sample_count = noised.shape[0]
    token_total = chains.shape[0]
    score_scale = 1.0 / math.sqrt(head_size)
    row_index = lax.axis_index("rows")
    group_index = lax.axis_index("grp")
    chain_rows = lax.dynamic_slice_in_dim(chains, row_index * row_count, row_count)
    chain_cols = lax.dynamic_slice_in_dim(chains, group_index * col_count, col_count)
    pair_norm, pair_inv = norm_rows(pair.astype(jnp.float32))
    projected = jnp.einsum(
        "ijc,ch->hij", pair_norm.astype(jnp.bfloat16), w_pair, preferred_element_type=jnp.float32
    )
    same_chain = (chain_rows[:, None] == chain_cols[None, :]).astype(jnp.float32)
    bias_block = (projected + chain_gain[:, None, None] * same_chain[None]).astype(jnp.bfloat16)
    bias_keys = lax.all_gather(bias_block, "rows", axis=1, tiled=True)
    single_norm, single_inv = norm_rows(single.astype(jnp.float32))
    single_b = single_norm.astype(jnp.bfloat16)
    cond_gamma = jax.nn.sigmoid(jnp.dot(single_b, w_gamma, preferred_element_type=jnp.float32))
    cond_beta = jnp.dot(single_b, w_beta, preferred_element_type=jnp.float32)
    out_gate = jax.nn.sigmoid(jnp.dot(single_b, w_outgate, preferred_element_type=jnp.float32))
    noised_f = noised.astype(jnp.float32)
    noised_norm, noised_inv = norm_rows(noised_f)
    x_b = (noised_norm * cond_gamma[None] + cond_beta[None]).astype(jnp.bfloat16)
    queries = project(x_b, w_query).astype(jnp.bfloat16)
    keys_own = project(x_b, w_key).astype(jnp.bfloat16)
    values_own = project(x_b, w_value).astype(jnp.bfloat16)
    queries_all = lax.all_gather(queries, "grp", axis=1, tiled=True)
    query_heads = queries_all.reshape(sample_count, token_total, head_count, head_size)
    key_heads = keys_own.reshape(sample_count, col_count, head_count, head_size)
    value_heads = values_own.reshape(sample_count, col_count, head_count, head_size)
    scores = (
        jnp.einsum("sihe,sjhe->shij", query_heads, key_heads, preferred_element_type=jnp.float32)
        * score_scale
        + bias_keys.astype(jnp.float32)[None]
    )
    exp_scores = jnp.exp(scores)
    exp_total = lax.psum(jnp.sum(exp_scores, axis=-1).astype(jnp.bfloat16), "grp").astype(
        jnp.float32
    )
    attn_prob = exp_scores / exp_total[..., None]
    prob_b = attn_prob.astype(jnp.bfloat16)
    attended_part = jnp.einsum(
        "shij,sjhe->sihe", prob_b, value_heads, preferred_element_type=jnp.float32
    )
    attended_part = attended_part.reshape(sample_count, token_total, model_width)
    attended = lax.psum_scatter(
        attended_part.astype(jnp.bfloat16), "grp", scatter_dimension=1, tiled=True
    )
    block_update = project(attended, w_out)
    updated = (noised_f + out_gate[None] * block_update).astype(jnp.bfloat16)
    grad_out = cotangent.astype(jnp.float32)
    gate_part = jnp.sum(grad_out * block_update, axis=0)
    grad_update = (grad_out * out_gate[None]).astype(jnp.bfloat16)
    grad_attn = project_back(grad_update, w_out).astype(jnp.bfloat16)
    grads_all = lax.all_gather(grad_attn, "grp", axis=1, tiled=True)
    grad_heads = grads_all.reshape(sample_count, token_total, head_count, head_size)
    grad_prob = jnp.einsum(
        "sihe,sjhe->shij", grad_heads, value_heads, preferred_element_type=jnp.float32
    )
    row_delta = lax.psum(
        jnp.sum(attn_prob * grad_prob, axis=-1).astype(jnp.bfloat16), "grp"
    ).astype(jnp.float32)
    grad_score = attn_prob * (grad_prob - row_delta[..., None])
    score_b = grad_score.astype(jnp.bfloat16)
    query_part = (
        jnp.einsum("shij,sjhe->sihe", score_b, key_heads, preferred_element_type=jnp.float32)
        * score_scale
    )
    query_part = query_part.reshape(sample_count, token_total, model_width)
    grad_query = lax.psum_scatter(
        query_part.astype(jnp.bfloat16), "grp", scatter_dimension=1, tiled=True
    )
    grad_key = (
        jnp.einsum("shij,sihe->sjhe", score_b, query_heads, preferred_element_type=jnp.float32)
        * score_scale
    )
    grad_value = jnp.einsum(
        "shij,sihe->sjhe", prob_b, grad_heads, preferred_element_type=jnp.float32
    )
    grad_key = grad_key.reshape(sample_count, col_count, model_width).astype(jnp.bfloat16)
    grad_value = grad_value.reshape(sample_count, col_count, model_width).astype(jnp.bfloat16)
    grad_input = (
        project_back(grad_query, w_query)
        + project_back(grad_key, w_key)
        + project_back(grad_value, w_value)
    )
    gamma_part = jnp.sum(grad_input * noised_norm, axis=0)
    beta_part = jnp.sum(grad_input, axis=0)
    gamma_sum, beta_sum, gate_sum = lax.psum((gamma_part, beta_part, gate_part), "rows")
    pre_gamma = (gamma_sum * cond_gamma * (1.0 - cond_gamma)).astype(jnp.bfloat16)
    pre_gate = (gate_sum * out_gate * (1.0 - out_gate)).astype(jnp.bfloat16)
    grad_snorm = jnp.dot(pre_gamma, w_gamma.T, preferred_element_type=jnp.float32)
    grad_snorm = grad_snorm + jnp.dot(
        beta_sum.astype(jnp.bfloat16), w_beta.T, preferred_element_type=jnp.float32
    )
    grad_snorm = grad_snorm + jnp.dot(pre_gate, w_outgate.T, preferred_element_type=jnp.float32)
    d_single = norm_back(grad_snorm, single_norm, single_inv)
    bias_part = jnp.sum(score_b, axis=0, dtype=jnp.float32)
    bias_own = lax.psum_scatter(bias_part, "rows", scatter_dimension=1, tiled=True)
    bias_grad = (bias_own * token_total).astype(jnp.bfloat16)
    grad_pairn = jnp.einsum("hij,ch->ijc", bias_grad, w_pair, preferred_element_type=jnp.float32)
    d_pair = norm_back(grad_pairn, pair_norm, pair_inv).astype(jnp.bfloat16)
    return (updated, d_single, d_pair)


def solution(mesh):
    in_specs = (
        P("grp", None),
        P("rows", "grp", None),
        P(),
        P("rows", "grp", None),
        P(),
        P(),
        P(),
        P(),
        P(),
        P(),
        P(),
        P(),
        P(),
        P("rows", "grp", None),
    )
    out_specs = (P("rows", "grp", None), P("grp", None), P("rows", "grp", None))
    groups = mesh.shape["grp"]
    row_total = mesh.shape["rows"]

    def on_device(*args):
        pair, noised, w_pair = args[1], args[3], args[11]
        fits = (
            groups in (2, 4)
            and pair.shape[0] % 32 == 0
            and pair.shape[1] % pair.shape[0] == 0
            and row_total == 8
            and noised.shape[0] == 1
            and noised.shape[1] == 192
            and w_pair.shape[1] % (2 * groups) == 0
        )
        if fits:
            return split_heads(*args, groups=groups, row_total=row_total)
        return split_keys(*args)

    return jax.shard_map(
        on_device, mesh=mesh, in_specs=in_specs, out_specs=out_specs, check_vma=False
    )
```

```python
import functools
import math

import jax
import jax.numpy as jnp
from jax import lax
from jax.experimental import pallas as pl
from jax.experimental.pallas import tpu as pltpu
from jax.sharding import PartitionSpec as P

EPSILON = 1e-05
BF16 = jnp.bfloat16
F32 = jnp.float32
LOG2_E = math.log2(math.e)
VMEM_LIMIT = 56 * 1024 * 1024


def norm_rows(values):
    center = values - jnp.mean(values, axis=-1, keepdims=True)
    inverse = lax.rsqrt(jnp.mean(center * center, axis=-1, keepdims=True) + EPSILON)
    return (center * inverse, inverse)


def norm_back(grad_in, normed, inverse):
    grad_mean = jnp.mean(grad_in, axis=-1, keepdims=True)
    cross_mean = jnp.mean(grad_in * normed, axis=-1, keepdims=True)
    return inverse * (grad_in - grad_mean - normed * cross_mean)


def mm(left, right):
    return lax.dot_general(left, right, (((1,), (0,)), ((), ())), preferred_element_type=F32)


def mm_nt(left, right):
    return lax.dot_general(left, right, (((1,), (1,)), ((), ())), preferred_element_type=F32)


def mm_tn(left, right):
    return lax.dot_general(left, right, (((0,), (0,)), ((), ())), preferred_element_type=F32)


def sigmoid(values):
    return 1.0 / (1.0 + jnp.exp(-values))


def params():
    return pltpu.CompilerParams(vmem_limit_bytes=VMEM_LIMIT)


def smem():
    return pl.BlockSpec(memory_space=pltpu.SMEM)


def vmem():
    return pl.BlockSpec(memory_space=pltpu.VMEM)


def project_kernel(
    group_ref,
    single_ref,
    noised_ref,
    cot_ref,
    w_gamma_ref,
    w_beta_ref,
    w_outgate_ref,
    w_query_ref,
    w_key_ref,
    w_value_ref,
    w_out_ref,
    *rest,
    groups,
    calls,
    head_size,
):
    send_refs = rest[:groups]
    gamma_ref, gate_ref, stage_ref = rest[groups:]
    width = stage_ref.shape[2]
    part = width // (4 * calls)
    group_own = group_ref[0]
    single_norm, _ = norm_rows(single_ref[...].astype(F32))
    single_b = single_norm.astype(BF16)
    cond_gamma = sigmoid(mm(single_b, w_gamma_ref[...]))
    gamma_ref[...] = cond_gamma
    out_gate = sigmoid(mm(single_b, w_outgate_ref[...]))
    gate_ref[...] = out_gate
    cond_beta = mm(single_b, w_beta_ref[...])
    noised_norm, _ = norm_rows(noised_ref[...].astype(F32))
    x_b = (noised_norm * cond_gamma + cond_beta).astype(BF16)

    def put(kind, values):
        rounded = values.astype(BF16)
        for group in range(groups):
            slot = group_own ^ group
            for call in range(calls):
                feature = (group * calls + call) * part
                lane = (call * 4 + kind) * part
                stage_ref[slot, :, lane : lane + part] = rounded[:, feature : feature + part]

    put(0, mm(x_b, w_query_ref[...]) * (LOG2_E / math.sqrt(head_size)))
    put(1, mm(x_b, w_key_ref[...]))
    put(2, mm(x_b, w_value_ref[...]))
    grad_update = (cot_ref[...].astype(F32) * out_gate).astype(BF16)
    put(3, mm_nt(grad_update, w_out_ref[...]))
    for slot in range(groups):
        send_refs[slot][...] = stage_ref[slot]


def lane_tiles(cols):
    return [(tile, tile * 128, min(cols, tile * 128 + 128)) for tile in range(-(-cols // 128))]


def mean_matrix(channels):
    first = lax.broadcasted_iota(jnp.int32, (2 * channels, 2 * channels), 0) >= channels
    second = lax.broadcasted_iota(jnp.int32, (2 * channels, 2 * channels), 1) >= channels
    return jnp.where(first == second, 1.0 / channels, 0.0).astype(BF16)


def center_rows(pair_ref, first, batch, means):
    _, _, cols, channels = pair_ref.shape
    both = jnp.concatenate(
        [pair_ref[side, first : first + batch].reshape(batch * cols, channels) for side in range(2)],
        axis=1,
    )
    return both.astype(F32) - mm(both, means)


def lane_pad(block, before, total):
    rows, width = block.shape
    pieces = [block]
    if before:
        pieces = [jnp.zeros((rows, before), block.dtype)] + pieces
    if total > before + width:
        pieces = pieces + [jnp.zeros((rows, total - before - width), block.dtype)]
    return jnp.concatenate(pieces, axis=1)


def bias_kernel(
    group_ref,
    rows_ref,
    chains_ref,
    gain_ref,
    pair_ref,
    w_pair_ref,
    cols_ref,
    *rest,
    groups,
    batch,
):
    send_refs = rest[:groups]
    stats_ref, flat_ref, gains_ref, stage_ref = rest[groups:]
    _, step, cols, channels = pair_ref.shape
    heads = gain_ref.shape[0]
    per_group = heads // groups
    half = step * pl.num_programs(0)
    group_own = group_ref[0]
    row_base = rows_ref[0] * 2 * half + pl.program_id(0) * step
    means = mean_matrix(channels)
    weight = w_pair_ref[...].astype(F32).T.astype(BF16)
    mean_part = jnp.full((channels, heads), 1.0 / channels, BF16)
    mixed = []
    for inner in range(2):
        for part, offset in ((weight, 0), (mean_part, heads)):
            for side in range(2):
                mixed.append(lane_pad(part, 2 * heads * (2 * inner + side) + offset, 8 * heads))
    mixed = jnp.concatenate(mixed, axis=0)
    chain_all = cols_ref[...].reshape(1, groups * cols)
    chain_cols = chain_all[:, :cols]
    for group in range(1, groups):
        here = chain_all[:, group * cols : (group + 1) * cols]
        chain_cols = jnp.where(group_own == group, here, chain_cols)
    for head in range(heads):
        gains_ref[head : head + 1, :] = jnp.full((1, cols), gain_ref[head] * LOG2_E, F32)

    for first in range(0, step, batch):
        center = center_rows(pair_ref, first, batch, means)
        center_b = center.astype(BF16)
        square = (center * center).astype(BF16)
        for base in range(0, batch, 2):
            one = slice(base * cols, (base + 1) * cols)
            two = slice((base + 1) * cols, (base + 2) * cols)
            left = jnp.concatenate(
                [center_b[one], square[one], center_b[two], square[two]], axis=1
            )
            sums = mm(left, mixed).T
            for inner in range(2):
                row = first + base + inner
                for side in range(2):
                    top = 2 * heads * (2 * inner + side)
                    inverse = lax.rsqrt(sums[top + heads : top + 2 * heads] + EPSILON)
                    projected = sums[top : top + heads] * inverse
                    stats_ref[side, row, :heads, :] = projected
                    stats_ref[side, row, heads:, :] = inverse[:8]
                    chain = chains_ref[row_base + side * half + row]
                    same = (chain_cols == chain).astype(F32)
                    values = projected * LOG2_E + gains_ref[...] * same
                    for tile, start, end in lane_tiles(cols):
                        piece = lane_pad(values[:, start:end], 0, 128)
                        flat_ref[side, tile, pl.ds(row, heads, stride=step), :] = piece
    for head in range(heads):
        slot = group_own ^ (head // per_group)
        tops = slice(head * step, (head + 1) * step)
        rest_lanes = [flat_ref[side, 1, tops, : cols - 128] for side in range(2)]
        stage_ref[slot, head % per_group, 0] = flat_ref[0, 0, tops, :].astype(BF16)
        stage_ref[slot, head % per_group, 1] = flat_ref[1, 0, tops, :].astype(BF16)
        stage_ref[slot, head % per_group, 2] = jnp.concatenate(rest_lanes, axis=1).astype(BF16)
    for slot in range(groups):
        send_refs[slot][...] = stage_ref[slot]


def pair_bias(pair, w_pair, chain_gain, chains, group_index, row_index, groups):
    rows, cols, channels = pair.shape
    heads = w_pair.shape[1]
    per_group = heads // groups
    half = rows // 2
    step = 16
    tiles = -(-cols // 128)
    *sends, stats = pl.pallas_call(
        functools.partial(bias_kernel, groups=groups, batch=4),
        grid=(half // step,),
        in_specs=[
            smem(),
            smem(),
            smem(),
            smem(),
            pl.BlockSpec((2, step, cols, channels), lambda t: (0, t, 0, 0)),
            pl.BlockSpec((heads, channels), lambda t: (0, 0)),
            pl.BlockSpec((groups * cols,), lambda t: (0,)),
        ],
        out_specs=[
            pl.BlockSpec((per_group, 3, step, 128), lambda t: (0, 0, t, 0)) for _ in range(groups)
        ]
        + [pl.BlockSpec((2, step, heads + 8, cols), lambda t: (0, t, 0, 0))],
        out_shape=[
            jax.ShapeDtypeStruct((per_group, 3, half, 128), BF16) for _ in range(groups)
        ]
        + [jax.ShapeDtypeStruct((2, half, heads + 8, cols), F32)],
        scratch_shapes=[
            pltpu.VMEM((2, tiles, heads * step, 128), F32),
            pltpu.VMEM((heads, cols), F32),
            pltpu.VMEM((groups, per_group, 3, step, 128), BF16),
        ],
        compiler_params=params(),
    )(
        group_index,
        row_index,
        chains,
        chain_gain,
        pair.reshape(2, half, cols, channels),
        w_pair.T,
        chains,
    )
    return sends, stats


def pair_back_kernel(
    group_ref, pair_ref, stats_ref, w_pair_ref, *rest, groups, calls, factor, batch
):
    grad_refs = rest[: groups * calls]
    out_ref, flat_ref = rest[groups * calls :]
    _, step, cols, channels = pair_ref.shape
    per_call = grad_refs[0].shape[0]
    heads = groups * calls * per_call
    group_own = group_ref[0]
    means = mean_matrix(channels)
    weight = w_pair_ref[...].astype(F32)
    weight = (weight - jnp.mean(weight, axis=-1, keepdims=True)).astype(BF16)
    spread = lax.broadcasted_iota(jnp.int32, (heads, channels), 0)
    spread = (spread < 2).astype(F32).astype(BF16)
    block = jnp.concatenate(
        [lane_pad(weight, 0, 2 * channels), lane_pad(spread, channels, 2 * channels)], axis=0
    )
    weights = jnp.concatenate(
        [lane_pad(block, 2 * channels * place, 8 * channels) for place in range(4)], axis=0
    )
    blank = jnp.zeros((heads - 2, cols), F32)
    for number in range(groups * calls):
        call, slot = divmod(number, groups)
        source = (group_own ^ slot) * calls + call
        for head in range(per_call):
            values = grad_refs[number][head].astype(F32)
            top = pl.multiple_of((source * per_call + head) * step, step)
            for side in range(2):
                flat_ref[side, 0, pl.ds(top, step), :] = values[side]
                flat_ref[side, 1, pl.ds(top, step), : cols - 128] = values[2][
                    :, side * (cols - 128) : (side + 1) * (cols - 128)
                ]

    for first in range(0, step, batch):
        center = center_rows(pair_ref, first, batch, means)
        for base in range(0, batch, 2):
            places = [(base + inner, side) for inner in range(2) for side in range(2)]
            left = []
            for inner, side in places:
                grads = jnp.concatenate(
                    [
                        flat_ref[side, tile, pl.ds(first + inner, heads, stride=step), :][
                            :, : end - start
                        ]
                        for tile, start, end in lane_tiles(cols)
                    ],
                    axis=1,
                )
                projected = stats_ref[side, first + inner, :heads, :]
                inverse = stats_ref[side, first + inner, heads : heads + 1, :]
                cross = jnp.sum(grads * projected, axis=0, keepdims=True) * (1.0 / channels)
                scaled = grads * (inverse * factor)
                cross = cross * (inverse * inverse * factor)
                cross_high = cross.astype(BF16).astype(F32)
                left += [scaled, cross_high, cross - cross_high, blank]
            both = mm_tn(jnp.concatenate(left, axis=0).astype(BF16), weights)
            for place, (inner, side) in enumerate(places):
                rows = slice(inner * cols, (inner + 1) * cols)
                lanes = slice(side * channels, (side + 1) * channels)
                start = 2 * channels * place
                middle, end = start + channels, start + 2 * channels
                out_ref[side, first + inner] = (
                    both[:, start:middle] - center[rows, lanes] * both[:, middle:end]
                ).astype(BF16)


def pair_back(pair, stats, grads, w_pair, group_index, groups, factor):
    rows, cols, channels = pair.shape
    per_call = grads[0].shape[0]
    heads = len(grads) * per_call
    half = rows // 2
    step = 16
    tiles = -(-cols // 128)
    out = pl.pallas_call(
        functools.partial(
            pair_back_kernel, groups=groups, calls=len(grads) // groups, factor=factor, batch=4
        ),
        grid=(half // step,),
        in_specs=[
            smem(),
            pl.BlockSpec((2, step, cols, channels), lambda t: (0, t, 0, 0)),
            pl.BlockSpec((2, step, heads + 8, cols), lambda t: (0, t, 0, 0)),
            pl.BlockSpec((heads, channels), lambda t: (0, 0)),
        ]
        + [pl.BlockSpec((per_call, 3, step, 128), lambda t: (0, 0, t, 0)) for _ in grads],
        out_specs=pl.BlockSpec((2, step, cols, channels), lambda t: (0, t, 0, 0)),
        out_shape=jax.ShapeDtypeStruct((2, half, cols, channels), BF16),
        scratch_shapes=[pltpu.VMEM((2, tiles, heads * step, 128), F32)],
        compiler_params=params(),
    )(group_index, pair.reshape(2, half, cols, channels), stats, w_pair.T, *grads)
    return out.reshape(rows, cols, channels)


def unit_order(heads):
    first, second = range(heads // 2), range(heads // 2, heads)
    order = [(1, head) for head in first] + [(3, head) for head in first]
    order += [(2, head) for head in second] + [(3, head) for head in second]
    order += [(0, head) for head in range(heads)]
    order += [(2, head) for head in first] + [(1, head) for head in second]
    return order


def attention_kernel(group_ref, row_ref, *rest, groups, row_parts, head_size, row_block):
    bias_refs = rest[: row_parts + 2]
    acts_refs = rest[row_parts + 2 : row_parts + 2 + groups]
    rest = rest[row_parts + 2 + groups :]
    out_refs = rest[:groups]
    (
        keep_ref,
        give_ref,
        query_ref,
        keys_ref,
        values_ref,
        grads_ref,
        query_t_ref,
        keys_t_ref,
        values_t_ref,
        bias_full,
        score_full,
        att_sum,
        gq_sum,
        gk_sum,
        gv_sum,
    ) = rest[groups:]
    head = pl.program_id(0)
    heads = keep_ref.shape[0] * 2 // row_parts
    group_own = group_ref[0]
    cols, width = acts_refs[0].shape
    tokens = groups * cols
    part = width // 4
    half = bias_refs[0].shape[3]
    rest_lanes = cols - 128
    scale = 1.0 / math.sqrt(head_size)
    extra = att_sum.shape[1] - part
    plain = (query_ref, keys_ref, values_ref, grads_ref)
    turned = (query_t_ref, keys_t_ref, values_t_ref)

    turns = [(slot * cols, slot * 128, 128) for slot in range(groups)]
    turns += [
        (slot * cols + 128, groups * 128 + slot * rest_lanes, rest_lanes) for slot in range(groups)
    ]

    @pl.when(head == 0)
    def _():
        for kind in range(4):
            lanes = slice(kind * part, (kind + 1) * part)
            if kind in (0, 3):
                for slot in range(groups):
                    plain[kind][slot * cols : (slot + 1) * cols, :] = acts_refs[slot][:, lanes]
            else:
                for token, place, count in turns:
                    slot, inside = divmod(token, cols)
                    plain[kind][place : place + count, :] = acts_refs[slot][
                        inside : inside + count, lanes
                    ]
            if kind < len(turned):
                turned[kind][...] = plain[kind][...].T
        att_sum[...] = jnp.zeros_like(att_sum)
        gq_sum[...] = jnp.zeros_like(gq_sum)
        gv_sum[...] = jnp.zeros_like(gv_sum)

    def places(row_part):
        first = row_part * (2 * half)
        slot = group_own ^ (first // cols)
        for side in range(2):
            top = slot * cols + lax.rem(first, cols) + side * half
            yield side, pl.ds(pl.multiple_of(top, 16), half)

    for other in range(row_parts):

        def block(column, which, other=other):
            if other >= row_parts - 2 and column >= groups // 2:
                return bias_refs[other + 2][column - groups // 2, 0, which]
            return bias_refs[other][column, 0, which]

        for side, rows in places(row_ref[0] ^ other):
            lanes = slice(side * rest_lanes, (side + 1) * rest_lanes)
            tiles = [block(column, side) for column in range(groups)]
            tiles += [block(column, 2)[:, lanes] for column in range(groups)]
            bias_full[rows, :] = jnp.concatenate(tiles, axis=1)

    lane = lax.broadcasted_iota(jnp.int32, (1, part), 1)
    mine = (lane >= head * head_size) & (lane < (head + 1) * head_size)
    zero = jnp.zeros((), BF16)
    keys_m = jnp.where(mine, keys_ref[...], zero)
    values_m = jnp.concatenate(
        [jnp.where(mine, values_ref[...], zero), jnp.ones((tokens, extra), BF16)], axis=1
    )
    feature = pl.multiple_of(head * head_size, head_size)
    query_t = query_t_ref[pl.ds(feature, head_size), :]
    gk_t = jnp.zeros((head_size, tokens), F32)
    gv_t = jnp.zeros((part, tokens), F32)
    for top in range(0, tokens, row_block):
        rows = slice(top, top + row_block)
        query = jnp.where(mine, query_ref[rows, :], zero)
        grads = jnp.where(mine, grads_ref[rows, :], zero)
        weights = jnp.exp2(mm(query, keys_t_ref[...]) + bias_full[rows, :].astype(F32))
        weights_b = weights.astype(BF16)
        attended = mm(weights_b, values_m)
        inverse = 1.0 / attended[:, part : part + 1]
        attended = attended[:, :part] * inverse
        att_sum[rows, :part] += attended
        grads = (grads.astype(F32) * inverse).astype(BF16)
        delta = jnp.sum(attended * grads.astype(F32), axis=-1, keepdims=True)
        score = (weights * (mm(grads, values_t_ref[...]) - delta)).astype(BF16)
        score_full[rows, :] = score
        gq_sum[rows, :] += mm(score, keys_m)
        gk_t = gk_t + mm(query_t[:, rows], score)
        gv_t = gv_t + mm_tn(grads, weights_b)
    gk_sum[pl.ds(feature, head_size), :] = gk_t
    gv_sum[...] += gv_t

    order = unit_order(heads)

    def give_back(some_heads):
        for other in range(row_parts):
            unit = order.index((other // 2, some_heads[0]))
            dbias_ref = give_ref if other % 2 else keep_ref
            unit = unit + head - some_heads[0]
            scores = [score_full[rows, :] for _, rows in places(row_ref[0] ^ other)]
            blocks = []
            for column in range(groups):
                start = groups * 128 + column * rest_lanes
                blocks += [score[:, column * 128 : (column + 1) * 128] for score in scores]
                blocks.append(
                    jnp.concatenate(
                        [score[:, start : start + rest_lanes] for score in scores], axis=1
                    )
                )
            dbias_ref[unit] = jnp.stack(blocks).reshape(dbias_ref.shape[1:])

    @pl.when(head < heads // 2)
    def _():
        give_back(range(heads // 2))

    @pl.when(head >= heads // 2)
    def _():
        give_back(range(heads // 2, heads))

    @pl.when(head == heads - 1)
    def _():
        results = (
            gq_sum[...] * scale,
            (gk_sum[...] * math.log(2.0)).T,
            gv_sum[...].T,
            att_sum[:, :part],
        )
        for kind, values in enumerate(results):
            rounded = values.astype(BF16)
            lanes = slice(kind * part, (kind + 1) * part)
            if kind in (0, 3):
                for slot in range(groups):
                    out_refs[slot][:, lanes] = rounded[slot * cols : (slot + 1) * cols]
            else:
                for token, place, count in turns:
                    slot, inside = divmod(token, cols)
                    out_refs[slot][inside : inside + count, lanes] = rounded[place : place + count]


def attention(group_index, row_index, acts, bias, head_size):
    groups = len(acts)
    row_parts = len(bias) - 2
    cols, width = acts[0].shape
    tokens = groups * cols
    part = width // 4
    _, heads, _, half, lanes = bias[0].shape
    row_block = tokens
    padded = (part // 128 + 1) * 128
    units = (row_parts // 2 * heads, groups, 3, half, lanes)
    *grads, keep, give = pl.pallas_call(
        functools.partial(
            attention_kernel,
            groups=groups,
            row_parts=row_parts,
            head_size=head_size,
            row_block=row_block,
        ),
        grid=(heads,),
        in_specs=[smem(), smem()]
        + [
            pl.BlockSpec((block.shape[0], 1, 3, half, lanes), lambda h: (0, h, 0, 0, 0))
            for block in bias
        ]
        + [pl.BlockSpec((cols, width), lambda h: (0, 0))] * groups,
        out_specs=[pl.BlockSpec((cols, width), lambda h: (0, 0))] * groups
        + [pl.BlockSpec(shape, lambda h: (0, 0, 0, 0, 0)) for shape in (units, units)],
        out_shape=[jax.ShapeDtypeStruct((cols, width), BF16)] * groups
        + [jax.ShapeDtypeStruct(shape, BF16) for shape in (units, units)],
        scratch_shapes=[pltpu.VMEM((tokens, part), BF16) for _ in range(4)]
        + [pltpu.VMEM((part, tokens), BF16) for _ in range(3)]
        + [
            pltpu.VMEM((tokens, tokens), BF16),
            pltpu.VMEM((tokens, tokens), BF16),
            pltpu.VMEM((tokens, padded), F32),
            pltpu.VMEM((tokens, part), F32),
            pltpu.VMEM((part, tokens), F32),
            pltpu.VMEM((part, tokens), F32),
        ],
        compiler_params=params(),
    )(group_index, row_index, *bias, *acts)
    return grads, keep, give


def finish_kernel(
    group_ref,
    single_ref,
    noised_ref,
    cot_ref,
    gamma_ref,
    gate_ref,
    w_gamma_ref,
    w_beta_ref,
    w_outgate_ref,
    w_query_ref,
    w_key_ref,
    w_value_ref,
    w_out_ref,
    *rest,
    groups,
    calls,
):
    got_refs = rest[: groups * calls]
    updated_ref, d_single_ref, stage_ref = rest[groups * calls :]
    width = stage_ref.shape[3]
    part = width // 4
    for slot in range(groups):
        for call in range(calls):
            stage_ref[group_ref[0] ^ slot, call] = got_refs[
                call * groups + slot
            ][...]

    def take(kind):
        return jnp.concatenate(
            [
                stage_ref[group, call, :, kind * part : (kind + 1) * part]
                for group in range(groups)
                for call in range(calls)
            ],
            axis=1,
        )

    out_gate = gate_ref[...]
    cond_gamma = gamma_ref[...]
    block_update = mm(take(3), w_out_ref[...])
    noised = noised_ref[...].astype(F32)
    updated_ref[...] = (noised + out_gate * block_update).astype(BF16)
    gate_part = cot_ref[...].astype(F32) * block_update
    pre_gate = (gate_part * out_gate * (1.0 - out_gate)).astype(BF16)
    grad_input = mm_nt(take(0), w_query_ref[...])
    grad_input += mm_nt(take(1), w_key_ref[...])
    grad_input += mm_nt(take(2), w_value_ref[...])
    noised_norm, _ = norm_rows(noised)
    pre_gamma = (grad_input * noised_norm * cond_gamma * (1.0 - cond_gamma)).astype(BF16)
    grad_snorm = mm_nt(pre_gamma, w_gamma_ref[...])
    grad_snorm += mm_nt(grad_input.astype(BF16), w_beta_ref[...])
    grad_snorm += mm_nt(pre_gate, w_outgate_ref[...])
    single_norm, single_inv = norm_rows(single_ref[...].astype(F32))
    d_single_ref[...] = norm_back(grad_snorm, single_norm, single_inv).astype(BF16)


def swap_groups(sends):
    groups = len(sends)
    order = (*range(2, groups), 1)
    got = []
    for bits in order:
        perm = [(index, index ^ bits) for index in range(groups)]
        got.append(lax.ppermute(sends[bits], "grp", perm))
    got = dict(zip(order, got))
    return [sends[0]] + [got[bits] for bits in range(1, groups)]


def flip_rows(values, bits, row_total):
    return lax.ppermute(values, "rows", [(index, index ^ bits) for index in range(row_total)])


def gather_rows(own, acts, row_total):
    half = own.shape[0] // 2
    near = flip_rows(own, 2, row_total)
    far = flip_rows(own, 4, row_total)
    first = flip_rows(near[:half], 4, row_total)
    second = flip_rows(far[half:], 2, row_total)
    first, second, acts = lax.optimization_barrier((first, second, acts))
    blocks = []
    for block in (own, near, far, first, second):
        blocks += [block, flip_rows(block, 1, row_total)]
    return blocks, acts


def add_last_kernel(own_ref, far_ref, near_ref, *out_refs):
    heads = own_ref.shape[0]
    half = heads // 2
    for head in range(heads):
        other = far_ref[head] if head < half else near_ref[head - half]
        total = (own_ref[head].astype(F32) + other.astype(F32)).astype(BF16)
        for slot, out_ref in enumerate(out_refs):
            out_ref[head] = total[slot]


def scatter_rows(keep, give, row_total):
    got = flip_rows(give, 1, row_total)
    early = keep.shape[0] // 2
    heads = early // 2
    part = heads // 2

    def add(first, count, *others):
        total = keep[first : first + count].astype(F32) + got[first : first + count].astype(F32)
        for other in others:
            total += other.astype(F32)
        return total.astype(BF16)

    near = flip_rows(add(0, heads), 2, row_total)
    far = flip_rows(add(heads, heads), 4, row_total)
    far_two = flip_rows(add(early + heads, part, near[part:]), 4, row_total)
    near_two = flip_rows(add(early + heads + part, part, far[part:]), 2, row_total)
    own = add(early, heads, jnp.concatenate([near[:part], far[:part]]))
    return own, far_two, near_two


def add_last(own, far_two, near_two):
    heads, groups = own.shape[:2]
    return pl.pallas_call(
        add_last_kernel,
        in_specs=[vmem()] * 3,
        out_specs=[vmem()] * groups,
        out_shape=[jax.ShapeDtypeStruct((heads,) + own.shape[2:], BF16)] * groups,
        compiler_params=params(),
    )(own, far_two, near_two)


def sum_cores(mine, row_total):
    return (mine.astype(F32) + flip_rows(mine, 1, row_total).astype(F32)).astype(BF16)


def sum_chips(both, row_total):
    near, far, last = (flip_rows(both, bits, row_total).astype(F32) for bits in (2, 4, 6))
    return (both.astype(F32) + near) + (far + last)


def split_heads(
    single,
    pair,
    chains,
    noised,
    w_gamma,
    w_beta,
    w_outgate,
    w_query,
    w_key,
    w_value,
    w_out,
    w_pair,
    chain_gain,
    cotangent,
    *,
    groups,
    row_total,
):
    cols, _ = single.shape
    tokens = chains.shape[0]
    width = noised.shape[2]
    head_size = width // w_pair.shape[1]
    calls = 1
    row_index = lax.axis_index("rows").reshape(1)
    group_index = lax.axis_index("grp").reshape(1)
    bias_send, stats = pair_bias(
        pair, w_pair, chain_gain, chains, group_index, row_index, groups
    )
    bias_got = swap_groups(bias_send)
    noised = noised[0]
    cotangent = cotangent[0]
    *acts_send, cond_gamma, out_gate = pl.pallas_call(
        functools.partial(
            project_kernel, groups=groups, calls=calls, head_size=head_size
        ),
        in_specs=[smem()] + [vmem()] * 10,
        out_shape=[
            jax.ShapeDtypeStruct((cols, 4 * width // groups), BF16) for _ in range(groups)
        ]
        + [
            jax.ShapeDtypeStruct((cols, width), F32),
            jax.ShapeDtypeStruct((cols, width), F32),
        ],
        scratch_shapes=[pltpu.VMEM((groups, cols, 4 * width // groups), BF16)],
        compiler_params=params(),
    )(
        group_index,
        single,
        noised,
        cotangent,
        w_gamma,
        w_beta,
        w_outgate,
        w_query,
        w_key,
        w_value,
        w_out,
    )
    bias_got, _ = lax.optimization_barrier((bias_got, acts_send))
    acts = swap_groups(acts_send)
    bias_all, acts = gather_rows(jnp.stack(bias_got), acts, row_total)
    grads_send, keep, give = attention(group_index, row_index, acts, bias_all, head_size)
    grads = swap_groups(grads_send)
    own, far_two, near_two = scatter_rows(keep, give, row_total)
    far_two, near_two, grads = lax.optimization_barrier((far_two, near_two, grads))
    dbias_own, grads = lax.optimization_barrier((add_last(own, far_two, near_two), grads))
    dbias_back = swap_groups(dbias_own)
    updated, d_part = pl.pallas_call(
        functools.partial(finish_kernel, groups=groups, calls=calls),
        in_specs=[smem()] + [vmem()] * (12 + groups * calls),
        out_shape=[
            jax.ShapeDtypeStruct((cols, width), BF16),
            jax.ShapeDtypeStruct(single.shape, BF16),
        ],
        scratch_shapes=[pltpu.VMEM((groups, calls, cols, 4 * width // (groups * calls)), BF16)],
        compiler_params=params(),
    )(
        group_index,
        single,
        noised,
        cotangent,
        cond_gamma,
        out_gate,
        w_gamma,
        w_beta,
        w_outgate,
        w_query,
        w_key,
        w_value,
        w_out,
        *grads,
    )
    d_part, dbias_back = lax.optimization_barrier((d_part, dbias_back))
    d_both = sum_cores(d_part, row_total)
    d_single = sum_chips(d_both, row_total)
    d_pair = pair_back(pair, stats, dbias_back, w_pair, group_index, groups, float(tokens))
    return (updated[None], d_single, d_pair)


def project(acts, weight):
    return jnp.einsum("std,de->ste", acts, weight, preferred_element_type=F32)


def project_back(acts, weight):
    return jnp.einsum("ste,de->std", acts, weight, preferred_element_type=F32)


def split_keys(
    single,
    pair,
    chains,
    noised,
    w_gamma,
    w_beta,
    w_outgate,
    w_query,
    w_key,
    w_value,
    w_out,
    w_pair,
    chain_gain,
    cotangent,
):
    col_count = single.shape[0]
    row_count = pair.shape[0]
    head_count = w_pair.shape[1]
    model_width = w_query.shape[0]
    head_size = model_width // head_count
    sample_count = noised.shape[0]
    token_total = chains.shape[0]
    score_scale = 1.0 / math.sqrt(head_size)
    row_index = lax.axis_index("rows")
    group_index = lax.axis_index("grp")
    chain_rows = lax.dynamic_slice_in_dim(chains, row_index * row_count, row_count)
    chain_cols = lax.dynamic_slice_in_dim(chains, group_index * col_count, col_count)
    pair_norm, pair_inv = norm_rows(pair.astype(jnp.float32))
    projected = jnp.einsum(
        "ijc,ch->hij", pair_norm.astype(jnp.bfloat16), w_pair, preferred_element_type=jnp.float32
    )
    same_chain = (chain_rows[:, None] == chain_cols[None, :]).astype(jnp.float32)
    bias_block = (projected + chain_gain[:, None, None] * same_chain[None]).astype(jnp.bfloat16)
    bias_keys = lax.all_gather(bias_block, "rows", axis=1, tiled=True)
    single_norm, single_inv = norm_rows(single.astype(jnp.float32))
    single_b = single_norm.astype(jnp.bfloat16)
    cond_gamma = jax.nn.sigmoid(jnp.dot(single_b, w_gamma, preferred_element_type=jnp.float32))
    cond_beta = jnp.dot(single_b, w_beta, preferred_element_type=jnp.float32)
    out_gate = jax.nn.sigmoid(jnp.dot(single_b, w_outgate, preferred_element_type=jnp.float32))
    noised_f = noised.astype(jnp.float32)
    noised_norm, noised_inv = norm_rows(noised_f)
    x_b = (noised_norm * cond_gamma[None] + cond_beta[None]).astype(jnp.bfloat16)
    queries = project(x_b, w_query).astype(jnp.bfloat16)
    keys_own = project(x_b, w_key).astype(jnp.bfloat16)
    values_own = project(x_b, w_value).astype(jnp.bfloat16)
    queries_all = lax.all_gather(queries, "grp", axis=1, tiled=True)
    query_heads = queries_all.reshape(sample_count, token_total, head_count, head_size)
    key_heads = keys_own.reshape(sample_count, col_count, head_count, head_size)
    value_heads = values_own.reshape(sample_count, col_count, head_count, head_size)
    scores = (
        jnp.einsum("sihe,sjhe->shij", query_heads, key_heads, preferred_element_type=jnp.float32)
        * score_scale
        + bias_keys.astype(jnp.float32)[None]
    )
    exp_scores = jnp.exp(scores)
    exp_total = lax.psum(jnp.sum(exp_scores, axis=-1).astype(jnp.bfloat16), "grp").astype(
        jnp.float32
    )
    attn_prob = exp_scores / exp_total[..., None]
    prob_b = attn_prob.astype(jnp.bfloat16)
    attended_part = jnp.einsum(
        "shij,sjhe->sihe", prob_b, value_heads, preferred_element_type=jnp.float32
    )
    attended_part = attended_part.reshape(sample_count, token_total, model_width)
    attended = lax.psum_scatter(
        attended_part.astype(jnp.bfloat16), "grp", scatter_dimension=1, tiled=True
    )
    block_update = project(attended, w_out)
    updated = (noised_f + out_gate[None] * block_update).astype(jnp.bfloat16)
    grad_out = cotangent.astype(jnp.float32)
    gate_part = jnp.sum(grad_out * block_update, axis=0)
    grad_update = (grad_out * out_gate[None]).astype(jnp.bfloat16)
    grad_attn = project_back(grad_update, w_out).astype(jnp.bfloat16)
    grads_all = lax.all_gather(grad_attn, "grp", axis=1, tiled=True)
    grad_heads = grads_all.reshape(sample_count, token_total, head_count, head_size)
    grad_prob = jnp.einsum(
        "sihe,sjhe->shij", grad_heads, value_heads, preferred_element_type=jnp.float32
    )
    row_delta = lax.psum(
        jnp.sum(attn_prob * grad_prob, axis=-1).astype(jnp.bfloat16), "grp"
    ).astype(jnp.float32)
    grad_score = attn_prob * (grad_prob - row_delta[..., None])
    score_b = grad_score.astype(jnp.bfloat16)
    query_part = (
        jnp.einsum("shij,sjhe->sihe", score_b, key_heads, preferred_element_type=jnp.float32)
        * score_scale
    )
    query_part = query_part.reshape(sample_count, token_total, model_width)
    grad_query = lax.psum_scatter(
        query_part.astype(jnp.bfloat16), "grp", scatter_dimension=1, tiled=True
    )
    grad_key = (
        jnp.einsum("shij,sihe->sjhe", score_b, query_heads, preferred_element_type=jnp.float32)
        * score_scale
    )
    grad_value = jnp.einsum(
        "shij,sihe->sjhe", prob_b, grad_heads, preferred_element_type=jnp.float32
    )
    grad_key = grad_key.reshape(sample_count, col_count, model_width).astype(jnp.bfloat16)
    grad_value = grad_value.reshape(sample_count, col_count, model_width).astype(jnp.bfloat16)
    grad_input = (
        project_back(grad_query, w_query)
        + project_back(grad_key, w_key)
        + project_back(grad_value, w_value)
    )
    gamma_part = jnp.sum(grad_input * noised_norm, axis=0)
    beta_part = jnp.sum(grad_input, axis=0)
    gamma_sum, beta_sum, gate_sum = lax.psum((gamma_part, beta_part, gate_part), "rows")
    pre_gamma = (gamma_sum * cond_gamma * (1.0 - cond_gamma)).astype(jnp.bfloat16)
    pre_gate = (gate_sum * out_gate * (1.0 - out_gate)).astype(jnp.bfloat16)
    grad_snorm = jnp.dot(pre_gamma, w_gamma.T, preferred_element_type=jnp.float32)
    grad_snorm = grad_snorm + jnp.dot(
        beta_sum.astype(jnp.bfloat16), w_beta.T, preferred_element_type=jnp.float32
    )
    grad_snorm = grad_snorm + jnp.dot(pre_gate, w_outgate.T, preferred_element_type=jnp.float32)
    d_single = norm_back(grad_snorm, single_norm, single_inv)
    bias_part = jnp.sum(score_b, axis=0, dtype=jnp.float32)
    bias_own = lax.psum_scatter(bias_part, "rows", scatter_dimension=1, tiled=True)
    bias_grad = (bias_own * token_total).astype(jnp.bfloat16)
    grad_pairn = jnp.einsum("hij,ch->ijc", bias_grad, w_pair, preferred_element_type=jnp.float32)
    d_pair = norm_back(grad_pairn, pair_norm, pair_inv).astype(jnp.bfloat16)
    return (updated, d_single, d_pair)


def solution(mesh):
    in_specs = (
        P("grp", None),
        P("rows", "grp", None),
        P(),
        P("rows", "grp", None),
        P(),
        P(),
        P(),
        P(),
        P(),
        P(),
        P(),
        P(),
        P(),
        P("rows", "grp", None),
    )
    out_specs = (P("rows", "grp", None), P("grp", None), P("rows", "grp", None))
    groups = mesh.shape["grp"]
    row_total = mesh.shape["rows"]

    def on_device(*args):
        pair, noised, w_pair = args[1], args[3], args[11]
        fits = (
            groups == 4
            and pair.shape[0] % 32 == 0
            and pair.shape[1] % pair.shape[0] == 0
            and row_total == 8
            and noised.shape[0] == 1
            and noised.shape[1] == 192
            and w_pair.shape[1] % (2 * groups) == 0
        )
        if fits:
            return split_heads(*args, groups=groups, row_total=row_total)
        return split_keys(*args)

    return jax.shard_map(
        on_device, mesh=mesh, in_specs=in_specs, out_specs=out_specs, check_vma=False
    )
```

```python
import functools
import math

import jax
import jax.numpy as jnp
from jax import lax
from jax.experimental import pallas as pl
from jax.experimental.pallas import tpu as pltpu
from jax.sharding import PartitionSpec as P

EPSILON = 1e-05
BF16 = jnp.bfloat16
F32 = jnp.float32
LOG2_E = math.log2(math.e)
VMEM_LIMIT = 56 * 1024 * 1024


def norm_rows(values):
    center = values - jnp.mean(values, axis=-1, keepdims=True)
    inverse = lax.rsqrt(jnp.mean(center * center, axis=-1, keepdims=True) + EPSILON)
    return (center * inverse, inverse)


def norm_back(grad_in, normed, inverse):
    grad_mean = jnp.mean(grad_in, axis=-1, keepdims=True)
    cross_mean = jnp.mean(grad_in * normed, axis=-1, keepdims=True)
    return inverse * (grad_in - grad_mean - normed * cross_mean)


def mm(left, right):
    return lax.dot_general(left, right, (((1,), (0,)), ((), ())), preferred_element_type=F32)


def mm_nt(left, right):
    return lax.dot_general(left, right, (((1,), (1,)), ((), ())), preferred_element_type=F32)


def mm_tn(left, right):
    return lax.dot_general(left, right, (((0,), (0,)), ((), ())), preferred_element_type=F32)


def sigmoid(values):
    return 1.0 / (1.0 + jnp.exp(-values))


def params():
    return pltpu.CompilerParams(vmem_limit_bytes=VMEM_LIMIT)


def smem():
    return pl.BlockSpec(memory_space=pltpu.SMEM)


def vmem():
    return pl.BlockSpec(memory_space=pltpu.VMEM)


def project_kernel(
    group_ref,
    single_ref,
    noised_ref,
    cot_ref,
    w_gamma_ref,
    w_beta_ref,
    w_outgate_ref,
    w_query_ref,
    w_key_ref,
    w_value_ref,
    w_out_ref,
    *rest,
    groups,
    calls,
    head_size,
):
    send_refs = rest[:groups]
    gamma_ref, gate_ref, stage_ref = rest[groups:]
    width = stage_ref.shape[2]
    part = width // (4 * calls)
    group_own = group_ref[0]
    single_norm, _ = norm_rows(single_ref[...].astype(F32))
    single_b = single_norm.astype(BF16)
    cond_gamma = sigmoid(mm(single_b, w_gamma_ref[...]))
    gamma_ref[...] = cond_gamma
    out_gate = sigmoid(mm(single_b, w_outgate_ref[...]))
    gate_ref[...] = out_gate
    cond_beta = mm(single_b, w_beta_ref[...])
    noised_norm, _ = norm_rows(noised_ref[...].astype(F32))
    x_b = (noised_norm * cond_gamma + cond_beta).astype(BF16)

    def put(kind, values):
        rounded = values.astype(BF16)
        for group in range(groups):
            slot = group_own ^ group
            for call in range(calls):
                feature = (group * calls + call) * part
                lane = (call * 4 + kind) * part
                stage_ref[slot, :, lane : lane + part] = rounded[:, feature : feature + part]

    put(0, mm(x_b, w_query_ref[...]) * (LOG2_E / math.sqrt(head_size)))
    put(1, mm(x_b, w_key_ref[...]))
    put(2, mm(x_b, w_value_ref[...]))
    grad_update = (cot_ref[...].astype(F32) * out_gate).astype(BF16)
    put(3, mm_nt(grad_update, w_out_ref[...]))
    for slot in range(groups):
        send_refs[slot][...] = stage_ref[slot]


def lane_tiles(cols):
    return [(tile, tile * 128, min(cols, tile * 128 + 128)) for tile in range(-(-cols // 128))]


def mean_matrix(channels):
    first = lax.broadcasted_iota(jnp.int32, (2 * channels, 2 * channels), 0) >= channels
    second = lax.broadcasted_iota(jnp.int32, (2 * channels, 2 * channels), 1) >= channels
    return jnp.where(first == second, 1.0 / channels, 0.0).astype(BF16)


def center_rows(pair_ref, first, batch, means):
    _, _, cols, channels = pair_ref.shape
    both = jnp.concatenate(
        [pair_ref[side, first : first + batch].reshape(batch * cols, channels) for side in range(2)],
        axis=1,
    )
    return both.astype(F32) - mm(both, means)


def lane_pad(block, before, total):
    rows, width = block.shape
    pieces = [block]
    if before:
        pieces = [jnp.zeros((rows, before), block.dtype)] + pieces
    if total > before + width:
        pieces = pieces + [jnp.zeros((rows, total - before - width), block.dtype)]
    return jnp.concatenate(pieces, axis=1)


def bias_kernel(
    group_ref,
    rows_ref,
    chains_ref,
    gain_ref,
    pair_ref,
    w_pair_ref,
    cols_ref,
    *rest,
    groups,
    batch,
):
    send_refs = rest[:groups]
    stats_ref, flat_ref, gains_ref, stage_ref = rest[groups:]
    _, step, cols, channels = pair_ref.shape
    heads = gain_ref.shape[0]
    per_group = heads // groups
    half = step * pl.num_programs(0)
    group_own = group_ref[0]
    row_base = rows_ref[0] * 2 * half + pl.program_id(0) * step
    means = mean_matrix(channels)
    weight = w_pair_ref[...].astype(F32).T.astype(BF16)
    mean_part = jnp.full((channels, heads), 1.0 / channels, BF16)
    mixed = []
    for inner in range(2):
        for part, offset in ((weight, 0), (mean_part, heads)):
            for side in range(2):
                mixed.append(lane_pad(part, 2 * heads * (2 * inner + side) + offset, 8 * heads))
    mixed = jnp.concatenate(mixed, axis=0)
    chain_all = cols_ref[...].reshape(1, groups * cols)
    chain_cols = chain_all[:, :cols]
    for group in range(1, groups):
        here = chain_all[:, group * cols : (group + 1) * cols]
        chain_cols = jnp.where(group_own == group, here, chain_cols)
    for head in range(heads):
        gains_ref[head : head + 1, :] = jnp.full((1, cols), gain_ref[head] * LOG2_E, F32)

    for first in range(0, step, batch):
        center = center_rows(pair_ref, first, batch, means)
        center_b = center.astype(BF16)
        square = (center * center).astype(BF16)
        for base in range(0, batch, 2):
            one = slice(base * cols, (base + 1) * cols)
            two = slice((base + 1) * cols, (base + 2) * cols)
            left = jnp.concatenate(
                [center_b[one], square[one], center_b[two], square[two]], axis=1
            )
            sums = mm(left, mixed).T
            for inner in range(2):
                row = first + base + inner
                for side in range(2):
                    top = 2 * heads * (2 * inner + side)
                    inverse = lax.rsqrt(sums[top + heads : top + 2 * heads] + EPSILON)
                    projected = sums[top : top + heads] * inverse
                    stats_ref[side, row, :heads, :] = projected
                    stats_ref[side, row, heads:, :] = inverse[:8]
                    chain = chains_ref[row_base + side * half + row]
                    same = (chain_cols == chain).astype(F32)
                    values = projected * LOG2_E + gains_ref[...] * same
                    for tile, start, end in lane_tiles(cols):
                        piece = lane_pad(values[:, start:end], 0, 128)
                        flat_ref[side, tile, pl.ds(row, heads, stride=step), :] = piece
    for head in range(heads):
        slot = group_own ^ (head // per_group)
        tops = slice(head * step, (head + 1) * step)
        rest_lanes = [flat_ref[side, 1, tops, : cols - 128] for side in range(2)]
        stage_ref[slot, head % per_group, 0] = flat_ref[0, 0, tops, :].astype(BF16)
        stage_ref[slot, head % per_group, 1] = flat_ref[1, 0, tops, :].astype(BF16)
        stage_ref[slot, head % per_group, 2] = jnp.concatenate(rest_lanes, axis=1).astype(BF16)
    for slot in range(groups):
        send_refs[slot][...] = stage_ref[slot]


def pair_bias(pair, w_pair, chain_gain, chains, group_index, row_index, groups):
    rows, cols, channels = pair.shape
    heads = w_pair.shape[1]
    per_group = heads // groups
    half = rows // 2
    step = 16
    tiles = -(-cols // 128)
    *sends, stats = pl.pallas_call(
        functools.partial(bias_kernel, groups=groups, batch=4),
        grid=(half // step,),
        in_specs=[
            smem(),
            smem(),
            smem(),
            smem(),
            pl.BlockSpec((2, step, cols, channels), lambda t: (0, t, 0, 0)),
            pl.BlockSpec((heads, channels), lambda t: (0, 0)),
            pl.BlockSpec((groups * cols,), lambda t: (0,)),
        ],
        out_specs=[
            pl.BlockSpec((per_group, 3, step, 128), lambda t: (0, 0, t, 0)) for _ in range(groups)
        ]
        + [pl.BlockSpec((2, step, heads + 8, cols), lambda t: (0, t, 0, 0))],
        out_shape=[
            jax.ShapeDtypeStruct((per_group, 3, half, 128), BF16) for _ in range(groups)
        ]
        + [jax.ShapeDtypeStruct((2, half, heads + 8, cols), F32)],
        scratch_shapes=[
            pltpu.VMEM((2, tiles, heads * step, 128), F32),
            pltpu.VMEM((heads, cols), F32),
            pltpu.VMEM((groups, per_group, 3, step, 128), BF16),
        ],
        compiler_params=params(),
    )(
        group_index,
        row_index,
        chains,
        chain_gain,
        pair.reshape(2, half, cols, channels),
        w_pair.T,
        chains,
    )
    return sends, stats


def pair_back_kernel(
    group_ref, pair_ref, stats_ref, w_pair_ref, *rest, groups, calls, factor, batch
):
    grad_refs = rest[: groups * calls]
    out_ref, flat_ref = rest[groups * calls :]
    _, step, cols, channels = pair_ref.shape
    per_call = grad_refs[0].shape[0]
    heads = groups * calls * per_call
    group_own = group_ref[0]
    means = mean_matrix(channels)
    weight = w_pair_ref[...].astype(F32)
    weight = (weight - jnp.mean(weight, axis=-1, keepdims=True)).astype(BF16)
    spread = lax.broadcasted_iota(jnp.int32, (heads, channels), 0)
    spread = (spread < 2).astype(F32).astype(BF16)
    block = jnp.concatenate(
        [lane_pad(weight, 0, 2 * channels), lane_pad(spread, channels, 2 * channels)], axis=0
    )
    weights = jnp.concatenate(
        [lane_pad(block, 2 * channels * place, 8 * channels) for place in range(4)], axis=0
    )
    blank = jnp.zeros((heads - 2, cols), F32)
    for number in range(groups * calls):
        call, slot = divmod(number, groups)
        source = (group_own ^ slot) * calls + call
        for head in range(per_call):
            values = grad_refs[number][head].astype(F32)
            top = pl.multiple_of((source * per_call + head) * step, step)
            for side in range(2):
                flat_ref[side, 0, pl.ds(top, step), :] = values[side]
                flat_ref[side, 1, pl.ds(top, step), : cols - 128] = values[2][
                    :, side * (cols - 128) : (side + 1) * (cols - 128)
                ]

    for first in range(0, step, batch):
        center = center_rows(pair_ref, first, batch, means)
        for base in range(0, batch, 2):
            places = [(base + inner, side) for inner in range(2) for side in range(2)]
            left = []
            for inner, side in places:
                grads = jnp.concatenate(
                    [
                        flat_ref[side, tile, pl.ds(first + inner, heads, stride=step), :][
                            :, : end - start
                        ]
                        for tile, start, end in lane_tiles(cols)
                    ],
                    axis=1,
                )
                projected = stats_ref[side, first + inner, :heads, :]
                inverse = stats_ref[side, first + inner, heads : heads + 1, :]
                cross = jnp.sum(grads * projected, axis=0, keepdims=True) * (1.0 / channels)
                scaled = grads * (inverse * factor)
                cross = cross * (inverse * inverse * factor)
                cross_high = cross.astype(BF16).astype(F32)
                left += [scaled, cross_high, cross - cross_high, blank]
            both = mm_tn(jnp.concatenate(left, axis=0).astype(BF16), weights)
            for place, (inner, side) in enumerate(places):
                rows = slice(inner * cols, (inner + 1) * cols)
                lanes = slice(side * channels, (side + 1) * channels)
                start = 2 * channels * place
                middle, end = start + channels, start + 2 * channels
                out_ref[side, first + inner] = (
                    both[:, start:middle] - center[rows, lanes] * both[:, middle:end]
                ).astype(BF16)


def pair_back(pair, stats, grads, w_pair, group_index, groups, factor):
    rows, cols, channels = pair.shape
    per_call = grads[0].shape[0]
    heads = len(grads) * per_call
    half = rows // 2
    step = 16
    tiles = -(-cols // 128)
    out = pl.pallas_call(
        functools.partial(
            pair_back_kernel, groups=groups, calls=len(grads) // groups, factor=factor, batch=4
        ),
        grid=(half // step,),
        in_specs=[
            smem(),
            pl.BlockSpec((2, step, cols, channels), lambda t: (0, t, 0, 0)),
            pl.BlockSpec((2, step, heads + 8, cols), lambda t: (0, t, 0, 0)),
            pl.BlockSpec((heads, channels), lambda t: (0, 0)),
        ]
        + [pl.BlockSpec((per_call, 3, step, 128), lambda t: (0, 0, t, 0)) for _ in grads],
        out_specs=pl.BlockSpec((2, step, cols, channels), lambda t: (0, t, 0, 0)),
        out_shape=jax.ShapeDtypeStruct((2, half, cols, channels), BF16),
        scratch_shapes=[pltpu.VMEM((2, tiles, heads * step, 128), F32)],
        compiler_params=params(),
    )(group_index, pair.reshape(2, half, cols, channels), stats, w_pair.T, *grads)
    return out.reshape(rows, cols, channels)


def unit_order(heads):
    first, second = range(heads // 2), range(heads // 2, heads)
    order = [(1, head) for head in first] + [(3, head) for head in first]
    order += [(2, head) for head in second] + [(3, head) for head in second]
    order += [(0, head) for head in range(heads)]
    order += [(2, head) for head in first] + [(1, head) for head in second]
    return order


def attention_kernel(group_ref, row_ref, *rest, groups, row_parts, head_size, row_block):
    bias_refs = rest[: row_parts + 2]
    acts_refs = rest[row_parts + 2 : row_parts + 2 + groups]
    rest = rest[row_parts + 2 + groups :]
    out_refs = rest[:groups]
    (
        keep_ref,
        give_ref,
        query_ref,
        keys_ref,
        values_ref,
        grads_ref,
        query_t_ref,
        keys_t_ref,
        values_t_ref,
        bias_full,
        score_full,
        att_sum,
        gq_sum,
        gk_sum,
        gv_sum,
    ) = rest[groups:]
    head = pl.program_id(0)
    heads = keep_ref.shape[1] * 2 // row_parts
    group_own = group_ref[0]
    cols, width = acts_refs[0].shape
    tokens = groups * cols
    part = width // 4
    half = bias_refs[0].shape[3]
    rest_lanes = cols - 128
    scale = 1.0 / math.sqrt(head_size)
    extra = att_sum.shape[1] - part
    plain = (query_ref, keys_ref, values_ref, grads_ref)
    turned = (query_t_ref, keys_t_ref, values_t_ref)

    turns = [(slot * cols, slot * 128, 128) for slot in range(groups)]
    turns += [
        (slot * cols + 128, groups * 128 + slot * rest_lanes, rest_lanes) for slot in range(groups)
    ]

    @pl.when(head == 0)
    def _():
        for kind in range(4):
            lanes = slice(kind * part, (kind + 1) * part)
            if kind in (0, 3):
                for slot in range(groups):
                    plain[kind][slot * cols : (slot + 1) * cols, :] = acts_refs[slot][:, lanes]
            else:
                for token, place, count in turns:
                    slot, inside = divmod(token, cols)
                    plain[kind][place : place + count, :] = acts_refs[slot][
                        inside : inside + count, lanes
                    ]
            if kind < len(turned):
                turned[kind][...] = plain[kind][...].T
        att_sum[...] = jnp.zeros_like(att_sum)
        gq_sum[...] = jnp.zeros_like(gq_sum)
        gv_sum[...] = jnp.zeros_like(gv_sum)

    def places(row_part):
        first = row_part * (2 * half)
        slot = group_own ^ (first // cols)
        for side in range(2):
            top = slot * cols + lax.rem(first, cols) + side * half
            yield side, pl.ds(pl.multiple_of(top, 16), half)

    for other in range(row_parts):

        def block(column, which, other=other):
            if other >= row_parts - 2 and column >= groups // 2:
                return bias_refs[other + 2][column - groups // 2, 0, which]
            return bias_refs[other][column, 0, which]

        for side, rows in places(row_ref[0] ^ other):
            lanes = slice(side * rest_lanes, (side + 1) * rest_lanes)
            tiles = [block(column, side) for column in range(groups)]
            tiles += [block(column, 2)[:, lanes] for column in range(groups)]
            bias_full[rows, :] = jnp.concatenate(tiles, axis=1)

    lane = lax.broadcasted_iota(jnp.int32, (1, part), 1)
    mine = (lane >= head * head_size) & (lane < (head + 1) * head_size)
    zero = jnp.zeros((), BF16)
    keys_m = jnp.where(mine, keys_ref[...], zero)
    values_m = jnp.concatenate(
        [jnp.where(mine, values_ref[...], zero), jnp.ones((tokens, extra), BF16)], axis=1
    )
    feature = pl.multiple_of(head * head_size, head_size)
    query_t = query_t_ref[pl.ds(feature, head_size), :]
    gk_t = jnp.zeros((head_size, tokens), F32)
    gv_t = jnp.zeros((part, tokens), F32)
    for top in range(0, tokens, row_block):
        rows = slice(top, top + row_block)
        query = jnp.where(mine, query_ref[rows, :], zero)
        grads = jnp.where(mine, grads_ref[rows, :], zero)
        weights = jnp.exp2(mm(query, keys_t_ref[...]) + bias_full[rows, :].astype(F32))
        weights_b = weights.astype(BF16)
        attended = mm(weights_b, values_m)
        inverse = 1.0 / attended[:, part : part + 1]
        attended = attended[:, :part] * inverse
        att_sum[rows, :part] += attended
        grads = (grads.astype(F32) * inverse).astype(BF16)
        delta = jnp.sum(attended * grads.astype(F32), axis=-1, keepdims=True)
        score = (weights * (mm(grads, values_t_ref[...]) - delta)).astype(BF16)
        score_full[rows, :] = score
        gq_sum[rows, :] += mm(score, keys_m)
        gk_t = gk_t + mm(query_t[:, rows], score)
        gv_t = gv_t + mm_tn(grads, weights_b)
    gk_sum[pl.ds(feature, head_size), :] = gk_t
    gv_sum[...] += gv_t

    order = unit_order(heads)

    def give_back(some_heads):
        for other in range(row_parts):
            unit = order.index((other // 2, some_heads[0]))
            dbias_ref = give_ref if other % 2 else keep_ref
            unit = unit + head - some_heads[0]
            scores = [score_full[rows, :] for _, rows in places(row_ref[0] ^ other)]
            blocks = []
            for column in range(groups):
                start = groups * 128 + column * rest_lanes
                blocks += [score[:, column * 128 : (column + 1) * 128] for score in scores]
                blocks.append(
                    jnp.concatenate(
                        [score[:, start : start + rest_lanes] for score in scores], axis=1
                    )
                )
            for column in range(groups):
                dbias_ref[column, unit] = jnp.stack(blocks[3 * column : 3 * column + 3])

    @pl.when(head < heads // 2)
    def _():
        give_back(range(heads // 2))

    @pl.when(head >= heads // 2)
    def _():
        give_back(range(heads // 2, heads))

    @pl.when(head == heads - 1)
    def _():
        results = (
            gq_sum[...] * scale,
            (gk_sum[...] * math.log(2.0)).T,
            gv_sum[...].T,
            att_sum[:, :part],
        )
        for kind, values in enumerate(results):
            rounded = values.astype(BF16)
            lanes = slice(kind * part, (kind + 1) * part)
            if kind in (0, 3):
                for slot in range(groups):
                    out_refs[slot][:, lanes] = rounded[slot * cols : (slot + 1) * cols]
            else:
                for token, place, count in turns:
                    slot, inside = divmod(token, cols)
                    out_refs[slot][inside : inside + count, lanes] = rounded[place : place + count]


def attention(group_index, row_index, acts, bias, head_size):
    groups = len(acts)
    row_parts = len(bias) - 2
    cols, width = acts[0].shape
    tokens = groups * cols
    part = width // 4
    _, heads, _, half, lanes = bias[0].shape
    row_block = tokens
    padded = (part // 128 + 1) * 128
    units = (groups, row_parts // 2 * heads, 3, half, lanes)
    *grads, keep, give = pl.pallas_call(
        functools.partial(
            attention_kernel,
            groups=groups,
            row_parts=row_parts,
            head_size=head_size,
            row_block=row_block,
        ),
        grid=(heads,),
        in_specs=[smem(), smem()]
        + [
            pl.BlockSpec((block.shape[0], 1, 3, half, lanes), lambda h: (0, h, 0, 0, 0))
            for block in bias
        ]
        + [pl.BlockSpec((cols, width), lambda h: (0, 0))] * groups,
        out_specs=[pl.BlockSpec((cols, width), lambda h: (0, 0))] * groups
        + [pl.BlockSpec(shape, lambda h: (0, 0, 0, 0, 0)) for shape in (units, units)],
        out_shape=[jax.ShapeDtypeStruct((cols, width), BF16)] * groups
        + [jax.ShapeDtypeStruct(shape, BF16) for shape in (units, units)],
        scratch_shapes=[pltpu.VMEM((tokens, part), BF16) for _ in range(4)]
        + [pltpu.VMEM((part, tokens), BF16) for _ in range(3)]
        + [
            pltpu.VMEM((tokens, tokens), BF16),
            pltpu.VMEM((tokens, tokens), BF16),
            pltpu.VMEM((tokens, padded), F32),
            pltpu.VMEM((tokens, part), F32),
            pltpu.VMEM((part, tokens), F32),
            pltpu.VMEM((part, tokens), F32),
        ],
        compiler_params=params(),
    )(group_index, row_index, *bias, *acts)
    return grads, keep, give


def finish_kernel(
    group_ref,
    single_ref,
    noised_ref,
    cot_ref,
    gamma_ref,
    gate_ref,
    w_gamma_ref,
    w_beta_ref,
    w_outgate_ref,
    w_query_ref,
    w_key_ref,
    w_value_ref,
    w_out_ref,
    *rest,
    groups,
    calls,
):
    got_refs = rest[: groups * calls]
    updated_ref, d_single_ref, stage_ref = rest[groups * calls :]
    width = stage_ref.shape[3]
    part = width // 4
    for slot in range(groups):
        for call in range(calls):
            stage_ref[group_ref[0] ^ slot, call] = got_refs[
                call * groups + slot
            ][...]

    def take(kind):
        return jnp.concatenate(
            [
                stage_ref[group, call, :, kind * part : (kind + 1) * part]
                for group in range(groups)
                for call in range(calls)
            ],
            axis=1,
        )

    out_gate = gate_ref[...]
    cond_gamma = gamma_ref[...]
    block_update = mm(take(3), w_out_ref[...])
    noised = noised_ref[...].astype(F32)
    updated_ref[...] = (noised + out_gate * block_update).astype(BF16)
    gate_part = cot_ref[...].astype(F32) * block_update
    pre_gate = (gate_part * out_gate * (1.0 - out_gate)).astype(BF16)
    grad_input = mm_nt(take(0), w_query_ref[...])
    grad_input += mm_nt(take(1), w_key_ref[...])
    grad_input += mm_nt(take(2), w_value_ref[...])
    noised_norm, _ = norm_rows(noised)
    pre_gamma = (grad_input * noised_norm * cond_gamma * (1.0 - cond_gamma)).astype(BF16)
    grad_snorm = mm_nt(pre_gamma, w_gamma_ref[...])
    grad_snorm += mm_nt(grad_input.astype(BF16), w_beta_ref[...])
    grad_snorm += mm_nt(pre_gate, w_outgate_ref[...])
    single_norm, single_inv = norm_rows(single_ref[...].astype(F32))
    d_single_ref[...] = norm_back(grad_snorm, single_norm, single_inv).astype(BF16)


def swap_groups(sends):
    groups = len(sends)
    order = (*range(2, groups), 1)
    got = []
    for bits in order:
        perm = [(index, index ^ bits) for index in range(groups)]
        got.append(lax.ppermute(sends[bits], "grp", perm))
    got = dict(zip(order, lax.optimization_barrier(got)))
    return [sends[0]] + [got[bits] for bits in range(1, groups)]


def flip_rows(values, bits, row_total):
    return lax.ppermute(values, "rows", [(index, index ^ bits) for index in range(row_total)])


def gather_rows(own, acts, row_total):
    half = own.shape[0] // 2
    near = flip_rows(own, 2, row_total)
    far = flip_rows(own, 4, row_total)
    first = flip_rows(near[:half], 4, row_total)
    second = flip_rows(far[half:], 2, row_total)
    acts[2], acts[3], acts[1], first, second = lax.optimization_barrier(
        (acts[2], acts[3], acts[1], first, second)
    )
    blocks = []
    for block in (own, near, far, first, second):
        blocks += [block, flip_rows(block, 1, row_total)]
    return blocks, acts


def scatter_rows(keep, give, row_total):
    got = flip_rows(give, 1, row_total)
    early = keep.shape[1] // 2
    heads = early // 2
    part = heads // 2

    def add(first, count, *others):
        total = keep[:, first : first + count].astype(F32)
        total += got[:, first : first + count].astype(F32)
        for other in others:
            total += other.astype(F32)
        return total.astype(BF16)

    near = flip_rows(add(0, heads), 2, row_total)
    far = flip_rows(add(heads, heads), 4, row_total)
    far_two = flip_rows(add(early + heads, part, near[:, part:]), 4, row_total)
    near_two = flip_rows(add(early + heads + part, part, far[:, part:]), 2, row_total)
    own = add(early, heads, jnp.concatenate([near[:, :part], far[:, :part]], axis=1))
    return own, far_two, near_two


def add_last(own, far_two, near_two):
    last = jnp.concatenate([far_two, near_two], axis=1)
    total = (own.astype(F32) + last.astype(F32)).astype(BF16)
    return [total[slot] for slot in range(total.shape[0])]


def sum_cores(mine, row_total):
    return (mine.astype(F32) + flip_rows(mine, 1, row_total).astype(F32)).astype(BF16)


def sum_chips(both, row_total):
    near, far, last = (flip_rows(both, bits, row_total).astype(F32) for bits in (2, 4, 6))
    return (both.astype(F32) + near) + (far + last)


def split_heads(
    single,
    pair,
    chains,
    noised,
    w_gamma,
    w_beta,
    w_outgate,
    w_query,
    w_key,
    w_value,
    w_out,
    w_pair,
    chain_gain,
    cotangent,
    *,
    groups,
    row_total,
):
    cols, _ = single.shape
    tokens = chains.shape[0]
    width = noised.shape[2]
    head_size = width // w_pair.shape[1]
    calls = 1
    row_index = lax.axis_index("rows").reshape(1)
    group_index = lax.axis_index("grp").reshape(1)
    bias_send, stats = pair_bias(
        pair, w_pair, chain_gain, chains, group_index, row_index, groups
    )
    bias_got = swap_groups(bias_send)
    noised = noised[0]
    cotangent = cotangent[0]
    *acts_send, cond_gamma, out_gate = pl.pallas_call(
        functools.partial(
            project_kernel, groups=groups, calls=calls, head_size=head_size
        ),
        in_specs=[smem()] + [vmem()] * 10,
        out_shape=[
            jax.ShapeDtypeStruct((cols, 4 * width // groups), BF16) for _ in range(groups)
        ]
        + [
            jax.ShapeDtypeStruct((cols, width), F32),
            jax.ShapeDtypeStruct((cols, width), F32),
        ],
        scratch_shapes=[pltpu.VMEM((groups, cols, 4 * width // groups), BF16)],
        compiler_params=params(),
    )(
        group_index,
        single,
        noised,
        cotangent,
        w_gamma,
        w_beta,
        w_outgate,
        w_query,
        w_key,
        w_value,
        w_out,
    )
    bias_got, _ = lax.optimization_barrier((bias_got, acts_send))
    acts = swap_groups(acts_send)
    bias_all, acts = gather_rows(jnp.stack(bias_got), acts, row_total)
    grads_send, keep, give = attention(group_index, row_index, acts, bias_all, head_size)
    grads = swap_groups(grads_send)
    own, far_two, near_two = scatter_rows(keep, give, row_total)
    far_two, near_two, grads = lax.optimization_barrier((far_two, near_two, grads))
    dbias_own, grads = lax.optimization_barrier((add_last(own, far_two, near_two), grads))
    dbias_back = swap_groups(dbias_own)
    updated, d_part = pl.pallas_call(
        functools.partial(finish_kernel, groups=groups, calls=calls),
        in_specs=[smem()] + [vmem()] * (12 + groups * calls),
        out_shape=[
            jax.ShapeDtypeStruct((cols, width), BF16),
            jax.ShapeDtypeStruct(single.shape, BF16),
        ],
        scratch_shapes=[pltpu.VMEM((groups, calls, cols, 4 * width // (groups * calls)), BF16)],
        compiler_params=params(),
    )(
        group_index,
        single,
        noised,
        cotangent,
        cond_gamma,
        out_gate,
        w_gamma,
        w_beta,
        w_outgate,
        w_query,
        w_key,
        w_value,
        w_out,
        *grads,
    )
    d_part, dbias_back = lax.optimization_barrier((d_part, dbias_back))
    d_both = sum_cores(d_part, row_total)
    d_single = sum_chips(d_both, row_total)
    d_pair = pair_back(pair, stats, dbias_back, w_pair, group_index, groups, float(tokens))
    return (updated[None], d_single, d_pair)


def project(acts, weight):
    return jnp.einsum("std,de->ste", acts, weight, preferred_element_type=F32)


def project_back(acts, weight):
    return jnp.einsum("ste,de->std", acts, weight, preferred_element_type=F32)


def split_keys(
    single,
    pair,
    chains,
    noised,
    w_gamma,
    w_beta,
    w_outgate,
    w_query,
    w_key,
    w_value,
    w_out,
    w_pair,
    chain_gain,
    cotangent,
):
    col_count = single.shape[0]
    row_count = pair.shape[0]
    head_count = w_pair.shape[1]
    model_width = w_query.shape[0]
    head_size = model_width // head_count
    sample_count = noised.shape[0]
    token_total = chains.shape[0]
    score_scale = 1.0 / math.sqrt(head_size)
    row_index = lax.axis_index("rows")
    group_index = lax.axis_index("grp")
    chain_rows = lax.dynamic_slice_in_dim(chains, row_index * row_count, row_count)
    chain_cols = lax.dynamic_slice_in_dim(chains, group_index * col_count, col_count)
    pair_norm, pair_inv = norm_rows(pair.astype(jnp.float32))
    projected = jnp.einsum(
        "ijc,ch->hij", pair_norm.astype(jnp.bfloat16), w_pair, preferred_element_type=jnp.float32
    )
    same_chain = (chain_rows[:, None] == chain_cols[None, :]).astype(jnp.float32)
    bias_block = (projected + chain_gain[:, None, None] * same_chain[None]).astype(jnp.bfloat16)
    bias_keys = lax.all_gather(bias_block, "rows", axis=1, tiled=True)
    single_norm, single_inv = norm_rows(single.astype(jnp.float32))
    single_b = single_norm.astype(jnp.bfloat16)
    cond_gamma = jax.nn.sigmoid(jnp.dot(single_b, w_gamma, preferred_element_type=jnp.float32))
    cond_beta = jnp.dot(single_b, w_beta, preferred_element_type=jnp.float32)
    out_gate = jax.nn.sigmoid(jnp.dot(single_b, w_outgate, preferred_element_type=jnp.float32))
    noised_f = noised.astype(jnp.float32)
    noised_norm, noised_inv = norm_rows(noised_f)
    x_b = (noised_norm * cond_gamma[None] + cond_beta[None]).astype(jnp.bfloat16)
    queries = project(x_b, w_query).astype(jnp.bfloat16)
    keys_own = project(x_b, w_key).astype(jnp.bfloat16)
    values_own = project(x_b, w_value).astype(jnp.bfloat16)
    queries_all = lax.all_gather(queries, "grp", axis=1, tiled=True)
    query_heads = queries_all.reshape(sample_count, token_total, head_count, head_size)
    key_heads = keys_own.reshape(sample_count, col_count, head_count, head_size)
    value_heads = values_own.reshape(sample_count, col_count, head_count, head_size)
    scores = (
        jnp.einsum("sihe,sjhe->shij", query_heads, key_heads, preferred_element_type=jnp.float32)
        * score_scale
        + bias_keys.astype(jnp.float32)[None]
    )
    exp_scores = jnp.exp(scores)
    exp_total = lax.psum(jnp.sum(exp_scores, axis=-1).astype(jnp.bfloat16), "grp").astype(
        jnp.float32
    )
    attn_prob = exp_scores / exp_total[..., None]
    prob_b = attn_prob.astype(jnp.bfloat16)
    attended_part = jnp.einsum(
        "shij,sjhe->sihe", prob_b, value_heads, preferred_element_type=jnp.float32
    )
    attended_part = attended_part.reshape(sample_count, token_total, model_width)
    attended = lax.psum_scatter(
        attended_part.astype(jnp.bfloat16), "grp", scatter_dimension=1, tiled=True
    )
    block_update = project(attended, w_out)
    updated = (noised_f + out_gate[None] * block_update).astype(jnp.bfloat16)
    grad_out = cotangent.astype(jnp.float32)
    gate_part = jnp.sum(grad_out * block_update, axis=0)
    grad_update = (grad_out * out_gate[None]).astype(jnp.bfloat16)
    grad_attn = project_back(grad_update, w_out).astype(jnp.bfloat16)
    grads_all = lax.all_gather(grad_attn, "grp", axis=1, tiled=True)
    grad_heads = grads_all.reshape(sample_count, token_total, head_count, head_size)
    grad_prob = jnp.einsum(
        "sihe,sjhe->shij", grad_heads, value_heads, preferred_element_type=jnp.float32
    )
    row_delta = lax.psum(
        jnp.sum(attn_prob * grad_prob, axis=-1).astype(jnp.bfloat16), "grp"
    ).astype(jnp.float32)
    grad_score = attn_prob * (grad_prob - row_delta[..., None])
    score_b = grad_score.astype(jnp.bfloat16)
    query_part = (
        jnp.einsum("shij,sjhe->sihe", score_b, key_heads, preferred_element_type=jnp.float32)
        * score_scale
    )
    query_part = query_part.reshape(sample_count, token_total, model_width)
    grad_query = lax.psum_scatter(
        query_part.astype(jnp.bfloat16), "grp", scatter_dimension=1, tiled=True
    )
    grad_key = (
        jnp.einsum("shij,sihe->sjhe", score_b, query_heads, preferred_element_type=jnp.float32)
        * score_scale
    )
    grad_value = jnp.einsum(
        "shij,sihe->sjhe", prob_b, grad_heads, preferred_element_type=jnp.float32
    )
    grad_key = grad_key.reshape(sample_count, col_count, model_width).astype(jnp.bfloat16)
    grad_value = grad_value.reshape(sample_count, col_count, model_width).astype(jnp.bfloat16)
    grad_input = (
        project_back(grad_query, w_query)
        + project_back(grad_key, w_key)
        + project_back(grad_value, w_value)
    )
    gamma_part = jnp.sum(grad_input * noised_norm, axis=0)
    beta_part = jnp.sum(grad_input, axis=0)
    gamma_sum, beta_sum, gate_sum = lax.psum((gamma_part, beta_part, gate_part), "rows")
    pre_gamma = (gamma_sum * cond_gamma * (1.0 - cond_gamma)).astype(jnp.bfloat16)
    pre_gate = (gate_sum * out_gate * (1.0 - out_gate)).astype(jnp.bfloat16)
    grad_snorm = jnp.dot(pre_gamma, w_gamma.T, preferred_element_type=jnp.float32)
    grad_snorm = grad_snorm + jnp.dot(
        beta_sum.astype(jnp.bfloat16), w_beta.T, preferred_element_type=jnp.float32
    )
    grad_snorm = grad_snorm + jnp.dot(pre_gate, w_outgate.T, preferred_element_type=jnp.float32)
    d_single = norm_back(grad_snorm, single_norm, single_inv)
    bias_part = jnp.sum(score_b, axis=0, dtype=jnp.float32)
    bias_own = lax.psum_scatter(bias_part, "rows", scatter_dimension=1, tiled=True)
    bias_grad = (bias_own * token_total).astype(jnp.bfloat16)
    grad_pairn = jnp.einsum("hij,ch->ijc", bias_grad, w_pair, preferred_element_type=jnp.float32)
    d_pair = norm_back(grad_pairn, pair_norm, pair_inv).astype(jnp.bfloat16)
    return (updated, d_single, d_pair)


def solution(mesh):
    in_specs = (
        P("grp", None),
        P("rows", "grp", None),
        P(),
        P("rows", "grp", None),
        P(),
        P(),
        P(),
        P(),
        P(),
        P(),
        P(),
        P(),
        P(),
        P("rows", "grp", None),
    )
    out_specs = (P("rows", "grp", None), P("grp", None), P("rows", "grp", None))
    groups = mesh.shape["grp"]
    row_total = mesh.shape["rows"]

    def on_device(*args):
        pair, noised, w_pair = args[1], args[3], args[11]
        fits = (
            groups == 4
            and pair.shape[0] % 32 == 0
            and pair.shape[1] % pair.shape[0] == 0
            and row_total == 8
            and noised.shape[0] == 1
            and noised.shape[1] == 192
            and w_pair.shape[1] % (2 * groups) == 0
        )
        if fits:
            return split_heads(*args, groups=groups, row_total=row_total)
        return split_keys(*args)

    return jax.shard_map(
        on_device, mesh=mesh, in_specs=in_specs, out_specs=out_specs, check_vma=False
    )
```

```python
import functools
import math

import jax
import jax.numpy as jnp
from jax import lax
from jax.experimental import pallas as pl
from jax.experimental.pallas import tpu as pltpu
from jax.sharding import PartitionSpec as P

EPSILON = 1e-05
BF16 = jnp.bfloat16
F32 = jnp.float32
LOG2_E = math.log2(math.e)
SLOT_ORDER = (0, 2, 3, 1)
VMEM_LIMIT = 56 * 1024 * 1024


def norm_rows(values):
    center = values - jnp.mean(values, axis=-1, keepdims=True)
    inverse = lax.rsqrt(jnp.mean(center * center, axis=-1, keepdims=True) + EPSILON)
    return (center * inverse, inverse)


def norm_back(grad_in, normed, inverse):
    grad_mean = jnp.mean(grad_in, axis=-1, keepdims=True)
    cross_mean = jnp.mean(grad_in * normed, axis=-1, keepdims=True)
    return inverse * (grad_in - grad_mean - normed * cross_mean)


def mm(left, right):
    return lax.dot_general(left, right, (((1,), (0,)), ((), ())), preferred_element_type=F32)


def mm_nt(left, right):
    return lax.dot_general(left, right, (((1,), (1,)), ((), ())), preferred_element_type=F32)


def mm_tn(left, right):
    return lax.dot_general(left, right, (((0,), (0,)), ((), ())), preferred_element_type=F32)


def sigmoid(values):
    return 1.0 / (1.0 + jnp.exp(-values))


def params():
    return pltpu.CompilerParams(vmem_limit_bytes=VMEM_LIMIT)


def smem():
    return pl.BlockSpec(memory_space=pltpu.SMEM)


def vmem():
    return pl.BlockSpec(memory_space=pltpu.VMEM)


def project_kernel(
    group_ref,
    single_ref,
    noised_ref,
    cot_ref,
    w_gamma_ref,
    w_beta_ref,
    w_outgate_ref,
    w_query_ref,
    w_key_ref,
    w_value_ref,
    w_out_ref,
    *rest,
    groups,
    calls,
    head_size,
):
    send_refs = rest[:groups]
    gamma_ref, gate_ref, stage_ref = rest[groups:]
    width = stage_ref.shape[2]
    part = width // (4 * calls)
    group_own = group_ref[0]
    single_norm, _ = norm_rows(single_ref[...].astype(F32))
    single_b = single_norm.astype(BF16)
    cond_gamma = sigmoid(mm(single_b, w_gamma_ref[...]))
    gamma_ref[...] = cond_gamma
    out_gate = sigmoid(mm(single_b, w_outgate_ref[...]))
    gate_ref[...] = out_gate
    cond_beta = mm(single_b, w_beta_ref[...])
    noised_norm, _ = norm_rows(noised_ref[...].astype(F32))
    x_b = (noised_norm * cond_gamma + cond_beta).astype(BF16)

    def put(kind, values):
        rounded = values.astype(BF16)
        for group in range(groups):
            slot = group_own ^ group
            for call in range(calls):
                feature = (group * calls + call) * part
                lane = (call * 4 + kind) * part
                stage_ref[slot, :, lane : lane + part] = rounded[:, feature : feature + part]

    put(0, mm(x_b, w_query_ref[...]) * (LOG2_E / math.sqrt(head_size)))
    put(1, mm(x_b, w_key_ref[...]))
    put(2, mm(x_b, w_value_ref[...]))
    grad_update = (cot_ref[...].astype(F32) * out_gate).astype(BF16)
    put(3, mm_nt(grad_update, w_out_ref[...]))
    for slot in range(groups):
        send_refs[SLOT_ORDER.index(slot)][...] = stage_ref[slot]


def lane_tiles(cols):
    return [(tile, tile * 128, min(cols, tile * 128 + 128)) for tile in range(-(-cols // 128))]


def mean_matrix(channels):
    first = lax.broadcasted_iota(jnp.int32, (2 * channels, 2 * channels), 0) >= channels
    second = lax.broadcasted_iota(jnp.int32, (2 * channels, 2 * channels), 1) >= channels
    return jnp.where(first == second, 1.0 / channels, 0.0).astype(BF16)


def center_rows(pair_ref, first, batch, means):
    _, _, cols, channels = pair_ref.shape
    both = jnp.concatenate(
        [pair_ref[side, first : first + batch].reshape(batch * cols, channels) for side in range(2)],
        axis=1,
    )
    return both.astype(F32) - mm(both, means)


def lane_pad(block, before, total):
    rows, width = block.shape
    pieces = [block]
    if before:
        pieces = [jnp.zeros((rows, before), block.dtype)] + pieces
    if total > before + width:
        pieces = pieces + [jnp.zeros((rows, total - before - width), block.dtype)]
    return jnp.concatenate(pieces, axis=1)


def bias_kernel(
    group_ref,
    rows_ref,
    chains_ref,
    gain_ref,
    pair_ref,
    w_pair_ref,
    cols_ref,
    *rest,
    groups,
    batch,
):
    send_refs = rest[:groups]
    stats_ref, flat_ref, gains_ref, stage_ref = rest[groups:]
    _, step, cols, channels = pair_ref.shape
    heads = gain_ref.shape[0]
    per_group = heads // groups
    half = step * pl.num_programs(0)
    group_own = group_ref[0]
    row_base = rows_ref[0] * 2 * half + pl.program_id(0) * step
    means = mean_matrix(channels)
    weight = w_pair_ref[...].astype(F32).T.astype(BF16)
    mean_part = jnp.full((channels, heads), 1.0 / channels, BF16)
    mixed = []
    for inner in range(2):
        for part, offset in ((weight, 0), (mean_part, heads)):
            for side in range(2):
                mixed.append(lane_pad(part, 2 * heads * (2 * inner + side) + offset, 8 * heads))
    mixed = jnp.concatenate(mixed, axis=0)
    chain_all = cols_ref[...].reshape(1, groups * cols)
    chain_cols = chain_all[:, :cols]
    for group in range(1, groups):
        here = chain_all[:, group * cols : (group + 1) * cols]
        chain_cols = jnp.where(group_own == group, here, chain_cols)
    for head in range(heads):
        gains_ref[head : head + 1, :] = jnp.full((1, cols), gain_ref[head] * LOG2_E, F32)

    for first in range(0, step, batch):
        center = center_rows(pair_ref, first, batch, means)
        center_b = center.astype(BF16)
        square = (center * center).astype(BF16)
        for base in range(0, batch, 2):
            one = slice(base * cols, (base + 1) * cols)
            two = slice((base + 1) * cols, (base + 2) * cols)
            left = jnp.concatenate(
                [center_b[one], square[one], center_b[two], square[two]], axis=1
            )
            sums = mm(left, mixed).T
            for inner in range(2):
                row = first + base + inner
                for side in range(2):
                    top = 2 * heads * (2 * inner + side)
                    inverse = lax.rsqrt(sums[top + heads : top + 2 * heads] + EPSILON)
                    projected = sums[top : top + heads] * inverse
                    stats_ref[side, row, :heads, :] = projected
                    stats_ref[side, row, heads:, :] = inverse[:8]
                    chain = chains_ref[row_base + side * half + row]
                    same = (chain_cols == chain).astype(F32)
                    values = projected * LOG2_E + gains_ref[...] * same
                    for tile, start, end in lane_tiles(cols):
                        piece = lane_pad(values[:, start:end], 0, 128)
                        flat_ref[side, tile, pl.ds(row, heads, stride=step), :] = piece
    for head in range(heads):
        slot = group_own ^ (head // per_group)
        tops = slice(head * step, (head + 1) * step)
        rest_lanes = [flat_ref[side, 1, tops, : cols - 128] for side in range(2)]
        stage_ref[slot, head % per_group, 0] = flat_ref[0, 0, tops, :].astype(BF16)
        stage_ref[slot, head % per_group, 1] = flat_ref[1, 0, tops, :].astype(BF16)
        stage_ref[slot, head % per_group, 2] = jnp.concatenate(rest_lanes, axis=1).astype(BF16)
    for slot in range(groups):
        send_refs[slot][...] = stage_ref[slot]


def pair_bias(pair, w_pair, chain_gain, chains, group_index, row_index, groups):
    rows, cols, channels = pair.shape
    heads = w_pair.shape[1]
    per_group = heads // groups
    half = rows // 2
    step = 16
    tiles = -(-cols // 128)
    *sends, stats = pl.pallas_call(
        functools.partial(bias_kernel, groups=groups, batch=2),
        grid=(half // step,),
        in_specs=[
            smem(),
            smem(),
            smem(),
            smem(),
            pl.BlockSpec((2, step, cols, channels), lambda t: (0, t, 0, 0)),
            pl.BlockSpec((heads, channels), lambda t: (0, 0)),
            pl.BlockSpec((groups * cols,), lambda t: (0,)),
        ],
        out_specs=[
            pl.BlockSpec((per_group, 3, step, 128), lambda t: (0, 0, t, 0)) for _ in range(groups)
        ]
        + [pl.BlockSpec((2, step, heads + 8, cols), lambda t: (0, t, 0, 0))],
        out_shape=[
            jax.ShapeDtypeStruct((per_group, 3, half, 128), BF16) for _ in range(groups)
        ]
        + [jax.ShapeDtypeStruct((2, half, heads + 8, cols), F32)],
        scratch_shapes=[
            pltpu.VMEM((2, tiles, heads * step, 128), F32),
            pltpu.VMEM((heads, cols), F32),
            pltpu.VMEM((groups, per_group, 3, step, 128), BF16),
        ],
        compiler_params=params(),
    )(
        group_index,
        row_index,
        chains,
        chain_gain,
        pair.reshape(2, half, cols, channels),
        w_pair.T,
        chains,
    )
    return sends, stats


def pair_back_kernel(
    group_ref, pair_ref, stats_ref, w_pair_ref, *rest, groups, calls, factor, batch
):
    grad_refs = rest[: groups * calls]
    out_ref, flat_ref = rest[groups * calls :]
    _, step, cols, channels = pair_ref.shape
    per_call = grad_refs[0].shape[0]
    heads = groups * calls * per_call
    group_own = group_ref[0]
    means = mean_matrix(channels)
    weight = w_pair_ref[...].astype(F32)
    weight = (weight - jnp.mean(weight, axis=-1, keepdims=True)).astype(BF16)
    spread = lax.broadcasted_iota(jnp.int32, (heads, channels), 0)
    spread = (spread < 2).astype(F32).astype(BF16)
    block = jnp.concatenate(
        [lane_pad(weight, 0, 2 * channels), lane_pad(spread, channels, 2 * channels)], axis=0
    )
    weights = jnp.concatenate(
        [lane_pad(block, 2 * channels * place, 8 * channels) for place in range(4)], axis=0
    )
    blank = jnp.zeros((heads - 2, cols), F32)
    for number in range(groups * calls):
        call, slot = divmod(number, groups)
        source = (group_own ^ slot) * calls + call
        for head in range(per_call):
            values = grad_refs[number][head].astype(F32)
            top = pl.multiple_of((source * per_call + head) * step, step)
            for side in range(2):
                flat_ref[side, 0, pl.ds(top, step), :] = values[side]
                flat_ref[side, 1, pl.ds(top, step), : cols - 128] = values[2][
                    :, side * (cols - 128) : (side + 1) * (cols - 128)
                ]

    for first in range(0, step, batch):
        center = center_rows(pair_ref, first, batch, means)
        for base in range(0, batch, 2):
            places = [(base + inner, side) for inner in range(2) for side in range(2)]
            left = []
            for inner, side in places:
                grads = jnp.concatenate(
                    [
                        flat_ref[side, tile, pl.ds(first + inner, heads, stride=step), :][
                            :, : end - start
                        ]
                        for tile, start, end in lane_tiles(cols)
                    ],
                    axis=1,
                )
                projected = stats_ref[side, first + inner, :heads, :]
                inverse = stats_ref[side, first + inner, heads : heads + 1, :]
                cross = jnp.sum(grads * projected, axis=0, keepdims=True) * (1.0 / channels)
                scaled = grads * (inverse * factor)
                cross = cross * (inverse * inverse * factor)
                cross_high = cross.astype(BF16).astype(F32)
                left += [scaled, cross_high, cross - cross_high, blank]
            both = mm_tn(jnp.concatenate(left, axis=0).astype(BF16), weights)
            for place, (inner, side) in enumerate(places):
                rows = slice(inner * cols, (inner + 1) * cols)
                lanes = slice(side * channels, (side + 1) * channels)
                start = 2 * channels * place
                middle, end = start + channels, start + 2 * channels
                out_ref[side, first + inner] = (
                    both[:, start:middle] - center[rows, lanes] * both[:, middle:end]
                ).astype(BF16)


def pair_back(pair, stats, grads, w_pair, group_index, groups, factor):
    rows, cols, channels = pair.shape
    per_call = grads[0].shape[0]
    heads = len(grads) * per_call
    half = rows // 2
    step = 16
    tiles = -(-cols // 128)
    out = pl.pallas_call(
        functools.partial(
            pair_back_kernel, groups=groups, calls=len(grads) // groups, factor=factor, batch=2
        ),
        grid=(half // step,),
        in_specs=[
            smem(),
            pl.BlockSpec((2, step, cols, channels), lambda t: (0, t, 0, 0)),
            pl.BlockSpec((2, step, heads + 8, cols), lambda t: (0, t, 0, 0)),
            pl.BlockSpec((heads, channels), lambda t: (0, 0)),
        ]
        + [pl.BlockSpec((per_call, 3, step, 128), lambda t: (0, 0, t, 0)) for _ in grads],
        out_specs=pl.BlockSpec((2, step, cols, channels), lambda t: (0, t, 0, 0)),
        out_shape=jax.ShapeDtypeStruct((2, half, cols, channels), BF16),
        scratch_shapes=[pltpu.VMEM((2, tiles, heads * step, 128), F32)],
        compiler_params=params(),
    )(group_index, pair.reshape(2, half, cols, channels), stats, w_pair.T, *grads)
    return out.reshape(rows, cols, channels)


def unit_order(heads):
    first, second = range(heads // 2), range(heads // 2, heads)
    order = [(1, head) for head in first] + [(3, head) for head in first]
    order += [(2, head) for head in second] + [(3, head) for head in second]
    order += [(0, head) for head in range(heads)]
    order += [(2, head) for head in first] + [(1, head) for head in second]
    return order


def attention_kernel(group_ref, row_ref, *rest, groups, row_parts, head_size, row_block):
    bias_refs = rest[: row_parts + 2]
    acts_refs = rest[row_parts + 2 : row_parts + 2 + groups]
    acts_refs = acts_refs[:1] + acts_refs[-1:] + acts_refs[1:-1]
    rest = rest[row_parts + 2 + groups :]
    out_refs = rest[:groups]
    (
        keep_ref,
        give_ref,
        query_ref,
        keys_ref,
        values_ref,
        grads_ref,
        query_t_ref,
        keys_t_ref,
        values_t_ref,
        bias_full,
        score_full,
        att_sum,
        gq_sum,
        gk_sum,
        gv_sum,
    ) = rest[groups:]
    head = pl.program_id(0)
    heads = keep_ref.shape[1] * 2 // row_parts
    group_own = group_ref[0]
    cols, width = acts_refs[0].shape
    tokens = groups * cols
    part = width // 4
    half = bias_refs[0].shape[3]
    rest_lanes = cols - 128
    scale = 1.0 / math.sqrt(head_size)
    extra = att_sum.shape[1] - part
    plain = (query_ref, keys_ref, values_ref, grads_ref)
    turned = (query_t_ref, keys_t_ref, values_t_ref)

    turns = [(slot * cols, slot * 128, 128) for slot in range(groups)]
    turns += [
        (slot * cols + 128, groups * 128 + slot * rest_lanes, rest_lanes) for slot in range(groups)
    ]

    @pl.when(head == 0)
    def _():
        for kind in range(4):
            lanes = slice(kind * part, (kind + 1) * part)
            if kind in (0, 3):
                for slot in range(groups):
                    plain[kind][slot * cols : (slot + 1) * cols, :] = acts_refs[slot][:, lanes]
            else:
                for token, place, count in turns:
                    slot, inside = divmod(token, cols)
                    plain[kind][place : place + count, :] = acts_refs[slot][
                        inside : inside + count, lanes
                    ]
            if kind < len(turned):
                turned[kind][...] = plain[kind][...].T
        att_sum[...] = jnp.zeros_like(att_sum)
        gq_sum[...] = jnp.zeros_like(gq_sum)
        gv_sum[...] = jnp.zeros_like(gv_sum)

    def places(row_part):
        first = row_part * (2 * half)
        slot = group_own ^ (first // cols)
        for side in range(2):
            top = slot * cols + lax.rem(first, cols) + side * half
            yield side, pl.ds(pl.multiple_of(top, 16), half)

    for other in range(row_parts):

        def block(column, which, other=other):
            if other >= row_parts - 2 and column >= groups // 2:
                return bias_refs[other + 2][column - groups // 2, 0, which]
            return bias_refs[other][column, 0, which]

        for side, rows in places(row_ref[0] ^ other):
            lanes = slice(side * rest_lanes, (side + 1) * rest_lanes)
            tiles = [block(column, side) for column in range(groups)]
            tiles += [block(column, 2)[:, lanes] for column in range(groups)]
            bias_full[rows, :] = jnp.concatenate(tiles, axis=1)

    lane = lax.broadcasted_iota(jnp.int32, (1, part), 1)
    mine = (lane >= head * head_size) & (lane < (head + 1) * head_size)
    zero = jnp.zeros((), BF16)
    keys_m = jnp.where(mine, keys_ref[...], zero)
    values_m = jnp.concatenate(
        [jnp.where(mine, values_ref[...], zero), jnp.ones((tokens, extra), BF16)], axis=1
    )
    feature = pl.multiple_of(head * head_size, head_size)
    query_t = query_t_ref[pl.ds(feature, head_size), :]
    gk_t = jnp.zeros((head_size, tokens), F32)
    gv_t = jnp.zeros((part, tokens), F32)
    for top in range(0, tokens, row_block):
        rows = slice(top, top + row_block)
        query = jnp.where(mine, query_ref[rows, :], zero)
        grads = jnp.where(mine, grads_ref[rows, :], zero)
        weights = jnp.exp2(mm(query, keys_t_ref[...]) + bias_full[rows, :].astype(F32))
        weights_b = weights.astype(BF16)
        attended = mm(weights_b, values_m)
        inverse = 1.0 / attended[:, part : part + 1]
        attended = attended[:, :part] * inverse
        att_sum[rows, :part] += attended
        grads = (grads.astype(F32) * inverse).astype(BF16)
        delta = jnp.sum(attended * grads.astype(F32), axis=-1, keepdims=True)
        score = (weights * (mm(grads, values_t_ref[...]) - delta)).astype(BF16)
        score_full[rows, :] = score
        gq_sum[rows, :] += mm(score, keys_m)
        gk_t = gk_t + mm(query_t[:, rows], score)
        gv_t = gv_t + mm_tn(grads, weights_b)
    gk_sum[pl.ds(feature, head_size), :] = gk_t
    gv_sum[...] += gv_t

    order = unit_order(heads)

    def give_back(some_heads):
        for other in range(row_parts):
            unit = order.index((other // 2, some_heads[0]))
            dbias_ref = give_ref if other % 2 else keep_ref
            unit = unit + head - some_heads[0]
            scores = [score_full[rows, :] for _, rows in places(row_ref[0] ^ other)]
            blocks = []
            for column in range(groups):
                start = groups * 128 + column * rest_lanes
                blocks += [score[:, column * 128 : (column + 1) * 128] for score in scores]
                blocks.append(
                    jnp.concatenate(
                        [score[:, start : start + rest_lanes] for score in scores], axis=1
                    )
                )
            for column in range(groups):
                dbias_ref[column, unit] = jnp.stack(blocks[3 * column : 3 * column + 3])

    @pl.when(head < heads // 2)
    def _():
        give_back(range(heads // 2))

    @pl.when(head >= heads // 2)
    def _():
        give_back(range(heads // 2, heads))

    @pl.when(head == heads - 1)
    def _():
        results = (
            gq_sum[...] * scale,
            (gk_sum[...] * math.log(2.0)).T,
            gv_sum[...].T,
            att_sum[:, :part],
        )
        for kind, values in enumerate(results):
            rounded = values.astype(BF16)
            lanes = slice(kind * part, (kind + 1) * part)
            if kind in (0, 3):
                for slot in range(groups):
                    out_refs[slot][:, lanes] = rounded[slot * cols : (slot + 1) * cols]
            else:
                for token, place, count in turns:
                    slot, inside = divmod(token, cols)
                    out_refs[slot][inside : inside + count, lanes] = rounded[place : place + count]


def attention(group_index, row_index, acts, bias, head_size):
    groups = len(acts)
    row_parts = len(bias) - 2
    cols, width = acts[0].shape
    tokens = groups * cols
    part = width // 4
    _, heads, _, half, lanes = bias[0].shape
    row_block = tokens
    padded = (part // 128 + 1) * 128
    units = (groups, row_parts // 2 * heads, 3, half, lanes)
    *grads, keep, give = pl.pallas_call(
        functools.partial(
            attention_kernel,
            groups=groups,
            row_parts=row_parts,
            head_size=head_size,
            row_block=row_block,
        ),
        grid=(heads,),
        in_specs=[smem(), smem()]
        + [
            pl.BlockSpec((block.shape[0], 1, 3, half, lanes), lambda h: (0, h, 0, 0, 0))
            for block in bias
        ]
        + [pl.BlockSpec((cols, width), lambda h: (0, 0))] * groups,
        out_specs=[pl.BlockSpec((cols, width), lambda h: (0, 0))] * groups
        + [pl.BlockSpec(shape, lambda h: (0, 0, 0, 0, 0)) for shape in (units, units)],
        out_shape=[jax.ShapeDtypeStruct((cols, width), BF16)] * groups
        + [jax.ShapeDtypeStruct(shape, BF16) for shape in (units, units)],
        scratch_shapes=[pltpu.VMEM((tokens, part), BF16) for _ in range(4)]
        + [pltpu.VMEM((part, tokens), BF16) for _ in range(3)]
        + [
            pltpu.VMEM((tokens, tokens), BF16),
            pltpu.VMEM((tokens, tokens), BF16),
            pltpu.VMEM((tokens, padded), F32),
            pltpu.VMEM((tokens, part), F32),
            pltpu.VMEM((part, tokens), F32),
            pltpu.VMEM((part, tokens), F32),
        ],
        compiler_params=params(),
    )(group_index, row_index, *bias, acts[0], *acts[2:], acts[1])
    return grads, keep, give


def finish_kernel(
    group_ref,
    single_ref,
    noised_ref,
    cot_ref,
    gamma_ref,
    gate_ref,
    w_gamma_ref,
    w_beta_ref,
    w_outgate_ref,
    w_query_ref,
    w_key_ref,
    w_value_ref,
    w_out_ref,
    *rest,
    groups,
    calls,
):
    got_refs = rest[: groups * calls]
    updated_ref, d_single_ref, stage_ref = rest[groups * calls :]
    width = stage_ref.shape[3]
    part = width // 4
    for slot in range(groups):
        for call in range(calls):
            stage_ref[group_ref[0] ^ slot, call] = got_refs[
                call * groups + slot
            ][...]

    def take(kind):
        return jnp.concatenate(
            [
                stage_ref[group, call, :, kind * part : (kind + 1) * part]
                for group in range(groups)
                for call in range(calls)
            ],
            axis=1,
        )

    out_gate = gate_ref[...]
    cond_gamma = gamma_ref[...]
    block_update = mm(take(3), w_out_ref[...])
    noised = noised_ref[...].astype(F32)
    updated_ref[...] = (noised + out_gate * block_update).astype(BF16)
    gate_part = cot_ref[...].astype(F32) * block_update
    pre_gate = (gate_part * out_gate * (1.0 - out_gate)).astype(BF16)
    grad_input = mm_nt(take(0), w_query_ref[...])
    grad_input += mm_nt(take(1), w_key_ref[...])
    grad_input += mm_nt(take(2), w_value_ref[...])
    noised_norm, _ = norm_rows(noised)
    pre_gamma = (grad_input * noised_norm * cond_gamma * (1.0 - cond_gamma)).astype(BF16)
    grad_snorm = mm_nt(pre_gamma, w_gamma_ref[...])
    grad_snorm += mm_nt(grad_input.astype(BF16), w_beta_ref[...])
    grad_snorm += mm_nt(pre_gate, w_outgate_ref[...])
    single_norm, single_inv = norm_rows(single_ref[...].astype(F32))
    d_single_ref[...] = norm_back(grad_snorm, single_norm, single_inv).astype(BF16)


def swap_groups(sends):
    groups = len(sends)
    order = SLOT_ORDER[1:]
    got = []
    for bits in order:
        perm = [(index, index ^ bits) for index in range(groups)]
        got.append(lax.ppermute(sends[bits], "grp", perm))
    got = dict(zip(order, lax.optimization_barrier(got)))
    return [sends[0]] + [got[bits] for bits in range(1, groups)]


def flip_rows(values, bits, row_total):
    return lax.ppermute(values, "rows", [(index, index ^ bits) for index in range(row_total)])


def gather_rows(own, acts, row_total):
    half = own.shape[0] // 2
    near = flip_rows(own, 2, row_total)
    far = flip_rows(own, 4, row_total)
    first = flip_rows(near[:half], 4, row_total)
    second = flip_rows(far[half:], 2, row_total)
    acts[2], acts[3], acts[1], first, second = lax.optimization_barrier(
        (acts[2], acts[3], acts[1], first, second)
    )
    blocks = []
    for block in (own, near, far, first, second):
        blocks += [block, flip_rows(block, 1, row_total)]
    return blocks, acts


def scatter_rows(keep, give, row_total):
    got = flip_rows(give, 1, row_total)
    early = keep.shape[1] // 2
    heads = early // 2
    part = heads // 2

    def add(first, count, *others):
        total = keep[:, first : first + count].astype(F32)
        total += got[:, first : first + count].astype(F32)
        for other in others:
            total += other.astype(F32)
        return total.astype(BF16)

    near = flip_rows(add(0, heads), 2, row_total)
    far = flip_rows(add(heads, heads), 4, row_total)
    far_two = flip_rows(add(early + heads, part, near[:, part:]), 4, row_total)
    near_two = flip_rows(add(early + heads + part, part, far[:, part:]), 2, row_total)
    own = add(early, heads, jnp.concatenate([near[:, :part], far[:, :part]], axis=1))
    return own, far_two, near_two


def add_last(own, far_two, near_two):
    last = jnp.concatenate([far_two, near_two], axis=1)
    total = (own.astype(F32) + last.astype(F32)).astype(BF16)
    return [total[slot] for slot in range(total.shape[0])]


def sum_rows(mine, d_pair, row_total):
    parts = [flip_rows(mine, bits, row_total) for bits in (2, 4, 6)]
    parts, d_pair = lax.optimization_barrier((parts, d_pair))
    near, far, last = (part.astype(F32) for part in parts)
    chips = ((mine.astype(F32) + near) + (far + last)).astype(BF16)
    return chips.astype(F32) + flip_rows(chips, 1, row_total).astype(F32), d_pair


def split_heads(
    single,
    pair,
    chains,
    noised,
    w_gamma,
    w_beta,
    w_outgate,
    w_query,
    w_key,
    w_value,
    w_out,
    w_pair,
    chain_gain,
    cotangent,
    *,
    groups,
    row_total,
):
    cols, _ = single.shape
    tokens = chains.shape[0]
    width = noised.shape[2]
    head_size = width // w_pair.shape[1]
    calls = 1
    row_index = lax.axis_index("rows").reshape(1)
    group_index = lax.axis_index("grp").reshape(1)
    bias_send, stats = pair_bias(
        pair, w_pair, chain_gain, chains, group_index, row_index, groups
    )
    bias_got = swap_groups(bias_send)
    noised = noised[0]
    cotangent = cotangent[0]
    *acts_send, cond_gamma, out_gate = pl.pallas_call(
        functools.partial(
            project_kernel, groups=groups, calls=calls, head_size=head_size
        ),
        in_specs=[smem()] + [vmem()] * 10,
        out_shape=[
            jax.ShapeDtypeStruct((cols, 4 * width // groups), BF16) for _ in range(groups)
        ]
        + [
            jax.ShapeDtypeStruct((cols, width), F32),
            jax.ShapeDtypeStruct((cols, width), F32),
        ],
        scratch_shapes=[pltpu.VMEM((groups, cols, 4 * width // groups), BF16)],
        compiler_params=params(),
    )(
        group_index,
        single,
        noised,
        cotangent,
        w_gamma,
        w_beta,
        w_outgate,
        w_query,
        w_key,
        w_value,
        w_out,
    )
    bias_got, _ = lax.optimization_barrier((bias_got, acts_send))
    acts_send = [acts_send[SLOT_ORDER.index(slot)] for slot in range(groups)]
    acts = swap_groups(acts_send)
    bias_all, acts = gather_rows(jnp.stack(bias_got), acts, row_total)
    grads_send, keep, give = attention(group_index, row_index, acts, bias_all, head_size)
    grads = swap_groups(grads_send)
    own, far_two, near_two = scatter_rows(keep, give, row_total)
    far_two, near_two, grads = lax.optimization_barrier((far_two, near_two, grads))
    dbias_own, grads = lax.optimization_barrier((add_last(own, far_two, near_two), grads))
    dbias_back = swap_groups(dbias_own)
    updated, d_part = pl.pallas_call(
        functools.partial(finish_kernel, groups=groups, calls=calls),
        in_specs=[smem()] + [vmem()] * (12 + groups * calls),
        out_shape=[
            jax.ShapeDtypeStruct((cols, width), BF16),
            jax.ShapeDtypeStruct(single.shape, BF16),
        ],
        scratch_shapes=[pltpu.VMEM((groups, calls, cols, 4 * width // (groups * calls)), BF16)],
        compiler_params=params(),
    )(
        group_index,
        single,
        noised,
        cotangent,
        cond_gamma,
        out_gate,
        w_gamma,
        w_beta,
        w_outgate,
        w_query,
        w_key,
        w_value,
        w_out,
        *grads,
    )
    d_pair = pair_back(pair, stats, dbias_back, w_pair, group_index, groups, float(tokens))
    d_single, d_pair = sum_rows(d_part, d_pair, row_total)
    return (updated[None], d_single, d_pair)


def project(acts, weight):
    return jnp.einsum("std,de->ste", acts, weight, preferred_element_type=F32)


def project_back(acts, weight):
    return jnp.einsum("ste,de->std", acts, weight, preferred_element_type=F32)


def split_keys(
    single,
    pair,
    chains,
    noised,
    w_gamma,
    w_beta,
    w_outgate,
    w_query,
    w_key,
    w_value,
    w_out,
    w_pair,
    chain_gain,
    cotangent,
):
    col_count = single.shape[0]
    row_count = pair.shape[0]
    head_count = w_pair.shape[1]
    model_width = w_query.shape[0]
    head_size = model_width // head_count
    sample_count = noised.shape[0]
    token_total = chains.shape[0]
    score_scale = 1.0 / math.sqrt(head_size)
    row_index = lax.axis_index("rows")
    group_index = lax.axis_index("grp")
    chain_rows = lax.dynamic_slice_in_dim(chains, row_index * row_count, row_count)
    chain_cols = lax.dynamic_slice_in_dim(chains, group_index * col_count, col_count)
    pair_norm, pair_inv = norm_rows(pair.astype(jnp.float32))
    projected = jnp.einsum(
        "ijc,ch->hij", pair_norm.astype(jnp.bfloat16), w_pair, preferred_element_type=jnp.float32
    )
    same_chain = (chain_rows[:, None] == chain_cols[None, :]).astype(jnp.float32)
    bias_block = (projected + chain_gain[:, None, None] * same_chain[None]).astype(jnp.bfloat16)
    bias_keys = lax.all_gather(bias_block, "rows", axis=1, tiled=True)
    single_norm, single_inv = norm_rows(single.astype(jnp.float32))
    single_b = single_norm.astype(jnp.bfloat16)
    cond_gamma = jax.nn.sigmoid(jnp.dot(single_b, w_gamma, preferred_element_type=jnp.float32))
    cond_beta = jnp.dot(single_b, w_beta, preferred_element_type=jnp.float32)
    out_gate = jax.nn.sigmoid(jnp.dot(single_b, w_outgate, preferred_element_type=jnp.float32))
    noised_f = noised.astype(jnp.float32)
    noised_norm, noised_inv = norm_rows(noised_f)
    x_b = (noised_norm * cond_gamma[None] + cond_beta[None]).astype(jnp.bfloat16)
    queries = project(x_b, w_query).astype(jnp.bfloat16)
    keys_own = project(x_b, w_key).astype(jnp.bfloat16)
    values_own = project(x_b, w_value).astype(jnp.bfloat16)
    queries_all = lax.all_gather(queries, "grp", axis=1, tiled=True)
    query_heads = queries_all.reshape(sample_count, token_total, head_count, head_size)
    key_heads = keys_own.reshape(sample_count, col_count, head_count, head_size)
    value_heads = values_own.reshape(sample_count, col_count, head_count, head_size)
    scores = (
        jnp.einsum("sihe,sjhe->shij", query_heads, key_heads, preferred_element_type=jnp.float32)
        * score_scale
        + bias_keys.astype(jnp.float32)[None]
    )
    exp_scores = jnp.exp(scores)
    exp_total = lax.psum(jnp.sum(exp_scores, axis=-1).astype(jnp.bfloat16), "grp").astype(
        jnp.float32
    )
    attn_prob = exp_scores / exp_total[..., None]
    prob_b = attn_prob.astype(jnp.bfloat16)
    attended_part = jnp.einsum(
        "shij,sjhe->sihe", prob_b, value_heads, preferred_element_type=jnp.float32
    )
    attended_part = attended_part.reshape(sample_count, token_total, model_width)
    attended = lax.psum_scatter(
        attended_part.astype(jnp.bfloat16), "grp", scatter_dimension=1, tiled=True
    )
    block_update = project(attended, w_out)
    updated = (noised_f + out_gate[None] * block_update).astype(jnp.bfloat16)
    grad_out = cotangent.astype(jnp.float32)
    gate_part = jnp.sum(grad_out * block_update, axis=0)
    grad_update = (grad_out * out_gate[None]).astype(jnp.bfloat16)
    grad_attn = project_back(grad_update, w_out).astype(jnp.bfloat16)
    grads_all = lax.all_gather(grad_attn, "grp", axis=1, tiled=True)
    grad_heads = grads_all.reshape(sample_count, token_total, head_count, head_size)
    grad_prob = jnp.einsum(
        "sihe,sjhe->shij", grad_heads, value_heads, preferred_element_type=jnp.float32
    )
    row_delta = lax.psum(
        jnp.sum(attn_prob * grad_prob, axis=-1).astype(jnp.bfloat16), "grp"
    ).astype(jnp.float32)
    grad_score = attn_prob * (grad_prob - row_delta[..., None])
    score_b = grad_score.astype(jnp.bfloat16)
    query_part = (
        jnp.einsum("shij,sjhe->sihe", score_b, key_heads, preferred_element_type=jnp.float32)
        * score_scale
    )
    query_part = query_part.reshape(sample_count, token_total, model_width)
    grad_query = lax.psum_scatter(
        query_part.astype(jnp.bfloat16), "grp", scatter_dimension=1, tiled=True
    )
    grad_key = (
        jnp.einsum("shij,sihe->sjhe", score_b, query_heads, preferred_element_type=jnp.float32)
        * score_scale
    )
    grad_value = jnp.einsum(
        "shij,sihe->sjhe", prob_b, grad_heads, preferred_element_type=jnp.float32
    )
    grad_key = grad_key.reshape(sample_count, col_count, model_width).astype(jnp.bfloat16)
    grad_value = grad_value.reshape(sample_count, col_count, model_width).astype(jnp.bfloat16)
    grad_input = (
        project_back(grad_query, w_query)
        + project_back(grad_key, w_key)
        + project_back(grad_value, w_value)
    )
    gamma_part = jnp.sum(grad_input * noised_norm, axis=0)
    beta_part = jnp.sum(grad_input, axis=0)
    gamma_sum, beta_sum, gate_sum = lax.psum((gamma_part, beta_part, gate_part), "rows")
    pre_gamma = (gamma_sum * cond_gamma * (1.0 - cond_gamma)).astype(jnp.bfloat16)
    pre_gate = (gate_sum * out_gate * (1.0 - out_gate)).astype(jnp.bfloat16)
    grad_snorm = jnp.dot(pre_gamma, w_gamma.T, preferred_element_type=jnp.float32)
    grad_snorm = grad_snorm + jnp.dot(
        beta_sum.astype(jnp.bfloat16), w_beta.T, preferred_element_type=jnp.float32
    )
    grad_snorm = grad_snorm + jnp.dot(pre_gate, w_outgate.T, preferred_element_type=jnp.float32)
    d_single = norm_back(grad_snorm, single_norm, single_inv)
    bias_part = jnp.sum(score_b, axis=0, dtype=jnp.float32)
    bias_own = lax.psum_scatter(bias_part, "rows", scatter_dimension=1, tiled=True)
    bias_grad = (bias_own * token_total).astype(jnp.bfloat16)
    grad_pairn = jnp.einsum("hij,ch->ijc", bias_grad, w_pair, preferred_element_type=jnp.float32)
    d_pair = norm_back(grad_pairn, pair_norm, pair_inv).astype(jnp.bfloat16)
    return (updated, d_single, d_pair)


def solution(mesh):
    in_specs = (
        P("grp", None),
        P("rows", "grp", None),
        P(),
        P("rows", "grp", None),
        P(),
        P(),
        P(),
        P(),
        P(),
        P(),
        P(),
        P(),
        P(),
        P("rows", "grp", None),
    )
    out_specs = (P("rows", "grp", None), P("grp", None), P("rows", "grp", None))
    groups = mesh.shape["grp"]
    row_total = mesh.shape["rows"]

    def on_device(*args):
        pair, noised, w_pair = args[1], args[3], args[11]
        fits = (
            groups == 4
            and pair.shape[0] % 32 == 0
            and pair.shape[1] % pair.shape[0] == 0
            and row_total == 8
            and noised.shape[0] == 1
            and noised.shape[1] == 192
            and w_pair.shape[1] % (2 * groups) == 0
        )
        if fits:
            return split_heads(*args, groups=groups, row_total=row_total)
        return split_keys(*args)

    return jax.shard_map(
        on_device, mesh=mesh, in_specs=in_specs, out_specs=out_specs, check_vma=False
    )
```

```python
import functools
import math

import jax
import jax.numpy as jnp
from jax import lax
from jax.experimental import pallas as pl
from jax.experimental.pallas import tpu as pltpu
from jax.sharding import PartitionSpec as P

EPSILON = 1e-05
BF16 = jnp.bfloat16
F32 = jnp.float32
LOG2_E = math.log2(math.e)
SLOT_ORDER = (0, 2, 3, 1)
VMEM_LIMIT = 56 * 1024 * 1024


def norm_rows(values):
    center = values - jnp.mean(values, axis=-1, keepdims=True)
    inverse = lax.rsqrt(jnp.mean(center * center, axis=-1, keepdims=True) + EPSILON)
    return (center * inverse, inverse)


def norm_back(grad_in, normed, inverse):
    grad_mean = jnp.mean(grad_in, axis=-1, keepdims=True)
    cross_mean = jnp.mean(grad_in * normed, axis=-1, keepdims=True)
    return inverse * (grad_in - grad_mean - normed * cross_mean)


def mm(left, right):
    return lax.dot_general(left, right, (((1,), (0,)), ((), ())), preferred_element_type=F32)


def mm_nt(left, right):
    return lax.dot_general(left, right, (((1,), (1,)), ((), ())), preferred_element_type=F32)


def mm_tn(left, right):
    return lax.dot_general(left, right, (((0,), (0,)), ((), ())), preferred_element_type=F32)


def sigmoid(values):
    return 1.0 / (1.0 + jnp.exp(-values))


def params():
    return pltpu.CompilerParams(vmem_limit_bytes=VMEM_LIMIT)


def smem():
    return pl.BlockSpec(memory_space=pltpu.SMEM)


def vmem():
    return pl.BlockSpec(memory_space=pltpu.VMEM)


def project_kernel(
    group_ref,
    single_ref,
    noised_ref,
    cot_ref,
    w_gamma_ref,
    w_beta_ref,
    w_outgate_ref,
    w_query_ref,
    w_key_ref,
    w_value_ref,
    w_out_ref,
    *rest,
    groups,
    calls,
    head_size,
):
    send_refs = rest[:groups]
    gamma_ref, gate_ref, stage_ref = rest[groups:]
    width = stage_ref.shape[2]
    part = width // (4 * calls)
    group_own = group_ref[0]
    single_norm, _ = norm_rows(single_ref[...].astype(F32))
    single_b = single_norm.astype(BF16)
    cond_gamma = sigmoid(mm(single_b, w_gamma_ref[...]))
    gamma_ref[...] = cond_gamma
    out_gate = sigmoid(mm(single_b, w_outgate_ref[...]))
    gate_ref[...] = out_gate
    cond_beta = mm(single_b, w_beta_ref[...])
    noised_norm, _ = norm_rows(noised_ref[...].astype(F32))
    x_b = (noised_norm * cond_gamma + cond_beta).astype(BF16)

    def put(kind, values):
        rounded = values.astype(BF16)
        for group in range(groups):
            slot = group_own ^ group
            for call in range(calls):
                feature = (group * calls + call) * part
                lane = (call * 4 + kind) * part
                stage_ref[slot, :, lane : lane + part] = rounded[:, feature : feature + part]

    put(0, mm(x_b, w_query_ref[...]) * (LOG2_E / math.sqrt(head_size)))
    put(1, mm(x_b, w_key_ref[...]))
    put(2, mm(x_b, w_value_ref[...]))
    grad_update = (cot_ref[...].astype(F32) * out_gate).astype(BF16)
    put(3, mm_nt(grad_update, w_out_ref[...]))
    for slot in range(groups):
        send_refs[SLOT_ORDER.index(slot)][...] = stage_ref[slot]


def lane_tiles(cols):
    return [(tile, tile * 128, min(cols, tile * 128 + 128)) for tile in range(-(-cols // 128))]


def mean_matrix(channels):
    first = lax.broadcasted_iota(jnp.int32, (2 * channels, 2 * channels), 0) >= channels
    second = lax.broadcasted_iota(jnp.int32, (2 * channels, 2 * channels), 1) >= channels
    return jnp.where(first == second, 1.0 / channels, 0.0).astype(BF16)


def center_rows(pair_ref, first, batch, means):
    _, _, cols, channels = pair_ref.shape
    both = jnp.concatenate(
        [pair_ref[side, first : first + batch].reshape(batch * cols, channels) for side in range(2)],
        axis=1,
    )
    return both.astype(F32) - mm(both, means)


def lane_pad(block, before, total):
    rows, width = block.shape
    pieces = [block]
    if before:
        pieces = [jnp.zeros((rows, before), block.dtype)] + pieces
    if total > before + width:
        pieces = pieces + [jnp.zeros((rows, total - before - width), block.dtype)]
    return jnp.concatenate(pieces, axis=1)


def bias_kernel(
    group_ref,
    rows_ref,
    chains_ref,
    gain_ref,
    pair_ref,
    w_pair_ref,
    cols_ref,
    *rest,
    groups,
    batch,
):
    send_refs = rest[:groups]
    stats_ref, flat_ref, gains_ref, stage_ref = rest[groups:]
    _, step, cols, channels = pair_ref.shape
    heads = gain_ref.shape[0]
    per_group = heads // groups
    half = step * pl.num_programs(0)
    group_own = group_ref[0]
    row_base = rows_ref[0] * 2 * half + pl.program_id(0) * step
    means = mean_matrix(channels)
    weight = w_pair_ref[...].astype(F32).T.astype(BF16)
    mean_part = jnp.full((channels, heads), 1.0 / channels, BF16)
    mixed = []
    for inner in range(2):
        for part, offset in ((weight, 0), (mean_part, heads)):
            for side in range(2):
                mixed.append(lane_pad(part, 2 * heads * (2 * inner + side) + offset, 8 * heads))
    mixed = jnp.concatenate(mixed, axis=0)
    chain_all = cols_ref[...].reshape(1, groups * cols)
    chain_cols = chain_all[:, :cols]
    for group in range(1, groups):
        here = chain_all[:, group * cols : (group + 1) * cols]
        chain_cols = jnp.where(group_own == group, here, chain_cols)
    for head in range(heads):
        gains_ref[head : head + 1, :] = jnp.full((1, cols), gain_ref[head] * LOG2_E, F32)

    for first in range(0, step, batch):
        center = center_rows(pair_ref, first, batch, means)
        center_b = center.astype(BF16)
        square = (center * center).astype(BF16)
        for base in range(0, batch, 2):
            one = slice(base * cols, (base + 1) * cols)
            two = slice((base + 1) * cols, (base + 2) * cols)
            left = jnp.concatenate(
                [center_b[one], square[one], center_b[two], square[two]], axis=1
            )
            sums = mm(left, mixed).T
            for inner in range(2):
                row = first + base + inner
                for side in range(2):
                    top = 2 * heads * (2 * inner + side)
                    inverse = lax.rsqrt(sums[top + heads : top + 2 * heads] + EPSILON)
                    projected = sums[top : top + heads] * inverse
                    stats_ref[side, row, :heads, :] = projected
                    stats_ref[side, row, heads:, :] = inverse[:8]
                    chain = chains_ref[row_base + side * half + row]
                    same = (chain_cols == chain).astype(F32)
                    values = projected * LOG2_E + gains_ref[...] * same
                    for tile, start, end in lane_tiles(cols):
                        piece = lane_pad(values[:, start:end], 0, 128)
                        flat_ref[side, tile, pl.ds(row, heads, stride=step), :] = piece
    for head in range(heads):
        slot = group_own ^ (head // per_group)
        tops = slice(head * step, (head + 1) * step)
        rest_lanes = [flat_ref[side, 1, tops, : cols - 128] for side in range(2)]
        stage_ref[slot, head % per_group, 0] = flat_ref[0, 0, tops, :].astype(BF16)
        stage_ref[slot, head % per_group, 1] = flat_ref[1, 0, tops, :].astype(BF16)
        stage_ref[slot, head % per_group, 2] = jnp.concatenate(rest_lanes, axis=1).astype(BF16)
    for slot in range(groups):
        send_refs[slot][...] = stage_ref[slot]


def pair_bias(pair, w_pair, chain_gain, chains, group_index, row_index, groups):
    rows, cols, channels = pair.shape
    heads = w_pair.shape[1]
    per_group = heads // groups
    half = rows // 2
    step = 16
    tiles = -(-cols // 128)
    *sends, stats = pl.pallas_call(
        functools.partial(bias_kernel, groups=groups, batch=16),
        grid=(half // step,),
        in_specs=[
            smem(),
            smem(),
            smem(),
            smem(),
            pl.BlockSpec((2, step, cols, channels), lambda t: (0, t, 0, 0)),
            pl.BlockSpec((heads, channels), lambda t: (0, 0)),
            pl.BlockSpec((groups * cols,), lambda t: (0,)),
        ],
        out_specs=[
            pl.BlockSpec((per_group, 3, step, 128), lambda t: (0, 0, t, 0)) for _ in range(groups)
        ]
        + [pl.BlockSpec((2, step, heads + 8, cols), lambda t: (0, t, 0, 0))],
        out_shape=[
            jax.ShapeDtypeStruct((per_group, 3, half, 128), BF16) for _ in range(groups)
        ]
        + [jax.ShapeDtypeStruct((2, half, heads + 8, cols), F32)],
        scratch_shapes=[
            pltpu.VMEM((2, tiles, heads * step, 128), F32),
            pltpu.VMEM((heads, cols), F32),
            pltpu.VMEM((groups, per_group, 3, step, 128), BF16),
        ],
        compiler_params=params(),
    )(
        group_index,
        row_index,
        chains,
        chain_gain,
        pair.reshape(2, half, cols, channels),
        w_pair.T,
        chains,
    )
    return sends, stats


def pair_back_kernel(
    group_ref, pair_ref, stats_ref, w_pair_ref, *rest, groups, calls, factor, batch
):
    grad_refs = rest[: groups * calls]
    out_ref, flat_ref = rest[groups * calls :]
    _, step, cols, channels = pair_ref.shape
    per_call = grad_refs[0].shape[0]
    heads = groups * calls * per_call
    group_own = group_ref[0]
    means = mean_matrix(channels)
    weight = w_pair_ref[...].astype(F32)
    weight = (weight - jnp.mean(weight, axis=-1, keepdims=True)).astype(BF16)
    spread = lax.broadcasted_iota(jnp.int32, (heads, channels), 0)
    spread = (spread < 2).astype(F32).astype(BF16)
    block = jnp.concatenate(
        [lane_pad(weight, 0, 2 * channels), lane_pad(spread, channels, 2 * channels)], axis=0
    )
    weights = jnp.concatenate(
        [lane_pad(block, 2 * channels * place, 8 * channels) for place in range(4)], axis=0
    )
    blank = jnp.zeros((heads - 2, cols), F32)
    for number in range(groups * calls):
        call, slot = divmod(number, groups)
        source = (group_own ^ slot) * calls + call
        for head in range(per_call):
            values = grad_refs[number][head].astype(F32)
            top = pl.multiple_of((source * per_call + head) * step, step)
            for side in range(2):
                flat_ref[side, 0, pl.ds(top, step), :] = values[side]
                flat_ref[side, 1, pl.ds(top, step), : cols - 128] = values[2][
                    :, side * (cols - 128) : (side + 1) * (cols - 128)
                ]

    for first in range(0, step, batch):
        center = center_rows(pair_ref, first, batch, means)
        for base in range(0, batch, 2):
            places = [(base + inner, side) for inner in range(2) for side in range(2)]
            left = []
            for inner, side in places:
                grads = jnp.concatenate(
                    [
                        flat_ref[side, tile, pl.ds(first + inner, heads, stride=step), :][
                            :, : end - start
                        ]
                        for tile, start, end in lane_tiles(cols)
                    ],
                    axis=1,
                )
                projected = stats_ref[side, first + inner, :heads, :]
                inverse = stats_ref[side, first + inner, heads : heads + 1, :]
                cross = jnp.sum(grads * projected, axis=0, keepdims=True) * (1.0 / channels)
                scaled = grads * (inverse * factor)
                cross = cross * (inverse * inverse * factor)
                cross_high = cross.astype(BF16).astype(F32)
                left += [scaled, cross_high, cross - cross_high, blank]
            both = mm_tn(jnp.concatenate(left, axis=0).astype(BF16), weights)
            for place, (inner, side) in enumerate(places):
                rows = slice(inner * cols, (inner + 1) * cols)
                lanes = slice(side * channels, (side + 1) * channels)
                start = 2 * channels * place
                middle, end = start + channels, start + 2 * channels
                out_ref[side, first + inner] = (
                    both[:, start:middle] - center[rows, lanes] * both[:, middle:end]
                ).astype(BF16)


def pair_back(pair, stats, grads, w_pair, group_index, groups, factor):
    rows, cols, channels = pair.shape
    per_call = grads[0].shape[0]
    heads = len(grads) * per_call
    half = rows // 2
    step = 16
    tiles = -(-cols // 128)
    out = pl.pallas_call(
        functools.partial(
            pair_back_kernel, groups=groups, calls=len(grads) // groups, factor=factor, batch=8
        ),
        grid=(half // step,),
        in_specs=[
            smem(),
            pl.BlockSpec((2, step, cols, channels), lambda t: (0, t, 0, 0)),
            pl.BlockSpec((2, step, heads + 8, cols), lambda t: (0, t, 0, 0)),
            pl.BlockSpec((heads, channels), lambda t: (0, 0)),
        ]
        + [pl.BlockSpec((per_call, 3, step, 128), lambda t: (0, 0, t, 0)) for _ in grads],
        out_specs=pl.BlockSpec((2, step, cols, channels), lambda t: (0, t, 0, 0)),
        out_shape=jax.ShapeDtypeStruct((2, half, cols, channels), BF16),
        scratch_shapes=[pltpu.VMEM((2, tiles, heads * step, 128), F32)],
        compiler_params=params(),
    )(group_index, pair.reshape(2, half, cols, channels), stats, w_pair.T, *grads)
    return out.reshape(rows, cols, channels)


def unit_order(heads):
    first, second = range(heads // 2), range(heads // 2, heads)
    order = [(1, head) for head in first] + [(3, head) for head in first]
    order += [(2, head) for head in second] + [(3, head) for head in second]
    order += [(0, head) for head in range(heads)]
    order += [(2, head) for head in first] + [(1, head) for head in second]
    return order


def attention_kernel(group_ref, row_ref, *rest, groups, row_parts, head_size):
    bias_refs = rest[: row_parts + 2]
    acts_refs = rest[row_parts + 2 : row_parts + 2 + groups]
    acts_refs = acts_refs[:1] + acts_refs[-1:] + acts_refs[1:-1]
    rest = rest[row_parts + 2 + groups :]
    out_refs = rest[:groups]
    (
        keep_ref,
        give_ref,
        query_ref,
        keys_ref,
        values_ref,
        grads_ref,
        query_t_ref,
        keys_t_ref,
        values_t_ref,
        bias_full,
        score_full,
        att_sum,
        gq_sum,
        gk_sum,
        gv_sum,
    ) = rest[groups:]
    heads = keep_ref.shape[1] * 2 // row_parts
    group_own = group_ref[0]
    cols, width = acts_refs[0].shape
    tokens = groups * cols
    part = width // 4
    half = bias_refs[0].shape[3]
    rest_lanes = cols - 128
    scale = 1.0 / math.sqrt(head_size)
    extra = 128 - part % 128
    plain = (query_ref, keys_ref, values_ref, grads_ref)
    turned = (query_t_ref, keys_t_ref, values_t_ref)

    turns = [(slot * cols, slot * 128, 128) for slot in range(groups)]
    turns += [
        (slot * cols + 128, groups * 128 + slot * rest_lanes, rest_lanes) for slot in range(groups)
    ]
    for kind in range(4):
        lanes = slice(kind * part, (kind + 1) * part)
        if kind in (0, 3):
            for slot in range(groups):
                plain[kind][slot * cols : (slot + 1) * cols, :] = acts_refs[slot][:, lanes]
        else:
            for token, place, count in turns:
                slot, inside = divmod(token, cols)
                plain[kind][place : place + count, :] = acts_refs[slot][
                    inside : inside + count, lanes
                ]
        if kind < len(turned):
            turned[kind][...] = plain[kind][...].T

    def places(row_part):
        first = row_part * (2 * half)
        slot = group_own ^ (first // cols)
        for side in range(2):
            top = slot * cols + lax.rem(first, cols) + side * half
            yield side, pl.ds(pl.multiple_of(top, 16), half)

    def block(other, column, head, which):
        if other >= row_parts - 2 and column >= groups // 2:
            return bias_refs[other + 2][column - groups // 2, head, which]
        return bias_refs[other][column, head, which]

    lane = lax.broadcasted_iota(jnp.int32, (1, part), 1)
    zero = jnp.zeros((), BF16)
    order = unit_order(heads)
    for head in range(heads):
        bias_head, score_head = bias_full.at[head % 2], score_full.at[head % 2]
        for other in range(row_parts):
            for side, rows in places(row_ref[0] ^ other):
                lanes = slice(side * rest_lanes, (side + 1) * rest_lanes)
                tiles = [block(other, column, head, side) for column in range(groups)]
                tiles += [block(other, column, head, 2)[:, lanes] for column in range(groups)]
                bias_head[rows, :] = jnp.concatenate(tiles, axis=1)

        features = slice(head * head_size, (head + 1) * head_size)
        mine = (lane >= features.start) & (lane < features.stop)
        query = jnp.where(mine, query_ref[...], zero)
        grads = jnp.where(mine, grads_ref[...], zero)
        keys_m = jnp.where(mine, keys_ref[...], zero)
        values_m = jnp.concatenate(
            [jnp.where(mine, values_ref[...], zero), jnp.ones((tokens, extra), BF16)], axis=1
        )
        weights = jnp.exp2(mm(query, keys_t_ref[...]) + bias_head[...].astype(F32))
        weights_b = weights.astype(BF16)
        attended = mm(weights_b, values_m)
        inverse = 1.0 / attended[:, part : part + 1]
        attended = attended[:, :part] * inverse
        grads = (grads.astype(F32) * inverse).astype(BF16)
        delta = jnp.sum(attended * grads.astype(F32), axis=-1, keepdims=True)
        score = (weights * (mm(grads, values_t_ref[...]) - delta)).astype(BF16)
        score_head[...] = score
        grad_query = mm(score, keys_m)
        grad_value = mm_tn(grads, weights_b)
        if head == 0:
            att_sum[...] = attended
            gq_sum[...] = grad_query
            gv_sum[...] = grad_value
        else:
            att_sum[...] += attended
            gq_sum[...] += grad_query
            gv_sum[...] += grad_value
        gk_sum[features, :] = mm(query_t_ref[features, :], score)

        for other in range(row_parts):
            unit = order.index((other // 2, head))
            dbias_ref = give_ref if other % 2 else keep_ref
            scores = [score_head[rows, :] for _, rows in places(row_ref[0] ^ other)]
            for column in range(groups):
                start = groups * 128 + column * rest_lanes
                blocks = [score[:, column * 128 : (column + 1) * 128] for score in scores]
                blocks.append(
                    jnp.concatenate(
                        [score[:, start : start + rest_lanes] for score in scores], axis=1
                    )
                )
                dbias_ref[column, unit] = jnp.stack(blocks)

    results = (
        gq_sum[...] * scale,
        (gk_sum[...] * math.log(2.0)).T,
        gv_sum[...].T,
        att_sum[...],
    )
    for kind, values in enumerate(results):
        rounded = values.astype(BF16)
        lanes = slice(kind * part, (kind + 1) * part)
        if kind in (0, 3):
            for slot in range(groups):
                out_refs[slot][:, lanes] = rounded[slot * cols : (slot + 1) * cols]
        else:
            for token, place, count in turns:
                slot, inside = divmod(token, cols)
                out_refs[slot][inside : inside + count, lanes] = rounded[place : place + count]


def attention(group_index, row_index, acts, bias, head_size):
    groups = len(acts)
    row_parts = len(bias) - 2
    cols, width = acts[0].shape
    tokens = groups * cols
    part = width // 4
    _, heads, _, half, _ = bias[0].shape
    units = (groups, row_parts // 2 * heads, 3, half, 128)
    *grads, keep, give = pl.pallas_call(
        functools.partial(
            attention_kernel, groups=groups, row_parts=row_parts, head_size=head_size
        ),
        in_specs=[smem(), smem()] + [vmem()] * (len(bias) + groups),
        out_shape=[jax.ShapeDtypeStruct((cols, width), BF16)] * groups
        + [jax.ShapeDtypeStruct(units, BF16)] * 2,
        scratch_shapes=[pltpu.VMEM((tokens, part), BF16) for _ in range(4)]
        + [pltpu.VMEM((part, tokens), BF16) for _ in range(3)]
        + [
            pltpu.VMEM((2, tokens, tokens), BF16),
            pltpu.VMEM((2, tokens, tokens), BF16),
            pltpu.VMEM((tokens, part), F32),
            pltpu.VMEM((tokens, part), F32),
            pltpu.VMEM((part, tokens), F32),
            pltpu.VMEM((part, tokens), F32),
        ],
        compiler_params=params(),
    )(group_index, row_index, *bias, acts[0], *acts[2:], acts[1])
    return grads, keep, give


def finish_kernel(
    group_ref,
    single_ref,
    noised_ref,
    cot_ref,
    gamma_ref,
    gate_ref,
    w_gamma_ref,
    w_beta_ref,
    w_outgate_ref,
    w_query_ref,
    w_key_ref,
    w_value_ref,
    w_out_ref,
    *rest,
    groups,
    calls,
):
    got_refs = rest[: groups * calls]
    updated_ref, d_single_ref, stage_ref, *held_refs, copied = rest[groups * calls :]
    sources = (
        w_out_ref,
        w_query_ref,
        w_key_ref,
        w_value_ref,
        w_gamma_ref,
        w_beta_ref,
        w_outgate_ref,
    )
    copies = [
        pltpu.make_async_copy(source, held, copied.at[number])
        for number, (source, held) in enumerate(zip(sources, held_refs))
    ]
    for copy in copies:
        copy.start()

    def weight(number):
        copies[number].wait()
        return held_refs[number][...]

    width = stage_ref.shape[3]
    part = width // 4
    for slot in range(groups):
        for call in range(calls):
            stage_ref[group_ref[0] ^ slot, call] = got_refs[
                call * groups + slot
            ][...]

    def take(kind):
        return jnp.concatenate(
            [
                stage_ref[group, call, :, kind * part : (kind + 1) * part]
                for group in range(groups)
                for call in range(calls)
            ],
            axis=1,
        )

    out_gate = gate_ref[...]
    cond_gamma = gamma_ref[...]
    block_update = mm(take(3), weight(0))
    noised = noised_ref[...].astype(F32)
    updated_ref[...] = (noised + out_gate * block_update).astype(BF16)
    gate_part = cot_ref[...].astype(F32) * block_update
    pre_gate = (gate_part * out_gate * (1.0 - out_gate)).astype(BF16)
    grad_input = mm_nt(take(0), weight(1))
    grad_input += mm_nt(take(1), weight(2))
    grad_input += mm_nt(take(2), weight(3))
    noised_norm, _ = norm_rows(noised)
    pre_gamma = (grad_input * noised_norm * cond_gamma * (1.0 - cond_gamma)).astype(BF16)
    grad_snorm = mm_nt(pre_gamma, weight(4))
    grad_snorm += mm_nt(grad_input.astype(BF16), weight(5))
    grad_snorm += mm_nt(pre_gate, weight(6))
    single_norm, single_inv = norm_rows(single_ref[...].astype(F32))
    d_single_ref[...] = norm_back(grad_snorm, single_norm, single_inv).astype(BF16)


def swap_groups(sends):
    groups = len(sends)
    order = SLOT_ORDER[1:]
    got = []
    for bits in order:
        perm = [(index, index ^ bits) for index in range(groups)]
        got.append(lax.ppermute(sends[bits], "grp", perm))
    got = dict(zip(order, lax.optimization_barrier(got)))
    return [sends[0]] + [got[bits] for bits in range(1, groups)]


def flip_rows(values, bits, row_total):
    return lax.ppermute(values, "rows", [(index, index ^ bits) for index in range(row_total)])


def gather_rows(own, acts, row_total):
    half = own.shape[0] // 2
    near = flip_rows(own, 2, row_total)
    far = flip_rows(own, 4, row_total)
    first = flip_rows(near[:half], 4, row_total)
    second = flip_rows(far[half:], 2, row_total)
    acts[2], acts[3], acts[1], first, second = lax.optimization_barrier(
        (acts[2], acts[3], acts[1], first, second)
    )
    blocks = []
    for block in (own, near, far, first, second):
        blocks += [block, flip_rows(block, 1, row_total)]
    return blocks, acts


def scatter_rows(keep, give, row_total):
    got = flip_rows(give, 1, row_total)
    early = keep.shape[1] // 2
    heads = early // 2
    part = heads // 2

    def add(first, count, *others):
        total = keep[:, first : first + count].astype(F32)
        total += got[:, first : first + count].astype(F32)
        for other in others:
            total += other.astype(F32)
        return total.astype(BF16)

    near = flip_rows(add(0, heads), 2, row_total)
    far = flip_rows(add(heads, heads), 4, row_total)
    far_two = flip_rows(add(early + heads, part, near[:, part:]), 4, row_total)
    near_two = flip_rows(add(early + heads + part, part, far[:, part:]), 2, row_total)
    own = add(early, heads, jnp.concatenate([near[:, :part], far[:, :part]], axis=1))
    return own, far_two, near_two


def add_last(own, far_two, near_two):
    last = jnp.concatenate([far_two, near_two], axis=1)
    total = (own.astype(F32) + last.astype(F32)).astype(BF16)
    return [total[slot] for slot in range(total.shape[0])]


def sum_rows(mine, d_pair, row_total):
    parts = [flip_rows(mine, bits, row_total) for bits in (2, 4, 6)]
    parts, d_pair = lax.optimization_barrier((parts, d_pair))
    near, far, last = (part.astype(F32) for part in parts)
    chips = ((mine.astype(F32) + near) + (far + last)).astype(BF16)
    return chips.astype(F32) + flip_rows(chips, 1, row_total).astype(F32), d_pair


def split_heads(
    single,
    pair,
    chains,
    noised,
    w_gamma,
    w_beta,
    w_outgate,
    w_query,
    w_key,
    w_value,
    w_out,
    w_pair,
    chain_gain,
    cotangent,
    *,
    groups,
    row_total,
):
    cols, _ = single.shape
    tokens = chains.shape[0]
    width = noised.shape[2]
    head_size = width // w_pair.shape[1]
    calls = 1
    row_index = lax.axis_index("rows").reshape(1)
    group_index = lax.axis_index("grp").reshape(1)
    bias_send, stats = pair_bias(
        pair, w_pair, chain_gain, chains, group_index, row_index, groups
    )
    bias_got = swap_groups(bias_send)
    noised = noised[0]
    cotangent = cotangent[0]
    *acts_send, cond_gamma, out_gate = pl.pallas_call(
        functools.partial(
            project_kernel, groups=groups, calls=calls, head_size=head_size
        ),
        in_specs=[smem()] + [vmem()] * 10,
        out_shape=[
            jax.ShapeDtypeStruct((cols, 4 * width // groups), BF16) for _ in range(groups)
        ]
        + [
            jax.ShapeDtypeStruct((cols, width), F32),
            jax.ShapeDtypeStruct((cols, width), F32),
        ],
        scratch_shapes=[pltpu.VMEM((groups, cols, 4 * width // groups), BF16)],
        compiler_params=params(),
    )(
        group_index,
        single,
        noised,
        cotangent,
        w_gamma,
        w_beta,
        w_outgate,
        w_query,
        w_key,
        w_value,
        w_out,
    )
    bias_got, _ = lax.optimization_barrier((bias_got, acts_send))
    acts_send = [acts_send[SLOT_ORDER.index(slot)] for slot in range(groups)]
    acts = swap_groups(acts_send)
    bias_all, acts = gather_rows(jnp.stack(bias_got), acts, row_total)
    grads_send, keep, give = attention(group_index, row_index, acts, bias_all, head_size)
    grads = swap_groups(grads_send)
    own, far_two, near_two = scatter_rows(keep, give, row_total)
    far_two, near_two, grads = lax.optimization_barrier((far_two, near_two, grads))
    dbias_own, grads = lax.optimization_barrier((add_last(own, far_two, near_two), grads))
    dbias_back = swap_groups(dbias_own)
    updated, d_part = pl.pallas_call(
        functools.partial(finish_kernel, groups=groups, calls=calls),
        in_specs=[smem()]
        + [vmem()] * 5
        + [pl.BlockSpec(memory_space=pl.ANY)] * 7
        + [vmem()] * (groups * calls),
        out_shape=[
            jax.ShapeDtypeStruct((cols, width), BF16),
            jax.ShapeDtypeStruct(single.shape, BF16),
        ],
        scratch_shapes=[pltpu.VMEM((groups, calls, cols, 4 * width // (groups * calls)), BF16)]
        + [
            pltpu.VMEM(weight.shape, BF16)
            for weight in (w_out, w_query, w_key, w_value, w_gamma, w_beta, w_outgate)
        ]
        + [pltpu.SemaphoreType.DMA((7,))],
        compiler_params=params(),
    )(
        group_index,
        single,
        noised,
        cotangent,
        cond_gamma,
        out_gate,
        w_gamma,
        w_beta,
        w_outgate,
        w_query,
        w_key,
        w_value,
        w_out,
        *grads,
    )
    d_pair = pair_back(pair, stats, dbias_back, w_pair, group_index, groups, float(tokens))
    d_single, d_pair = sum_rows(d_part, d_pair, row_total)
    return (updated[None], d_single, d_pair)


def project(acts, weight):
    return jnp.einsum("std,de->ste", acts, weight, preferred_element_type=F32)


def project_back(acts, weight):
    return jnp.einsum("ste,de->std", acts, weight, preferred_element_type=F32)


def split_keys(
    single,
    pair,
    chains,
    noised,
    w_gamma,
    w_beta,
    w_outgate,
    w_query,
    w_key,
    w_value,
    w_out,
    w_pair,
    chain_gain,
    cotangent,
):
    col_count = single.shape[0]
    row_count = pair.shape[0]
    head_count = w_pair.shape[1]
    model_width = w_query.shape[0]
    head_size = model_width // head_count
    sample_count = noised.shape[0]
    token_total = chains.shape[0]
    score_scale = 1.0 / math.sqrt(head_size)
    row_index = lax.axis_index("rows")
    group_index = lax.axis_index("grp")
    chain_rows = lax.dynamic_slice_in_dim(chains, row_index * row_count, row_count)
    chain_cols = lax.dynamic_slice_in_dim(chains, group_index * col_count, col_count)
    pair_norm, pair_inv = norm_rows(pair.astype(jnp.float32))
    projected = jnp.einsum(
        "ijc,ch->hij", pair_norm.astype(jnp.bfloat16), w_pair, preferred_element_type=jnp.float32
    )
    same_chain = (chain_rows[:, None] == chain_cols[None, :]).astype(jnp.float32)
    bias_block = (projected + chain_gain[:, None, None] * same_chain[None]).astype(jnp.bfloat16)
    bias_keys = lax.all_gather(bias_block, "rows", axis=1, tiled=True)
    single_norm, single_inv = norm_rows(single.astype(jnp.float32))
    single_b = single_norm.astype(jnp.bfloat16)
    cond_gamma = jax.nn.sigmoid(jnp.dot(single_b, w_gamma, preferred_element_type=jnp.float32))
    cond_beta = jnp.dot(single_b, w_beta, preferred_element_type=jnp.float32)
    out_gate = jax.nn.sigmoid(jnp.dot(single_b, w_outgate, preferred_element_type=jnp.float32))
    noised_f = noised.astype(jnp.float32)
    noised_norm, noised_inv = norm_rows(noised_f)
    x_b = (noised_norm * cond_gamma[None] + cond_beta[None]).astype(jnp.bfloat16)
    queries = project(x_b, w_query).astype(jnp.bfloat16)
    keys_own = project(x_b, w_key).astype(jnp.bfloat16)
    values_own = project(x_b, w_value).astype(jnp.bfloat16)
    queries_all = lax.all_gather(queries, "grp", axis=1, tiled=True)
    query_heads = queries_all.reshape(sample_count, token_total, head_count, head_size)
    key_heads = keys_own.reshape(sample_count, col_count, head_count, head_size)
    value_heads = values_own.reshape(sample_count, col_count, head_count, head_size)
    scores = (
        jnp.einsum("sihe,sjhe->shij", query_heads, key_heads, preferred_element_type=jnp.float32)
        * score_scale
        + bias_keys.astype(jnp.float32)[None]
    )
    exp_scores = jnp.exp(scores)
    exp_total = lax.psum(jnp.sum(exp_scores, axis=-1).astype(jnp.bfloat16), "grp").astype(
        jnp.float32
    )
    attn_prob = exp_scores / exp_total[..., None]
    prob_b = attn_prob.astype(jnp.bfloat16)
    attended_part = jnp.einsum(
        "shij,sjhe->sihe", prob_b, value_heads, preferred_element_type=jnp.float32
    )
    attended_part = attended_part.reshape(sample_count, token_total, model_width)
    attended = lax.psum_scatter(
        attended_part.astype(jnp.bfloat16), "grp", scatter_dimension=1, tiled=True
    )
    block_update = project(attended, w_out)
    updated = (noised_f + out_gate[None] * block_update).astype(jnp.bfloat16)
    grad_out = cotangent.astype(jnp.float32)
    gate_part = jnp.sum(grad_out * block_update, axis=0)
    grad_update = (grad_out * out_gate[None]).astype(jnp.bfloat16)
    grad_attn = project_back(grad_update, w_out).astype(jnp.bfloat16)
    grads_all = lax.all_gather(grad_attn, "grp", axis=1, tiled=True)
    grad_heads = grads_all.reshape(sample_count, token_total, head_count, head_size)
    grad_prob = jnp.einsum(
        "sihe,sjhe->shij", grad_heads, value_heads, preferred_element_type=jnp.float32
    )
    row_delta = lax.psum(
        jnp.sum(attn_prob * grad_prob, axis=-1).astype(jnp.bfloat16), "grp"
    ).astype(jnp.float32)
    grad_score = attn_prob * (grad_prob - row_delta[..., None])
    score_b = grad_score.astype(jnp.bfloat16)
    query_part = (
        jnp.einsum("shij,sjhe->sihe", score_b, key_heads, preferred_element_type=jnp.float32)
        * score_scale
    )
    query_part = query_part.reshape(sample_count, token_total, model_width)
    grad_query = lax.psum_scatter(
        query_part.astype(jnp.bfloat16), "grp", scatter_dimension=1, tiled=True
    )
    grad_key = (
        jnp.einsum("shij,sihe->sjhe", score_b, query_heads, preferred_element_type=jnp.float32)
        * score_scale
    )
    grad_value = jnp.einsum(
        "shij,sihe->sjhe", prob_b, grad_heads, preferred_element_type=jnp.float32
    )
    grad_key = grad_key.reshape(sample_count, col_count, model_width).astype(jnp.bfloat16)
    grad_value = grad_value.reshape(sample_count, col_count, model_width).astype(jnp.bfloat16)
    grad_input = (
        project_back(grad_query, w_query)
        + project_back(grad_key, w_key)
        + project_back(grad_value, w_value)
    )
    gamma_part = jnp.sum(grad_input * noised_norm, axis=0)
    beta_part = jnp.sum(grad_input, axis=0)
    gamma_sum, beta_sum, gate_sum = lax.psum((gamma_part, beta_part, gate_part), "rows")
    pre_gamma = (gamma_sum * cond_gamma * (1.0 - cond_gamma)).astype(jnp.bfloat16)
    pre_gate = (gate_sum * out_gate * (1.0 - out_gate)).astype(jnp.bfloat16)
    grad_snorm = jnp.dot(pre_gamma, w_gamma.T, preferred_element_type=jnp.float32)
    grad_snorm = grad_snorm + jnp.dot(
        beta_sum.astype(jnp.bfloat16), w_beta.T, preferred_element_type=jnp.float32
    )
    grad_snorm = grad_snorm + jnp.dot(pre_gate, w_outgate.T, preferred_element_type=jnp.float32)
    d_single = norm_back(grad_snorm, single_norm, single_inv)
    bias_part = jnp.sum(score_b, axis=0, dtype=jnp.float32)
    bias_own = lax.psum_scatter(bias_part, "rows", scatter_dimension=1, tiled=True)
    bias_grad = (bias_own * token_total).astype(jnp.bfloat16)
    grad_pairn = jnp.einsum("hij,ch->ijc", bias_grad, w_pair, preferred_element_type=jnp.float32)
    d_pair = norm_back(grad_pairn, pair_norm, pair_inv).astype(jnp.bfloat16)
    return (updated, d_single, d_pair)


def solution(mesh):
    in_specs = (
        P("grp", None),
        P("rows", "grp", None),
        P(),
        P("rows", "grp", None),
        P(),
        P(),
        P(),
        P(),
        P(),
        P(),
        P(),
        P(),
        P(),
        P("rows", "grp", None),
    )
    out_specs = (P("rows", "grp", None), P("grp", None), P("rows", "grp", None))
    groups = mesh.shape["grp"]
    row_total = mesh.shape["rows"]

    def on_device(*args):
        pair, noised, w_pair = args[1], args[3], args[11]
        fits = (
            groups == 4
            and pair.shape[0] % 32 == 0
            and pair.shape[1] % pair.shape[0] == 0
            and row_total == 8
            and noised.shape[0] == 1
            and noised.shape[1] == 192
            and w_pair.shape[1] % (2 * groups) == 0
        )
        if fits:
            return split_heads(*args, groups=groups, row_total=row_total)
        return split_keys(*args)

    return jax.shard_map(
        on_device, mesh=mesh, in_specs=in_specs, out_specs=out_specs, check_vma=False
    )
```

```python
import functools
import math

import jax
import jax.numpy as jnp
from jax import lax
from jax.experimental import pallas as pl
from jax.experimental.pallas import tpu as pltpu
from jax.sharding import PartitionSpec as P

EPSILON = 1e-05
BF16 = jnp.bfloat16
F32 = jnp.float32
LOG2_E = math.log2(math.e)
SLOT_ORDER = (0, 2, 3, 1)
VMEM_LIMIT = 56 * 1024 * 1024


def norm_rows(values):
    center = values - jnp.mean(values, axis=-1, keepdims=True)
    inverse = lax.rsqrt(jnp.mean(center * center, axis=-1, keepdims=True) + EPSILON)
    return (center * inverse, inverse)


def norm_back(grad_in, normed, inverse):
    grad_mean = jnp.mean(grad_in, axis=-1, keepdims=True)
    cross_mean = jnp.mean(grad_in * normed, axis=-1, keepdims=True)
    return inverse * (grad_in - grad_mean - normed * cross_mean)


def mm(left, right):
    return lax.dot_general(left, right, (((1,), (0,)), ((), ())), preferred_element_type=F32)


def mm_nt(left, right):
    return lax.dot_general(left, right, (((1,), (1,)), ((), ())), preferred_element_type=F32)


def mm_tn(left, right):
    return lax.dot_general(left, right, (((0,), (0,)), ((), ())), preferred_element_type=F32)


def sigmoid(values):
    return 1.0 / (1.0 + jnp.exp(-values))


def params():
    return pltpu.CompilerParams(vmem_limit_bytes=VMEM_LIMIT)


def smem():
    return pl.BlockSpec(memory_space=pltpu.SMEM)


def vmem():
    return pl.BlockSpec(memory_space=pltpu.VMEM)


def project_kernel(
    group_ref,
    single_ref,
    noised_ref,
    cot_ref,
    w_gamma_ref,
    w_beta_ref,
    w_outgate_ref,
    w_query_ref,
    w_key_ref,
    w_value_ref,
    w_out_ref,
    *rest,
    groups,
    calls,
    head_size,
):
    send_refs = rest[:groups]
    gamma_ref, gate_ref, stage_ref = rest[groups:]
    width = stage_ref.shape[2]
    part = width // (4 * calls)
    group_own = group_ref[0]
    single_norm, _ = norm_rows(single_ref[...].astype(F32))
    single_b = single_norm.astype(BF16)
    cond_gamma = sigmoid(mm(single_b, w_gamma_ref[...]))
    gamma_ref[...] = cond_gamma
    out_gate = sigmoid(mm(single_b, w_outgate_ref[...]))
    gate_ref[...] = out_gate
    cond_beta = mm(single_b, w_beta_ref[...])
    noised_norm, _ = norm_rows(noised_ref[...].astype(F32))
    x_b = (noised_norm * cond_gamma + cond_beta).astype(BF16)

    def put(kind, values):
        rounded = values.astype(BF16)
        for group in range(groups):
            slot = group_own ^ group
            for call in range(calls):
                feature = (group * calls + call) * part
                lane = (call * 4 + kind) * part
                stage_ref[slot, :, lane : lane + part] = rounded[:, feature : feature + part]

    put(0, mm(x_b, w_query_ref[...]) * (LOG2_E / math.sqrt(head_size)))
    put(1, mm(x_b, w_key_ref[...]))
    put(2, mm(x_b, w_value_ref[...]))
    grad_update = (cot_ref[...].astype(F32) * out_gate).astype(BF16)
    put(3, mm_nt(grad_update, w_out_ref[...]))
    for slot in range(groups):
        send_refs[SLOT_ORDER.index(slot)][...] = stage_ref[slot]


def lane_tiles(cols):
    return [(tile, tile * 128, min(cols, tile * 128 + 128)) for tile in range(-(-cols // 128))]


def mean_matrix(channels):
    first = lax.broadcasted_iota(jnp.int32, (2 * channels, 2 * channels), 0) >= channels
    second = lax.broadcasted_iota(jnp.int32, (2 * channels, 2 * channels), 1) >= channels
    return jnp.where(first == second, 1.0 / channels, 0.0).astype(BF16)


def center_rows(pair_ref, first, batch, means):
    _, _, cols, channels = pair_ref.shape
    both = jnp.concatenate(
        [pair_ref[side, first : first + batch].reshape(batch * cols, channels) for side in range(2)],
        axis=1,
    )
    return both.astype(F32) - mm(both, means)


def lane_pad(block, before, total):
    rows, width = block.shape
    pieces = [block]
    if before:
        pieces = [jnp.zeros((rows, before), block.dtype)] + pieces
    if total > before + width:
        pieces = pieces + [jnp.zeros((rows, total - before - width), block.dtype)]
    return jnp.concatenate(pieces, axis=1)


def bias_kernel(
    group_ref,
    rows_ref,
    chains_ref,
    gain_ref,
    pair_ref,
    w_pair_ref,
    cols_ref,
    *rest,
    groups,
    batch,
):
    send_refs = rest[:groups]
    stats_ref, flat_ref, gains_ref, stage_ref = rest[groups:]
    _, step, cols, channels = pair_ref.shape
    heads = gain_ref.shape[0]
    per_group = heads // groups
    half = step * pl.num_programs(0)
    group_own = group_ref[0]
    row_base = rows_ref[0] * 2 * half + pl.program_id(0) * step
    means = mean_matrix(channels)
    weight = w_pair_ref[...].astype(F32).T.astype(BF16)
    mean_part = jnp.full((channels, heads), 1.0 / channels, BF16)
    mixed = []
    for inner in range(2):
        for part, offset in ((weight, 0), (mean_part, heads)):
            for side in range(2):
                mixed.append(lane_pad(part, 2 * heads * (2 * inner + side) + offset, 8 * heads))
    mixed = jnp.concatenate(mixed, axis=0)
    chain_all = cols_ref[...].reshape(1, groups * cols)
    chain_cols = chain_all[:, :cols]
    for group in range(1, groups):
        here = chain_all[:, group * cols : (group + 1) * cols]
        chain_cols = jnp.where(group_own == group, here, chain_cols)
    for head in range(heads):
        gains_ref[head : head + 1, :] = jnp.full((1, cols), gain_ref[head] * LOG2_E, F32)

    for first in range(0, step, batch):
        center = center_rows(pair_ref, first, batch, means)
        center_b = center.astype(BF16)
        square = (center * center).astype(BF16)
        for base in range(0, batch, 2):
            one = slice(base * cols, (base + 1) * cols)
            two = slice((base + 1) * cols, (base + 2) * cols)
            left = jnp.concatenate(
                [center_b[one], square[one], center_b[two], square[two]], axis=1
            )
            sums = mm(left, mixed).T
            for inner in range(2):
                row = first + base + inner
                for side in range(2):
                    top = 2 * heads * (2 * inner + side)
                    inverse = lax.rsqrt(sums[top + heads : top + 2 * heads] + EPSILON)
                    projected = sums[top : top + heads] * inverse
                    stats_ref[side, row, :heads, :] = projected
                    stats_ref[side, row, heads:, :] = inverse[:8]
                    chain = chains_ref[row_base + side * half + row]
                    same = (chain_cols == chain).astype(F32)
                    values = projected * LOG2_E + gains_ref[...] * same
                    for tile, start, end in lane_tiles(cols):
                        piece = lane_pad(values[:, start:end], 0, 128)
                        flat_ref[side, tile, pl.ds(row, heads, stride=step), :] = piece
    for head in range(heads):
        slot = group_own ^ (head // per_group)
        tops = slice(head * step, (head + 1) * step)
        rest_lanes = [flat_ref[side, 1, tops, : cols - 128] for side in range(2)]
        stage_ref[slot, head % per_group, 0] = flat_ref[0, 0, tops, :].astype(BF16)
        stage_ref[slot, head % per_group, 1] = flat_ref[1, 0, tops, :].astype(BF16)
        stage_ref[slot, head % per_group, 2] = jnp.concatenate(rest_lanes, axis=1).astype(BF16)
    for slot in range(groups):
        send_refs[slot][...] = stage_ref[slot]


def pair_bias(pair, w_pair, chain_gain, chains, group_index, row_index, groups):
    rows, cols, channels = pair.shape
    heads = w_pair.shape[1]
    per_group = heads // groups
    half = rows // 2
    step = 16
    tiles = -(-cols // 128)
    *sends, stats = pl.pallas_call(
        functools.partial(bias_kernel, groups=groups, batch=16),
        grid=(half // step,),
        in_specs=[
            smem(),
            smem(),
            smem(),
            smem(),
            pl.BlockSpec((2, step, cols, channels), lambda t: (0, t, 0, 0)),
            pl.BlockSpec((heads, channels), lambda t: (0, 0)),
            pl.BlockSpec((groups * cols,), lambda t: (0,)),
        ],
        out_specs=[
            pl.BlockSpec((per_group, 3, step, 128), lambda t: (0, 0, t, 0)) for _ in range(groups)
        ]
        + [pl.BlockSpec((2, step, heads + 8, cols), lambda t: (0, t, 0, 0))],
        out_shape=[
            jax.ShapeDtypeStruct((per_group, 3, half, 128), BF16) for _ in range(groups)
        ]
        + [jax.ShapeDtypeStruct((2, half, heads + 8, cols), F32)],
        scratch_shapes=[
            pltpu.VMEM((2, tiles, heads * step, 128), F32),
            pltpu.VMEM((heads, cols), F32),
            pltpu.VMEM((groups, per_group, 3, step, 128), BF16),
        ],
        compiler_params=params(),
    )(
        group_index,
        row_index,
        chains,
        chain_gain,
        pair.reshape(2, half, cols, channels),
        w_pair.T,
        chains,
    )
    return sends, stats


def pair_back_kernel(
    group_ref, pair_ref, stats_ref, w_pair_ref, *rest, groups, calls, factor, batch
):
    grad_refs = rest[: groups * calls]
    out_ref, flat_ref = rest[groups * calls :]
    _, step, cols, channels = pair_ref.shape
    per_call = grad_refs[0].shape[0]
    heads = groups * calls * per_call
    group_own = group_ref[0]
    means = mean_matrix(channels)
    weight = w_pair_ref[...].astype(F32)
    weight = (weight - jnp.mean(weight, axis=-1, keepdims=True)).astype(BF16)
    spread = lax.broadcasted_iota(jnp.int32, (heads, channels), 0)
    spread = (spread < 2).astype(F32).astype(BF16)
    block = jnp.concatenate(
        [lane_pad(weight, 0, 2 * channels), lane_pad(spread, channels, 2 * channels)], axis=0
    )
    weights = jnp.concatenate(
        [lane_pad(block, 2 * channels * place, 8 * channels) for place in range(4)], axis=0
    )
    blank = jnp.zeros((heads - 2, cols), F32)
    for number in range(groups * calls):
        call, slot = divmod(number, groups)
        source = (group_own ^ slot) * calls + call
        for head in range(per_call):
            values = grad_refs[number][head].astype(F32)
            top = pl.multiple_of((source * per_call + head) * step, step)
            for side in range(2):
                flat_ref[side, 0, pl.ds(top, step), :] = values[side]
                flat_ref[side, 1, pl.ds(top, step), : cols - 128] = values[2][
                    :, side * (cols - 128) : (side + 1) * (cols - 128)
                ]

    for first in range(0, step, batch):
        center = center_rows(pair_ref, first, batch, means)
        for base in range(0, batch, 2):
            places = [(base + inner, side) for inner in range(2) for side in range(2)]
            left = []
            for inner, side in places:
                grads = jnp.concatenate(
                    [
                        flat_ref[side, tile, pl.ds(first + inner, heads, stride=step), :][
                            :, : end - start
                        ]
                        for tile, start, end in lane_tiles(cols)
                    ],
                    axis=1,
                )
                projected = stats_ref[side, first + inner, :heads, :]
                inverse = stats_ref[side, first + inner, heads : heads + 1, :]
                cross = jnp.sum(grads * projected, axis=0, keepdims=True) * (1.0 / channels)
                scaled = grads * (inverse * factor)
                cross = cross * (inverse * inverse * factor)
                cross_high = cross.astype(BF16).astype(F32)
                left += [scaled, cross_high, cross - cross_high, blank]
            both = mm_tn(jnp.concatenate(left, axis=0).astype(BF16), weights)
            for place, (inner, side) in enumerate(places):
                rows = slice(inner * cols, (inner + 1) * cols)
                lanes = slice(side * channels, (side + 1) * channels)
                start = 2 * channels * place
                middle, end = start + channels, start + 2 * channels
                out_ref[side, first + inner] = (
                    both[:, start:middle] - center[rows, lanes] * both[:, middle:end]
                ).astype(BF16)


def pair_back(pair, stats, grads, w_pair, group_index, groups, factor):
    rows, cols, channels = pair.shape
    per_call = grads[0].shape[0]
    heads = len(grads) * per_call
    half = rows // 2
    step = 16
    tiles = -(-cols // 128)
    out = pl.pallas_call(
        functools.partial(
            pair_back_kernel, groups=groups, calls=len(grads) // groups, factor=factor, batch=8
        ),
        grid=(half // step,),
        in_specs=[
            smem(),
            pl.BlockSpec((2, step, cols, channels), lambda t: (0, t, 0, 0)),
            pl.BlockSpec((2, step, heads + 8, cols), lambda t: (0, t, 0, 0)),
            pl.BlockSpec((heads, channels), lambda t: (0, 0)),
        ]
        + [pl.BlockSpec((per_call, 3, step, 128), lambda t: (0, 0, t, 0)) for _ in grads],
        out_specs=pl.BlockSpec((2, step, cols, channels), lambda t: (0, t, 0, 0)),
        out_shape=jax.ShapeDtypeStruct((2, half, cols, channels), BF16),
        scratch_shapes=[pltpu.VMEM((2, tiles, heads * step, 128), F32)],
        compiler_params=params(),
    )(group_index, pair.reshape(2, half, cols, channels), stats, w_pair.T, *grads)
    return out.reshape(rows, cols, channels)


def unit_order(heads):
    first, second = range(heads // 2), range(heads // 2, heads)
    order = [(1, head) for head in first] + [(3, head) for head in first]
    order += [(2, head) for head in second] + [(3, head) for head in second]
    order += [(0, head) for head in range(heads)]
    order += [(2, head) for head in first] + [(1, head) for head in second]
    return order


def attention_kernel(group_ref, row_ref, *rest, groups, row_parts, head_size):
    bias_sources = rest[: row_parts + 2]
    acts_refs = rest[row_parts + 2 : row_parts + 2 + groups]
    acts_refs = acts_refs[:1] + acts_refs[-1:] + acts_refs[1:-1]
    rest = rest[row_parts + 2 + groups :]
    out_refs = rest[:groups]
    bias_refs = rest[-row_parts - 4 : -2]
    bias_done, back_done = rest[-2:]
    (
        keep_out,
        give_out,
        keep_ref,
        give_ref,
        query_ref,
        keys_ref,
        values_ref,
        grads_ref,
        query_t_ref,
        keys_t_ref,
        values_t_ref,
        bias_full,
        score_full,
        att_sum,
        gq_sum,
        gk_sum,
        gv_sum,
    ) = rest[groups : -row_parts - 4]
    heads = keep_ref.shape[1] * 2 // row_parts
    coming = [
        [
            pltpu.make_async_copy(
                source.at[:, head], bias_refs[number].at[:, head], bias_done.at[head, number]
            )
            for number, source in enumerate(bias_sources)
        ]
        for head in range(heads)
    ]
    for head_copies in coming:
        for copy in head_copies:
            copy.start()
    going = []
    group_own = group_ref[0]
    cols, width = acts_refs[0].shape
    tokens = groups * cols
    part = width // 4
    half = bias_refs[0].shape[3]
    rest_lanes = cols - 128
    scale = 1.0 / math.sqrt(head_size)
    extra = 128 - part % 128
    plain = (query_ref, keys_ref, values_ref, grads_ref)
    turned = (query_t_ref, keys_t_ref, values_t_ref)

    turns = [(slot * cols, slot * 128, 128) for slot in range(groups)]
    turns += [
        (slot * cols + 128, groups * 128 + slot * rest_lanes, rest_lanes) for slot in range(groups)
    ]
    for kind in range(4):
        lanes = slice(kind * part, (kind + 1) * part)
        if kind in (0, 3):
            for slot in range(groups):
                plain[kind][slot * cols : (slot + 1) * cols, :] = acts_refs[slot][:, lanes]
        else:
            for token, place, count in turns:
                slot, inside = divmod(token, cols)
                plain[kind][place : place + count, :] = acts_refs[slot][
                    inside : inside + count, lanes
                ]
        if kind < len(turned):
            turned[kind][...] = plain[kind][...].T

    def places(row_part):
        first = row_part * (2 * half)
        slot = group_own ^ (first // cols)
        for side in range(2):
            top = slot * cols + lax.rem(first, cols) + side * half
            yield side, pl.ds(pl.multiple_of(top, 16), half)

    def block(other, column, head, which):
        if other >= row_parts - 2 and column >= groups // 2:
            return bias_refs[other + 2][column - groups // 2, head, which]
        return bias_refs[other][column, head, which]

    lane = lax.broadcasted_iota(jnp.int32, (1, part), 1)
    zero = jnp.zeros((), BF16)
    order = unit_order(heads)
    for head in range(heads):
        bias_head, score_head = bias_full.at[head % 2], score_full.at[head % 2]
        for copy in coming[head]:
            copy.wait()
        for other in range(row_parts):
            for side, rows in places(row_ref[0] ^ other):
                lanes = slice(side * rest_lanes, (side + 1) * rest_lanes)
                tiles = [block(other, column, head, side) for column in range(groups)]
                tiles += [block(other, column, head, 2)[:, lanes] for column in range(groups)]
                bias_head[rows, :] = jnp.concatenate(tiles, axis=1)

        features = slice(head * head_size, (head + 1) * head_size)
        mine = (lane >= features.start) & (lane < features.stop)
        query = jnp.where(mine, query_ref[...], zero)
        grads = jnp.where(mine, grads_ref[...], zero)
        keys_m = jnp.where(mine, keys_ref[...], zero)
        values_m = jnp.concatenate(
            [jnp.where(mine, values_ref[...], zero), jnp.ones((tokens, extra), BF16)], axis=1
        )
        weights = jnp.exp2(mm(query, keys_t_ref[...]) + bias_head[...].astype(F32))
        weights_b = weights.astype(BF16)
        attended = mm(weights_b, values_m)
        inverse = 1.0 / attended[:, part : part + 1]
        attended = attended[:, :part] * inverse
        grads = (grads.astype(F32) * inverse).astype(BF16)
        delta = jnp.sum(attended * grads.astype(F32), axis=-1, keepdims=True)
        score = (weights * (mm(grads, values_t_ref[...]) - delta)).astype(BF16)
        score_head[...] = score
        grad_query = mm(score, keys_m)
        grad_value = mm_tn(grads, weights_b)
        if head == 0:
            att_sum[...] = attended
            gq_sum[...] = grad_query
            gv_sum[...] = grad_value
        else:
            att_sum[...] += attended
            gq_sum[...] += grad_query
            gv_sum[...] += grad_value
        gk_sum[features, :] = mm(query_t_ref[features, :], score)

        for other in range(row_parts):
            unit = order.index((other // 2, head))
            dbias_ref = give_ref if other % 2 else keep_ref
            scores = [score_head[rows, :] for _, rows in places(row_ref[0] ^ other)]
            for column in range(groups):
                start = groups * 128 + column * rest_lanes
                blocks = [score[:, column * 128 : (column + 1) * 128] for score in scores]
                blocks.append(
                    jnp.concatenate(
                        [score[:, start : start + rest_lanes] for score in scores], axis=1
                    )
                )
                dbias_ref[column, unit] = jnp.stack(blocks)
            target = give_out if other % 2 else keep_out
            copy = pltpu.make_async_copy(
                dbias_ref.at[:, unit], target.at[:, unit], back_done.at[head, other]
            )
            copy.start()
            going.append(copy)

    results = (
        gq_sum[...] * scale,
        (gk_sum[...] * math.log(2.0)).T,
        gv_sum[...].T,
        att_sum[...],
    )
    for kind, values in enumerate(results):
        rounded = values.astype(BF16)
        lanes = slice(kind * part, (kind + 1) * part)
        if kind in (0, 3):
            for slot in range(groups):
                out_refs[slot][:, lanes] = rounded[slot * cols : (slot + 1) * cols]
        else:
            for token, place, count in turns:
                slot, inside = divmod(token, cols)
                out_refs[slot][inside : inside + count, lanes] = rounded[place : place + count]
    for copy in going:
        copy.wait()


def attention(group_index, row_index, acts, bias, head_size):
    groups = len(acts)
    row_parts = len(bias) - 2
    cols, width = acts[0].shape
    tokens = groups * cols
    part = width // 4
    _, heads, _, half, _ = bias[0].shape
    units = (groups, row_parts // 2 * heads, 3, half, 128)
    anywhere = pl.BlockSpec(memory_space=pl.ANY)
    *grads, keep, give = pl.pallas_call(
        functools.partial(
            attention_kernel, groups=groups, row_parts=row_parts, head_size=head_size
        ),
        in_specs=[smem(), smem()] + [anywhere] * len(bias) + [vmem()] * groups,
        out_specs=[vmem()] * groups + [anywhere] * 2,
        out_shape=[jax.ShapeDtypeStruct((cols, width), BF16)] * groups
        + [jax.ShapeDtypeStruct(units, BF16)] * 2,
        scratch_shapes=[pltpu.VMEM(units, BF16) for _ in range(2)]
        + [pltpu.VMEM((tokens, part), BF16) for _ in range(4)]
        + [pltpu.VMEM((part, tokens), BF16) for _ in range(3)]
        + [
            pltpu.VMEM((2, tokens, tokens), BF16),
            pltpu.VMEM((2, tokens, tokens), BF16),
            pltpu.VMEM((tokens, part), F32),
            pltpu.VMEM((tokens, part), F32),
            pltpu.VMEM((part, tokens), F32),
            pltpu.VMEM((part, tokens), F32),
        ]
        + [pltpu.VMEM(block.shape, BF16) for block in bias]
        + [
            pltpu.SemaphoreType.DMA((heads, len(bias))),
            pltpu.SemaphoreType.DMA((heads, row_parts)),
        ],
        compiler_params=params(),
    )(group_index, row_index, *bias, acts[0], *acts[2:], acts[1])
    return grads, keep, give


def finish_kernel(
    group_ref,
    single_ref,
    noised_ref,
    cot_ref,
    gamma_ref,
    gate_ref,
    w_gamma_ref,
    w_beta_ref,
    w_outgate_ref,
    w_query_ref,
    w_key_ref,
    w_value_ref,
    w_out_ref,
    *rest,
    groups,
    calls,
):
    got_refs = rest[: groups * calls]
    updated_ref, d_single_ref, stage_ref = rest[groups * calls :]
    width = stage_ref.shape[3]
    part = width // 4
    for slot in range(groups):
        for call in range(calls):
            stage_ref[group_ref[0] ^ slot, call] = got_refs[
                call * groups + slot
            ][...]

    def take(kind):
        return jnp.concatenate(
            [
                stage_ref[group, call, :, kind * part : (kind + 1) * part]
                for group in range(groups)
                for call in range(calls)
            ],
            axis=1,
        )

    out_gate = gate_ref[...]
    cond_gamma = gamma_ref[...]
    block_update = mm(take(3), w_out_ref[...])
    noised = noised_ref[...].astype(F32)
    updated_ref[...] = (noised + out_gate * block_update).astype(BF16)
    gate_part = cot_ref[...].astype(F32) * block_update
    pre_gate = (gate_part * out_gate * (1.0 - out_gate)).astype(BF16)
    grad_input = mm_nt(take(0), w_query_ref[...])
    grad_input += mm_nt(take(1), w_key_ref[...])
    grad_input += mm_nt(take(2), w_value_ref[...])
    noised_norm, _ = norm_rows(noised)
    pre_gamma = (grad_input * noised_norm * cond_gamma * (1.0 - cond_gamma)).astype(BF16)
    grad_snorm = mm_nt(pre_gamma, w_gamma_ref[...])
    grad_snorm += mm_nt(grad_input.astype(BF16), w_beta_ref[...])
    grad_snorm += mm_nt(pre_gate, w_outgate_ref[...])
    single_norm, single_inv = norm_rows(single_ref[...].astype(F32))
    d_single_ref[...] = norm_back(grad_snorm, single_norm, single_inv).astype(BF16)


def swap_groups(sends):
    groups = len(sends)
    order = SLOT_ORDER[1:]
    got = []
    for bits in order:
        perm = [(index, index ^ bits) for index in range(groups)]
        got.append(lax.ppermute(sends[bits], "grp", perm))
    got = dict(zip(order, lax.optimization_barrier(got)))
    return [sends[0]] + [got[bits] for bits in range(1, groups)]


def flip_rows(values, bits, row_total):
    return lax.ppermute(values, "rows", [(index, index ^ bits) for index in range(row_total)])


def gather_rows(own, acts, row_total):
    half = own.shape[0] // 2
    near = flip_rows(own, 2, row_total)
    far = flip_rows(own, 4, row_total)
    first = flip_rows(near[:half], 4, row_total)
    second = flip_rows(far[half:], 2, row_total)
    acts[2], acts[3], acts[1], first, second = lax.optimization_barrier(
        (acts[2], acts[3], acts[1], first, second)
    )
    blocks = []
    for block in (own, near, far, first, second):
        blocks += [block, flip_rows(block, 1, row_total)]
    return blocks, acts


def scatter_rows(keep, give, row_total):
    got = flip_rows(give, 1, row_total)
    early = keep.shape[1] // 2
    heads = early // 2
    part = heads // 2

    def add(first, count, *others):
        total = keep[:, first : first + count].astype(F32)
        total += got[:, first : first + count].astype(F32)
        for other in others:
            total += other.astype(F32)
        return total.astype(BF16)

    near = flip_rows(add(0, heads), 2, row_total)
    far = flip_rows(add(heads, heads), 4, row_total)
    far_two = flip_rows(add(early + heads, part, near[:, part:]), 4, row_total)
    near_two = flip_rows(add(early + heads + part, part, far[:, part:]), 2, row_total)
    own = add(early, heads, jnp.concatenate([near[:, :part], far[:, :part]], axis=1))
    return own, far_two, near_two


def add_last(own, far_two, near_two):
    last = jnp.concatenate([far_two, near_two], axis=1)
    total = (own.astype(F32) + last.astype(F32)).astype(BF16)
    return [total[slot] for slot in range(total.shape[0])]


def sum_rows(mine, d_pair, row_total):
    parts = [flip_rows(mine, bits, row_total) for bits in (2, 4, 6)]
    parts, d_pair = lax.optimization_barrier((parts, d_pair))
    near, far, last = (part.astype(F32) for part in parts)
    chips = ((mine.astype(F32) + near) + (far + last)).astype(BF16)
    return chips.astype(F32) + flip_rows(chips, 1, row_total).astype(F32), d_pair


def split_heads(
    single,
    pair,
    chains,
    noised,
    w_gamma,
    w_beta,
    w_outgate,
    w_query,
    w_key,
    w_value,
    w_out,
    w_pair,
    chain_gain,
    cotangent,
    *,
    groups,
    row_total,
):
    cols, _ = single.shape
    tokens = chains.shape[0]
    width = noised.shape[2]
    head_size = width // w_pair.shape[1]
    calls = 1
    row_index = lax.axis_index("rows").reshape(1)
    group_index = lax.axis_index("grp").reshape(1)
    bias_send, stats = pair_bias(
        pair, w_pair, chain_gain, chains, group_index, row_index, groups
    )
    bias_got = swap_groups(bias_send)
    noised = noised[0]
    cotangent = cotangent[0]
    *acts_send, cond_gamma, out_gate = pl.pallas_call(
        functools.partial(
            project_kernel, groups=groups, calls=calls, head_size=head_size
        ),
        in_specs=[smem()] + [vmem()] * 10,
        out_shape=[
            jax.ShapeDtypeStruct((cols, 4 * width // groups), BF16) for _ in range(groups)
        ]
        + [
            jax.ShapeDtypeStruct((cols, width), F32),
            jax.ShapeDtypeStruct((cols, width), F32),
        ],
        scratch_shapes=[pltpu.VMEM((groups, cols, 4 * width // groups), BF16)],
        compiler_params=params(),
    )(
        group_index,
        single,
        noised,
        cotangent,
        w_gamma,
        w_beta,
        w_outgate,
        w_query,
        w_key,
        w_value,
        w_out,
    )
    bias_got, _ = lax.optimization_barrier((bias_got, acts_send))
    acts_send = [acts_send[SLOT_ORDER.index(slot)] for slot in range(groups)]
    acts = swap_groups(acts_send)
    bias_all, acts = gather_rows(jnp.stack(bias_got), acts, row_total)
    grads_send, keep, give = attention(group_index, row_index, acts, bias_all, head_size)
    grads = swap_groups(grads_send)
    own, far_two, near_two = scatter_rows(keep, give, row_total)
    far_two, near_two, grads = lax.optimization_barrier((far_two, near_two, grads))
    dbias_own, grads = lax.optimization_barrier((add_last(own, far_two, near_two), grads))
    dbias_back = swap_groups(dbias_own)
    updated, d_part = pl.pallas_call(
        functools.partial(finish_kernel, groups=groups, calls=calls),
        in_specs=[smem()] + [vmem()] * (12 + groups * calls),
        out_shape=[
            jax.ShapeDtypeStruct((cols, width), BF16),
            jax.ShapeDtypeStruct(single.shape, BF16),
        ],
        scratch_shapes=[pltpu.VMEM((groups, calls, cols, 4 * width // (groups * calls)), BF16)],
        compiler_params=params(),
    )(
        group_index,
        single,
        noised,
        cotangent,
        cond_gamma,
        out_gate,
        w_gamma,
        w_beta,
        w_outgate,
        w_query,
        w_key,
        w_value,
        w_out,
        *grads,
    )
    d_pair = pair_back(pair, stats, dbias_back, w_pair, group_index, groups, float(tokens))
    d_single, d_pair = sum_rows(d_part, d_pair, row_total)
    return (updated[None], d_single, d_pair)


def project(acts, weight):
    return jnp.einsum("std,de->ste", acts, weight, preferred_element_type=F32)


def project_back(acts, weight):
    return jnp.einsum("ste,de->std", acts, weight, preferred_element_type=F32)


def split_keys(
    single,
    pair,
    chains,
    noised,
    w_gamma,
    w_beta,
    w_outgate,
    w_query,
    w_key,
    w_value,
    w_out,
    w_pair,
    chain_gain,
    cotangent,
):
    col_count = single.shape[0]
    row_count = pair.shape[0]
    head_count = w_pair.shape[1]
    model_width = w_query.shape[0]
    head_size = model_width // head_count
    sample_count = noised.shape[0]
    token_total = chains.shape[0]
    score_scale = 1.0 / math.sqrt(head_size)
    row_index = lax.axis_index("rows")
    group_index = lax.axis_index("grp")
    chain_rows = lax.dynamic_slice_in_dim(chains, row_index * row_count, row_count)
    chain_cols = lax.dynamic_slice_in_dim(chains, group_index * col_count, col_count)
    pair_norm, pair_inv = norm_rows(pair.astype(jnp.float32))
    projected = jnp.einsum(
        "ijc,ch->hij", pair_norm.astype(jnp.bfloat16), w_pair, preferred_element_type=jnp.float32
    )
    same_chain = (chain_rows[:, None] == chain_cols[None, :]).astype(jnp.float32)
    bias_block = (projected + chain_gain[:, None, None] * same_chain[None]).astype(jnp.bfloat16)
    bias_keys = lax.all_gather(bias_block, "rows", axis=1, tiled=True)
    single_norm, single_inv = norm_rows(single.astype(jnp.float32))
    single_b = single_norm.astype(jnp.bfloat16)
    cond_gamma = jax.nn.sigmoid(jnp.dot(single_b, w_gamma, preferred_element_type=jnp.float32))
    cond_beta = jnp.dot(single_b, w_beta, preferred_element_type=jnp.float32)
    out_gate = jax.nn.sigmoid(jnp.dot(single_b, w_outgate, preferred_element_type=jnp.float32))
    noised_f = noised.astype(jnp.float32)
    noised_norm, noised_inv = norm_rows(noised_f)
    x_b = (noised_norm * cond_gamma[None] + cond_beta[None]).astype(jnp.bfloat16)
    queries = project(x_b, w_query).astype(jnp.bfloat16)
    keys_own = project(x_b, w_key).astype(jnp.bfloat16)
    values_own = project(x_b, w_value).astype(jnp.bfloat16)
    queries_all = lax.all_gather(queries, "grp", axis=1, tiled=True)
    query_heads = queries_all.reshape(sample_count, token_total, head_count, head_size)
    key_heads = keys_own.reshape(sample_count, col_count, head_count, head_size)
    value_heads = values_own.reshape(sample_count, col_count, head_count, head_size)
    scores = (
        jnp.einsum("sihe,sjhe->shij", query_heads, key_heads, preferred_element_type=jnp.float32)
        * score_scale
        + bias_keys.astype(jnp.float32)[None]
    )
    exp_scores = jnp.exp(scores)
    exp_total = lax.psum(jnp.sum(exp_scores, axis=-1).astype(jnp.bfloat16), "grp").astype(
        jnp.float32
    )
    attn_prob = exp_scores / exp_total[..., None]
    prob_b = attn_prob.astype(jnp.bfloat16)
    attended_part = jnp.einsum(
        "shij,sjhe->sihe", prob_b, value_heads, preferred_element_type=jnp.float32
    )
    attended_part = attended_part.reshape(sample_count, token_total, model_width)
    attended = lax.psum_scatter(
        attended_part.astype(jnp.bfloat16), "grp", scatter_dimension=1, tiled=True
    )
    block_update = project(attended, w_out)
    updated = (noised_f + out_gate[None] * block_update).astype(jnp.bfloat16)
    grad_out = cotangent.astype(jnp.float32)
    gate_part = jnp.sum(grad_out * block_update, axis=0)
    grad_update = (grad_out * out_gate[None]).astype(jnp.bfloat16)
    grad_attn = project_back(grad_update, w_out).astype(jnp.bfloat16)
    grads_all = lax.all_gather(grad_attn, "grp", axis=1, tiled=True)
    grad_heads = grads_all.reshape(sample_count, token_total, head_count, head_size)
    grad_prob = jnp.einsum(
        "sihe,sjhe->shij", grad_heads, value_heads, preferred_element_type=jnp.float32
    )
    row_delta = lax.psum(
        jnp.sum(attn_prob * grad_prob, axis=-1).astype(jnp.bfloat16), "grp"
    ).astype(jnp.float32)
    grad_score = attn_prob * (grad_prob - row_delta[..., None])
    score_b = grad_score.astype(jnp.bfloat16)
    query_part = (
        jnp.einsum("shij,sjhe->sihe", score_b, key_heads, preferred_element_type=jnp.float32)
        * score_scale
    )
    query_part = query_part.reshape(sample_count, token_total, model_width)
    grad_query = lax.psum_scatter(
        query_part.astype(jnp.bfloat16), "grp", scatter_dimension=1, tiled=True
    )
    grad_key = (
        jnp.einsum("shij,sihe->sjhe", score_b, query_heads, preferred_element_type=jnp.float32)
        * score_scale
    )
    grad_value = jnp.einsum(
        "shij,sihe->sjhe", prob_b, grad_heads, preferred_element_type=jnp.float32
    )
    grad_key = grad_key.reshape(sample_count, col_count, model_width).astype(jnp.bfloat16)
    grad_value = grad_value.reshape(sample_count, col_count, model_width).astype(jnp.bfloat16)
    grad_input = (
        project_back(grad_query, w_query)
        + project_back(grad_key, w_key)
        + project_back(grad_value, w_value)
    )
    gamma_part = jnp.sum(grad_input * noised_norm, axis=0)
    beta_part = jnp.sum(grad_input, axis=0)
    gamma_sum, beta_sum, gate_sum = lax.psum((gamma_part, beta_part, gate_part), "rows")
    pre_gamma = (gamma_sum * cond_gamma * (1.0 - cond_gamma)).astype(jnp.bfloat16)
    pre_gate = (gate_sum * out_gate * (1.0 - out_gate)).astype(jnp.bfloat16)
    grad_snorm = jnp.dot(pre_gamma, w_gamma.T, preferred_element_type=jnp.float32)
    grad_snorm = grad_snorm + jnp.dot(
        beta_sum.astype(jnp.bfloat16), w_beta.T, preferred_element_type=jnp.float32
    )
    grad_snorm = grad_snorm + jnp.dot(pre_gate, w_outgate.T, preferred_element_type=jnp.float32)
    d_single = norm_back(grad_snorm, single_norm, single_inv)
    bias_part = jnp.sum(score_b, axis=0, dtype=jnp.float32)
    bias_own = lax.psum_scatter(bias_part, "rows", scatter_dimension=1, tiled=True)
    bias_grad = (bias_own * token_total).astype(jnp.bfloat16)
    grad_pairn = jnp.einsum("hij,ch->ijc", bias_grad, w_pair, preferred_element_type=jnp.float32)
    d_pair = norm_back(grad_pairn, pair_norm, pair_inv).astype(jnp.bfloat16)
    return (updated, d_single, d_pair)


def solution(mesh):
    in_specs = (
        P("grp", None),
        P("rows", "grp", None),
        P(),
        P("rows", "grp", None),
        P(),
        P(),
        P(),
        P(),
        P(),
        P(),
        P(),
        P(),
        P(),
        P("rows", "grp", None),
    )
    out_specs = (P("rows", "grp", None), P("grp", None), P("rows", "grp", None))
    groups = mesh.shape["grp"]
    row_total = mesh.shape["rows"]

    def on_device(*args):
        pair, noised, w_pair = args[1], args[3], args[11]
        fits = (
            groups == 4
            and pair.shape[0] % 32 == 0
            and pair.shape[1] % pair.shape[0] == 0
            and row_total == 8
            and noised.shape[0] == 1
            and noised.shape[1] == 192
            and w_pair.shape[1] % (2 * groups) == 0
        )
        if fits:
            return split_heads(*args, groups=groups, row_total=row_total)
        return split_keys(*args)

    return jax.shard_map(
        on_device, mesh=mesh, in_specs=in_specs, out_specs=out_specs, check_vma=False
    )
```

```python
import functools
import math

import jax
import jax.numpy as jnp
from jax import lax
from jax.experimental import pallas as pl
from jax.experimental.pallas import tpu as pltpu
from jax.sharding import PartitionSpec as P

EPSILON = 1e-05
BF16 = jnp.bfloat16
F32 = jnp.float32
LOG2_E = math.log2(math.e)
SLOT_ORDER = (0, 2, 3, 1)
VMEM_LIMIT = 56 * 1024 * 1024


def norm_rows(values):
    center = values - jnp.mean(values, axis=-1, keepdims=True)
    inverse = lax.rsqrt(jnp.mean(center * center, axis=-1, keepdims=True) + EPSILON)
    return (center * inverse, inverse)


def norm_back(grad_in, normed, inverse):
    grad_mean = jnp.mean(grad_in, axis=-1, keepdims=True)
    cross_mean = jnp.mean(grad_in * normed, axis=-1, keepdims=True)
    return inverse * (grad_in - grad_mean - normed * cross_mean)


def mm(left, right):
    return lax.dot_general(left, right, (((1,), (0,)), ((), ())), preferred_element_type=F32)


def mm_nt(left, right):
    return lax.dot_general(left, right, (((1,), (1,)), ((), ())), preferred_element_type=F32)


def mm_tn(left, right):
    return lax.dot_general(left, right, (((0,), (0,)), ((), ())), preferred_element_type=F32)


def sigmoid(values):
    return 1.0 / (1.0 + jnp.exp(-values))


def params():
    return pltpu.CompilerParams(vmem_limit_bytes=VMEM_LIMIT)


def smem():
    return pl.BlockSpec(memory_space=pltpu.SMEM)


def vmem():
    return pl.BlockSpec(memory_space=pltpu.VMEM)


def project_kernel(
    group_ref,
    single_ref,
    noised_ref,
    cot_ref,
    w_gamma_ref,
    w_beta_ref,
    w_outgate_ref,
    w_query_ref,
    w_key_ref,
    w_value_ref,
    w_out_ref,
    *rest,
    groups,
    calls,
    head_size,
):
    send_refs = rest[:groups]
    gamma_ref, gate_ref, stage_ref = rest[groups:]
    width = stage_ref.shape[2]
    part = width // (4 * calls)
    group_own = group_ref[0]
    single_norm, _ = norm_rows(single_ref[...].astype(F32))
    single_b = single_norm.astype(BF16)
    cond_gamma = sigmoid(mm(single_b, w_gamma_ref[...]))
    gamma_ref[...] = cond_gamma
    out_gate = sigmoid(mm(single_b, w_outgate_ref[...]))
    gate_ref[...] = out_gate
    cond_beta = mm(single_b, w_beta_ref[...])
    noised_norm, _ = norm_rows(noised_ref[...].astype(F32))
    x_b = (noised_norm * cond_gamma + cond_beta).astype(BF16)

    def put(kind, values):
        rounded = values.astype(BF16)
        for group in range(groups):
            slot = group_own ^ group
            for call in range(calls):
                feature = (group * calls + call) * part
                lane = (call * 4 + kind) * part
                stage_ref[slot, :, lane : lane + part] = rounded[:, feature : feature + part]

    put(0, mm(x_b, w_query_ref[...]) * (LOG2_E / math.sqrt(head_size)))
    put(1, mm(x_b, w_key_ref[...]))
    put(2, mm(x_b, w_value_ref[...]))
    grad_update = (cot_ref[...].astype(F32) * out_gate).astype(BF16)
    put(3, mm_nt(grad_update, w_out_ref[...]))
    for slot in range(groups):
        send_refs[SLOT_ORDER.index(slot)][...] = stage_ref[slot]


def lane_tiles(cols):
    return [(tile, tile * 128, min(cols, tile * 128 + 128)) for tile in range(-(-cols // 128))]


def center_rows(pair_ref, first, batch):
    _, _, cols, channels = pair_ref.shape
    halves = []
    for side in range(2):
        rows = pair_ref[side, first : first + batch].reshape(batch * cols, channels).astype(F32)
        halves.append(rows - jnp.sum(rows, axis=-1, keepdims=True) * (1.0 / channels))
    return jnp.concatenate(halves, axis=1)


def lane_pad(block, before, total):
    rows, width = block.shape
    pieces = [block]
    if before:
        pieces = [jnp.zeros((rows, before), block.dtype)] + pieces
    if total > before + width:
        pieces = pieces + [jnp.zeros((rows, total - before - width), block.dtype)]
    return jnp.concatenate(pieces, axis=1)


def bias_kernel(
    group_ref,
    rows_ref,
    chains_ref,
    gain_ref,
    pair_ref,
    w_pair_ref,
    cols_ref,
    *rest,
    groups,
    batch,
):
    send_refs = rest[:groups]
    stats_ref, flat_ref, gains_ref, stage_ref = rest[groups:]
    _, step, cols, channels = pair_ref.shape
    heads = gain_ref.shape[0]
    per_group = heads // groups
    half = step * pl.num_programs(0)
    group_own = group_ref[0]
    row_base = rows_ref[0] * 2 * half + pl.program_id(0) * step
    weight = w_pair_ref[...].astype(F32).T.astype(BF16)
    mean_part = jnp.full((channels, heads), 1.0 / channels, BF16)
    mixed = []
    for inner in range(2):
        for part, offset in ((weight, 0), (mean_part, heads)):
            for side in range(2):
                mixed.append(lane_pad(part, 2 * heads * (2 * inner + side) + offset, 8 * heads))
    mixed = jnp.concatenate(mixed, axis=0)
    chain_all = cols_ref[...].reshape(1, groups * cols)
    chain_cols = chain_all[:, :cols]
    for group in range(1, groups):
        here = chain_all[:, group * cols : (group + 1) * cols]
        chain_cols = jnp.where(group_own == group, here, chain_cols)
    for head in range(heads):
        gains_ref[head : head + 1, :] = jnp.full((1, cols), gain_ref[head] * LOG2_E, F32)

    for first in range(0, step, batch):
        center = center_rows(pair_ref, first, batch)
        center_b = center.astype(BF16)
        square = (center * center).astype(BF16)
        for base in range(0, batch, 2):
            one = slice(base * cols, (base + 1) * cols)
            two = slice((base + 1) * cols, (base + 2) * cols)
            left = jnp.concatenate(
                [center_b[one], square[one], center_b[two], square[two]], axis=1
            )
            sums = mm(left, mixed).T
            for inner in range(2):
                row = first + base + inner
                for side in range(2):
                    top = 2 * heads * (2 * inner + side)
                    inverse = lax.rsqrt(sums[top + heads : top + 2 * heads] + EPSILON)
                    projected = sums[top : top + heads] * inverse
                    stats_ref[side, row, :heads, :] = projected
                    stats_ref[side, row, heads:, :] = inverse[:8]
                    chain = chains_ref[row_base + side * half + row]
                    same = (chain_cols == chain).astype(F32)
                    values = projected * LOG2_E + gains_ref[...] * same
                    for tile, start, end in lane_tiles(cols):
                        piece = lane_pad(values[:, start:end], 0, 128)
                        flat_ref[side, tile, pl.ds(row, heads, stride=step), :] = piece
    for head in range(heads):
        slot = group_own ^ (head // per_group)
        tops = slice(head * step, (head + 1) * step)
        rest_lanes = [flat_ref[side, 1, tops, : cols - 128] for side in range(2)]
        stage_ref[slot, head % per_group, 0] = flat_ref[0, 0, tops, :].astype(BF16)
        stage_ref[slot, head % per_group, 1] = flat_ref[1, 0, tops, :].astype(BF16)
        stage_ref[slot, head % per_group, 2] = jnp.concatenate(rest_lanes, axis=1).astype(BF16)
    for slot in range(groups):
        send_refs[slot][...] = stage_ref[slot]


def pair_bias(pair, w_pair, chain_gain, chains, group_index, row_index, groups):
    rows, cols, channels = pair.shape
    heads = w_pair.shape[1]
    per_group = heads // groups
    half = rows // 2
    step = 16
    tiles = -(-cols // 128)
    *sends, stats = pl.pallas_call(
        functools.partial(bias_kernel, groups=groups, batch=16),
        grid=(half // step,),
        in_specs=[
            smem(),
            smem(),
            smem(),
            smem(),
            pl.BlockSpec((2, step, cols, channels), lambda t: (0, t, 0, 0)),
            pl.BlockSpec((heads, channels), lambda t: (0, 0)),
            pl.BlockSpec((groups * cols,), lambda t: (0,)),
        ],
        out_specs=[
            pl.BlockSpec((per_group, 3, step, 128), lambda t: (0, 0, t, 0)) for _ in range(groups)
        ]
        + [pl.BlockSpec((2, step, heads + 8, cols), lambda t: (0, t, 0, 0))],
        out_shape=[
            jax.ShapeDtypeStruct((per_group, 3, half, 128), BF16) for _ in range(groups)
        ]
        + [jax.ShapeDtypeStruct((2, half, heads + 8, cols), F32)],
        scratch_shapes=[
            pltpu.VMEM((2, tiles, heads * step, 128), F32),
            pltpu.VMEM((heads, cols), F32),
            pltpu.VMEM((groups, per_group, 3, step, 128), BF16),
        ],
        compiler_params=params(),
    )(
        group_index,
        row_index,
        chains,
        chain_gain,
        pair.reshape(2, half, cols, channels),
        w_pair.T,
        chains,
    )
    return sends, stats


def pair_back_kernel(
    group_ref, pair_ref, stats_ref, w_pair_ref, *rest, groups, calls, factor, batch
):
    grad_refs = rest[: groups * calls]
    out_ref, flat_ref = rest[groups * calls :]
    _, step, cols, channels = pair_ref.shape
    per_call = grad_refs[0].shape[0]
    heads = groups * calls * per_call
    group_own = group_ref[0]
    weight = w_pair_ref[...].astype(F32)
    weight = (weight - jnp.mean(weight, axis=-1, keepdims=True)).astype(BF16)
    spread = lax.broadcasted_iota(jnp.int32, (heads, channels), 0)
    spread = (spread < 2).astype(F32).astype(BF16)
    block = jnp.concatenate(
        [lane_pad(weight, 0, 2 * channels), lane_pad(spread, channels, 2 * channels)], axis=0
    )
    weights = jnp.concatenate(
        [lane_pad(block, 2 * channels * place, 8 * channels) for place in range(4)], axis=0
    )
    blank = jnp.zeros((heads - 2, cols), F32)
    for number in range(groups * calls):
        call, slot = divmod(number, groups)
        source = (group_own ^ slot) * calls + call
        for head in range(per_call):
            values = grad_refs[number][head].astype(F32)
            top = pl.multiple_of((source * per_call + head) * step, step)
            for side in range(2):
                flat_ref[side, 0, pl.ds(top, step), :] = values[side]
                flat_ref[side, 1, pl.ds(top, step), : cols - 128] = values[2][
                    :, side * (cols - 128) : (side + 1) * (cols - 128)
                ]

    for first in range(0, step, batch):
        center = center_rows(pair_ref, first, batch)
        for base in range(0, batch, 2):
            places = [(base + inner, side) for inner in range(2) for side in range(2)]
            left = []
            for inner, side in places:
                grads = jnp.concatenate(
                    [
                        flat_ref[side, tile, pl.ds(first + inner, heads, stride=step), :][
                            :, : end - start
                        ]
                        for tile, start, end in lane_tiles(cols)
                    ],
                    axis=1,
                )
                projected = stats_ref[side, first + inner, :heads, :]
                inverse = stats_ref[side, first + inner, heads : heads + 1, :]
                cross = jnp.sum(grads * projected, axis=0, keepdims=True) * (1.0 / channels)
                scaled = grads * (inverse * factor)
                cross = cross * (inverse * inverse * factor)
                cross_high = cross.astype(BF16).astype(F32)
                left += [scaled, cross_high, cross - cross_high, blank]
            both = mm_tn(jnp.concatenate(left, axis=0).astype(BF16), weights)
            for place, (inner, side) in enumerate(places):
                rows = slice(inner * cols, (inner + 1) * cols)
                lanes = slice(side * channels, (side + 1) * channels)
                start = 2 * channels * place
                middle, end = start + channels, start + 2 * channels
                out_ref[side, first + inner] = (
                    both[:, start:middle] - center[rows, lanes] * both[:, middle:end]
                ).astype(BF16)


def pair_back(pair, stats, grads, w_pair, group_index, groups, factor):
    rows, cols, channels = pair.shape
    per_call = grads[0].shape[0]
    heads = len(grads) * per_call
    half = rows // 2
    step = 16
    tiles = -(-cols // 128)
    out = pl.pallas_call(
        functools.partial(
            pair_back_kernel, groups=groups, calls=len(grads) // groups, factor=factor, batch=8
        ),
        grid=(half // step,),
        in_specs=[
            smem(),
            pl.BlockSpec((2, step, cols, channels), lambda t: (0, t, 0, 0)),
            pl.BlockSpec((2, step, heads + 8, cols), lambda t: (0, t, 0, 0)),
            pl.BlockSpec((heads, channels), lambda t: (0, 0)),
        ]
        + [pl.BlockSpec((per_call, 3, step, 128), lambda t: (0, 0, t, 0)) for _ in grads],
        out_specs=pl.BlockSpec((2, step, cols, channels), lambda t: (0, t, 0, 0)),
        out_shape=jax.ShapeDtypeStruct((2, half, cols, channels), BF16),
        scratch_shapes=[pltpu.VMEM((2, tiles, heads * step, 128), F32)],
        compiler_params=params(),
    )(group_index, pair.reshape(2, half, cols, channels), stats, w_pair.T, *grads)
    return out.reshape(rows, cols, channels)


def unit_order(heads):
    first, second = range(heads // 2), range(heads // 2, heads)
    order = [(1, head) for head in first] + [(3, head) for head in first]
    order += [(2, head) for head in second] + [(3, head) for head in second]
    order += [(0, head) for head in range(heads)]
    order += [(2, head) for head in first] + [(1, head) for head in second]
    return order


def attention_kernel(group_ref, row_ref, *rest, groups, row_parts, head_size):
    bias_refs = rest[: row_parts + 2]
    acts_refs = rest[row_parts + 2 : row_parts + 2 + groups]
    acts_refs = acts_refs[:1] + acts_refs[-1:] + acts_refs[1:-1]
    rest = rest[row_parts + 2 + groups :]
    out_refs = rest[:groups]
    (
        keep_ref,
        give_ref,
        query_ref,
        keys_ref,
        values_ref,
        grads_ref,
        query_t_ref,
        keys_t_ref,
        values_t_ref,
        bias_full,
        score_full,
        att_sum,
        gq_sum,
        gk_sum,
        gv_sum,
    ) = rest[groups:]
    heads = keep_ref.shape[1] * 2 // row_parts
    group_own = group_ref[0]
    cols, width = acts_refs[0].shape
    tokens = groups * cols
    part = width // 4
    half = bias_refs[0].shape[3]
    rest_lanes = cols - 128
    scale = 1.0 / math.sqrt(head_size)
    extra = 128 - part % 128
    plain = (query_ref, keys_ref, values_ref, grads_ref)
    turned = (query_t_ref, keys_t_ref, values_t_ref)

    turns = [(slot * cols, slot * 128, 128) for slot in range(groups)]
    turns += [
        (slot * cols + 128, groups * 128 + slot * rest_lanes, rest_lanes) for slot in range(groups)
    ]
    for kind in range(4):
        lanes = slice(kind * part, (kind + 1) * part)
        if kind in (0, 3):
            for slot in range(groups):
                plain[kind][slot * cols : (slot + 1) * cols, :] = acts_refs[slot][:, lanes]
        else:
            for token, place, count in turns:
                slot, inside = divmod(token, cols)
                plain[kind][place : place + count, :] = acts_refs[slot][
                    inside : inside + count, lanes
                ]
        if kind < len(turned):
            turned[kind][...] = plain[kind][...].T

    def places(row_part):
        first = row_part * (2 * half)
        slot = group_own ^ (first // cols)
        for side in range(2):
            top = slot * cols + lax.rem(first, cols) + side * half
            yield side, pl.ds(pl.multiple_of(top, 16), half)

    def block(other, column, head, which):
        if other >= row_parts - 2 and column >= groups // 2:
            return bias_refs[other + 2][column - groups // 2, head, which]
        return bias_refs[other][column, head, which]

    lane = lax.broadcasted_iota(jnp.int32, (1, part), 1)
    zero = jnp.zeros((), BF16)
    order = unit_order(heads)
    for head in range(heads):
        bias_head, score_head = bias_full.at[head % 2], score_full.at[head % 2]
        for other in range(row_parts):
            for side, rows in places(row_ref[0] ^ other):
                lanes = slice(side * rest_lanes, (side + 1) * rest_lanes)
                tiles = [block(other, column, head, side) for column in range(groups)]
                tiles += [block(other, column, head, 2)[:, lanes] for column in range(groups)]
                bias_head[rows, :] = jnp.concatenate(tiles, axis=1)

        features = slice(head * head_size, (head + 1) * head_size)
        mine = (lane >= features.start) & (lane < features.stop)
        query = jnp.where(mine, query_ref[...], zero)
        grads = jnp.where(mine, grads_ref[...], zero)
        keys_m = jnp.where(mine, keys_ref[...], zero)
        values_m = jnp.concatenate(
            [jnp.where(mine, values_ref[...], zero), jnp.ones((tokens, extra), BF16)], axis=1
        )
        weights = jnp.exp2(mm(query, keys_t_ref[...]) + bias_head[...].astype(F32))
        weights_b = weights.astype(BF16)
        attended = mm(weights_b, values_m)
        inverse = 1.0 / attended[:, part : part + 1]
        attended = attended[:, :part] * inverse
        grads = (grads.astype(F32) * inverse).astype(BF16)
        delta = jnp.sum(attended * grads.astype(F32), axis=-1, keepdims=True)
        score = (weights * (mm(grads, values_t_ref[...]) - delta)).astype(BF16)
        score_head[...] = score
        grad_query = mm(score, keys_m)
        grad_value = mm_tn(grads, weights_b)
        if head == 0:
            att_sum[...] = attended
            gq_sum[...] = grad_query
            gv_sum[...] = grad_value
        else:
            att_sum[...] += attended
            gq_sum[...] += grad_query
            gv_sum[...] += grad_value
        gk_sum[features, :] = mm(query_t_ref[features, :], score)

        for other in range(row_parts):
            unit = order.index((other // 2, head))
            dbias_ref = give_ref if other % 2 else keep_ref
            scores = [score_head[rows, :] for _, rows in places(row_ref[0] ^ other)]
            for column in range(groups):
                start = groups * 128 + column * rest_lanes
                blocks = [score[:, column * 128 : (column + 1) * 128] for score in scores]
                blocks.append(
                    jnp.concatenate(
                        [score[:, start : start + rest_lanes] for score in scores], axis=1
                    )
                )
                dbias_ref[column, unit] = jnp.stack(blocks)

    results = (
        gq_sum[...] * scale,
        (gk_sum[...] * math.log(2.0)).T,
        gv_sum[...].T,
        att_sum[...],
    )
    for kind, values in enumerate(results):
        rounded = values.astype(BF16)
        lanes = slice(kind * part, (kind + 1) * part)
        if kind in (0, 3):
            for slot in range(groups):
                out_refs[slot][:, lanes] = rounded[slot * cols : (slot + 1) * cols]
        else:
            for token, place, count in turns:
                slot, inside = divmod(token, cols)
                out_refs[slot][inside : inside + count, lanes] = rounded[place : place + count]


def attention(group_index, row_index, acts, bias, head_size):
    groups = len(acts)
    row_parts = len(bias) - 2
    cols, width = acts[0].shape
    tokens = groups * cols
    part = width // 4
    _, heads, _, half, _ = bias[0].shape
    units = (groups, row_parts // 2 * heads, 3, half, 128)
    *grads, keep, give = pl.pallas_call(
        functools.partial(
            attention_kernel, groups=groups, row_parts=row_parts, head_size=head_size
        ),
        in_specs=[smem(), smem()] + [vmem()] * (len(bias) + groups),
        out_shape=[jax.ShapeDtypeStruct((cols, width), BF16)] * groups
        + [jax.ShapeDtypeStruct(units, BF16)] * 2,
        scratch_shapes=[pltpu.VMEM((tokens, part), BF16) for _ in range(4)]
        + [pltpu.VMEM((part, tokens), BF16) for _ in range(3)]
        + [
            pltpu.VMEM((2, tokens, tokens), BF16),
            pltpu.VMEM((2, tokens, tokens), BF16),
            pltpu.VMEM((tokens, part), F32),
            pltpu.VMEM((tokens, part), F32),
            pltpu.VMEM((part, tokens), F32),
            pltpu.VMEM((part, tokens), F32),
        ],
        compiler_params=params(),
    )(group_index, row_index, *bias, acts[0], *acts[2:], acts[1])
    return grads, keep, give


def finish_kernel(
    group_ref,
    single_ref,
    noised_ref,
    cot_ref,
    gamma_ref,
    gate_ref,
    w_gamma_ref,
    w_beta_ref,
    w_outgate_ref,
    w_query_ref,
    w_key_ref,
    w_value_ref,
    w_out_ref,
    *rest,
    groups,
    calls,
):
    got_refs = rest[: groups * calls]
    updated_ref, d_single_ref, stage_ref = rest[groups * calls :]
    width = stage_ref.shape[3]
    part = width // 4
    for slot in range(groups):
        for call in range(calls):
            stage_ref[group_ref[0] ^ slot, call] = got_refs[
                call * groups + slot
            ][...]

    def take(kind):
        return jnp.concatenate(
            [
                stage_ref[group, call, :, kind * part : (kind + 1) * part]
                for group in range(groups)
                for call in range(calls)
            ],
            axis=1,
        )

    out_gate = gate_ref[...]
    cond_gamma = gamma_ref[...]
    block_update = mm(take(3), w_out_ref[...])
    noised = noised_ref[...].astype(F32)
    updated_ref[...] = (noised + out_gate * block_update).astype(BF16)
    gate_part = cot_ref[...].astype(F32) * block_update
    pre_gate = (gate_part * out_gate * (1.0 - out_gate)).astype(BF16)
    grad_input = mm_nt(take(0), w_query_ref[...])
    grad_input += mm_nt(take(1), w_key_ref[...])
    grad_input += mm_nt(take(2), w_value_ref[...])
    noised_norm, _ = norm_rows(noised)
    pre_gamma = (grad_input * noised_norm * cond_gamma * (1.0 - cond_gamma)).astype(BF16)
    grad_snorm = mm_nt(pre_gamma, w_gamma_ref[...])
    grad_snorm += mm_nt(grad_input.astype(BF16), w_beta_ref[...])
    grad_snorm += mm_nt(pre_gate, w_outgate_ref[...])
    single_norm, single_inv = norm_rows(single_ref[...].astype(F32))
    d_single_ref[...] = norm_back(grad_snorm, single_norm, single_inv).astype(BF16)


def swap_groups(sends):
    groups = len(sends)
    order = SLOT_ORDER[1:]
    got = []
    for bits in order:
        perm = [(index, index ^ bits) for index in range(groups)]
        got.append(lax.ppermute(sends[bits], "grp", perm))
    got = dict(zip(order, lax.optimization_barrier(got)))
    return [sends[0]] + [got[bits] for bits in range(1, groups)]


def flip_rows(values, bits, row_total):
    return lax.ppermute(values, "rows", [(index, index ^ bits) for index in range(row_total)])


def gather_rows(own, acts, row_total):
    half = own.shape[0] // 2
    near = flip_rows(own, 2, row_total)
    far = flip_rows(own, 4, row_total)
    first = flip_rows(near[:half], 4, row_total)
    second = flip_rows(far[half:], 2, row_total)
    acts[2], acts[3], acts[1], first, second = lax.optimization_barrier(
        (acts[2], acts[3], acts[1], first, second)
    )
    blocks = []
    for block in (own, near, far, first, second):
        blocks += [block, flip_rows(block, 1, row_total)]
    return blocks, acts


def scatter_rows(keep, give, row_total):
    got = flip_rows(give, 1, row_total)
    early = keep.shape[1] // 2
    heads = early // 2
    part = heads // 2

    def add(first, count, *others):
        total = keep[:, first : first + count].astype(F32)
        total += got[:, first : first + count].astype(F32)
        for other in others:
            total += other.astype(F32)
        return total.astype(BF16)

    near = flip_rows(add(0, heads), 2, row_total)
    far = flip_rows(add(heads, heads), 4, row_total)
    far_two = flip_rows(add(early + heads, part, near[:, part:]), 4, row_total)
    near_two = flip_rows(add(early + heads + part, part, far[:, part:]), 2, row_total)
    own = add(early, heads, jnp.concatenate([near[:, :part], far[:, :part]], axis=1))
    return own, far_two, near_two


def add_last(own, far_two, near_two):
    last = jnp.concatenate([far_two, near_two], axis=1)
    total = (own.astype(F32) + last.astype(F32)).astype(BF16)
    return [total[slot] for slot in range(total.shape[0])]


def sum_rows(mine, d_pair, row_total):
    parts = [flip_rows(mine, bits, row_total) for bits in (2, 4, 6)]
    parts, d_pair = lax.optimization_barrier((parts, d_pair))
    near, far, last = (part.astype(F32) for part in parts)
    chips = ((mine.astype(F32) + near) + (far + last)).astype(BF16)
    return chips.astype(F32) + flip_rows(chips, 1, row_total).astype(F32), d_pair


def split_heads(
    single,
    pair,
    chains,
    noised,
    w_gamma,
    w_beta,
    w_outgate,
    w_query,
    w_key,
    w_value,
    w_out,
    w_pair,
    chain_gain,
    cotangent,
    *,
    groups,
    row_total,
):
    cols, _ = single.shape
    tokens = chains.shape[0]
    width = noised.shape[2]
    head_size = width // w_pair.shape[1]
    calls = 1
    row_index = lax.axis_index("rows").reshape(1)
    group_index = lax.axis_index("grp").reshape(1)
    bias_send, stats = pair_bias(
        pair, w_pair, chain_gain, chains, group_index, row_index, groups
    )
    bias_got = swap_groups(bias_send)
    noised = noised[0]
    cotangent = cotangent[0]
    *acts_send, cond_gamma, out_gate = pl.pallas_call(
        functools.partial(
            project_kernel, groups=groups, calls=calls, head_size=head_size
        ),
        in_specs=[smem()] + [vmem()] * 10,
        out_shape=[
            jax.ShapeDtypeStruct((cols, 4 * width // groups), BF16) for _ in range(groups)
        ]
        + [
            jax.ShapeDtypeStruct((cols, width), F32),
            jax.ShapeDtypeStruct((cols, width), F32),
        ],
        scratch_shapes=[pltpu.VMEM((groups, cols, 4 * width // groups), BF16)],
        compiler_params=params(),
    )(
        group_index,
        single,
        noised,
        cotangent,
        w_gamma,
        w_beta,
        w_outgate,
        w_query,
        w_key,
        w_value,
        w_out,
    )
    bias_got, _ = lax.optimization_barrier((bias_got, acts_send))
    acts_send = [acts_send[SLOT_ORDER.index(slot)] for slot in range(groups)]
    acts = swap_groups(acts_send)
    bias_all, acts = gather_rows(jnp.stack(bias_got), acts, row_total)
    grads_send, keep, give = attention(group_index, row_index, acts, bias_all, head_size)
    grads = swap_groups(grads_send)
    own, far_two, near_two = scatter_rows(keep, give, row_total)
    far_two, near_two, grads = lax.optimization_barrier((far_two, near_two, grads))
    dbias_own, grads = lax.optimization_barrier((add_last(own, far_two, near_two), grads))
    dbias_back = swap_groups(dbias_own)
    updated, d_part = pl.pallas_call(
        functools.partial(finish_kernel, groups=groups, calls=calls),
        in_specs=[smem()] + [vmem()] * (12 + groups * calls),
        out_shape=[
            jax.ShapeDtypeStruct((cols, width), BF16),
            jax.ShapeDtypeStruct(single.shape, BF16),
        ],
        scratch_shapes=[pltpu.VMEM((groups, calls, cols, 4 * width // (groups * calls)), BF16)],
        compiler_params=params(),
    )(
        group_index,
        single,
        noised,
        cotangent,
        cond_gamma,
        out_gate,
        w_gamma,
        w_beta,
        w_outgate,
        w_query,
        w_key,
        w_value,
        w_out,
        *grads,
    )
    d_pair = pair_back(pair, stats, dbias_back, w_pair, group_index, groups, float(tokens))
    d_single, d_pair = sum_rows(d_part, d_pair, row_total)
    return (updated[None], d_single, d_pair)


def project(acts, weight):
    return jnp.einsum("std,de->ste", acts, weight, preferred_element_type=F32)


def project_back(acts, weight):
    return jnp.einsum("ste,de->std", acts, weight, preferred_element_type=F32)


def split_keys(
    single,
    pair,
    chains,
    noised,
    w_gamma,
    w_beta,
    w_outgate,
    w_query,
    w_key,
    w_value,
    w_out,
    w_pair,
    chain_gain,
    cotangent,
):
    col_count = single.shape[0]
    row_count = pair.shape[0]
    head_count = w_pair.shape[1]
    model_width = w_query.shape[0]
    head_size = model_width // head_count
    sample_count = noised.shape[0]
    token_total = chains.shape[0]
    score_scale = 1.0 / math.sqrt(head_size)
    row_index = lax.axis_index("rows")
    group_index = lax.axis_index("grp")
    chain_rows = lax.dynamic_slice_in_dim(chains, row_index * row_count, row_count)
    chain_cols = lax.dynamic_slice_in_dim(chains, group_index * col_count, col_count)
    pair_norm, pair_inv = norm_rows(pair.astype(jnp.float32))
    projected = jnp.einsum(
        "ijc,ch->hij", pair_norm.astype(jnp.bfloat16), w_pair, preferred_element_type=jnp.float32
    )
    same_chain = (chain_rows[:, None] == chain_cols[None, :]).astype(jnp.float32)
    bias_block = (projected + chain_gain[:, None, None] * same_chain[None]).astype(jnp.bfloat16)
    bias_keys = lax.all_gather(bias_block, "rows", axis=1, tiled=True)
    single_norm, single_inv = norm_rows(single.astype(jnp.float32))
    single_b = single_norm.astype(jnp.bfloat16)
    cond_gamma = jax.nn.sigmoid(jnp.dot(single_b, w_gamma, preferred_element_type=jnp.float32))
    cond_beta = jnp.dot(single_b, w_beta, preferred_element_type=jnp.float32)
    out_gate = jax.nn.sigmoid(jnp.dot(single_b, w_outgate, preferred_element_type=jnp.float32))
    noised_f = noised.astype(jnp.float32)
    noised_norm, noised_inv = norm_rows(noised_f)
    x_b = (noised_norm * cond_gamma[None] + cond_beta[None]).astype(jnp.bfloat16)
    queries = project(x_b, w_query).astype(jnp.bfloat16)
    keys_own = project(x_b, w_key).astype(jnp.bfloat16)
    values_own = project(x_b, w_value).astype(jnp.bfloat16)
    queries_all = lax.all_gather(queries, "grp", axis=1, tiled=True)
    query_heads = queries_all.reshape(sample_count, token_total, head_count, head_size)
    key_heads = keys_own.reshape(sample_count, col_count, head_count, head_size)
    value_heads = values_own.reshape(sample_count, col_count, head_count, head_size)
    scores = (
        jnp.einsum("sihe,sjhe->shij", query_heads, key_heads, preferred_element_type=jnp.float32)
        * score_scale
        + bias_keys.astype(jnp.float32)[None]
    )
    exp_scores = jnp.exp(scores)
    exp_total = lax.psum(jnp.sum(exp_scores, axis=-1).astype(jnp.bfloat16), "grp").astype(
        jnp.float32
    )
    attn_prob = exp_scores / exp_total[..., None]
    prob_b = attn_prob.astype(jnp.bfloat16)
    attended_part = jnp.einsum(
        "shij,sjhe->sihe", prob_b, value_heads, preferred_element_type=jnp.float32
    )
    attended_part = attended_part.reshape(sample_count, token_total, model_width)
    attended = lax.psum_scatter(
        attended_part.astype(jnp.bfloat16), "grp", scatter_dimension=1, tiled=True
    )
    block_update = project(attended, w_out)
    updated = (noised_f + out_gate[None] * block_update).astype(jnp.bfloat16)
    grad_out = cotangent.astype(jnp.float32)
    gate_part = jnp.sum(grad_out * block_update, axis=0)
    grad_update = (grad_out * out_gate[None]).astype(jnp.bfloat16)
    grad_attn = project_back(grad_update, w_out).astype(jnp.bfloat16)
    grads_all = lax.all_gather(grad_attn, "grp", axis=1, tiled=True)
    grad_heads = grads_all.reshape(sample_count, token_total, head_count, head_size)
    grad_prob = jnp.einsum(
        "sihe,sjhe->shij", grad_heads, value_heads, preferred_element_type=jnp.float32
    )
    row_delta = lax.psum(
        jnp.sum(attn_prob * grad_prob, axis=-1).astype(jnp.bfloat16), "grp"
    ).astype(jnp.float32)
    grad_score = attn_prob * (grad_prob - row_delta[..., None])
    score_b = grad_score.astype(jnp.bfloat16)
    query_part = (
        jnp.einsum("shij,sjhe->sihe", score_b, key_heads, preferred_element_type=jnp.float32)
        * score_scale
    )
    query_part = query_part.reshape(sample_count, token_total, model_width)
    grad_query = lax.psum_scatter(
        query_part.astype(jnp.bfloat16), "grp", scatter_dimension=1, tiled=True
    )
    grad_key = (
        jnp.einsum("shij,sihe->sjhe", score_b, query_heads, preferred_element_type=jnp.float32)
        * score_scale
    )
    grad_value = jnp.einsum(
        "shij,sihe->sjhe", prob_b, grad_heads, preferred_element_type=jnp.float32
    )
    grad_key = grad_key.reshape(sample_count, col_count, model_width).astype(jnp.bfloat16)
    grad_value = grad_value.reshape(sample_count, col_count, model_width).astype(jnp.bfloat16)
    grad_input = (
        project_back(grad_query, w_query)
        + project_back(grad_key, w_key)
        + project_back(grad_value, w_value)
    )
    gamma_part = jnp.sum(grad_input * noised_norm, axis=0)
    beta_part = jnp.sum(grad_input, axis=0)
    gamma_sum, beta_sum, gate_sum = lax.psum((gamma_part, beta_part, gate_part), "rows")
    pre_gamma = (gamma_sum * cond_gamma * (1.0 - cond_gamma)).astype(jnp.bfloat16)
    pre_gate = (gate_sum * out_gate * (1.0 - out_gate)).astype(jnp.bfloat16)
    grad_snorm = jnp.dot(pre_gamma, w_gamma.T, preferred_element_type=jnp.float32)
    grad_snorm = grad_snorm + jnp.dot(
        beta_sum.astype(jnp.bfloat16), w_beta.T, preferred_element_type=jnp.float32
    )
    grad_snorm = grad_snorm + jnp.dot(pre_gate, w_outgate.T, preferred_element_type=jnp.float32)
    d_single = norm_back(grad_snorm, single_norm, single_inv)
    bias_part = jnp.sum(score_b, axis=0, dtype=jnp.float32)
    bias_own = lax.psum_scatter(bias_part, "rows", scatter_dimension=1, tiled=True)
    bias_grad = (bias_own * token_total).astype(jnp.bfloat16)
    grad_pairn = jnp.einsum("hij,ch->ijc", bias_grad, w_pair, preferred_element_type=jnp.float32)
    d_pair = norm_back(grad_pairn, pair_norm, pair_inv).astype(jnp.bfloat16)
    return (updated, d_single, d_pair)


def solution(mesh):
    in_specs = (
        P("grp", None),
        P("rows", "grp", None),
        P(),
        P("rows", "grp", None),
        P(),
        P(),
        P(),
        P(),
        P(),
        P(),
        P(),
        P(),
        P(),
        P("rows", "grp", None),
    )
    out_specs = (P("rows", "grp", None), P("grp", None), P("rows", "grp", None))
    groups = mesh.shape["grp"]
    row_total = mesh.shape["rows"]

    def on_device(*args):
        pair, noised, w_pair = args[1], args[3], args[11]
        fits = (
            groups == 4
            and pair.shape[0] % 32 == 0
            and pair.shape[1] % pair.shape[0] == 0
            and row_total == 8
            and noised.shape[0] == 1
            and noised.shape[1] == 192
            and w_pair.shape[1] % (2 * groups) == 0
        )
        if fits:
            return split_heads(*args, groups=groups, row_total=row_total)
        return split_keys(*args)

    return jax.shard_map(
        on_device, mesh=mesh, in_specs=in_specs, out_specs=out_specs, check_vma=False
    )
```

```python
import functools
import math

import jax
import jax.numpy as jnp
from jax import lax
from jax.experimental import pallas as pl
from jax.experimental.pallas import tpu as pltpu
from jax.sharding import PartitionSpec as P

EPSILON = 1e-05
BF16 = jnp.bfloat16
F32 = jnp.float32
LOG2_E = math.log2(math.e)
SLOT_ORDER = (0, 2, 3, 1)
VMEM_LIMIT = 56 * 1024 * 1024


def norm_rows(values):
    center = values - jnp.mean(values, axis=-1, keepdims=True)
    inverse = lax.rsqrt(jnp.mean(center * center, axis=-1, keepdims=True) + EPSILON)
    return (center * inverse, inverse)


def norm_back(grad_in, normed, inverse):
    grad_mean = jnp.mean(grad_in, axis=-1, keepdims=True)
    cross_mean = jnp.mean(grad_in * normed, axis=-1, keepdims=True)
    return inverse * (grad_in - grad_mean - normed * cross_mean)


def mm(left, right):
    return lax.dot_general(left, right, (((1,), (0,)), ((), ())), preferred_element_type=F32)


def mm_nt(left, right):
    return lax.dot_general(left, right, (((1,), (1,)), ((), ())), preferred_element_type=F32)


def mm_tn(left, right):
    return lax.dot_general(left, right, (((0,), (0,)), ((), ())), preferred_element_type=F32)


def sigmoid(values):
    return 1.0 / (1.0 + jnp.exp(-values))


def params():
    return pltpu.CompilerParams(vmem_limit_bytes=VMEM_LIMIT)


def smem():
    return pl.BlockSpec(memory_space=pltpu.SMEM)


def vmem():
    return pl.BlockSpec(memory_space=pltpu.VMEM)


def project_kernel(
    group_ref,
    single_ref,
    noised_ref,
    cot_ref,
    w_gamma_ref,
    w_beta_ref,
    w_outgate_ref,
    w_query_ref,
    w_key_ref,
    w_value_ref,
    w_out_ref,
    *rest,
    groups,
    calls,
    head_size,
):
    send_refs = rest[:groups]
    gamma_ref, gate_ref, stage_ref = rest[groups:]
    width = stage_ref.shape[2]
    part = width // (4 * calls)
    group_own = group_ref[0]
    single_norm, _ = norm_rows(single_ref[...].astype(F32))
    single_b = single_norm.astype(BF16)
    cond_gamma = sigmoid(mm(single_b, w_gamma_ref[...]))
    gamma_ref[...] = cond_gamma
    out_gate = sigmoid(mm(single_b, w_outgate_ref[...]))
    gate_ref[...] = out_gate
    cond_beta = mm(single_b, w_beta_ref[...])
    noised_norm, _ = norm_rows(noised_ref[...].astype(F32))
    x_b = (noised_norm * cond_gamma + cond_beta).astype(BF16)

    def put(kind, values):
        rounded = values.astype(BF16)
        for group in range(groups):
            slot = group_own ^ group
            for call in range(calls):
                feature = (group * calls + call) * part
                lane = (call * 4 + kind) * part
                stage_ref[slot, :, lane : lane + part] = rounded[:, feature : feature + part]

    put(0, mm(x_b, w_query_ref[...]) * (LOG2_E / math.sqrt(head_size)))
    put(1, mm(x_b, w_key_ref[...]))
    put(2, mm(x_b, w_value_ref[...]))
    grad_update = (cot_ref[...].astype(F32) * out_gate).astype(BF16)
    put(3, mm_nt(grad_update, w_out_ref[...]))
    for slot in range(groups):
        send_refs[SLOT_ORDER.index(slot)][...] = stage_ref[slot]


def lane_tiles(cols):
    return [(tile, tile * 128, min(cols, tile * 128 + 128)) for tile in range(-(-cols // 128))]


def center_rows(pair_ref, first, batch):
    _, _, cols, channels = pair_ref.shape
    halves = []
    for side in range(2):
        rows = pair_ref[side, first : first + batch].reshape(batch * cols, channels).astype(F32)
        halves.append(rows - jnp.sum(rows, axis=-1, keepdims=True) * (1.0 / channels))
    return jnp.concatenate(halves, axis=1)


def lane_pad(block, before, total):
    rows, width = block.shape
    pieces = [block]
    if before:
        pieces = [jnp.zeros((rows, before), block.dtype)] + pieces
    if total > before + width:
        pieces = pieces + [jnp.zeros((rows, total - before - width), block.dtype)]
    return jnp.concatenate(pieces, axis=1)


def bias_kernel(
    group_ref,
    rows_ref,
    chains_ref,
    gain_ref,
    pair_ref,
    w_pair_ref,
    cols_ref,
    *rest,
    groups,
    batch,
):
    send_refs = rest[:groups]
    stats_ref, flat_ref, gains_ref, stage_ref = rest[groups:]
    _, step, cols, channels = pair_ref.shape
    heads = gain_ref.shape[0]
    per_group = heads // groups
    half = step * pl.num_programs(0)
    group_own = group_ref[0]
    row_base = rows_ref[0] * 2 * half + pl.program_id(0) * step
    weight = w_pair_ref[...].astype(F32).T.astype(BF16)
    mean_part = jnp.full((channels, heads), 1.0 / channels, BF16)
    mixed = []
    for inner in range(2):
        for part, offset in ((weight, 0), (mean_part, heads)):
            for side in range(2):
                mixed.append(lane_pad(part, 2 * heads * (2 * inner + side) + offset, 8 * heads))
    mixed = jnp.concatenate(mixed, axis=0)
    chain_all = cols_ref[...].reshape(1, groups * cols)
    chain_cols = chain_all[:, :cols]
    for group in range(1, groups):
        here = chain_all[:, group * cols : (group + 1) * cols]
        chain_cols = jnp.where(group_own == group, here, chain_cols)
    for head in range(heads):
        gains_ref[head : head + 1, :] = jnp.full((1, cols), gain_ref[head] * LOG2_E, F32)

    for first in range(0, step, batch):
        center = center_rows(pair_ref, first, batch)
        center_b = center.astype(BF16)
        square = (center * center).astype(BF16)
        for base in range(0, batch, 2):
            one = slice(base * cols, (base + 1) * cols)
            two = slice((base + 1) * cols, (base + 2) * cols)
            left = jnp.concatenate(
                [center_b[one], square[one], center_b[two], square[two]], axis=1
            )
            sums = mm(left, mixed).T
            for inner in range(2):
                row = first + base + inner
                for side in range(2):
                    top = 2 * heads * (2 * inner + side)
                    inverse = lax.rsqrt(sums[top + heads : top + 2 * heads] + EPSILON)
                    projected = sums[top : top + heads] * inverse
                    stats_ref[side, row, :heads, :] = projected
                    stats_ref[side, row, heads:, :] = inverse[:8]
                    chain = chains_ref[row_base + side * half + row]
                    same = (chain_cols == chain).astype(F32)
                    values = projected * LOG2_E + gains_ref[...] * same
                    for tile, start, end in lane_tiles(cols):
                        piece = lane_pad(values[:, start:end], 0, 128)
                        flat_ref[side, tile, pl.ds(row, heads, stride=step), :] = piece
    for head in range(heads):
        slot = group_own ^ (head // per_group)
        tops = slice(head * step, (head + 1) * step)
        rest_lanes = [flat_ref[side, 1, tops, : cols - 128] for side in range(2)]
        stage_ref[slot, head % per_group, 0] = flat_ref[0, 0, tops, :].astype(BF16)
        stage_ref[slot, head % per_group, 1] = flat_ref[1, 0, tops, :].astype(BF16)
        stage_ref[slot, head % per_group, 2] = jnp.concatenate(rest_lanes, axis=1).astype(BF16)
    for slot in range(groups):
        send_refs[slot][...] = stage_ref[slot]


def pair_bias(pair, w_pair, chain_gain, chains, group_index, row_index, groups):
    rows, cols, channels = pair.shape
    heads = w_pair.shape[1]
    per_group = heads // groups
    half = rows // 2
    step = 16
    tiles = -(-cols // 128)
    *sends, stats = pl.pallas_call(
        functools.partial(bias_kernel, groups=groups, batch=16),
        grid=(half // step,),
        in_specs=[
            smem(),
            smem(),
            smem(),
            smem(),
            pl.BlockSpec((2, step, cols, channels), lambda t: (0, t, 0, 0)),
            pl.BlockSpec((heads, channels), lambda t: (0, 0)),
            pl.BlockSpec((groups * cols,), lambda t: (0,)),
        ],
        out_specs=[
            pl.BlockSpec((per_group, 3, step, 128), lambda t: (0, 0, t, 0)) for _ in range(groups)
        ]
        + [pl.BlockSpec((2, step, heads + 8, cols), lambda t: (0, t, 0, 0))],
        out_shape=[
            jax.ShapeDtypeStruct((per_group, 3, half, 128), BF16) for _ in range(groups)
        ]
        + [jax.ShapeDtypeStruct((2, half, heads + 8, cols), F32)],
        scratch_shapes=[
            pltpu.VMEM((2, tiles, heads * step, 128), F32),
            pltpu.VMEM((heads, cols), F32),
            pltpu.VMEM((groups, per_group, 3, step, 128), BF16),
        ],
        compiler_params=params(),
    )(
        group_index,
        row_index,
        chains,
        chain_gain,
        pair.reshape(2, half, cols, channels),
        w_pair.T,
        chains,
    )
    return sends, stats


def pair_back_kernel(
    group_ref, pair_ref, stats_ref, w_pair_ref, *rest, groups, calls, factor, batch
):
    grad_refs = rest[: groups * calls]
    out_ref, flat_ref = rest[groups * calls :]
    _, step, cols, channels = pair_ref.shape
    per_call = grad_refs[0].shape[0]
    heads = groups * calls * per_call
    group_own = group_ref[0]
    weight = w_pair_ref[...].astype(F32)
    weight = (weight - jnp.mean(weight, axis=-1, keepdims=True)).astype(BF16)
    spread = lax.broadcasted_iota(jnp.int32, (heads, channels), 0)
    spread = (spread < 2).astype(F32).astype(BF16)
    block = jnp.concatenate(
        [lane_pad(weight, 0, 2 * channels), lane_pad(spread, channels, 2 * channels)], axis=0
    )
    weights = jnp.concatenate(
        [lane_pad(block, 2 * channels * place, 8 * channels) for place in range(4)], axis=0
    )
    blank = jnp.zeros((heads - 2, cols), F32)
    for number in range(groups * calls):
        call, slot = divmod(number, groups)
        source = (group_own ^ slot) * calls + call
        for head in range(per_call):
            values = grad_refs[number][head].astype(F32)
            top = pl.multiple_of((source * per_call + head) * step, step)
            for side in range(2):
                flat_ref[side, 0, pl.ds(top, step), :] = values[side]
                flat_ref[side, 1, pl.ds(top, step), : cols - 128] = values[2][
                    :, side * (cols - 128) : (side + 1) * (cols - 128)
                ]

    for first in range(0, step, batch):
        center = center_rows(pair_ref, first, batch)
        for base in range(0, batch, 2):
            places = [(base + inner, side) for inner in range(2) for side in range(2)]
            left = []
            for inner, side in places:
                grads = jnp.concatenate(
                    [
                        flat_ref[side, tile, pl.ds(first + inner, heads, stride=step), :][
                            :, : end - start
                        ]
                        for tile, start, end in lane_tiles(cols)
                    ],
                    axis=1,
                )
                projected = stats_ref[side, first + inner, :heads, :]
                inverse = stats_ref[side, first + inner, heads : heads + 1, :]
                cross = jnp.sum(grads * projected, axis=0, keepdims=True) * (1.0 / channels)
                scaled = grads * (inverse * factor)
                cross = cross * (inverse * inverse * factor)
                cross_high = cross.astype(BF16).astype(F32)
                left += [scaled, cross_high, cross - cross_high, blank]
            both = mm_tn(jnp.concatenate(left, axis=0).astype(BF16), weights)
            for place, (inner, side) in enumerate(places):
                rows = slice(inner * cols, (inner + 1) * cols)
                lanes = slice(side * channels, (side + 1) * channels)
                start = 2 * channels * place
                middle, end = start + channels, start + 2 * channels
                out_ref[side, first + inner] = (
                    both[:, start:middle] - center[rows, lanes] * both[:, middle:end]
                ).astype(BF16)


def pair_back(pair, stats, grads, w_pair, group_index, groups, factor):
    rows, cols, channels = pair.shape
    per_call = grads[0].shape[0]
    heads = len(grads) * per_call
    half = rows // 2
    step = 16
    tiles = -(-cols // 128)
    out = pl.pallas_call(
        functools.partial(
            pair_back_kernel, groups=groups, calls=len(grads) // groups, factor=factor, batch=8
        ),
        grid=(half // step,),
        in_specs=[
            smem(),
            pl.BlockSpec((2, step, cols, channels), lambda t: (0, t, 0, 0)),
            pl.BlockSpec((2, step, heads + 8, cols), lambda t: (0, t, 0, 0)),
            pl.BlockSpec((heads, channels), lambda t: (0, 0)),
        ]
        + [pl.BlockSpec((per_call, 3, step, 128), lambda t: (0, 0, t, 0)) for _ in grads],
        out_specs=pl.BlockSpec((2, step, cols, channels), lambda t: (0, t, 0, 0)),
        out_shape=jax.ShapeDtypeStruct((2, half, cols, channels), BF16),
        scratch_shapes=[pltpu.VMEM((2, tiles, heads * step, 128), F32)],
        compiler_params=params(),
    )(group_index, pair.reshape(2, half, cols, channels), stats, w_pair.T, *grads)
    return out.reshape(rows, cols, channels)


def unit_order(heads):
    first, second = range(heads // 2), range(heads // 2, heads)
    order = [(1, head) for head in first] + [(3, head) for head in first]
    order += [(2, head) for head in second] + [(3, head) for head in second]
    order += [(0, head) for head in range(heads)]
    order += [(2, head) for head in first] + [(1, head) for head in second]
    return order


def attention_kernel(group_ref, row_ref, *rest, groups, row_parts, head_size):
    bias_refs = rest[: row_parts + 2]
    acts_refs = rest[row_parts + 2 : row_parts + 2 + groups]
    acts_refs = acts_refs[:1] + acts_refs[-1:] + acts_refs[1:-1]
    rest = rest[row_parts + 2 + groups :]
    out_refs = rest[:groups]
    (
        keep_ref,
        give_ref,
        give_late_ref,
        query_ref,
        keys_ref,
        values_ref,
        grads_ref,
        query_t_ref,
        keys_t_ref,
        values_t_ref,
        bias_full,
        score_full,
        att_sum,
        gq_sum,
        gk_sum,
        gv_sum,
    ) = rest[groups:]
    heads = keep_ref.shape[1] * 2 // row_parts
    group_own = group_ref[0]
    cols, width = acts_refs[0].shape
    tokens = groups * cols
    part = width // 4
    half = bias_refs[0].shape[3]
    rest_lanes = cols - 128
    scale = 1.0 / math.sqrt(head_size)
    extra = 128 - part % 128
    plain = (query_ref, keys_ref, values_ref, grads_ref)
    turned = (query_t_ref, keys_t_ref, values_t_ref)

    turns = [(slot * cols, slot * 128, 128) for slot in range(groups)]
    turns += [
        (slot * cols + 128, groups * 128 + slot * rest_lanes, rest_lanes) for slot in range(groups)
    ]
    for kind in range(4):
        lanes = slice(kind * part, (kind + 1) * part)
        if kind in (0, 3):
            for slot in range(groups):
                plain[kind][slot * cols : (slot + 1) * cols, :] = acts_refs[slot][:, lanes]
        else:
            for token, place, count in turns:
                slot, inside = divmod(token, cols)
                plain[kind][place : place + count, :] = acts_refs[slot][
                    inside : inside + count, lanes
                ]
        if kind < len(turned):
            turned[kind][...] = plain[kind][...].T

    def places(row_part):
        first = row_part * (2 * half)
        slot = group_own ^ (first // cols)
        for side in range(2):
            top = slot * cols + lax.rem(first, cols) + side * half
            yield side, pl.ds(pl.multiple_of(top, 16), half)

    def block(other, column, head, which):
        if other >= row_parts - 2 and column >= groups // 2:
            return bias_refs[other + 2][column - groups // 2, head, which]
        return bias_refs[other][column, head, which]

    lane = lax.broadcasted_iota(jnp.int32, (1, part), 1)
    zero = jnp.zeros((), BF16)
    order = unit_order(heads)
    for head in range(heads):
        bias_head, score_head = bias_full.at[head % 2], score_full.at[head % 2]
        for other in range(row_parts):
            for side, rows in places(row_ref[0] ^ other):
                lanes = slice(side * rest_lanes, (side + 1) * rest_lanes)
                tiles = [block(other, column, head, side) for column in range(groups)]
                tiles += [block(other, column, head, 2)[:, lanes] for column in range(groups)]
                bias_head[rows, :] = jnp.concatenate(tiles, axis=1)

        features = slice(head * head_size, (head + 1) * head_size)
        mine = (lane >= features.start) & (lane < features.stop)
        query = jnp.where(mine, query_ref[...], zero)
        grads = jnp.where(mine, grads_ref[...], zero)
        keys_m = jnp.where(mine, keys_ref[...], zero)
        values_m = jnp.concatenate(
            [jnp.where(mine, values_ref[...], zero), jnp.ones((tokens, extra), BF16)], axis=1
        )
        weights = jnp.exp2(mm(query, keys_t_ref[...]) + bias_head[...].astype(F32))
        weights_b = weights.astype(BF16)
        attended = mm(weights_b, values_m)
        inverse = 1.0 / attended[:, part : part + 1]
        attended = attended[:, :part] * inverse
        grads = (grads.astype(F32) * inverse).astype(BF16)
        delta = jnp.sum(attended * grads.astype(F32), axis=-1, keepdims=True)
        score = (weights * (mm(grads, values_t_ref[...]) - delta)).astype(BF16)
        score_head[...] = score
        grad_query = mm(score, keys_m)
        grad_value = mm_tn(grads, weights_b)
        if head == 0:
            att_sum[...] = attended
            gq_sum[...] = grad_query
            gv_sum[...] = grad_value
        else:
            att_sum[...] += attended
            gq_sum[...] += grad_query
            gv_sum[...] += grad_value
        gk_sum[features, :] = mm(query_t_ref[features, :], score)

        for other in range(row_parts):
            unit = order.index((other // 2, head))
            dbias_ref = keep_ref
            if other % 2:
                early = len(order) // 2
                dbias_ref = give_ref if unit < early else give_late_ref
                unit = unit % early
            scores = [score_head[rows, :] for _, rows in places(row_ref[0] ^ other)]
            for column in range(groups):
                start = groups * 128 + column * rest_lanes
                blocks = [score[:, column * 128 : (column + 1) * 128] for score in scores]
                blocks.append(
                    jnp.concatenate(
                        [score[:, start : start + rest_lanes] for score in scores], axis=1
                    )
                )
                dbias_ref[column, unit] = jnp.stack(blocks)

    results = (
        gq_sum[...] * scale,
        (gk_sum[...] * math.log(2.0)).T,
        gv_sum[...].T,
        att_sum[...],
    )
    for kind, values in enumerate(results):
        rounded = values.astype(BF16)
        lanes = slice(kind * part, (kind + 1) * part)
        if kind in (0, 3):
            for slot in range(groups):
                out_refs[slot][:, lanes] = rounded[slot * cols : (slot + 1) * cols]
        else:
            for token, place, count in turns:
                slot, inside = divmod(token, cols)
                out_refs[slot][inside : inside + count, lanes] = rounded[place : place + count]


def attention(group_index, row_index, acts, bias, head_size):
    groups = len(acts)
    row_parts = len(bias) - 2
    cols, width = acts[0].shape
    tokens = groups * cols
    part = width // 4
    _, heads, _, half, _ = bias[0].shape
    units = (groups, row_parts // 2 * heads, 3, half, 128)
    some = (groups, row_parts // 4 * heads, 3, half, 128)
    *grads, keep, give, give_late = pl.pallas_call(
        functools.partial(
            attention_kernel, groups=groups, row_parts=row_parts, head_size=head_size
        ),
        in_specs=[smem(), smem()] + [vmem()] * (len(bias) + groups),
        out_shape=[jax.ShapeDtypeStruct((cols, width), BF16)] * groups
        + [jax.ShapeDtypeStruct(shape, BF16) for shape in (units, some, some)],
        scratch_shapes=[pltpu.VMEM((tokens, part), BF16) for _ in range(4)]
        + [pltpu.VMEM((part, tokens), BF16) for _ in range(3)]
        + [
            pltpu.VMEM((2, tokens, tokens), BF16),
            pltpu.VMEM((2, tokens, tokens), BF16),
            pltpu.VMEM((tokens, part), F32),
            pltpu.VMEM((tokens, part), F32),
            pltpu.VMEM((part, tokens), F32),
            pltpu.VMEM((part, tokens), F32),
        ],
        compiler_params=params(),
    )(group_index, row_index, *bias, acts[0], *acts[2:], acts[1])
    return grads, keep, give, give_late


def finish_kernel(
    group_ref,
    single_ref,
    noised_ref,
    cot_ref,
    gamma_ref,
    gate_ref,
    w_gamma_ref,
    w_beta_ref,
    w_outgate_ref,
    w_query_ref,
    w_key_ref,
    w_value_ref,
    w_out_ref,
    *rest,
    groups,
    calls,
):
    got_refs = rest[: groups * calls]
    updated_ref, d_single_ref, stage_ref = rest[groups * calls :]
    width = stage_ref.shape[3]
    part = width // 4
    for slot in range(groups):
        for call in range(calls):
            stage_ref[group_ref[0] ^ slot, call] = got_refs[
                call * groups + slot
            ][...]

    def take(kind):
        return jnp.concatenate(
            [
                stage_ref[group, call, :, kind * part : (kind + 1) * part]
                for group in range(groups)
                for call in range(calls)
            ],
            axis=1,
        )

    out_gate = gate_ref[...]
    cond_gamma = gamma_ref[...]
    block_update = mm(take(3), w_out_ref[...])
    noised = noised_ref[...].astype(F32)
    updated_ref[...] = (noised + out_gate * block_update).astype(BF16)
    gate_part = cot_ref[...].astype(F32) * block_update
    pre_gate = (gate_part * out_gate * (1.0 - out_gate)).astype(BF16)
    grad_input = mm_nt(take(0), w_query_ref[...])
    grad_input += mm_nt(take(1), w_key_ref[...])
    grad_input += mm_nt(take(2), w_value_ref[...])
    noised_norm, _ = norm_rows(noised)
    pre_gamma = (grad_input * noised_norm * cond_gamma * (1.0 - cond_gamma)).astype(BF16)
    grad_snorm = mm_nt(pre_gamma, w_gamma_ref[...])
    grad_snorm += mm_nt(grad_input.astype(BF16), w_beta_ref[...])
    grad_snorm += mm_nt(pre_gate, w_outgate_ref[...])
    single_norm, single_inv = norm_rows(single_ref[...].astype(F32))
    d_single_ref[...] = norm_back(grad_snorm, single_norm, single_inv).astype(BF16)


def swap_groups(sends):
    groups = len(sends)
    order = SLOT_ORDER[1:]
    got = []
    for bits in order:
        perm = [(index, index ^ bits) for index in range(groups)]
        got.append(lax.ppermute(sends[bits], "grp", perm))
    got = dict(zip(order, lax.optimization_barrier(got)))
    return [sends[0]] + [got[bits] for bits in range(1, groups)]


def flip_rows(values, bits, row_total):
    return lax.ppermute(values, "rows", [(index, index ^ bits) for index in range(row_total)])


def gather_rows(own, acts, row_total):
    half = own.shape[0] // 2
    near = flip_rows(own, 2, row_total)
    far = flip_rows(own, 4, row_total)
    first = flip_rows(near[:half], 4, row_total)
    second = flip_rows(far[half:], 2, row_total)
    acts[2], acts[3], acts[1], first, second = lax.optimization_barrier(
        (acts[2], acts[3], acts[1], first, second)
    )
    blocks = []
    for block in (own, near, far, first, second):
        blocks += [block, flip_rows(block, 1, row_total)]
    return blocks, acts


def swap_cores(give, give_late, row_total):
    got = flip_rows(give, 1, row_total)
    got, give_late = lax.optimization_barrier((got, give_late))
    return got, flip_rows(give_late, 1, row_total)


def scatter_rows(keep, got, got_late, row_total):
    early = got.shape[1]
    heads = early // 2
    part = heads // 2

    def add(first, count, *others):
        source, place = (got, first) if first < early else (got_late, first - early)
        total = keep[:, first : first + count].astype(F32)
        total += source[:, place : place + count].astype(F32)
        for other in others:
            total += other.astype(F32)
        return total.astype(BF16)

    near = flip_rows(add(0, heads), 2, row_total)
    far = flip_rows(add(heads, heads), 4, row_total)
    far_two = flip_rows(add(early + heads, part, near[:, part:]), 4, row_total)
    near_two = flip_rows(add(early + heads + part, part, far[:, part:]), 2, row_total)
    own = add(early, heads, jnp.concatenate([near[:, :part], far[:, :part]], axis=1))
    return own, far_two, near_two


def add_last(own, far_two, near_two):
    last = jnp.concatenate([far_two, near_two], axis=1)
    total = (own.astype(F32) + last.astype(F32)).astype(BF16)
    return [total[slot] for slot in range(total.shape[0])]


def sum_rows(mine, d_pair, row_total):
    parts = [flip_rows(mine, bits, row_total) for bits in (2, 4, 6)]
    parts, d_pair = lax.optimization_barrier((parts, d_pair))
    near, far, last = (part.astype(F32) for part in parts)
    chips = ((mine.astype(F32) + near) + (far + last)).astype(BF16)
    return chips.astype(F32) + flip_rows(chips, 1, row_total).astype(F32), d_pair


def split_heads(
    single,
    pair,
    chains,
    noised,
    w_gamma,
    w_beta,
    w_outgate,
    w_query,
    w_key,
    w_value,
    w_out,
    w_pair,
    chain_gain,
    cotangent,
    *,
    groups,
    row_total,
):
    cols, _ = single.shape
    tokens = chains.shape[0]
    width = noised.shape[2]
    head_size = width // w_pair.shape[1]
    calls = 1
    row_index = lax.axis_index("rows").reshape(1)
    group_index = lax.axis_index("grp").reshape(1)
    bias_send, stats = pair_bias(
        pair, w_pair, chain_gain, chains, group_index, row_index, groups
    )
    bias_got = swap_groups(bias_send)
    noised = noised[0]
    cotangent = cotangent[0]
    *acts_send, cond_gamma, out_gate = pl.pallas_call(
        functools.partial(
            project_kernel, groups=groups, calls=calls, head_size=head_size
        ),
        in_specs=[smem()] + [vmem()] * 10,
        out_shape=[
            jax.ShapeDtypeStruct((cols, 4 * width // groups), BF16) for _ in range(groups)
        ]
        + [
            jax.ShapeDtypeStruct((cols, width), F32),
            jax.ShapeDtypeStruct((cols, width), F32),
        ],
        scratch_shapes=[pltpu.VMEM((groups, cols, 4 * width // groups), BF16)],
        compiler_params=params(),
    )(
        group_index,
        single,
        noised,
        cotangent,
        w_gamma,
        w_beta,
        w_outgate,
        w_query,
        w_key,
        w_value,
        w_out,
    )
    bias_got, _ = lax.optimization_barrier((bias_got, acts_send))
    acts_send = [acts_send[SLOT_ORDER.index(slot)] for slot in range(groups)]
    acts = swap_groups(acts_send)
    bias_all, acts = gather_rows(jnp.stack(bias_got), acts, row_total)
    grads_send, keep, give, give_late = attention(
        group_index, row_index, acts, bias_all, head_size
    )
    got, got_late = swap_cores(give, give_late, row_total)
    got_late, grads_send[1] = lax.optimization_barrier((got_late, grads_send[1]))
    grads = swap_groups(grads_send)
    own, far_two, near_two = scatter_rows(keep, got, got_late, row_total)
    far_two, near_two, grads = lax.optimization_barrier((far_two, near_two, grads))
    dbias_own, grads = lax.optimization_barrier((add_last(own, far_two, near_two), grads))
    dbias_back = swap_groups(dbias_own)
    updated, d_part = pl.pallas_call(
        functools.partial(finish_kernel, groups=groups, calls=calls),
        in_specs=[smem()] + [vmem()] * (12 + groups * calls),
        out_shape=[
            jax.ShapeDtypeStruct((cols, width), BF16),
            jax.ShapeDtypeStruct(single.shape, BF16),
        ],
        scratch_shapes=[pltpu.VMEM((groups, calls, cols, 4 * width // (groups * calls)), BF16)],
        compiler_params=params(),
    )(
        group_index,
        single,
        noised,
        cotangent,
        cond_gamma,
        out_gate,
        w_gamma,
        w_beta,
        w_outgate,
        w_query,
        w_key,
        w_value,
        w_out,
        *grads,
    )
    d_pair = pair_back(pair, stats, dbias_back, w_pair, group_index, groups, float(tokens))
    d_single, d_pair = sum_rows(d_part, d_pair, row_total)
    return (updated[None], d_single, d_pair)


def project(acts, weight):
    return jnp.einsum("std,de->ste", acts, weight, preferred_element_type=F32)


def project_back(acts, weight):
    return jnp.einsum("ste,de->std", acts, weight, preferred_element_type=F32)


def split_keys(
    single,
    pair,
    chains,
    noised,
    w_gamma,
    w_beta,
    w_outgate,
    w_query,
    w_key,
    w_value,
    w_out,
    w_pair,
    chain_gain,
    cotangent,
):
    col_count = single.shape[0]
    row_count = pair.shape[0]
    head_count = w_pair.shape[1]
    model_width = w_query.shape[0]
    head_size = model_width // head_count
    sample_count = noised.shape[0]
    token_total = chains.shape[0]
    score_scale = 1.0 / math.sqrt(head_size)
    row_index = lax.axis_index("rows")
    group_index = lax.axis_index("grp")
    chain_rows = lax.dynamic_slice_in_dim(chains, row_index * row_count, row_count)
    chain_cols = lax.dynamic_slice_in_dim(chains, group_index * col_count, col_count)
    pair_norm, pair_inv = norm_rows(pair.astype(jnp.float32))
    projected = jnp.einsum(
        "ijc,ch->hij", pair_norm.astype(jnp.bfloat16), w_pair, preferred_element_type=jnp.float32
    )
    same_chain = (chain_rows[:, None] == chain_cols[None, :]).astype(jnp.float32)
    bias_block = (projected + chain_gain[:, None, None] * same_chain[None]).astype(jnp.bfloat16)
    bias_keys = lax.all_gather(bias_block, "rows", axis=1, tiled=True)
    single_norm, single_inv = norm_rows(single.astype(jnp.float32))
    single_b = single_norm.astype(jnp.bfloat16)
    cond_gamma = jax.nn.sigmoid(jnp.dot(single_b, w_gamma, preferred_element_type=jnp.float32))
    cond_beta = jnp.dot(single_b, w_beta, preferred_element_type=jnp.float32)
    out_gate = jax.nn.sigmoid(jnp.dot(single_b, w_outgate, preferred_element_type=jnp.float32))
    noised_f = noised.astype(jnp.float32)
    noised_norm, noised_inv = norm_rows(noised_f)
    x_b = (noised_norm * cond_gamma[None] + cond_beta[None]).astype(jnp.bfloat16)
    queries = project(x_b, w_query).astype(jnp.bfloat16)
    keys_own = project(x_b, w_key).astype(jnp.bfloat16)
    values_own = project(x_b, w_value).astype(jnp.bfloat16)
    queries_all = lax.all_gather(queries, "grp", axis=1, tiled=True)
    query_heads = queries_all.reshape(sample_count, token_total, head_count, head_size)
    key_heads = keys_own.reshape(sample_count, col_count, head_count, head_size)
    value_heads = values_own.reshape(sample_count, col_count, head_count, head_size)
    scores = (
        jnp.einsum("sihe,sjhe->shij", query_heads, key_heads, preferred_element_type=jnp.float32)
        * score_scale
        + bias_keys.astype(jnp.float32)[None]
    )
    exp_scores = jnp.exp(scores)
    exp_total = lax.psum(jnp.sum(exp_scores, axis=-1).astype(jnp.bfloat16), "grp").astype(
        jnp.float32
    )
    attn_prob = exp_scores / exp_total[..., None]
    prob_b = attn_prob.astype(jnp.bfloat16)
    attended_part = jnp.einsum(
        "shij,sjhe->sihe", prob_b, value_heads, preferred_element_type=jnp.float32
    )
    attended_part = attended_part.reshape(sample_count, token_total, model_width)
    attended = lax.psum_scatter(
        attended_part.astype(jnp.bfloat16), "grp", scatter_dimension=1, tiled=True
    )
    block_update = project(attended, w_out)
    updated = (noised_f + out_gate[None] * block_update).astype(jnp.bfloat16)
    grad_out = cotangent.astype(jnp.float32)
    gate_part = jnp.sum(grad_out * block_update, axis=0)
    grad_update = (grad_out * out_gate[None]).astype(jnp.bfloat16)
    grad_attn = project_back(grad_update, w_out).astype(jnp.bfloat16)
    grads_all = lax.all_gather(grad_attn, "grp", axis=1, tiled=True)
    grad_heads = grads_all.reshape(sample_count, token_total, head_count, head_size)
    grad_prob = jnp.einsum(
        "sihe,sjhe->shij", grad_heads, value_heads, preferred_element_type=jnp.float32
    )
    row_delta = lax.psum(
        jnp.sum(attn_prob * grad_prob, axis=-1).astype(jnp.bfloat16), "grp"
    ).astype(jnp.float32)
    grad_score = attn_prob * (grad_prob - row_delta[..., None])
    score_b = grad_score.astype(jnp.bfloat16)
    query_part = (
        jnp.einsum("shij,sjhe->sihe", score_b, key_heads, preferred_element_type=jnp.float32)
        * score_scale
    )
    query_part = query_part.reshape(sample_count, token_total, model_width)
    grad_query = lax.psum_scatter(
        query_part.astype(jnp.bfloat16), "grp", scatter_dimension=1, tiled=True
    )
    grad_key = (
        jnp.einsum("shij,sihe->sjhe", score_b, query_heads, preferred_element_type=jnp.float32)
        * score_scale
    )
    grad_value = jnp.einsum(
        "shij,sihe->sjhe", prob_b, grad_heads, preferred_element_type=jnp.float32
    )
    grad_key = grad_key.reshape(sample_count, col_count, model_width).astype(jnp.bfloat16)
    grad_value = grad_value.reshape(sample_count, col_count, model_width).astype(jnp.bfloat16)
    grad_input = (
        project_back(grad_query, w_query)
        + project_back(grad_key, w_key)
        + project_back(grad_value, w_value)
    )
    gamma_part = jnp.sum(grad_input * noised_norm, axis=0)
    beta_part = jnp.sum(grad_input, axis=0)
    gamma_sum, beta_sum, gate_sum = lax.psum((gamma_part, beta_part, gate_part), "rows")
    pre_gamma = (gamma_sum * cond_gamma * (1.0 - cond_gamma)).astype(jnp.bfloat16)
    pre_gate = (gate_sum * out_gate * (1.0 - out_gate)).astype(jnp.bfloat16)
    grad_snorm = jnp.dot(pre_gamma, w_gamma.T, preferred_element_type=jnp.float32)
    grad_snorm = grad_snorm + jnp.dot(
        beta_sum.astype(jnp.bfloat16), w_beta.T, preferred_element_type=jnp.float32
    )
    grad_snorm = grad_snorm + jnp.dot(pre_gate, w_outgate.T, preferred_element_type=jnp.float32)
    d_single = norm_back(grad_snorm, single_norm, single_inv)
    bias_part = jnp.sum(score_b, axis=0, dtype=jnp.float32)
    bias_own = lax.psum_scatter(bias_part, "rows", scatter_dimension=1, tiled=True)
    bias_grad = (bias_own * token_total).astype(jnp.bfloat16)
    grad_pairn = jnp.einsum("hij,ch->ijc", bias_grad, w_pair, preferred_element_type=jnp.float32)
    d_pair = norm_back(grad_pairn, pair_norm, pair_inv).astype(jnp.bfloat16)
    return (updated, d_single, d_pair)


def solution(mesh):
    in_specs = (
        P("grp", None),
        P("rows", "grp", None),
        P(),
        P("rows", "grp", None),
        P(),
        P(),
        P(),
        P(),
        P(),
        P(),
        P(),
        P(),
        P(),
        P("rows", "grp", None),
    )
    out_specs = (P("rows", "grp", None), P("grp", None), P("rows", "grp", None))
    groups = mesh.shape["grp"]
    row_total = mesh.shape["rows"]

    def on_device(*args):
        pair, noised, w_pair = args[1], args[3], args[11]
        fits = (
            groups == 4
            and pair.shape[0] % 32 == 0
            and pair.shape[1] % pair.shape[0] == 0
            and row_total == 8
            and noised.shape[0] == 1
            and noised.shape[1] == 192
            and w_pair.shape[1] % (2 * groups) == 0
        )
        if fits:
            return split_heads(*args, groups=groups, row_total=row_total)
        return split_keys(*args)

    return jax.shard_map(
        on_device, mesh=mesh, in_specs=in_specs, out_specs=out_specs, check_vma=False
    )
```

```python
import functools
import math

import jax
import jax.numpy as jnp
from jax import lax
from jax.experimental import pallas as pl
from jax.experimental.pallas import tpu as pltpu
from jax.sharding import PartitionSpec as P

EPSILON = 1e-05
BF16 = jnp.bfloat16
F32 = jnp.float32
LOG2_E = math.log2(math.e)
SLOT_ORDER = (0, 2, 3, 1)
VMEM_LIMIT = 56 * 1024 * 1024


def norm_rows(values):
    center = values - jnp.mean(values, axis=-1, keepdims=True)
    inverse = lax.rsqrt(jnp.mean(center * center, axis=-1, keepdims=True) + EPSILON)
    return (center * inverse, inverse)


def norm_back(grad_in, normed, inverse):
    grad_mean = jnp.mean(grad_in, axis=-1, keepdims=True)
    cross_mean = jnp.mean(grad_in * normed, axis=-1, keepdims=True)
    return inverse * (grad_in - grad_mean - normed * cross_mean)


def mm(left, right):
    return lax.dot_general(left, right, (((1,), (0,)), ((), ())), preferred_element_type=F32)


def mm_nt(left, right):
    return lax.dot_general(left, right, (((1,), (1,)), ((), ())), preferred_element_type=F32)


def mm_tn(left, right):
    return lax.dot_general(left, right, (((0,), (0,)), ((), ())), preferred_element_type=F32)


def sigmoid(values):
    return 1.0 / (1.0 + jnp.exp(-values))


def params():
    return pltpu.CompilerParams(vmem_limit_bytes=VMEM_LIMIT)


def smem():
    return pl.BlockSpec(memory_space=pltpu.SMEM)


def vmem():
    return pl.BlockSpec(memory_space=pltpu.VMEM)


def project_kernel(
    group_ref,
    single_ref,
    noised_ref,
    cot_ref,
    w_gamma_ref,
    w_beta_ref,
    w_outgate_ref,
    w_query_ref,
    w_key_ref,
    w_value_ref,
    w_out_ref,
    *rest,
    groups,
    calls,
    head_size,
):
    send_refs = rest[:groups]
    gamma_ref, gate_ref, stage_ref = rest[groups:]
    width = stage_ref.shape[2]
    part = width // (4 * calls)
    group_own = group_ref[0]
    single_norm, _ = norm_rows(single_ref[...].astype(F32))
    single_b = single_norm.astype(BF16)
    cond_gamma = sigmoid(mm(single_b, w_gamma_ref[...]))
    gamma_ref[...] = cond_gamma
    out_gate = sigmoid(mm(single_b, w_outgate_ref[...]))
    gate_ref[...] = out_gate
    cond_beta = mm(single_b, w_beta_ref[...])
    noised_norm, _ = norm_rows(noised_ref[...].astype(F32))
    x_b = (noised_norm * cond_gamma + cond_beta).astype(BF16)

    def put(kind, values):
        rounded = values.astype(BF16)
        for group in range(groups):
            slot = group_own ^ group
            for call in range(calls):
                feature = (group * calls + call) * part
                lane = (call * 4 + kind) * part
                stage_ref[slot, :, lane : lane + part] = rounded[:, feature : feature + part]

    put(0, mm(x_b, w_query_ref[...]) * (LOG2_E / math.sqrt(head_size)))
    put(1, mm(x_b, w_key_ref[...]))
    put(2, mm(x_b, w_value_ref[...]))
    grad_update = (cot_ref[...].astype(F32) * out_gate).astype(BF16)
    put(3, mm_nt(grad_update, w_out_ref[...]))
    for slot in range(groups):
        send_refs[SLOT_ORDER.index(slot)][...] = stage_ref[slot]


def lane_tiles(cols):
    return [(tile, tile * 128, min(cols, tile * 128 + 128)) for tile in range(-(-cols // 128))]


def center_rows(pair_ref, first, batch):
    _, _, cols, channels = pair_ref.shape
    halves = []
    for side in range(2):
        rows = pair_ref[side, first : first + batch].reshape(batch * cols, channels).astype(F32)
        halves.append(rows - jnp.sum(rows, axis=-1, keepdims=True) * (1.0 / channels))
    return jnp.concatenate(halves, axis=1)


def lane_pad(block, before, total):
    rows, width = block.shape
    pieces = [block]
    if before:
        pieces = [jnp.zeros((rows, before), block.dtype)] + pieces
    if total > before + width:
        pieces = pieces + [jnp.zeros((rows, total - before - width), block.dtype)]
    return jnp.concatenate(pieces, axis=1)


def bias_kernel(
    group_ref,
    rows_ref,
    chains_ref,
    gain_ref,
    pair_ref,
    w_pair_ref,
    cols_ref,
    *rest,
    groups,
    batch,
):
    send_refs = rest[:groups]
    stats_ref, flat_ref, gains_ref, stage_ref = rest[groups:]
    _, step, cols, channels = pair_ref.shape
    heads = gain_ref.shape[0]
    per_group = heads // groups
    half = step * pl.num_programs(0)
    group_own = group_ref[0]
    row_base = rows_ref[0] * 2 * half + pl.program_id(0) * step
    weight = w_pair_ref[...].astype(F32).T.astype(BF16)
    mean_part = jnp.full((channels, heads), 1.0 / channels, BF16)
    mixed = []
    for inner in range(2):
        for part, offset in ((weight, 0), (mean_part, heads)):
            for side in range(2):
                mixed.append(lane_pad(part, 2 * heads * (2 * inner + side) + offset, 8 * heads))
    mixed = jnp.concatenate(mixed, axis=0)
    chain_all = cols_ref[...].reshape(1, groups * cols)
    chain_cols = chain_all[:, :cols]
    for group in range(1, groups):
        here = chain_all[:, group * cols : (group + 1) * cols]
        chain_cols = jnp.where(group_own == group, here, chain_cols)
    for head in range(heads):
        gains_ref[head : head + 1, :] = jnp.full((1, cols), gain_ref[head] * LOG2_E, F32)

    for first in range(0, step, batch):
        center = center_rows(pair_ref, first, batch)
        center_b = center.astype(BF16)
        square = (center * center).astype(BF16)
        for base in range(0, batch, 2):
            one = slice(base * cols, (base + 1) * cols)
            two = slice((base + 1) * cols, (base + 2) * cols)
            left = jnp.concatenate(
                [center_b[one], square[one], center_b[two], square[two]], axis=1
            )
            sums = mm(left, mixed).T
            for inner in range(2):
                row = first + base + inner
                for side in range(2):
                    top = 2 * heads * (2 * inner + side)
                    inverse = lax.rsqrt(sums[top + heads : top + 2 * heads] + EPSILON)
                    projected = sums[top : top + heads] * inverse
                    stats_ref[side, row, :heads, :] = projected
                    stats_ref[side, row, heads:, :] = inverse[:8]
                    chain = chains_ref[row_base + side * half + row]
                    same = (chain_cols == chain).astype(F32)
                    values = projected * LOG2_E + gains_ref[...] * same
                    for tile, start, end in lane_tiles(cols):
                        piece = lane_pad(values[:, start:end], 0, 128)
                        flat_ref[side, tile, pl.ds(row, heads, stride=step), :] = piece
    for head in range(heads):
        slot = group_own ^ (head // per_group)
        tops = slice(head * step, (head + 1) * step)
        rest_lanes = [flat_ref[side, 1, tops, : cols - 128] for side in range(2)]
        stage_ref[slot, head % per_group, 0] = flat_ref[0, 0, tops, :].astype(BF16)
        stage_ref[slot, head % per_group, 1] = flat_ref[1, 0, tops, :].astype(BF16)
        stage_ref[slot, head % per_group, 2] = jnp.concatenate(rest_lanes, axis=1).astype(BF16)
    for slot in range(groups):
        send_refs[slot][...] = stage_ref[slot]


def pair_bias(pair, w_pair, chain_gain, chains, group_index, row_index, groups):
    rows, cols, channels = pair.shape
    heads = w_pair.shape[1]
    per_group = heads // groups
    half = rows // 2
    step = 16
    tiles = -(-cols // 128)
    *sends, stats = pl.pallas_call(
        functools.partial(bias_kernel, groups=groups, batch=2),
        grid=(half // step,),
        in_specs=[
            smem(),
            smem(),
            smem(),
            smem(),
            pl.BlockSpec((2, step, cols, channels), lambda t: (0, t, 0, 0)),
            pl.BlockSpec((heads, channels), lambda t: (0, 0)),
            pl.BlockSpec((groups * cols,), lambda t: (0,)),
        ],
        out_specs=[
            pl.BlockSpec((per_group, 3, step, 128), lambda t: (0, 0, t, 0)) for _ in range(groups)
        ]
        + [pl.BlockSpec((2, step, heads + 8, cols), lambda t: (0, t, 0, 0))],
        out_shape=[
            jax.ShapeDtypeStruct((per_group, 3, half, 128), BF16) for _ in range(groups)
        ]
        + [jax.ShapeDtypeStruct((2, half, heads + 8, cols), F32)],
        scratch_shapes=[
            pltpu.VMEM((2, tiles, heads * step, 128), F32),
            pltpu.VMEM((heads, cols), F32),
            pltpu.VMEM((groups, per_group, 3, step, 128), BF16),
        ],
        compiler_params=params(),
    )(
        group_index,
        row_index,
        chains,
        chain_gain,
        pair.reshape(2, half, cols, channels),
        w_pair.T,
        chains,
    )
    return sends, stats


def pair_back_kernel(
    group_ref, pair_ref, stats_ref, w_pair_ref, *rest, groups, calls, factor, batch
):
    grad_refs = rest[: groups * calls]
    out_ref, flat_ref = rest[groups * calls :]
    _, step, cols, channels = pair_ref.shape
    per_call = grad_refs[0].shape[0]
    heads = groups * calls * per_call
    group_own = group_ref[0]
    weight = w_pair_ref[...].astype(F32)
    weight = (weight - jnp.mean(weight, axis=-1, keepdims=True)).astype(BF16)
    spread = lax.broadcasted_iota(jnp.int32, (heads, channels), 0)
    spread = (spread < 2).astype(F32).astype(BF16)
    block = jnp.concatenate(
        [lane_pad(weight, 0, 2 * channels), lane_pad(spread, channels, 2 * channels)], axis=0
    )
    weights = jnp.concatenate(
        [lane_pad(block, 2 * channels * place, 8 * channels) for place in range(4)], axis=0
    )
    blank = jnp.zeros((heads - 2, cols), F32)
    for number in range(groups * calls):
        call, slot = divmod(number, groups)
        source = (group_own ^ slot) * calls + call
        for head in range(per_call):
            values = grad_refs[number][head].astype(F32)
            top = pl.multiple_of((source * per_call + head) * step, step)
            for side in range(2):
                flat_ref[side, 0, pl.ds(top, step), :] = values[side]
                flat_ref[side, 1, pl.ds(top, step), : cols - 128] = values[2][
                    :, side * (cols - 128) : (side + 1) * (cols - 128)
                ]

    for first in range(0, step, batch):
        center = center_rows(pair_ref, first, batch)
        for base in range(0, batch, 2):
            places = [(base + inner, side) for inner in range(2) for side in range(2)]
            left = []
            for inner, side in places:
                grads = jnp.concatenate(
                    [
                        flat_ref[side, tile, pl.ds(first + inner, heads, stride=step), :][
                            :, : end - start
                        ]
                        for tile, start, end in lane_tiles(cols)
                    ],
                    axis=1,
                )
                projected = stats_ref[side, first + inner, :heads, :]
                inverse = stats_ref[side, first + inner, heads : heads + 1, :]
                cross = jnp.sum(grads * projected, axis=0, keepdims=True) * (1.0 / channels)
                scaled = grads * (inverse * factor)
                cross = cross * (inverse * inverse * factor)
                cross_high = cross.astype(BF16).astype(F32)
                left += [scaled, cross_high, cross - cross_high, blank]
            both = mm_tn(jnp.concatenate(left, axis=0).astype(BF16), weights)
            for place, (inner, side) in enumerate(places):
                rows = slice(inner * cols, (inner + 1) * cols)
                lanes = slice(side * channels, (side + 1) * channels)
                start = 2 * channels * place
                middle, end = start + channels, start + 2 * channels
                out_ref[side, first + inner] = (
                    both[:, start:middle] - center[rows, lanes] * both[:, middle:end]
                ).astype(BF16)


def pair_back(pair, stats, grads, w_pair, group_index, groups, factor):
    rows, cols, channels = pair.shape
    per_call = grads[0].shape[0]
    heads = len(grads) * per_call
    half = rows // 2
    step = 16
    tiles = -(-cols // 128)
    out = pl.pallas_call(
        functools.partial(
            pair_back_kernel, groups=groups, calls=len(grads) // groups, factor=factor, batch=2
        ),
        grid=(half // step,),
        in_specs=[
            smem(),
            pl.BlockSpec((2, step, cols, channels), lambda t: (0, t, 0, 0)),
            pl.BlockSpec((2, step, heads + 8, cols), lambda t: (0, t, 0, 0)),
            pl.BlockSpec((heads, channels), lambda t: (0, 0)),
        ]
        + [pl.BlockSpec((per_call, 3, step, 128), lambda t: (0, 0, t, 0)) for _ in grads],
        out_specs=pl.BlockSpec((2, step, cols, channels), lambda t: (0, t, 0, 0)),
        out_shape=jax.ShapeDtypeStruct((2, half, cols, channels), BF16),
        scratch_shapes=[pltpu.VMEM((2, tiles, heads * step, 128), F32)],
        compiler_params=params(),
    )(group_index, pair.reshape(2, half, cols, channels), stats, w_pair.T, *grads)
    return out.reshape(rows, cols, channels)


def unit_order(heads):
    first, second = range(heads // 2), range(heads // 2, heads)
    order = [(1, head) for head in first] + [(3, head) for head in first]
    order += [(2, head) for head in second] + [(3, head) for head in second]
    order += [(0, head) for head in range(heads)]
    order += [(2, head) for head in first] + [(1, head) for head in second]
    return order


def attention_kernel(group_ref, row_ref, *rest, groups, row_parts, head_size):
    bias_refs = rest[: row_parts + 2]
    acts_refs = rest[row_parts + 2 : row_parts + 2 + groups]
    acts_refs = acts_refs[:1] + acts_refs[-1:] + acts_refs[1:-1]
    rest = rest[row_parts + 2 + groups :]
    out_refs = rest[:groups]
    (
        keep_ref,
        give_ref,
        give_late_ref,
        query_ref,
        keys_ref,
        values_ref,
        grads_ref,
        query_t_ref,
        keys_t_ref,
        values_t_ref,
        bias_full,
        score_full,
        att_sum,
        gq_sum,
        gk_sum,
        gv_sum,
    ) = rest[groups:]
    heads = keep_ref.shape[1] * 2 // row_parts
    group_own = group_ref[0]
    cols, width = acts_refs[0].shape
    tokens = groups * cols
    part = width // 4
    half = bias_refs[0].shape[3]
    rest_lanes = cols - 128
    scale = 1.0 / math.sqrt(head_size)
    extra = 128 - part % 128
    plain = (query_ref, keys_ref, values_ref, grads_ref)
    turned = (query_t_ref, keys_t_ref, values_t_ref)

    turns = [(slot * cols, slot * 128, 128) for slot in range(groups)]
    turns += [
        (slot * cols + 128, groups * 128 + slot * rest_lanes, rest_lanes) for slot in range(groups)
    ]
    for kind in range(4):
        lanes = slice(kind * part, (kind + 1) * part)
        if kind in (0, 3):
            for slot in range(groups):
                plain[kind][slot * cols : (slot + 1) * cols, :] = acts_refs[slot][:, lanes]
        else:
            for token, place, count in turns:
                slot, inside = divmod(token, cols)
                plain[kind][place : place + count, :] = acts_refs[slot][
                    inside : inside + count, lanes
                ]
        if kind < len(turned):
            turned[kind][...] = plain[kind][...].T

    def places(row_part):
        first = row_part * (2 * half)
        slot = group_own ^ (first // cols)
        for side in range(2):
            top = slot * cols + lax.rem(first, cols) + side * half
            yield side, pl.ds(pl.multiple_of(top, 16), half)

    def block(other, column, head, which):
        if other >= row_parts - 2 and column >= groups // 2:
            return bias_refs[other + 2][column - groups // 2, head, which]
        return bias_refs[other][column, head, which]

    lane = lax.broadcasted_iota(jnp.int32, (1, part), 1)
    zero = jnp.zeros((), BF16)
    order = unit_order(heads)
    for head in range(heads):
        bias_head, score_head = bias_full.at[head % 2], score_full.at[head % 2]
        for other in range(row_parts):
            for side, rows in places(row_ref[0] ^ other):
                lanes = slice(side * rest_lanes, (side + 1) * rest_lanes)
                tiles = [block(other, column, head, side) for column in range(groups)]
                tiles += [block(other, column, head, 2)[:, lanes] for column in range(groups)]
                bias_head[rows, :] = jnp.concatenate(tiles, axis=1)

        features = slice(head * head_size, (head + 1) * head_size)
        mine = (lane >= features.start) & (lane < features.stop)
        query = jnp.where(mine, query_ref[...], zero)
        grads = jnp.where(mine, grads_ref[...], zero)
        keys_m = jnp.where(mine, keys_ref[...], zero)
        values_m = jnp.concatenate(
            [jnp.where(mine, values_ref[...], zero), jnp.ones((tokens, extra), BF16)], axis=1
        )
        weights = jnp.exp2(mm(query, keys_t_ref[...]) + bias_head[...].astype(F32))
        weights_b = weights.astype(BF16)
        attended = mm(weights_b, values_m)
        inverse = 1.0 / attended[:, part : part + 1]
        attended = attended[:, :part] * inverse
        grads = (grads.astype(F32) * inverse).astype(BF16)
        delta = jnp.sum(attended * grads.astype(F32), axis=-1, keepdims=True)
        score = (weights * (mm(grads, values_t_ref[...]) - delta)).astype(BF16)
        score_head[...] = score
        grad_query = mm(score, keys_m)
        grad_value = mm_tn(grads, weights_b)
        if head == 0:
            att_sum[...] = attended
            gq_sum[...] = grad_query
            gv_sum[...] = grad_value
        else:
            att_sum[...] += attended
            gq_sum[...] += grad_query
            gv_sum[...] += grad_value
        gk_sum[features, :] = mm(query_t_ref[features, :], score)

        for other in range(row_parts):
            unit = order.index((other // 2, head))
            dbias_ref = keep_ref
            if other % 2:
                early = len(order) // 2
                dbias_ref = give_ref if unit < early else give_late_ref
                unit = unit % early
            scores = [score_head[rows, :] for _, rows in places(row_ref[0] ^ other)]
            for column in range(groups):
                start = groups * 128 + column * rest_lanes
                blocks = [score[:, column * 128 : (column + 1) * 128] for score in scores]
                blocks.append(
                    jnp.concatenate(
                        [score[:, start : start + rest_lanes] for score in scores], axis=1
                    )
                )
                dbias_ref[column, unit] = jnp.stack(blocks)

    results = (
        gq_sum[...] * scale,
        (gk_sum[...] * math.log(2.0)).T,
        gv_sum[...].T,
        att_sum[...],
    )
    for kind, values in enumerate(results):
        rounded = values.astype(BF16)
        lanes = slice(kind * part, (kind + 1) * part)
        if kind in (0, 3):
            for slot in range(groups):
                out_refs[slot][:, lanes] = rounded[slot * cols : (slot + 1) * cols]
        else:
            for token, place, count in turns:
                slot, inside = divmod(token, cols)
                out_refs[slot][inside : inside + count, lanes] = rounded[place : place + count]


def attention(group_index, row_index, acts, bias, head_size):
    groups = len(acts)
    row_parts = len(bias) - 2
    cols, width = acts[0].shape
    tokens = groups * cols
    part = width // 4
    _, heads, _, half, _ = bias[0].shape
    units = (groups, row_parts // 2 * heads, 3, half, 128)
    some = (groups, row_parts // 4 * heads, 3, half, 128)
    *grads, keep, give, give_late = pl.pallas_call(
        functools.partial(
            attention_kernel, groups=groups, row_parts=row_parts, head_size=head_size
        ),
        in_specs=[smem(), smem()] + [vmem()] * (len(bias) + groups),
        out_shape=[jax.ShapeDtypeStruct((cols, width), BF16)] * groups
        + [jax.ShapeDtypeStruct(shape, BF16) for shape in (units, some, some)],
        scratch_shapes=[pltpu.VMEM((tokens, part), BF16) for _ in range(4)]
        + [pltpu.VMEM((part, tokens), BF16) for _ in range(3)]
        + [
            pltpu.VMEM((2, tokens, tokens), BF16),
            pltpu.VMEM((2, tokens, tokens), BF16),
            pltpu.VMEM((tokens, part), F32),
            pltpu.VMEM((tokens, part), F32),
            pltpu.VMEM((part, tokens), F32),
            pltpu.VMEM((part, tokens), F32),
        ],
        compiler_params=params(),
    )(group_index, row_index, *bias, acts[0], *acts[2:], acts[1])
    return grads, keep, give, give_late


def finish_kernel(
    group_ref,
    single_ref,
    noised_ref,
    cot_ref,
    gamma_ref,
    gate_ref,
    w_gamma_ref,
    w_beta_ref,
    w_outgate_ref,
    w_query_ref,
    w_key_ref,
    w_value_ref,
    w_out_ref,
    *rest,
    groups,
    calls,
):
    got_refs = rest[: groups * calls]
    updated_ref, d_single_ref, stage_ref = rest[groups * calls :]
    width = stage_ref.shape[3]
    part = width // 4
    for slot in range(groups):
        for call in range(calls):
            stage_ref[group_ref[0] ^ slot, call] = got_refs[
                call * groups + slot
            ][...]

    def take(kind):
        return jnp.concatenate(
            [
                stage_ref[group, call, :, kind * part : (kind + 1) * part]
                for group in range(groups)
                for call in range(calls)
            ],
            axis=1,
        )

    out_gate = gate_ref[...]
    cond_gamma = gamma_ref[...]
    block_update = mm(take(3), w_out_ref[...])
    noised = noised_ref[...].astype(F32)
    updated_ref[...] = (noised + out_gate * block_update).astype(BF16)
    gate_part = cot_ref[...].astype(F32) * block_update
    pre_gate = (gate_part * out_gate * (1.0 - out_gate)).astype(BF16)
    grad_input = mm_nt(take(0), w_query_ref[...])
    grad_input += mm_nt(take(1), w_key_ref[...])
    grad_input += mm_nt(take(2), w_value_ref[...])
    noised_norm, _ = norm_rows(noised)
    pre_gamma = (grad_input * noised_norm * cond_gamma * (1.0 - cond_gamma)).astype(BF16)
    grad_snorm = mm_nt(pre_gamma, w_gamma_ref[...])
    grad_snorm += mm_nt(grad_input.astype(BF16), w_beta_ref[...])
    grad_snorm += mm_nt(pre_gate, w_outgate_ref[...])
    single_norm, single_inv = norm_rows(single_ref[...].astype(F32))
    d_single_ref[...] = norm_back(grad_snorm, single_norm, single_inv).astype(BF16)


def swap_groups(sends):
    groups = len(sends)
    order = SLOT_ORDER[1:]
    got = []
    for bits in order:
        perm = [(index, index ^ bits) for index in range(groups)]
        got.append(lax.ppermute(sends[bits], "grp", perm))
    got = dict(zip(order, lax.optimization_barrier(got)))
    return [sends[0]] + [got[bits] for bits in range(1, groups)]


def flip_rows(values, bits, row_total):
    return lax.ppermute(values, "rows", [(index, index ^ bits) for index in range(row_total)])


def gather_rows(own, acts, row_total):
    half = own.shape[0] // 2
    near = flip_rows(own, 2, row_total)
    far = flip_rows(own, 4, row_total)
    first = flip_rows(near[:half], 4, row_total)
    second = flip_rows(far[half:], 2, row_total)
    acts[2], acts[3], acts[1], first, second = lax.optimization_barrier(
        (acts[2], acts[3], acts[1], first, second)
    )
    blocks = []
    for block in (own, near, far, first, second):
        blocks += [block, flip_rows(block, 1, row_total)]
    return blocks, acts


def swap_cores(give, give_late, row_total):
    got = flip_rows(give, 1, row_total)
    got, give_late = lax.optimization_barrier((got, give_late))
    return got, flip_rows(give_late, 1, row_total)


def scatter_rows(keep, got, got_late, row_total):
    early = got.shape[1]
    heads = early // 2
    part = heads // 2

    def add(first, count, *others):
        source, place = (got, first) if first < early else (got_late, first - early)
        total = keep[:, first : first + count].astype(F32)
        total += source[:, place : place + count].astype(F32)
        for other in others:
            total += other.astype(F32)
        return total.astype(BF16)

    near = flip_rows(add(0, heads), 2, row_total)
    far = flip_rows(add(heads, heads), 4, row_total)
    far_two = flip_rows(add(early + heads, part, near[:, part:]), 4, row_total)
    near_two = flip_rows(add(early + heads + part, part, far[:, part:]), 2, row_total)
    own = add(early, heads, jnp.concatenate([near[:, :part], far[:, :part]], axis=1))
    return own, far_two, near_two


def add_last(own, far_two, near_two):
    last = jnp.concatenate([far_two, near_two], axis=1)
    total = (own.astype(F32) + last.astype(F32)).astype(BF16)
    return [total[slot] for slot in range(total.shape[0])]


def sum_rows(mine, d_pair, row_total):
    parts = [flip_rows(mine, bits, row_total) for bits in (2, 4, 6)]
    parts, d_pair = lax.optimization_barrier((parts, d_pair))
    near, far, last = (part.astype(F32) for part in parts)
    chips = ((mine.astype(F32) + near) + (far + last)).astype(BF16)
    return chips.astype(F32) + flip_rows(chips, 1, row_total).astype(F32), d_pair


def split_heads(
    single,
    pair,
    chains,
    noised,
    w_gamma,
    w_beta,
    w_outgate,
    w_query,
    w_key,
    w_value,
    w_out,
    w_pair,
    chain_gain,
    cotangent,
    *,
    groups,
    row_total,
):
    cols, _ = single.shape
    tokens = chains.shape[0]
    width = noised.shape[2]
    head_size = width // w_pair.shape[1]
    calls = 1
    row_index = lax.axis_index("rows").reshape(1)
    group_index = lax.axis_index("grp").reshape(1)
    bias_send, stats = pair_bias(
        pair, w_pair, chain_gain, chains, group_index, row_index, groups
    )
    bias_got = swap_groups(bias_send)
    noised = noised[0]
    cotangent = cotangent[0]
    *acts_send, cond_gamma, out_gate = pl.pallas_call(
        functools.partial(
            project_kernel, groups=groups, calls=calls, head_size=head_size
        ),
        in_specs=[smem()] + [vmem()] * 10,
        out_shape=[
            jax.ShapeDtypeStruct((cols, 4 * width // groups), BF16) for _ in range(groups)
        ]
        + [
            jax.ShapeDtypeStruct((cols, width), F32),
            jax.ShapeDtypeStruct((cols, width), F32),
        ],
        scratch_shapes=[pltpu.VMEM((groups, cols, 4 * width // groups), BF16)],
        compiler_params=params(),
    )(
        group_index,
        single,
        noised,
        cotangent,
        w_gamma,
        w_beta,
        w_outgate,
        w_query,
        w_key,
        w_value,
        w_out,
    )
    bias_got, _ = lax.optimization_barrier((bias_got, acts_send))
    acts_send = [acts_send[SLOT_ORDER.index(slot)] for slot in range(groups)]
    acts = swap_groups(acts_send)
    bias_all, acts = gather_rows(jnp.stack(bias_got), acts, row_total)
    grads_send, keep, give, give_late = attention(
        group_index, row_index, acts, bias_all, head_size
    )
    got, got_late = swap_cores(give, give_late, row_total)
    got_late, grads_send[1] = lax.optimization_barrier((got_late, grads_send[1]))
    grads = swap_groups(grads_send)
    own, far_two, near_two = scatter_rows(keep, got, got_late, row_total)
    far_two, near_two, grads = lax.optimization_barrier((far_two, near_two, grads))
    dbias_own, grads = lax.optimization_barrier((add_last(own, far_two, near_two), grads))
    dbias_back = swap_groups(dbias_own)
    updated, d_part = pl.pallas_call(
        functools.partial(finish_kernel, groups=groups, calls=calls),
        in_specs=[smem()] + [vmem()] * (12 + groups * calls),
        out_shape=[
            jax.ShapeDtypeStruct((cols, width), BF16),
            jax.ShapeDtypeStruct(single.shape, BF16),
        ],
        scratch_shapes=[pltpu.VMEM((groups, calls, cols, 4 * width // (groups * calls)), BF16)],
        compiler_params=params(),
    )(
        group_index,
        single,
        noised,
        cotangent,
        cond_gamma,
        out_gate,
        w_gamma,
        w_beta,
        w_outgate,
        w_query,
        w_key,
        w_value,
        w_out,
        *grads,
    )
    d_pair = pair_back(pair, stats, dbias_back, w_pair, group_index, groups, float(tokens))
    d_single, d_pair = sum_rows(d_part, d_pair, row_total)
    return (updated[None], d_single, d_pair)


def project(acts, weight):
    return jnp.einsum("std,de->ste", acts, weight, preferred_element_type=F32)


def project_back(acts, weight):
    return jnp.einsum("ste,de->std", acts, weight, preferred_element_type=F32)


def split_keys(
    single,
    pair,
    chains,
    noised,
    w_gamma,
    w_beta,
    w_outgate,
    w_query,
    w_key,
    w_value,
    w_out,
    w_pair,
    chain_gain,
    cotangent,
):
    col_count = single.shape[0]
    row_count = pair.shape[0]
    head_count = w_pair.shape[1]
    model_width = w_query.shape[0]
    head_size = model_width // head_count
    sample_count = noised.shape[0]
    token_total = chains.shape[0]
    score_scale = 1.0 / math.sqrt(head_size)
    row_index = lax.axis_index("rows")
    group_index = lax.axis_index("grp")
    chain_rows = lax.dynamic_slice_in_dim(chains, row_index * row_count, row_count)
    chain_cols = lax.dynamic_slice_in_dim(chains, group_index * col_count, col_count)
    pair_norm, pair_inv = norm_rows(pair.astype(jnp.float32))
    projected = jnp.einsum(
        "ijc,ch->hij", pair_norm.astype(jnp.bfloat16), w_pair, preferred_element_type=jnp.float32
    )
    same_chain = (chain_rows[:, None] == chain_cols[None, :]).astype(jnp.float32)
    bias_block = (projected + chain_gain[:, None, None] * same_chain[None]).astype(jnp.bfloat16)
    bias_keys = lax.all_gather(bias_block, "rows", axis=1, tiled=True)
    single_norm, single_inv = norm_rows(single.astype(jnp.float32))
    single_b = single_norm.astype(jnp.bfloat16)
    cond_gamma = jax.nn.sigmoid(jnp.dot(single_b, w_gamma, preferred_element_type=jnp.float32))
    cond_beta = jnp.dot(single_b, w_beta, preferred_element_type=jnp.float32)
    out_gate = jax.nn.sigmoid(jnp.dot(single_b, w_outgate, preferred_element_type=jnp.float32))
    noised_f = noised.astype(jnp.float32)
    noised_norm, noised_inv = norm_rows(noised_f)
    x_b = (noised_norm * cond_gamma[None] + cond_beta[None]).astype(jnp.bfloat16)
    queries = project(x_b, w_query).astype(jnp.bfloat16)
    keys_own = project(x_b, w_key).astype(jnp.bfloat16)
    values_own = project(x_b, w_value).astype(jnp.bfloat16)
    queries_all = lax.all_gather(queries, "grp", axis=1, tiled=True)
    query_heads = queries_all.reshape(sample_count, token_total, head_count, head_size)
    key_heads = keys_own.reshape(sample_count, col_count, head_count, head_size)
    value_heads = values_own.reshape(sample_count, col_count, head_count, head_size)
    scores = (
        jnp.einsum("sihe,sjhe->shij", query_heads, key_heads, preferred_element_type=jnp.float32)
        * score_scale
        + bias_keys.astype(jnp.float32)[None]
    )
    exp_scores = jnp.exp(scores)
    exp_total = lax.psum(jnp.sum(exp_scores, axis=-1).astype(jnp.bfloat16), "grp").astype(
        jnp.float32
    )
    attn_prob = exp_scores / exp_total[..., None]
    prob_b = attn_prob.astype(jnp.bfloat16)
    attended_part = jnp.einsum(
        "shij,sjhe->sihe", prob_b, value_heads, preferred_element_type=jnp.float32
    )
    attended_part = attended_part.reshape(sample_count, token_total, model_width)
    attended = lax.psum_scatter(
        attended_part.astype(jnp.bfloat16), "grp", scatter_dimension=1, tiled=True
    )
    block_update = project(attended, w_out)
    updated = (noised_f + out_gate[None] * block_update).astype(jnp.bfloat16)
    grad_out = cotangent.astype(jnp.float32)
    gate_part = jnp.sum(grad_out * block_update, axis=0)
    grad_update = (grad_out * out_gate[None]).astype(jnp.bfloat16)
    grad_attn = project_back(grad_update, w_out).astype(jnp.bfloat16)
    grads_all = lax.all_gather(grad_attn, "grp", axis=1, tiled=True)
    grad_heads = grads_all.reshape(sample_count, token_total, head_count, head_size)
    grad_prob = jnp.einsum(
        "sihe,sjhe->shij", grad_heads, value_heads, preferred_element_type=jnp.float32
    )
    row_delta = lax.psum(
        jnp.sum(attn_prob * grad_prob, axis=-1).astype(jnp.bfloat16), "grp"
    ).astype(jnp.float32)
    grad_score = attn_prob * (grad_prob - row_delta[..., None])
    score_b = grad_score.astype(jnp.bfloat16)
    query_part = (
        jnp.einsum("shij,sjhe->sihe", score_b, key_heads, preferred_element_type=jnp.float32)
        * score_scale
    )
    query_part = query_part.reshape(sample_count, token_total, model_width)
    grad_query = lax.psum_scatter(
        query_part.astype(jnp.bfloat16), "grp", scatter_dimension=1, tiled=True
    )
    grad_key = (
        jnp.einsum("shij,sihe->sjhe", score_b, query_heads, preferred_element_type=jnp.float32)
        * score_scale
    )
    grad_value = jnp.einsum(
        "shij,sihe->sjhe", prob_b, grad_heads, preferred_element_type=jnp.float32
    )
    grad_key = grad_key.reshape(sample_count, col_count, model_width).astype(jnp.bfloat16)
    grad_value = grad_value.reshape(sample_count, col_count, model_width).astype(jnp.bfloat16)
    grad_input = (
        project_back(grad_query, w_query)
        + project_back(grad_key, w_key)
        + project_back(grad_value, w_value)
    )
    gamma_part = jnp.sum(grad_input * noised_norm, axis=0)
    beta_part = jnp.sum(grad_input, axis=0)
    gamma_sum, beta_sum, gate_sum = lax.psum((gamma_part, beta_part, gate_part), "rows")
    pre_gamma = (gamma_sum * cond_gamma * (1.0 - cond_gamma)).astype(jnp.bfloat16)
    pre_gate = (gate_sum * out_gate * (1.0 - out_gate)).astype(jnp.bfloat16)
    grad_snorm = jnp.dot(pre_gamma, w_gamma.T, preferred_element_type=jnp.float32)
    grad_snorm = grad_snorm + jnp.dot(
        beta_sum.astype(jnp.bfloat16), w_beta.T, preferred_element_type=jnp.float32
    )
    grad_snorm = grad_snorm + jnp.dot(pre_gate, w_outgate.T, preferred_element_type=jnp.float32)
    d_single = norm_back(grad_snorm, single_norm, single_inv)
    bias_part = jnp.sum(score_b, axis=0, dtype=jnp.float32)
    bias_own = lax.psum_scatter(bias_part, "rows", scatter_dimension=1, tiled=True)
    bias_grad = (bias_own * token_total).astype(jnp.bfloat16)
    grad_pairn = jnp.einsum("hij,ch->ijc", bias_grad, w_pair, preferred_element_type=jnp.float32)
    d_pair = norm_back(grad_pairn, pair_norm, pair_inv).astype(jnp.bfloat16)
    return (updated, d_single, d_pair)


def solution(mesh):
    in_specs = (
        P("grp", None),
        P("rows", "grp", None),
        P(),
        P("rows", "grp", None),
        P(),
        P(),
        P(),
        P(),
        P(),
        P(),
        P(),
        P(),
        P(),
        P("rows", "grp", None),
    )
    out_specs = (P("rows", "grp", None), P("grp", None), P("rows", "grp", None))
    groups = mesh.shape["grp"]
    row_total = mesh.shape["rows"]

    def on_device(*args):
        pair, noised, w_pair = args[1], args[3], args[11]
        fits = (
            groups == 4
            and pair.shape[0] % 32 == 0
            and pair.shape[1] % pair.shape[0] == 0
            and row_total == 8
            and noised.shape[0] == 1
            and noised.shape[1] == 192
            and w_pair.shape[1] % (2 * groups) == 0
        )
        if fits:
            return split_heads(*args, groups=groups, row_total=row_total)
        return split_keys(*args)

    return jax.shard_map(
        on_device, mesh=mesh, in_specs=in_specs, out_specs=out_specs, check_vma=False
    )
```
